128 devices in a mesh: head: 4 (over z), batch: 32 (over y, x, core).
Axes of the slice: x: 4, y: 4, z: 4, core: 2. Of those that a mesh axis runs over, the one named last changes fastest.
Arguments:
- tokens: bfloat16 [32, 2048, 1024], P('batch', 'head'), may hold values from -6 to 6
- ln_gain1: float32 [1024], replicated, may hold values from 0.5 to 1.5
- ln_bias1: float32 [1024], replicated, may hold values from -1.75 to 1.75
- w_query: bfloat16 [1024, 1024], replicated, may hold values from -0.1875 to 0.1875
- w_key: bfloat16 [1024, 1024], replicated, may hold values from -0.1875 to 0.1875
- w_value: bfloat16 [1024, 1728], replicated, may hold values from -0.1875 to 0.1875
- w_gate: bfloat16 [1024, 1728], replicated, may hold values from -0.1875 to 0.1875
- w_out: bfloat16 [1728, 1024], replicated, may hold values from -0.21875 to 0.21875
- ln_gain2: float32 [1024], replicated, may hold values from 0.5 to 1.5
- ln_bias2: float32 [1024], replicated, may hold values from -1.75 to 1.75
- w_up: bfloat16 [1024, 1728], replicated, may hold values from -0.1875 to 0.1875
- w_down: bfloat16 [1728, 1024], replicated, may hold values from -0.21875 to 0.21875
- doc_lengths: int32 [32, 6], P('batch'), may hold values from 1 to 1537, as said below
- windows: int32 [4], replicated, may hold values from 32 to 2048, as said below
- cotangent: bfloat16 [32, 2048, 1024], P('batch', 'head'), may hold values from -8 to 8
Outputs:
- mixed: bfloat16 [32, 2048, 1024], P('batch', 'head')
- grad_tokens: bfloat16 [32, 2048, 1024], P('batch', 'head')
- grad_ln_gain1: float32 [1024], P('head')
- grad_ln_bias1: float32 [1024], P('head')
- grad_query: float32 [1024, 1024], P('head')
- grad_key: float32 [1024, 1024], P('head')
- grad_value: float32 [1024, 1728], P('head')
- grad_gate: float32 [1024, 1728], P('head')
- grad_out: float32 [1728, 1024], P('head')
- grad_ln_gain2: float32 [1024], P('head')
- grad_ln_bias2: float32 [1024], P('head')
- grad_up: float32 [1024, 1728], P('head')
- grad_down: float32 [1728, 1024], P('head')
The draws below stay inside these ranges and needn't reach their ends.
Inputs may be any that keep to these rules, and one draw needn't show every extreme that they name: `doc_lengths`: each row holds the 6 document lengths of one sequence in order; they sum to 2048, and each is at least 1. `windows`: heads 2 and 3 have window 2048; heads 0 and 1 each have a window of at most 128.
All inputs are finite; a program needn't handle non-finite values.
Results may differ from the reference program's by a relative error of at most 0.028.
Values may be sent and summed in bfloat16 or wider, within the bound.
A program may use at most 192 MiB of HBM per device.

```python
import jax
import jax.numpy as jnp
from jax import lax

D = 1024
HEADS = 4
KEYH = 256
VH = 432
FF = 1728
SPAN = 512
NDOC = 6
TOK_DEV = 512
QK = 1024
VD = 1728
SEQ_LEN = 2048
SEQS = 32


def draw_doc_lengths(key, part):
    key = jax.random.fold_in(key, 11)
    row_keys = jax.random.split(key, SEQS)

    def one_row(row_key):
        first_key, second = jax.random.split(row_key)
        ordering = jax.random.permutation(first_key, TOK_DEV - 2) + 1
        cut_points = jnp.sort(ordering[:NDOC - 2]).astype(jnp.int32)
        bounds = jnp.concatenate([jnp.zeros((1,), jnp.int32), cut_points, jnp.full((1,), TOK_DEV - 1, jnp.int32)])
        short_docs = bounds[1:] - bounds[:-1]
        big_slot = jax.random.randint(second, (), 0, NDOC)
        doc_slot = jnp.arange(NDOC, dtype=jnp.int32)
        shifted = jnp.where(doc_slot < big_slot, doc_slot, doc_slot - 1)
        picked = short_docs[jnp.clip(shifted, 0, NDOC - 2)]
        return jnp.where(doc_slot == big_slot, SEQ_LEN - TOK_DEV + 1, picked).astype(jnp.int32)
    return jax.vmap(one_row)(row_keys)


def draw_windows(key, part):
    key = jax.random.fold_in(key, 23)
    first_key, second = jax.random.split(key)
    fast_heads = HEADS // 2
    fast_draws = jax.random.randint(first_key, (fast_heads,), SPAN // 16, SPAN // 4 + 1)
    exact_slot = jax.random.randint(second, (), 0, fast_heads)
    fast_windows = jnp.where(jnp.arange(fast_heads) == exact_slot, SPAN // 16, fast_draws)
    slow_windows = jnp.full((HEADS - fast_heads,), SEQ_LEN, jnp.int32)
    return jnp.concatenate([fast_windows.astype(jnp.int32), slow_windows]).astype(jnp.int32)


def spiked(drawn, own_key, source, target, shards_of, factor):
    def block_of(axis_at):
        return (jnp.arange(drawn.shape[axis_at]) // (drawn.shape[axis_at] // shards_of)).reshape((-1,) + (1,) * (drawn.ndim - 1 - axis_at))

    first = jax.random.permutation(own_key, shards_of)[block_of(target)]
    other_side = (block_of(target) + shards_of // 2) % shards_of
    return jnp.where((block_of(source) == first) | (block_of(source) == other_side), factor * drawn, drawn)


def shard_levels(stream_key, extent, shards, smallest, top_value):
    gain, own = 1.0, jax.random.fold_in(stream_key, 6)
    for dim, blocks in shards:
        steps = jnp.exp(jax.random.uniform(jax.random.fold_in(own, dim), (blocks,), jnp.float32, smallest / len(shards), top_value / len(shards)))
        gain = gain * jnp.repeat(steps, extent[dim] // blocks).reshape([-1 if axis == dim else 1 for axis in range(len(extent))])
    return gain


def normal_values(stream_key, extent, scale, most, shards=(), kind=jnp.bfloat16):
    drawn = jax.random.normal(stream_key, extent, jnp.float32) * scale
    if len(shards) > 0:
        drawn = shard_levels(stream_key, extent, shards, -0.22, 0.18) * drawn
    return jnp.clip(drawn, min=-most, max=most).astype(kind)


def gaussian_with(stream_key, dims, scale, most, cuts, heavy, kind=jnp.bfloat16):
    values = scale * jax.random.normal(stream_key, dims, jnp.float32)
    if cuts:
        values = values * shard_levels(stream_key, dims, cuts, -0.22, 0.18)
    return jnp.clip(spiked(values, jax.random.fold_in(stream_key, 3), *heavy), -most, most).astype(kind)


def setup_inputs(seed: int = 0) -> dict:
    splits = jax.random.split(jax.random.key(seed), 16)
    tokens = normal_values(splits[0], (SEQS, SEQ_LEN, D), 1.0, 6.0, ((0, 32), (1, 4)))
    ln_gain1 = jnp.clip(1.0 + 0.1 * jax.random.normal(splits[1], (D,), jnp.float32), 0.5, 1.5)
    ln_bias1 = normal_values(splits[2], (D,), 0.3, 1.75, (), jnp.float32)
    w_query = normal_values(splits[3], (D, QK), D ** -0.5, 0.1875)
    w_key = normal_values(splits[4], (D, QK), D ** -0.5, 0.1875)
    w_value = normal_values(splits[5], (D, VD), D ** -0.5, 0.1875)
    w_gate = normal_values(splits[6], (D, VD), D ** -0.5, 0.1875)
    w_out = normal_values(splits[7], (VD, D), (VD // 2) ** -0.5, 0.21875)
    ln_gain2 = jnp.clip(1.0 + 0.1 * jax.random.normal(splits[8], (D,), jnp.float32), 0.5, 1.5)
    ln_bias2 = normal_values(splits[9], (D,), 0.3, 1.75, (), jnp.float32)
    w_up = normal_values(splits[10], (D, FF), D ** -0.5, 0.1875)
    w_down = normal_values(splits[11], (FF, D), (FF // 2) ** -0.5, 0.21875)
    doc_lengths = draw_doc_lengths(jax.random.fold_in(splits[15], 71), 0)
    windows = draw_windows(jax.random.fold_in(splits[15], 71), 0)
    cotangent = gaussian_with(splits[14], (SEQS, SEQ_LEN, D), 1.0, 8.0, ((0, 32), (1, 4)), (1, 2, 4, 2.0))
    return dict(tokens=tokens, ln_gain1=ln_gain1, ln_bias1=ln_bias1, w_query=w_query, w_key=w_key, w_value=w_value, w_gate=w_gate, w_out=w_out, ln_gain2=ln_gain2, ln_bias2=ln_bias2, w_up=w_up, w_down=w_down, doc_lengths=doc_lengths, windows=windows, cotangent=cotangent)


@jax.custom_vjp
def low(v):
    return lax.optimization_barrier(v.astype(jnp.bfloat16)).astype(jnp.float32)

@jax.custom_vjp
def low_back(v):
    return v

def low_keep(v):
    return (low(v), None)

def low_pass(kept, grad):
    return (grad,)

def back_keep(v):
    return (v, None)

def back_low(kept, grad):
    return (low(grad),)
low.defvjp(low_keep, low_pass)
low_back.defvjp(back_keep, back_low)
precise = lax.Precision.HIGHEST
epsilon = 1e-05
retention_floor = 1.0

def product(left_side, right_side):
    return jnp.dot(left_side, right_side, precision=precise, preferred_element_type=jnp.float32)

def layer_norm(values, gain_row, shift_row):
    center = values - lax.optimization_barrier(jnp.mean(values, axis=-1, keepdims=True))
    spread = lax.optimization_barrier(jnp.mean(center * center, axis=-1, keepdims=True))
    return center * lax.rsqrt(spread + epsilon) * gain_row + shift_row

def rotary_tables(positions):
    half_keys = KEYH // 2
    ladder = jnp.arange(half_keys, dtype=jnp.float32)
    theta_rate = 10000.0 ** (-ladder / half_keys)
    angles = positions[:, None] * theta_rate[None, :]
    zeta_base = (2.0 * ladder + 0.4 * KEYH) / (1.4 * KEYH)
    growth = jnp.exp(positions[:, None] / 512.0 * jnp.log(zeta_base)[None, :])
    return (jnp.cos(angles)[:, None, :], jnp.sin(angles)[:, None, :], growth[:, None, :])

def rotate(values, cosine, sine_table, factor):
    half_keys = KEYH // 2
    front_half = values[..., :half_keys]
    behind = values[..., half_keys:]
    return jnp.concatenate([(front_half * cosine - behind * sine_table) * factor, (front_half * sine_table + behind * cosine) * factor], axis=-1)

def document_ids(lengths, total_rows):
    doc_ends = jnp.cumsum(lengths).astype(jnp.int32)
    places = jnp.arange(total_rows, dtype=jnp.int32)
    return lax.optimization_barrier(jnp.sum((places[:, None] >= doc_ends[None, :-1]).astype(jnp.int32), axis=1))

def decay_mask(row_ids, column_ids, row_docs, column_docs, window, log_gamma):
    offset = row_ids[:, None] - column_ids[None, :]
    inside = (offset >= 0) & (offset < window) & (row_docs[:, None] == column_docs[None, :])
    decay_value = jnp.exp(jnp.maximum(offset, 0).astype(jnp.float32) * log_gamma)
    return jnp.where(inside, decay_value, 0.0)

def forward_sequence(values, gain_one, bias_one, query_w, key_w, value_w, gate_w, out_w, gain_two, bias_two, up_w, down_w, lengths, windows):
    first_in = low(layer_norm(values, gain_one, bias_one))
    positions = jnp.arange(SEQ_LEN, dtype=jnp.float32)
    cosine, sine_table, growth = rotary_tables(positions)
    query_raw = low_back(product(first_in, query_w)).reshape(SEQ_LEN, HEADS, KEYH)
    key_raw = low_back(product(first_in, key_w)).reshape(SEQ_LEN, HEADS, KEYH)
    queries = low(low_back(rotate(query_raw, cosine, sine_table, growth)))
    keys_low = low(low_back(rotate(key_raw, cosine, sine_table, 1.0 / growth) * KEYH ** (-0.5)))
    values_low = low(low_back(product(first_in, value_w))).reshape(SEQ_LEN, HEADS, VH)
    gate_raw = low_back(product(first_in, gate_w))
    doc_ids = document_ids(lengths, SEQ_LEN)
    column_ids = jnp.arange(SEQ_LEN, dtype=jnp.int32)
    log_gamma = jnp.log(1.0 - 2.0 ** (-5.0 - jnp.arange(HEADS, dtype=jnp.float32)))

    def retain_block(block_start):
        row_ids = block_start + jnp.arange(SPAN, dtype=jnp.int32)
        row_docs = lax.dynamic_slice_in_dim(doc_ids, block_start, SPAN)
        query_block = lax.dynamic_slice_in_dim(queries, block_start, SPAN, 0)
        decay_grids = jax.vmap(decay_mask, in_axes=(None, None, None, None, 0, 0))(row_ids, column_ids, row_docs, doc_ids, windows, log_gamma)
        scores = low_back(jnp.einsum('chk,lhk->hcl', query_block, keys_low, precision=precise))
        weights = low(scores * decay_grids)
        return jnp.einsum('hcl,lhv->chv', weights, values_low, precision=precise)
    starts = jnp.arange(SEQ_LEN // SPAN, dtype=jnp.int32) * SPAN
    retained = lax.map(jax.checkpoint(retain_block), starts).reshape(SEQ_LEN, HEADS, VH)
    retained = low_back(retained)
    center = retained - lax.optimization_barrier(jnp.mean(retained, axis=-1, keepdims=True))
    spread = lax.optimization_barrier(jnp.mean(center * center, axis=-1, keepdims=True))
    normed = center * lax.rsqrt(spread + retention_floor)
    heads_low = low(low_back(normed)).reshape(SEQ_LEN, VD)
    mixed_in = low(jax.nn.silu(gate_raw) * heads_low)
    hidden = values + low_back(product(mixed_in, out_w))
    second_in = low(layer_norm(hidden, gain_two, bias_two))
    lifted = low_back(product(second_in, up_w))
    activated = low(jax.nn.gelu(lifted, approximate=False))
    return hidden + product(activated, down_w)

def reference(tokens, ln_gain1, ln_bias1, w_query, w_key, w_value, w_gate, w_out, ln_gain2, ln_bias2, w_up, w_down, doc_lengths, windows, cotangent):
    weights = tuple((element.astype(jnp.float32) for element in (ln_gain1, ln_bias1, w_query, w_key, w_value, w_gate, w_out, ln_gain2, ln_bias2, w_up, w_down)))
    inputs = tokens.astype(jnp.float32)
    cotangents = cotangent.astype(jnp.float32)

    def one_sequence(running, packed):
        values, cotangent_seq, lengths = packed

        def forward(seq_values, *params):
            return forward_sequence(seq_values, *params, lengths, windows)
        output, pullback = jax.vjp(forward, values, *weights)
        gradients = pullback(cotangent_seq)
        running = tuple((element + gradient for element, gradient in zip(running, gradients[1:])))
        return (running, (output.astype(jnp.bfloat16), gradients[0].astype(jnp.bfloat16)))
    initial = tuple((jnp.zeros_like(element) for element in weights))
    totals, (outputs, input_grads) = lax.scan(one_sequence, initial, (inputs, cotangents, doc_lengths))
    return (outputs, input_grads, totals[0], totals[1], totals[2], totals[3], totals[4], totals[5], totals[6], totals[7], totals[8], totals[9], totals[10])
```

```python
import functools

import jax
import jax.numpy as jnp
from jax import lax
from jax.experimental import pallas as pl
from jax.experimental.pallas import tpu as pltpu
from jax.sharding import PartitionSpec as P

D = 1024
HEADS = 4
KEYH = 256
VH = 432
FF = 1728
QK = 1024
VD = 1728
TOK = 512
SEQ = 2048
HALO = 128
WIDE = 1792

epsilon = 1e-05
retention_floor = 1.0
BF = jnp.bfloat16
F32 = jnp.float32
MESH = pl.DeviceIdType.MESH

ORDERS = ((0, 1, 2), (1, 2, 0), (2, 0, 1))
GATHERS = ((2, 1), (2, 1), (1, 2))


def matmul(left_side, right_side):
    return jnp.dot(left_side, right_side, preferred_element_type=F32)


def contract_rows(left_side, right_side):
    return lax.dot_general(left_side, right_side, (((0,), (0,)), ((), ())), preferred_element_type=F32)


def contract_cols(left_side, right_side):
    return lax.dot_general(left_side, right_side, (((1,), (1,)), ((), ())), preferred_element_type=F32)


def normalize(values, gain_row, shift_row):
    center = values - jnp.mean(values, axis=-1, keepdims=True)
    inverse = lax.rsqrt(jnp.mean(center * center, axis=-1, keepdims=True) + epsilon)
    scaled = center * inverse
    return (scaled * gain_row + shift_row, scaled, inverse)


def normalize_back(upstream, scaled, inverse, gain_row):
    weighted = upstream * gain_row
    inner_term = (
        weighted
        - jnp.mean(weighted, axis=-1, keepdims=True)
        - scaled * jnp.mean(weighted * scaled, axis=-1, keepdims=True)
    )
    return (inverse * inner_term, jnp.sum(upstream * scaled, axis=0), jnp.sum(upstream, axis=0))


def rotary_tables(positions):
    half_keys = KEYH // 2
    ladder = jnp.arange(half_keys, dtype=F32)
    theta_rate = 10000.0 ** (-ladder / half_keys)
    angles = positions[:, None] * theta_rate[None, :]
    zeta_base = (2.0 * ladder + 0.4 * KEYH) / (1.4 * KEYH)
    growth = jnp.exp(positions[:, None] / 512.0 * jnp.log(zeta_base)[None, :])
    return (jnp.cos(angles)[:, None, :], jnp.sin(angles)[:, None, :], growth[:, None, :])


def rotate(values, cosine, sine_table, factor):
    half_keys = KEYH // 2
    front_half = values[..., :half_keys]
    behind = values[..., half_keys:]
    return jnp.concatenate(
        [
            (front_half * cosine - behind * sine_table) * factor,
            (front_half * sine_table + behind * cosine) * factor,
        ],
        axis=-1,
    )


def rotate_back(gradient, cosine, sine_table, factor):
    half_keys = KEYH // 2
    front_half = gradient[..., :half_keys] * factor
    behind = gradient[..., half_keys:] * factor
    return jnp.concatenate(
        [front_half * cosine + behind * sine_table, behind * cosine - front_half * sine_table],
        axis=-1,
    )


def coordinates():
    z = lax.axis_index("head")
    b = lax.axis_index("batch")
    return [z, lax.div(b, 8), lax.rem(lax.div(b, 2), 4), lax.rem(b, 2)]


def shifted(at, axis, step):
    place = list(at)
    if axis == 3:
        place[3] = 1 - place[3]
    else:
        place[axis] = lax.rem(place[axis] + step, 4)
    return (place[0], (place[1] * 4 + place[2]) * 2 + place[3])


def pick(ref, axes):
    index = [slice(None)] * 3
    for axis, value in axes.items():
        index[axis] = value
    return ref.at[tuple(index)]


def landing_shapes(shape, order):
    a1, a2, a3 = order
    r, c = shape

    def without(kept):
        return tuple(kept[a] for a in (0, 1, 2) if a in kept) + (r, c)

    return [
        without({a2: 2, a3: 4}),
        without({a2: 2, a3: 4}),
        without({a2: 4, a3: 4}),
        without({a2: 4, a3: 4}),
        (2, r, c),
        (2, r, c),
        (4, r, c),
        (4, r, c),
        (3, r, c),
    ]


COPIES = 20


class Sender:
    def __init__(self, at, send_sems, recv_sems, base):
        self.at = at
        self.send_sems = send_sems
        self.recv_sems = recv_sems
        self.next_slot = base
        self.sent = []

    def send(self, source, target, axis, step):
        slot = self.next_slot
        self.next_slot += 1
        copy = pltpu.make_async_remote_copy(
            src_ref=source,
            dst_ref=target,
            send_sem=self.send_sems.at[slot],
            recv_sem=self.recv_sems.at[slot],
            device_id=shifted(self.at, axis, step),
            device_id_type=MESH,
        )
        copy.start()
        self.sent.append(copy)
        return copy

    def finish(self):
        for copy in self.sent:
            copy.wait_send()


def reduce_steps(sender, stage, lands, result, order, gather):
    at = sender.at
    a1, a2, a3 = order
    p1, p2, p3 = at[a1], at[a2], at[a3]

    def away(p, step):
        return lax.rem(p + step, 4)

    low, high = pl.ds(0, 2), pl.ds(2, 2)
    one = sender.send(pick(stage, {a1: away(p1, 2), a2: low}), lands[0], a1, 1)
    two = sender.send(pick(stage, {a1: away(p1, 2), a2: high}), lands[1], a1, 3)
    yield
    one.wait_recv()
    to_right = pick(stage, {a1: away(p1, 1), a2: low})
    to_right[...] = to_right[...] + lands[0][...]
    one = sender.send(pick(stage, {a1: away(p1, 1)}), lands[2], a1, 1)
    two.wait_recv()
    to_left = pick(stage, {a1: away(p1, 3), a2: high})
    to_left[...] = to_left[...] + lands[1][...]
    two = sender.send(pick(stage, {a1: away(p1, 3)}), lands[3], a1, 3)
    yield
    one.wait_recv()
    two.wait_recv()
    own = pick(stage, {a1: p1})
    own[...] = (own[...].astype(F32) + lands[2][...].astype(F32) + lands[3][...].astype(F32)).astype(BF)
    one = sender.send(pick(stage, {a1: p1, a2: away(p2, 2), a3: low}), lands[4], a2, 1)
    two = sender.send(pick(stage, {a1: p1, a2: away(p2, 2), a3: high}), lands[5], a2, 3)
    yield
    one.wait_recv()
    to_right = pick(stage, {a1: p1, a2: away(p2, 1), a3: low})
    to_right[...] = to_right[...] + lands[4][...]
    one = sender.send(pick(stage, {a1: p1, a2: away(p2, 1)}), lands[6], a2, 1)
    two.wait_recv()
    to_left = pick(stage, {a1: p1, a2: away(p2, 3), a3: high})
    to_left[...] = to_left[...] + lands[5][...]
    two = sender.send(pick(stage, {a1: p1, a2: away(p2, 3)}), lands[7], a2, 3)
    yield
    one.wait_recv()
    two.wait_recv()
    own = pick(stage, {a1: p1, a2: p2})
    own[...] = (own[...].astype(F32) + lands[6][...].astype(F32) + lands[7][...].astype(F32)).astype(BF)
    three = [
        sender.send(pick(stage, {a1: p1, a2: p2, a3: away(p3, step)}), lands[8].at[step - 1], a3, step)
        for step in (1, 2, 3)
    ]
    yield
    for copy in three:
        copy.wait_recv()
    total = pick(stage, {a1: p1, a2: p2, a3: p3})[...].astype(F32)
    for step in range(3):
        total = total + lands[8][step].astype(F32)
    mine = result.at[at[3], at[1], at[2]]
    mine[...] = total.astype(BF)
    g1, g2 = gather
    three = [sender.send(mine, mine, g1, step) for step in (1, 2, 3)]
    yield
    for copy in three:
        copy.wait_recv()

    def block(place, part=None):
        if g2 == 1:
            return result.at[at[3], place] if part is None else result.at[at[3], place, part]
        return result.at[at[3], :, place] if part is None else result.at[at[3], part, place]

    q = at[g2]
    one = sender.send(block(q), block(q), g2, 1)
    two = sender.send(block(q), block(q), g2, 3)
    yield
    one.wait_recv()
    three = sender.send(block(away(q, 3), low), block(away(q, 3), low), g2, 1)
    two.wait_recv()
    four = sender.send(block(away(q, 1), high), block(away(q, 1), high), g2, 3)
    yield
    three.wait_recv()
    four.wait_recv()
    whole = result.at[at[3]]
    one = sender.send(whole, whole, 3, 1)
    yield
    one.wait_recv()
    sender.finish()


def greet(at):
    barrier = pltpu.get_barrier_semaphore()
    partners = [(axis, step) for axis in (0, 1, 2) for step in (1, 2, 3)] + [(3, 1)]
    for axis, step in partners:
        pl.semaphore_signal(barrier, inc=1, device_id=shifted(at, axis, step), device_id_type=MESH)
    pl.semaphore_wait(barrier, len(partners))


def reduce_kernel(shapes, *refs):
    n = len(shapes)
    stages, results = refs[:n], refs[n : 2 * n]
    scratch = refs[2 * n :]
    send_sems, recv_sems = scratch[-2:]
    at = coordinates()
    greet(at)
    running, used = [], 0
    for i in range(n):
        count = len(landing_shapes(shapes[i], ORDERS[i % 3]))
        lands = scratch[used : used + count]
        used += count
        running.append(
            reduce_steps(
                Sender(at, send_sems, recv_sems, i * COPIES),
                stages[i],
                lands,
                results[i],
                ORDERS[i % 3],
                GATHERS[i % 3],
            )
        )
    while running:
        running = [steps for steps in running if next(steps, 0) is None]


def reduce_all(stages):
    shapes = [s.shape[3:] for s in stages]
    n = len(stages)
    scratch = []
    for i in range(n):
        scratch += [pltpu.VMEM(s, BF) for s in landing_shapes(shapes[i], ORDERS[i % 3])]
    scratch += [pltpu.SemaphoreType.DMA((n * COPIES,))] * 2
    return pl.pallas_call(
        functools.partial(reduce_kernel, shapes),
        out_shape=[jax.ShapeDtypeStruct((2, 4, 4) + tuple(s), BF) for s in shapes],
        in_specs=[pl.BlockSpec(memory_space=pltpu.VMEM)] * n,
        out_specs=[pl.BlockSpec(memory_space=pltpu.VMEM)] * n,
        scratch_shapes=scratch,
        input_output_aliases={},
        compiler_params=pltpu.CompilerParams(
            collective_id=0, has_side_effects=True, vmem_limit_bytes=56 * 2**20
        ),
        name="reduce_gradients",
    )(*stages)


U_SPLIT = (0, 10 * 128, 20 * 128, 29 * 128)
D_SPLIT = (0, 80, 144, 224)


def stage_wide(grads):
    joined = jnp.concatenate(grads, axis=1).astype(BF)
    joined = joined.reshape(4, 4, 4, 16, joined.shape[1])
    return [joined[..., U_SPLIT[i] : U_SPLIT[i + 1]] for i in range(3)]


def stage_tall(grads):
    pieces = []
    for g in grads:
        g = jnp.pad(g.astype(BF).reshape(4, VH, 512), ((0, 0), (0, 16), (0, 0)))
        pieces.append(g.reshape(4, 4, 112, 4, 128).transpose(0, 1, 3, 2, 4))
    joined = jnp.concatenate(pieces, axis=3)
    return [joined[:, :, :, D_SPLIT[i] : D_SPLIT[i + 1]] for i in range(3)]


def unstage_wide(results):
    joined = jnp.concatenate(results, axis=-1)
    return joined.reshape(2, 256, joined.shape[-1])


def unstage_tall(results):
    joined = jnp.concatenate(results, axis=3)

    def one(piece):
        piece = piece.transpose(1, 3, 0, 2, 4).reshape(448, 1024)
        return piece[:VH].astype(F32)

    return [one(joined[:, :, :, :112]), one(joined[:, :, :, 112:])]


def body(
    tokens,
    ln_gain1,
    ln_bias1,
    w_query,
    w_key,
    w_value,
    w_gate,
    w_out,
    ln_gain2,
    ln_bias2,
    w_up,
    w_down,
    doc_lengths,
    windows,
    cotangent,
):
    rank = lax.axis_index("head")
    core = lax.rem(lax.axis_index("batch"), 2)
    start = rank * TOK
    inputs = tokens[0].astype(F32)
    gained_one, scaled_one, inverse_one = normalize(inputs, ln_gain1, ln_bias1)
    first_in = gained_one.astype(BF)
    query_raw = matmul(first_in, w_query).reshape(TOK, HEADS, KEYH)
    key_raw = matmul(first_in, w_key).reshape(TOK, HEADS, KEYH)
    value_low = matmul(first_in, w_value).astype(BF)
    gate_raw = matmul(first_in, w_gate)
    places = start + jnp.arange(TOK, dtype=jnp.int32)
    cosine, sine_table, growth = rotary_tables(places.astype(F32))
    queries = rotate(query_raw, cosine, sine_table, growth).reshape(TOK, QK).astype(BF)
    keys_low = (
        (rotate(key_raw, cosine, sine_table, 1.0 / growth) * KEYH ** (-0.5)).reshape(TOK, QK).astype(BF)
    )

    ends = jnp.cumsum(doc_lengths[0])[:-1]

    def doc_of(where):
        return jnp.sum((where[:, None] >= ends[None, :]).astype(jnp.int32), axis=1)

    docs = doc_of(places)
    before = jnp.arange(HALO, dtype=jnp.int32) + start - HALO
    after = jnp.arange(HALO, dtype=jnp.int32) + start + TOK
    edge_docs = doc_of(jnp.arange(0, 5, dtype=jnp.int32) * TOK - 1)
    doc_before = edge_docs[rank]
    doc_last = edge_docs[rank + 1]

    def head_q(a, h):
        return a[:, h * KEYH : (h + 1) * KEYH]

    def head_v(a, h):
        return a[:, h * VH : (h + 1) * VH]

    def log_gamma(h):
        return jnp.log(1.0 - 2.0 ** (-5.0 - jnp.float32(h)))

    def grid(rows, cols, row_docs, col_docs, h):
        offset = rows[:, None] - cols[None, :]
        inside = (offset >= 0) & (row_docs[:, None] == col_docs[None, :]) & (cols >= 0)[None, :] & (rows < SEQ)[:, None]
        inside = inside & (offset < windows[h])
        return jnp.where(inside, jnp.exp(jnp.maximum(offset, 0).astype(F32) * log_gamma(h)), 0.0)

    def pass_z(a, step):
        pairs = [(i, i + step) for i in range(4) if 0 <= i + step < 4]
        return lax.ppermute(a, "head", pairs)

    local = jnp.arange(TOK, dtype=F32)
    keys_decayed, states = [], []
    for h in (2, 3):
        factor = jnp.where(docs == doc_last, jnp.exp((TOK - local) * log_gamma(h)), 0.0)
        keys_decayed.append(factor)
        scaled_keys = (head_q(keys_low, h).astype(F32) * factor[:, None]).astype(BF)
        states.append(contract_rows(scaled_keys, head_v(value_low, h)).astype(BF))
    states = jnp.stack(states)
    halo_k = pass_z(keys_low[TOK - HALO :, : 2 * KEYH], 1)
    halo_v = pass_z(value_low[TOK - HALO :, : 2 * VH], 1)
    chunk_decay = jnp.stack([jnp.exp(TOK * log_gamma(h)) for h in (2, 3)])[:, None, None]
    state_in = pass_z(states, 1).astype(F32)
    for far in (2, 3):
        same = (doc_before == edge_docs[jnp.maximum(rank - far + 1, 0)]).astype(F32)
        state_in = state_in + same * chunk_decay ** (far - 1) * pass_z(states, far).astype(F32)
    state_in = state_in.astype(BF)

    rows_decayed = []
    grids, weights, pieces = [], [], []
    key_side, value_side = [], []
    for h in range(4):
        k_h, v_h = head_q(keys_low, h), head_v(value_low, h)
        if h < 2:
            k_h = jnp.concatenate([halo_k[:, h * KEYH : (h + 1) * KEYH], k_h])
            v_h = jnp.concatenate([halo_v[:, h * VH : (h + 1) * VH], v_h])
            cols = jnp.concatenate([before, places])
            g = grid(places, cols, docs, jnp.concatenate([doc_of(before), docs]), h)
        else:
            g = grid(places, places, docs, docs, h)
        w = (contract_cols(head_q(queries, h), k_h) * g).astype(BF)
        piece = matmul(w, v_h)
        if h >= 2:
            factor = jnp.where(docs == doc_before, jnp.exp(local * log_gamma(h)), 0.0)
            rows_decayed.append(factor)
            piece = piece + factor[:, None] * matmul(head_q(queries, h), state_in[h - 2])
        grids.append(g)
        weights.append(w)
        key_side.append(k_h)
        value_side.append(v_h)
        pieces.append(piece)
    retained = jnp.stack(pieces, axis=1)
    center = retained - jnp.mean(retained, axis=-1, keepdims=True)
    inv_spread = lax.rsqrt(jnp.mean(center * center, axis=-1, keepdims=True) + retention_floor)
    normed = center * inv_spread
    heads_low = normed.reshape(TOK, VD).astype(BF)

    gate_act = jax.nn.silu(gate_raw)
    heads_float = heads_low.astype(F32)
    mixed_in = (gate_act * heads_float).astype(BF)
    hidden = inputs + matmul(mixed_in, w_out)
    gained_two, scaled_two, inverse_two = normalize(hidden, ln_gain2, ln_bias2)
    second_in = gained_two.astype(BF)
    lifted = matmul(second_in, w_up)
    activated, gelu_pull = jax.vjp(lambda v: jax.nn.gelu(v, approximate=False), lifted)
    activated_low = activated.astype(BF)
    result = (hidden + matmul(activated_low, w_down)).astype(BF)

    siblings = [(i, i ^ 1) for i in range(32)]

    def swap(a):
        return lax.ppermute(a, "batch", siblings)

    def my_half(a):
        if a.shape[1] == VD:
            a = jnp.pad(a, ((0, 0), (0, WIDE - VD)))
        halves = a.reshape(TOK, 2, a.shape[1] // 2)
        mine = lax.dynamic_index_in_dim(halves, core, 1, keepdims=False)
        other = lax.dynamic_index_in_dim(halves, 1 - core, 1, keepdims=False)
        return jnp.concatenate([mine, swap(other)])

    def both(a):
        return jnp.concatenate([a, swap(a)])

    upstream = cotangent[0]
    grad_down = contract_rows(both(activated_low), my_half(upstream))
    lifted_grad = gelu_pull(contract_cols(upstream, w_down))[0].astype(BF)
    grad_up = contract_rows(both(second_in), my_half(lifted_grad))
    back_two, gain_two_grad, bias_two_grad = normalize_back(
        contract_cols(lifted_grad, w_up), scaled_two, inverse_two, ln_gain2
    )
    hidden_grad = upstream.astype(F32) + back_two
    hidden_low = hidden_grad.astype(BF)
    grad_out = contract_rows(both(mixed_in), my_half(hidden_low))
    mixed_grad = contract_cols(hidden_low, w_out)
    sigmoid = jax.nn.sigmoid(gate_raw)
    heads_grad = (mixed_grad * gate_act).astype(BF)
    gate_grad = (mixed_grad * heads_float * sigmoid * (1.0 + gate_raw * (1.0 - sigmoid))).astype(BF)

    e = heads_grad.astype(F32).reshape(TOK, HEADS, VH)
    inner = e - jnp.mean(e, axis=-1, keepdims=True) - normed * jnp.mean(e * normed, axis=-1, keepdims=True)
    retained_grad = (inner * inv_spread).astype(BF).reshape(TOK, VD)

    next_q = pass_z(queries[:HALO, : 2 * KEYH], -1)
    next_g = pass_z(retained_grad[:HALO, : 2 * VH], -1)
    back_states = []
    for h in (2, 3):
        scaled_q = (head_q(queries, h).astype(F32) * rows_decayed[h - 2][:, None]).astype(BF)
        back_states.append(contract_rows(scaled_q, head_v(retained_grad, h)).astype(BF))
    back_states = jnp.stack(back_states)
    back_in = pass_z(back_states, -1).astype(F32)
    for far in (2, 3):
        same = (doc_last == edge_docs[jnp.minimum(rank + far, 4)]).astype(F32)
        back_in = back_in + same * chunk_decay ** (far - 1) * pass_z(back_states, -far).astype(F32)
    back_in = back_in.astype(BF)

    query_grads, key_grads, value_grads = [], [], []
    for h in range(4):
        g_h, q_h = head_v(retained_grad, h), head_q(queries, h)
        score_grad = (contract_cols(g_h, value_side[h]) * grids[h]).astype(BF)
        dq = matmul(score_grad, key_side[h])
        if h < 2:
            dv = contract_rows(weights[h][:, HALO:], g_h)
            dk = contract_rows(score_grad[:, HALO:], q_h)
            tail_k, tail_v = head_q(keys_low, h)[TOK - HALO :], head_v(value_low, h)[TOK - HALO :]
            nq = next_q[:, h * KEYH : (h + 1) * KEYH]
            ng = next_g[:, h * VH : (h + 1) * VH]
            far_grid = grid(after, places[TOK - HALO :], doc_of(after), docs[TOK - HALO :], h)
            far_w = (contract_cols(nq, tail_k) * far_grid).astype(BF)
            far_s = (contract_cols(ng, tail_v) * far_grid).astype(BF)
            dv = dv.at[TOK - HALO :].add(contract_rows(far_w, ng))
            dk = dk.at[TOK - HALO :].add(contract_rows(far_s, nq))
        else:
            dv = contract_rows(weights[h], g_h)
            dk = contract_rows(score_grad, q_h)
            dq = dq + rows_decayed[h - 2][:, None] * contract_cols(g_h, state_in[h - 2])
            factor = keys_decayed[h - 2][:, None]
            dv = dv + factor * matmul(head_q(keys_low, h), back_in[h - 2])
            dk = dk + factor * contract_cols(head_v(value_low, h), back_in[h - 2])
        query_grads.append(dq.astype(BF))
        key_grads.append(dk.astype(BF))
        value_grads.append(dv.astype(BF))
    query_back = jnp.stack(query_grads, axis=1).astype(F32)
    key_back = jnp.stack(key_grads, axis=1).astype(F32)
    value_back = jnp.concatenate(value_grads, axis=1)
    query_raw_grad = rotate_back(query_back, cosine, sine_table, growth).reshape(TOK, QK).astype(BF)
    key_raw_grad = (
        (rotate_back(key_back, cosine, sine_table, 1.0 / growth) * KEYH ** (-0.5)).reshape(TOK, QK).astype(BF)
    )
    both_first = both(first_in)
    grad_query = contract_rows(both_first, my_half(query_raw_grad))
    grad_key = contract_rows(both_first, my_half(key_raw_grad))
    grad_value = contract_rows(both_first, my_half(value_back))
    grad_gate = contract_rows(both_first, my_half(gate_grad))
    first_grad = (
        contract_cols(query_raw_grad, w_query)
        + contract_cols(key_raw_grad, w_key)
        + contract_cols(value_back, w_value)
        + contract_cols(gate_grad, w_gate)
    )
    back_one, gain_one_grad, bias_one_grad = normalize_back(first_grad, scaled_one, inverse_one, ln_gain1)
    input_grad = (hidden_grad + back_one).astype(BF)

    vectors = jnp.stack([gain_one_grad, bias_one_grad, gain_two_grad, bias_two_grad], axis=1)
    mine = vectors + swap(vectors.astype(BF)).astype(F32)
    lane = VD - WIDE // 2
    with_vectors = jnp.concatenate([grad_up[:, :lane], mine, grad_up[:, lane + 4 :]], axis=1)
    grad_up = jnp.where(core == 1, with_vectors, grad_up)

    wide = stage_wide([grad_up, grad_gate, grad_value, grad_query, grad_key])
    tall = stage_tall([grad_down, grad_out])
    reduced = reduce_all(wide + tall)
    wide = unstage_wide(reduced[:3])
    out_down, out_out = unstage_tall(reduced[3:])

    def across(first, width):
        return jnp.concatenate([wide[0][:, first : first + width], wide[1][:, first : first + width]], axis=1).astype(F32)

    half = WIDE // 2
    up_all = across(0, half)
    gate_all = across(half, half)
    value_all = across(2 * half, half)
    query_all = across(3 * half, 512)
    key_all = across(3 * half + 512, 512)
    return (
        result.reshape(1, TOK, D),
        input_grad.reshape(1, TOK, D),
        up_all[:, VD],
        up_all[:, VD + 1],
        query_all,
        key_all,
        value_all[:, :VD],
        gate_all[:, :VD],
        out_out,
        up_all[:, VD + 2],
        up_all[:, VD + 3],
        up_all[:, :FF],
        out_down,
    )


def solution(mesh):
    in_specs = (
        P("batch", "head", None),
        P(),
        P(),
        P(),
        P(),
        P(),
        P(),
        P(),
        P(),
        P(),
        P(),
        P(),
        P("batch", None),
        P(),
        P("batch", "head", None),
    )
    out_specs = (
        P("batch", "head", None),
        P("batch", "head", None),
        P("head"),
        P("head"),
        P("head", None),
        P("head", None),
        P("head", None),
        P("head", None),
        P("head", None),
        P("head"),
        P("head"),
        P("head", None),
        P("head", None),
    )
    return jax.shard_map(body, mesh=mesh, in_specs=in_specs, out_specs=out_specs, check_vma=False)
```

```python
import functools
import math

import jax
import jax.numpy as jnp
import numpy as np
from jax import lax
from jax.experimental import pallas as pl
from jax.experimental.pallas import tpu as pltpu
from jax.sharding import PartitionSpec as P

D = 1024
HEADS = 4
KEYH = 256
VH = 432
FF = 1728
QK = 1024
VD = 1728
TOK = 512
SEQ = 2048
HALO = 128
WIDE = 1792

epsilon = 1e-05
retention_floor = 1.0
BF = jnp.bfloat16
F32 = jnp.float32
MESH = pl.DeviceIdType.MESH


ORDERS = ((0, 1, 2), (1, 0, 2), (2, 0, 1))
GATHERS = ((1, 2), (2, 1), (1, 2))
BIG, PAIRED = 112, 128
CUTS = {BIG: ((0, 48), (48, 32), (80, 32)), PAIRED: ((0, 48), (48, 48), (96, 32))}
COPIES = 19


def coordinates():
    z = lax.axis_index("head")
    b = lax.axis_index("batch")
    return [z, lax.div(b, 8), lax.rem(lax.div(b, 2), 4), lax.rem(b, 2)]


def shifted(at, axis, step):
    place = list(at)
    if axis == 3:
        place[3] = 1 - place[3]
    else:
        place[axis] = lax.rem(place[axis] + step, 4)
    return (place[0], (place[1] * 4 + place[2]) * 2 + place[3])


def away(p, step):
    return lax.rem(p + step, 4)


LOW, HIGH = pl.ds(0, 2), pl.ds(2, 2)


def landing_shapes(r):
    return [(2, 4, r, 128)] * 2 + [(4, 4, r, 128)] * 2 + [(2, r, 128)] * 2 + [(4, r, 128)] * 2 + [(3, r, 128)]


class Part:
    def __init__(self, at, stage, lands, mine, out, rows, order, gather, sems, base, credit_in, credit_out):
        self.at, self.stage, self.out = at, stage, out
        self.first, self.count = rows
        self.lands = [land.at[..., pl.ds(0, self.count), :] for land in lands]
        self.mine = mine.at[pl.ds(0, self.count)]
        self.order, self.gather = order, gather
        self.send_sems, self.recv_sems, self.copy_sem = sems
        self.slot = base
        self.credit_in, self.credit_out = credit_in, credit_out
        self.pending = []

    def send(self, source, target, axis, step):
        copy = pltpu.make_async_remote_copy(
            src_ref=source, dst_ref=target, send_sem=self.send_sems.at[self.slot], recv_sem=self.recv_sems.at[self.slot],
            device_id=shifted(self.at, axis, step), device_id_type=MESH,
        )
        self.slot += 1
        copy.start()
        self.pending.append(copy)
        return copy

    def flush(self):
        for copy in self.pending:
            copy.wait_send()
        self.pending = []

    def pick(self, axes):
        index = [slice(None)] * 3
        for axis, value in axes.items():
            index[axis] = value
        return self.stage.at[tuple(index) + (pl.ds(self.first, self.count), slice(None))]

    def writers(self):
        a1, a2, a3 = self.order
        return [(a1, 1), (a1, 3), (a2, 1), (a2, 3), (a3, 1), (a3, 2), (a3, 3)]

    def steps(self):
        at, lands = self.at, self.lands
        a1, a2, a3 = self.order
        p1, p2, p3 = at[a1], at[a2], at[a3]
        if self.credit_in is not None:
            pl.semaphore_wait(self.credit_in, len(self.writers()))
        one = self.send(self.pick({a1: away(p1, 2), a2: LOW}), lands[0], a1, 1)
        two = self.send(self.pick({a1: away(p1, 2), a2: HIGH}), lands[1], a1, 3)
        yield
        one.wait_recv()
        there = self.pick({a1: away(p1, 1), a2: LOW})
        there[...] = there[...] + lands[0][...]
        one = self.send(self.pick({a1: away(p1, 1)}), lands[2], a1, 1)
        two.wait_recv()
        there = self.pick({a1: away(p1, 3), a2: HIGH})
        there[...] = there[...] + lands[1][...]
        two = self.send(self.pick({a1: away(p1, 3)}), lands[3], a1, 3)
        yield
        one.wait_recv()
        two.wait_recv()
        own = self.pick({a1: p1})
        own[...] = (own[...].astype(F32) + lands[2][...].astype(F32) + lands[3][...].astype(F32)).astype(BF)
        one = self.send(self.pick({a1: p1, a2: away(p2, 2), a3: LOW}), lands[4], a2, 1)
        two = self.send(self.pick({a1: p1, a2: away(p2, 2), a3: HIGH}), lands[5], a2, 3)
        yield
        one.wait_recv()
        there = self.pick({a1: p1, a2: away(p2, 1), a3: LOW})
        there[...] = there[...] + lands[4][...]
        one = self.send(self.pick({a1: p1, a2: away(p2, 1)}), lands[6], a2, 1)
        two.wait_recv()
        there = self.pick({a1: p1, a2: away(p2, 3), a3: HIGH})
        there[...] = there[...] + lands[5][...]
        two = self.send(self.pick({a1: p1, a2: away(p2, 3)}), lands[7], a2, 3)
        yield
        one.wait_recv()
        two.wait_recv()
        own = self.pick({a1: p1, a2: p2})
        own[...] = (own[...].astype(F32) + lands[6][...].astype(F32) + lands[7][...].astype(F32)).astype(BF)
        three = [self.send(self.pick({a1: p1, a2: p2, a3: away(p3, s)}), lands[8].at[s - 1], a3, s) for s in (1, 2, 3)]
        yield
        for copy in three:
            copy.wait_recv()
        total = self.pick({a1: p1, a2: p2, a3: p3})[...].astype(F32)
        for step in range(3):
            total = total + lands[8][step].astype(F32)
        self.mine[...] = total.astype(BF)
        self.flush()
        if self.credit_out is not None:
            for axis, step in self.writers():
                pl.semaphore_signal(self.credit_out, inc=1, device_id=shifted(at, axis, step), device_id_type=MESH)

        rows = pl.ds(self.first, self.count)
        g1, g2 = self.gather
        target = self.out.at[at[3], at[1], at[2], rows]
        local = pltpu.make_async_copy(self.mine, target, self.copy_sem)
        local.start()
        three = [self.send(self.mine, target, g1, step) for step in (1, 2, 3)]
        yield
        for copy in three:
            copy.wait_recv()
        local.wait()

        def block(place, part=slice(None)):
            if g2 == 1:
                return self.out.at[at[3], place, part, rows]
            return self.out.at[at[3], part, place, rows]

        q = at[g2]
        one = self.send(block(q), block(q), g2, 1)
        two = self.send(block(q), block(q), g2, 3)
        yield
        one.wait_recv()
        three = self.send(block(away(q, 3), LOW), block(away(q, 3), LOW), g2, 1)
        two.wait_recv()
        four = self.send(block(away(q, 1), HIGH), block(away(q, 1), HIGH), g2, 3)
        yield
        three.wait_recv()
        four.wait_recv()
        whole = self.out.at[at[3], :, :, rows]
        one = self.send(whole, whole, 3, 1)
        yield
        one.wait_recv()
        self.flush()


class Unit:
    RS_STEPS = 6

    def __init__(self, parts):
        self.parts = parts
        self.running = None
        self.done = 0

    def start(self):
        self.running = [part.steps() for part in self.parts]
        self.pump()

    def pump(self, times=1):
        for _ in range(times):
            if not self.running:
                return False
            self.running = [steps for steps in self.running if next(steps, 0) is None]
            self.done += 1
        return bool(self.running)

    def reduced(self):
        while self.done < self.RS_STEPS:
            self.pump()


def vector_steps(at, mine, land_core, land_z, land_y, land_x, final, sems, base):
    send_sems, recv_sems = sems
    slots = iter(range(base, base + 10))

    def send(source, target, axis, step):
        slot = next(slots)
        copy = pltpu.make_async_remote_copy(
            src_ref=source, dst_ref=target, send_sem=send_sems.at[slot], recv_sem=recv_sems.at[slot],
            device_id=shifted(at, axis, step), device_id_type=MESH,
        )
        copy.start()
        return copy

    z, y, x, _ = at
    copies = [send(mine, land_core, 3, 1)]
    yield
    copies[0].wait()
    mine[...] = mine[...] + land_core[...]
    copies = [send(mine.at[away(z, s)], land_z.at[z], 0, s) for s in (1, 2, 3)]
    land_z[z] = mine[z]
    yield
    for axis, here, land in ((1, y, land_y), (2, x, land_x)):
        for copy in copies:
            copy.wait()
        source = land_z if axis == 1 else land_y
        total = (source[0] + source[1]) + (source[2] + source[3])
        land[here] = total
        copies = [send(land.at[here], land.at[here], axis, s) for s in (1, 2, 3)]
        yield
    for copy in copies:
        copy.wait()
    final[...] = (land_x[0] + land_x[1]) + (land_x[2] + land_x[3])


def greet(at):
    barrier = pltpu.get_barrier_semaphore()
    partners = [(axis, step) for axis in (0, 1, 2) for step in (1, 2, 3)] + [(3, 1)]
    for axis, step in partners:
        pl.semaphore_signal(barrier, inc=1, device_id=shifted(at, axis, step), device_id_type=MESH)
    pl.semaphore_wait(barrier, len(partners))


LOG_GAMMA = tuple(math.log(1.0 - 2.0 ** (-5.0 - h)) for h in range(HEADS))
HALF = WIDE // 2


def rotary_constants():
    half = KEYH // 2
    ladder = np.arange(half, dtype=np.float64)
    theta = 10000.0 ** (-ladder / half)
    place = np.arange(SEQ, dtype=np.float64)[:, None]
    zeta = (2.0 * ladder + 0.4 * KEYH) / (1.4 * KEYH)
    grow = zeta[None, :] ** (place / 512.0)
    cosine, sine = np.cos(place * theta), np.sin(place * theta)
    small = KEYH ** (-0.5)
    return np.concatenate(
        [cosine * grow, sine * grow, cosine / grow * small, sine / grow * small], axis=1
    ).astype(np.float32)


def dot_nn(a, b):
    return lax.dot_general(a, b, (((1,), (0,)), ((), ())), preferred_element_type=F32)


def dot_nt(a, b):
    return lax.dot_general(a, b, (((1,), (1,)), ((), ())), preferred_element_type=F32)


def dot_tn(a, b):
    return lax.dot_general(a, b, (((0,), (0,)), ((), ())), preferred_element_type=F32)


def row_loop(total, step, work):
    def one(i, carry):
        work(pl.ds(pl.multiple_of(i * step, step), step))
        return carry

    lax.fori_loop(0, total // step, one, 0)


class Documents:
    def __init__(self, lengths_ref):
        ends = []
        total = 0
        for i in range(5):
            total = total + lengths_ref[0, i]
            ends.append(total)
        self.ends = ends

    def of(self, where):
        found = jnp.zeros(where.shape, jnp.int32) if hasattr(where, "shape") and where.shape else 0
        for end in self.ends:
            found = found + jnp.where(where >= end, 1, 0)
        return found


def column(count, first=0):
    return lax.broadcasted_iota(jnp.int32, (count, 1), 0) + first


def line(count, first=0):
    return lax.broadcasted_iota(jnp.int32, (1, count), 1) + first


def decay_block(h, rows, cols, row_first, col_first, start, docs, window):
    i, j = column(rows, row_first), line(cols, col_first)
    base = min(row_first, col_first)
    seen = (i >= j) & (docs.of(i + start) == docs.of(j + start))
    if window is not None:
        seen = seen & (i - j < window)
    if col_first < 0:
        seen = seen & (j + start >= 0)
    down = jnp.exp((i - base).astype(F32) * LOG_GAMMA[h])
    up = jnp.exp((j - base).astype(F32) * (-LOG_GAMMA[h]))
    return jnp.where(seen, down * up, 0.0)


def rotated(raw, cosine, sine):
    front, behind = raw[:, :128], raw[:, 128:]
    return jnp.concatenate([front * cosine - behind * sine, front * sine + behind * cosine], axis=1)


def forward_kernel(
    tokens_hbm, cot_hbm, gain1, bias1, gain2, bias2, lengths, windows, table_hbm,
    wq_hbm, wk_hbm, wv_hbm, wg_hbm, wo_hbm, wu_hbm, wd_hbm,
    out_result, out_first, out_second, out_mixed, out_act, out_cot, out_lhalf, out_lift,
    out_q, out_k, out_v, out_w01, out_w23, out_sin, out_heads, out_u, out_w, out_hidden, out_stats, out_qnext,
    tokens, cot, table, wq, wk, wv, wg, wo, wu, wd,
    first, queries, keys, values, wide_f32, down_grad, kept, w01, w23, state, state_land, state_in,
    heads, u_ref, w_ref, mixed, hidden, second, lift, act, stats, result,
    load_sems, save_sems, send_sems, recv_sems,
):
    at = coordinates()
    z, core = at[0], at[3]
    start = z * TOK
    loads = {}
    for slot, (name, source, target) in enumerate(
        [
            ("tokens", tokens_hbm, tokens),
            ("wk", wk_hbm, wk),
            ("table", table_hbm.at[pl.ds(pl.multiple_of(z * TOK, TOK), TOK)], table),
            ("wv", wv_hbm, wv),
            ("wq", wq_hbm, wq),
            ("wg", wg_hbm, wg),
            ("cot", cot_hbm, cot),
            ("wd", wd_hbm, wd),
            ("wo", wo_hbm, wo),
            ("wu", wu_hbm, wu),
        ]
    ):
        loads[name] = pltpu.make_async_copy(source, target, load_sems.at[slot])
        loads[name].start()
    partners = [(3, 1), (0, 1), (0, 2), (0, 3)]
    barrier = pltpu.get_barrier_semaphore()
    for axis, step in partners:
        pl.semaphore_signal(barrier, inc=1, device_id=shifted(at, axis, step), device_id_type=MESH)

    saves, sends = [], []

    def save(source, target):
        copy = pltpu.make_async_copy(source, target, save_sems.at[len(saves)])
        copy.start()
        saves.append(copy)

    def remote(source, target, axis, step):
        slot = len(sends)
        copy = pltpu.make_async_remote_copy(
            src_ref=source, dst_ref=target, send_sem=send_sems.at[slot], recv_sem=recv_sems.at[slot],
            device_id=shifted(at, axis, step), device_id_type=MESH,
        )
        sends.append(copy)
        return copy

    def share(source, target):
        save(source, target.at[core])
        remote(source, target.at[core], 3, 1).start()

    loads["tokens"].wait()

    def norm_one(rows):
        x = tokens[rows].astype(F32)
        mean = jnp.mean(x, axis=-1, keepdims=True)
        center = x - mean
        inverse = lax.rsqrt(jnp.mean(center * center, axis=-1, keepdims=True) + epsilon)
        first[rows] = (center * inverse * gain1[...] + bias1[...]).astype(BF)
        stats[rows, 0:1] = mean
        stats[rows, 1:2] = inverse

    row_loop(TOK, 32, norm_one)
    pl.semaphore_wait(barrier, len(partners))
    share(first, out_first)

    docs = Documents(lengths)
    doc_before = docs.of(start - 1)
    doc_last = docs.of(start + TOK - 1)
    place = column(TOK)
    doc_rows = docs.of(place + start)

    loads["wk"].wait()
    loads["table"].wait()
    for h in range(HEADS):
        raw = dot_nn(first[...], wk[:, h * KEYH : (h + 1) * KEYH])
        keys[HALO:, h * KEYH : (h + 1) * KEYH] = rotated(raw, table[:, 256:384], table[:, 384:512]).astype(BF)
    loads["wv"].wait()
    for h in range(HEADS):
        values[h, HALO:] = dot_nt(first[...], wv[h * VH : (h + 1) * VH]).astype(BF)

    k_halo = remote(keys.at[pl.ds(TOK, HALO), pl.ds(0, 2 * KEYH)], keys.at[pl.ds(0, HALO), pl.ds(0, 2 * KEYH)], 0, 1)
    v_halo = remote(values.at[pl.ds(0, 2), pl.ds(TOK, HALO)], values.at[pl.ds(0, 2), pl.ds(0, HALO)], 0, 1)

    @pl.when(z < 3)
    def _():
        k_halo.start()
        v_halo.start()

    @pl.when(z == 0)
    def _():
        keys[0:HALO, 0 : 2 * KEYH] = jnp.zeros((HALO, 2 * KEYH), BF)
        values[0:2, 0:HALO] = jnp.zeros((2, HALO, VH), BF)

    for h in (2, 3):
        factor = jnp.where(doc_rows == doc_last, jnp.exp((TOK - place).astype(F32) * LOG_GAMMA[h]), 0.0)
        scaled = (keys[HALO:, h * KEYH : (h + 1) * KEYH].astype(F32) * factor).astype(BF)
        state[h - 2] = dot_tn(scaled, values[h, HALO:]).astype(BF)
    passing = []
    for far in (1, 2, 3):
        copy = remote(state, state_land.at[far - 1], 0, far)
        passing.append(copy)

        @pl.when(z + far < 4)
        def _():
            copy.start()

        @pl.when(z < far)
        def _():
            state_land[far - 1] = jnp.zeros((2, KEYH, VH), BF)

    loads["wq"].wait()
    for h in range(HEADS):
        raw = dot_nn(first[...], wq[:, h * KEYH : (h + 1) * KEYH])
        queries[:, h * KEYH : (h + 1) * KEYH] = rotated(raw, table[:, 0:128], table[:, 128:256]).astype(BF)
    save(queries, out_q)
    q_halo = remote(queries.at[pl.ds(0, HALO), pl.ds(0, 2 * KEYH)], out_qnext, 0, 3)

    @pl.when(z > 0)
    def _():
        q_halo.start()

    loads["wg"].wait()
    wide_f32[...] = dot_nt(first[...], wg[...])
    loads["cot"].wait()
    save(cot.at[:, pl.ds(pl.multiple_of(core * 512, 512), 512)], out_cot.at[core])
    remote(cot.at[:, pl.ds(pl.multiple_of((1 - core) * 512, 512), 512)], out_cot.at[core], 3, 1).start()
    loads["wd"].wait()
    down_grad[...] = dot_nt(cot[...], wd[...])

    for h in (2, 3):
        for b in (0, 1):
            rows, cols = slice(256 * b, 256 * b + 256), 256 * b + 256
            q_h = queries[rows, h * KEYH : (h + 1) * KEYH]
            scores = dot_nt(q_h, keys[HALO : HALO + cols, h * KEYH : (h + 1) * KEYH])
            weight = (scores * decay_block(h, 256, cols, 256 * b, 0, start, docs, None)).astype(BF)
            w23[h - 2, rows, 0:cols] = weight
            kept[h, rows] = dot_nn(weight, values[h, HALO : HALO + cols])

    @pl.when(z > 0)
    def _():
        k_halo.wait_recv()
        v_halo.wait_recv()

    save(keys, out_k)
    save(values, out_v)
    for h in (0, 1):
        for b in (0, 1):
            rows = slice(256 * b, 256 * b + 256)
            q_h = queries[rows, h * KEYH : (h + 1) * KEYH]
            scores = dot_nt(q_h, keys[256 * b : 256 * b + 384, h * KEYH : (h + 1) * KEYH])
            decay = decay_block(h, 256, 384, 256 * b, 256 * b - HALO, start, docs, windows[0, h])
            weight = (scores * decay).astype(BF)
            w01[h, b] = weight
            kept[h, rows] = dot_nn(weight, values[h, 256 * b : 256 * b + 384])
    save(w01, out_w01)
    save(w23, out_w23)

    for far in (1, 2, 3):

        @pl.when(z >= far)
        def _():
            passing[far - 1].wait_recv()

    for h in (2, 3):
        total = state_land[0, h - 2].astype(F32)
        for far in (2, 3):
            same = docs.of(start - (far - 1) * TOK - 1) == doc_before
            total = total + state_land[far - 1, h - 2].astype(F32) * jnp.where(
                same, math.exp(LOG_GAMMA[h] * TOK * (far - 1)), 0.0
            )
        state_in[h - 2] = total.astype(BF)
        factor = jnp.where(doc_rows == doc_before, jnp.exp(place.astype(F32) * LOG_GAMMA[h]), 0.0)
        kept[h] = kept[h] + factor * dot_nn(queries[:, h * KEYH : (h + 1) * KEYH], state_in[h - 2])
    save(state_in, out_sin)

    def mix(rows):
        parts = []
        for h in range(HEADS):
            x = kept[h, rows]
            center = x - jnp.mean(x, axis=-1, keepdims=True)
            inverse = lax.rsqrt(jnp.mean(center * center, axis=-1, keepdims=True) + retention_floor)
            stats[rows, 4 + h : 5 + h] = inverse
            parts.append(center * inverse)
        low = jnp.concatenate(parts, axis=1).astype(BF)
        heads[rows] = low
        low = low.astype(F32)
        gate = wide_f32[rows]
        sigma = 1.0 / (1.0 + jnp.exp(-gate))
        swish = gate * sigma
        u_ref[rows, 0:VD] = swish.astype(BF)
        w_ref[rows, 0:VD] = (low * (sigma * (1.0 + gate * (1.0 - sigma)))).astype(BF)
        mixed[rows] = (swish * low).astype(BF)

    row_loop(TOK, 32, mix)
    share(mixed, out_mixed)
    save(heads, out_heads)
    save(u_ref, out_u)
    save(w_ref, out_w)

    loads["wo"].wait()
    hidden[...] = dot_nn(mixed[...], wo[...])

    def norm_two(rows):
        x = hidden[rows] + tokens[rows].astype(F32)
        hidden[rows] = x
        mean = jnp.mean(x, axis=-1, keepdims=True)
        center = x - mean
        inverse = lax.rsqrt(jnp.mean(center * center, axis=-1, keepdims=True) + epsilon)
        second[rows] = (center * inverse * gain2[...] + bias2[...]).astype(BF)
        stats[rows, 2:3] = mean
        stats[rows, 3:4] = inverse

    row_loop(TOK, 32, norm_two)
    share(second, out_second)
    save(hidden, out_hidden)
    save(stats, out_stats)

    loads["wu"].wait()
    for first_col in range(0, FF, 256):
        width = min(256, FF - first_col)
        cols = slice(first_col, first_col + width)
        wide_f32[:, cols] = dot_nt(second[...], wu[cols])

    def activate(rows):
        x = wide_f32[rows]
        phi = 0.5 * (1.0 + lax.erf(x * math.sqrt(0.5)))
        slope = phi + x * jnp.exp(-0.5 * x * x) * (1.0 / math.sqrt(2.0 * math.pi))
        act[rows] = (x * phi).astype(BF)
        grad = (down_grad[rows] * slope).astype(BF)
        lift[rows] = jnp.concatenate([grad, jnp.zeros((grad.shape[0], WIDE - FF), BF)], axis=1)

    row_loop(TOK, 32, activate)
    share(act, out_act)
    save(lift, out_lift)
    save(lift.at[:, pl.ds(pl.multiple_of(core * HALF, HALF), HALF)], out_lhalf.at[core])
    remote(lift.at[:, pl.ds(pl.multiple_of((1 - core) * HALF, HALF), HALF)], out_lhalf.at[core], 3, 1).start()
    result[...] = (hidden[...] + dot_nn(act[...], wd[...])).astype(BF)
    save(result, out_result)

    def conditional(copy):
        return any(copy is other for other in [k_halo, v_halo, q_halo] + passing)

    for copy in sends:
        if not conditional(copy):
            copy.wait()

    @pl.when(z > 0)
    def _():
        q_halo.wait_send()

    @pl.when(z < 3)
    def _():
        q_halo.wait_recv()
        k_halo.wait_send()
        v_halo.wait_send()

    for far in (1, 2, 3):

        @pl.when(z + far < 4)
        def _():
            passing[far - 1].wait_send()

    for copy in saves:
        copy.wait()


def forward(tokens, cot, gain1, bias1, gain2, bias2, lengths, windows, table, wq, wk, wv, wg, wo, wu, wd):
    vmem = pl.BlockSpec(memory_space=pltpu.VMEM)
    smem = pl.BlockSpec(memory_space=pltpu.SMEM)
    anywhere = pl.BlockSpec(memory_space=pl.ANY)
    shape = jax.ShapeDtypeStruct
    outs = [
        shape((TOK, D), BF), shape((2, TOK, D), BF), shape((2, TOK, D), BF), shape((2, TOK, VD), BF), shape((2, TOK, FF), BF),
        shape((2, TOK, 512), BF), shape((2, TOK, HALF), BF), shape((TOK, WIDE), BF),
        shape((TOK, QK), BF), shape((HALO + TOK, QK), BF), shape((HEADS, HALO + TOK, VH), BF),
        shape((2, 2, 256, 384), BF), shape((2, TOK, TOK), BF), shape((2, KEYH, VH), BF),
        shape((TOK, VD), BF), shape((TOK, WIDE), BF), shape((TOK, WIDE), BF), shape((TOK, D), F32), shape((TOK, 128), F32),
        shape((HALO, 2 * KEYH), BF),
    ]
    scratch = [
        pltpu.VMEM((TOK, D), BF), pltpu.VMEM((TOK, D), BF), pltpu.VMEM((TOK, 512), F32),
        pltpu.VMEM((D, QK), BF), pltpu.VMEM((D, QK), BF), pltpu.VMEM((VD, D), BF), pltpu.VMEM((VD, D), BF),
        pltpu.VMEM((VD, D), BF), pltpu.VMEM((FF, D), BF), pltpu.VMEM((FF, D), BF),
        pltpu.VMEM((TOK, D), BF), pltpu.VMEM((TOK, QK), BF), pltpu.VMEM((HALO + TOK, QK), BF),
        pltpu.VMEM((HEADS, HALO + TOK, VH), BF), pltpu.VMEM((TOK, VD), F32), pltpu.VMEM((TOK, FF), F32),
        pltpu.VMEM((HEADS, TOK, VH), F32), pltpu.VMEM((2, 2, 256, 384), BF), pltpu.VMEM((2, TOK, TOK), BF),
        pltpu.VMEM((2, KEYH, VH), BF), pltpu.VMEM((3, 2, KEYH, VH), BF), pltpu.VMEM((2, KEYH, VH), BF),
        pltpu.VMEM((TOK, VD), BF), pltpu.VMEM((TOK, WIDE), BF), pltpu.VMEM((TOK, WIDE), BF), pltpu.VMEM((TOK, VD), BF),
        pltpu.VMEM((TOK, D), F32), pltpu.VMEM((TOK, D), BF), pltpu.VMEM((TOK, WIDE), BF), pltpu.VMEM((TOK, FF), BF),
        pltpu.VMEM((TOK, 128), F32), pltpu.VMEM((TOK, D), BF),
        pltpu.SemaphoreType.DMA((10,)), pltpu.SemaphoreType.DMA((20,)),
        pltpu.SemaphoreType.DMA((16,)), pltpu.SemaphoreType.DMA((16,)),
    ]
    return pl.pallas_call(
        forward_kernel,
        out_shape=outs,
        in_specs=[anywhere] * 2 + [vmem] * 4 + [smem] * 2 + [anywhere] * 8,
        out_specs=[anywhere] * len(outs),
        scratch_shapes=scratch,
        compiler_params=pltpu.CompilerParams(collective_id=1, has_side_effects=True, vmem_limit_bytes=62 * 2**20),
        cost_estimate=pl.CostEstimate(flops=14 * 10**9, bytes_accessed=50 * 10**6, transcendentals=2 * 10**6),
        name="forward",
    )(
        tokens, cot, gain1.reshape(1, D), bias1.reshape(1, D), gain2.reshape(1, D), bias2.reshape(1, D),
        lengths, windows.reshape(1, HEADS), table, wq, wk, wv.T, wg.T, wo, wu.T, wd,
    )


UNITS = ("down", "up", "out", "gate", "value", "qk")
UNIT_ROWS = {"down": BIG, "up": BIG, "out": BIG, "gate": BIG, "value": BIG, "qk": PAIRED}
UNIT_SET = {"down": 0, "up": 1, "out": 2, "gate": 0, "value": 1, "qk": 2}
SET_ROWS = (BIG, BIG, PAIRED)
PART_ROWS = {BIG: (48, 32, 32), PAIRED: (48, 48, 32)}


def stage_rows(stage, result, first_x):
    for z in range(4):
        for y in range(4):
            n = min(BIG, VH - BIG * y)
            for i in range(result.shape[1] // 128):
                piece = result[VH * z + BIG * y : VH * z + BIG * y + n, 128 * i : 128 * i + 128].astype(BF)
                stage[z, y, first_x + i, 0:n] = piece
                if n < BIG:
                    stage[z, y, first_x + i, n:BIG] = jnp.zeros((BIG - n, 128), BF)


def stage_columns(stage, result, first_z):
    for i in range(result.shape[1] // 128):
        z, xc = first_z + i // 2, i % 2
        for y in range(4):
            for xr in range(2):
                first = 224 * y + BIG * xr
                stage[z, y, 2 * xr + xc, 0:BIG] = result[first : first + BIG, 128 * i : 128 * i + 128].astype(BF)


def stage_square(stage, result, first_row):
    for z in range(4):
        for y in range(4):
            for x in range(4):
                piece = result[256 * z + 64 * y : 256 * z + 64 * y + 64, 128 * x : 128 * x + 128].astype(BF)
                stage[z, y, x, first_row : first_row + 64] = piece


def fold(rows):
    return jnp.sum(rows.reshape(rows.shape[0] // 8, 8, rows.shape[1]), axis=0)


def unrotated(grad, cosine, sine):
    grad = grad.astype(BF).astype(F32)
    front, behind = grad[:, :128], grad[:, 128:]
    return jnp.concatenate([front * cosine + behind * sine, behind * cosine - front * sine], axis=1).astype(BF)


def backward_kernel(
    act_hbm, coth_hbm, lhalf_hbm, second_hbm, first_hbm, mixed_hbm, lift_hbm, cot_hbm, hidden_hbm, stats_hbm,
    u_hbm, w_hbm, heads_hbm, q_hbm, k_hbm, v_hbm, w01_hbm, w23_hbm, sin_hbm, qnext_hbm, tokens_hbm, table_hbm,
    wq_hbm, wk_hbm, wv_hbm, wg_hbm, wo_hbm, wu_hbm, gain1, gain2, lengths, windows,
    out_tokens, out_vec, out_down, out_up, out_out, out_gate, out_value, out_qk,
    x1, x2, x3, y1, ch, wide, cot, heads, u_ref, w_ref, queries, keys, values, w01, w23, state_in, back_in,
    back_state, back_land, rgrad, hidden, wf, wu, wo, table, stats, qnext, gnext, vec_rows,
    vec, vec_core, vec_z, vec_y, vec_x, vec_out,
    stage0, stage1, stage2, *rest,
):
    lands = [[rest[27 * s + 9 * p : 27 * s + 9 * p + 9] for p in range(3)] for s in range(3)]
    rest = rest[81:]
    mines = rest[0:18]
    load_sems, save_sems, pair_send, pair_recv, z_send, z_recv, vec_send, vec_recv = rest[18:26]
    unit_send, unit_recv, unit_copy, credits, pair_credit = rest[26:]
    stages = (stage0, stage1, stage2)
    at = coordinates()
    z, core = at[0], at[3]
    start = z * TOK

    loading = {}

    def load(name, source, target):
        copy = pltpu.make_async_copy(source, target, load_sems.at[len(loading)])
        copy.start()
        loading[name] = copy

    def ready(*names):
        for name in names:
            loading[name].wait()

    load("act", act_hbm, x1)
    load("coth", coth_hbm, ch)
    load("lhalf", lhalf_hbm, y1)
    load("second", second_hbm, x2)
    load("lift", lift_hbm, wide)
    load("wu", wu_hbm, wu)
    greet(at)

    outs = dict(zip(UNITS, (out_down, out_up, out_out, out_gate, out_value, out_qk)))
    units = {}
    for n, name in enumerate(UNITS):
        s, parts = UNIT_SET[name], []
        for p in range(3):
            slot = 3 * n + p
            parts.append(
                Part(
                    at, stages[s], lands[s][p], mines[slot], outs[name], CUTS[UNIT_ROWS[name]][p], ORDERS[p], GATHERS[p],
                    (unit_send, unit_recv, unit_copy.at[slot]), slot * COPIES,
                    credits.at[slot - 9] if n >= 3 else None, credits.at[slot] if n < 3 else None,
                )
            )
        units[name] = Unit(parts)
    down, up, out, gate, value, qk = (units[name] for name in UNITS)

    pairs = []

    def to_sibling(source, target):
        copy = pltpu.make_async_remote_copy(
            src_ref=source, dst_ref=target, send_sem=pair_send.at[len(pairs)], recv_sem=pair_recv.at[len(pairs)],
            device_id=shifted(at, 3, 1), device_id_type=MESH,
        )
        copy.start()
        pairs.append(copy)
        return copy

    local_copies = []

    def halves(source, width, landing, lane):
        rows = pl.ds(pl.multiple_of(core * TOK, TOK), TOK)
        lanes = pl.ds(lane, width)
        mine = source.at[:, pl.ds(pl.multiple_of(core * width, width), width)]
        other = source.at[:, pl.ds(pl.multiple_of((1 - core) * width, width), width)]
        remote = to_sibling(other, landing.at[rows, lanes])
        local = pltpu.make_async_copy(mine, landing.at[rows, lanes], save_sems.at[len(local_copies)])
        local.start()
        local_copies.append(local)
        return remote, local

    def arrived(pair):
        pair[0].wait()
        pair[1].wait()

    def tell_sibling(slot):
        pl.semaphore_signal(pair_credit.at[slot], inc=1, device_id=shifted(at, 3, 1), device_id_type=MESH)

    ready("act", "coth")
    load("cot", cot_hbm, cot)
    load("hidden", hidden_hbm, hidden)
    load("stats", stats_hbm, stats)
    load("wo", wo_hbm, wo)
    for half in (0, 1):
        stage_rows(stage0, dot_tn(x1[...], ch[:, 256 * half : 256 * half + 256]), 2 * half)
    down.start()
    load("mixed", mixed_hbm, x1)
    load("u", u_hbm, u_ref)
    load("w", w_hbm, w_ref)
    load("heads", heads_hbm, heads)
    tell_sibling(0)

    ready("lhalf", "second")
    for half in (0, 1):
        stage_columns(stage1, dot_tn(y1[...], x2[:, 512 * half : 512 * half + 512]), 2 * half)
    up.start()
    tell_sibling(1)
    load("first", first_hbm, x3)
    load("q", q_hbm, queries)
    load("k", k_hbm, keys)
    load("v", v_hbm, values)
    load("w01", w01_hbm, w01)
    load("w23", w23_hbm, w23)
    load("sin", sin_hbm, state_in)
    load("qnext", qnext_hbm, qnext)
    load("table", table_hbm.at[pl.ds(pl.multiple_of(z * TOK, TOK), TOK)], table)

    ready("lift", "wu")
    wf[:, 0:D] = dot_nn(wide[:, 0:FF], wu[...])
    load("wg", wg_hbm, wu)
    down.pump()
    ready("cot", "hidden", "stats")

    def back_two(i, sums):
        rows = pl.ds(pl.multiple_of(i * 32, 32), 32)
        grad = wf[rows, 0:D]
        inverse = stats[rows, 3:4]
        scaled = (hidden[rows] - stats[rows, 2:3]) * inverse
        e = grad * gain2[...]
        inner = e - jnp.mean(e, axis=-1, keepdims=True) - scaled * jnp.mean(e * scaled, axis=-1, keepdims=True)
        total = cot[rows].astype(F32) + inverse * inner
        hidden[rows] = total
        cot[rows] = total.astype(BF)
        return (sums[0] + fold(grad * scaled), sums[1] + fold(grad))

    zero = jnp.zeros((8, D), F32)
    gain_sum, bias_sum = lax.fori_loop(0, TOK // 32, back_two, (zero, zero))
    vec_rows[2:3] = jnp.sum(gain_sum, axis=0, keepdims=True)
    vec_rows[3:4] = jnp.sum(bias_sum, axis=0, keepdims=True)
    pl.semaphore_wait(pair_credit.at[0], 1)
    low_pair = halves(cot, 512, ch, 0)
    up.pump()

    ready("wo")
    wf[:, 0:VD] = dot_nt(cot[...], wo[...])
    load("wv", wv_hbm, wo)
    down.pump()
    ready("u", "w", "heads")

    def back_mix(rows):
        grad = wf[rows, 0:VD]
        low = heads[rows].astype(F32)
        gated = (grad * w_ref[rows, 0:VD].astype(F32)).astype(BF)
        wide[rows] = jnp.concatenate([gated, jnp.zeros((32, WIDE - VD), BF)], axis=1)
        e_all = (grad * u_ref[rows, 0:VD].astype(F32)).astype(BF).astype(F32)
        for h in range(HEADS):
            e = e_all[:, h * VH : (h + 1) * VH]
            c = low[:, h * VH : (h + 1) * VH]
            inner = e - jnp.mean(e, axis=-1, keepdims=True) - c * jnp.mean(e * c, axis=-1, keepdims=True)
            rgrad[h, rows] = (inner * stats[rows, 4 + h : 5 + h]).astype(BF)

    row_loop(TOK, 32, back_mix)
    pl.semaphore_wait(pair_credit.at[1], 1)
    gate_pair = halves(wide, HALF, y1, 0)
    up.pump()

    ready("qnext", "q")

    def earlier(source, target, slot, far):
        return pltpu.make_async_remote_copy(
            src_ref=source, dst_ref=target, send_sem=z_send.at[slot], recv_sem=z_recv.at[slot],
            device_id=shifted(at, 0, 4 - far), device_id_type=MESH,
        )

    g_halo = earlier(rgrad.at[pl.ds(0, 2), pl.ds(0, HALO)], gnext, 0, 1)

    @pl.when(z > 0)
    def _():
        g_halo.start()

    @pl.when(z == 3)
    def _():
        gnext[...] = jnp.zeros((2, HALO, VH), BF)
        qnext[...] = jnp.zeros((HALO, 2 * KEYH), BF)

    docs = Documents(lengths)
    doc_before = docs.of(start - 1)
    doc_last = docs.of(start + TOK - 1)
    place = column(TOK)
    doc_rows = docs.of(place + start)

    def row_factor(h):
        return jnp.where(doc_rows == doc_before, jnp.exp(place.astype(F32) * LOG_GAMMA[h]), 0.0)

    for h in (2, 3):
        scaled = (queries[:, h * KEYH : (h + 1) * KEYH].astype(F32) * row_factor(h)).astype(BF)
        back_state[h - 2] = dot_tn(scaled, rgrad[h]).astype(BF)
    passing = []
    for far in (1, 2, 3):
        copy = earlier(back_state, back_land.at[far - 1], far, far)
        passing.append(copy)

        @pl.when(z >= far)
        def _():
            copy.start()

        @pl.when(z + far > 3)
        def _():
            back_land[far - 1] = jnp.zeros((2, KEYH, VH), BF)

    ready("mixed")
    arrived(low_pair)
    for half in (0, 1):
        stage_rows(stage2, dot_tn(x1[...], ch[:, 256 * half : 256 * half + 256]), 2 * half)
    out.start()
    tell_sibling(2)
    down.pump()

    ready("first")
    arrived(gate_pair)
    down.reduced()
    for half in (0, 1):
        stage_columns(stage0, dot_tn(y1[...], x3[:, 512 * half : 512 * half + 512]), 2 * half)
    gate.start()
    up.pump()
    out.pump()

    ready("k", "v", "w01", "w23", "sin", "table")

    def finish_query(h, grad):
        w_ref[:, h * KEYH : (h + 1) * KEYH] = unrotated(grad, table[:, 0:128], table[:, 128:256])

    def finish_key(h, grad):
        cot[:, h * KEYH : (h + 1) * KEYH] = unrotated(grad, table[:, 256:384], table[:, 384:512])

    ready_far = False
    for h in (2, 3):
        k_h = lambda rows: keys[rows, h * KEYH : (h + 1) * KEYH]
        q_h = lambda rows: queries[rows, h * KEYH : (h + 1) * KEYH]
        score = []
        for b in (0, 1):
            rows, cols = slice(256 * b, 256 * b + 256), 256 * b + 256
            grad = dot_nt(rgrad[h, rows], values[h, HALO : HALO + cols])
            grad = (grad * decay_block(h, 256, cols, 256 * b, 0, start, docs, None)).astype(BF)
            score.append(grad)
        query = jnp.concatenate(
            [dot_nn(score[b], k_h(slice(HALO, HALO + 256 * b + 256))) for b in (0, 1)], axis=0
        )
        query = query + row_factor(h) * dot_nt(rgrad[h], state_in[h - 2])
        finish_query(h, query)
        late = dot_tn(score[1], q_h(slice(256, 512)))
        early = dot_tn(score[0], q_h(slice(0, 256)))
        key = jnp.concatenate([early + late[:256], late[256:]], axis=0)
        late = dot_tn(w23[h - 2, 256:512], rgrad[h, 256:512])
        early = dot_tn(w23[h - 2, 0:256, 0:256], rgrad[h, 0:256])
        grad_v = jnp.concatenate([early + late[:256], late[256:]], axis=0)
        if not ready_far:
            ready_far = True
            for far in (1, 2, 3):

                @pl.when(z + far < 4)
                def _():
                    passing[far - 1].wait_recv()

        total = back_land[0, h - 2].astype(F32)
        for far in (2, 3):
            same = docs.of(start + far * TOK - 1) == doc_last
            total = total + back_land[far - 1, h - 2].astype(F32) * jnp.where(
                same, math.exp(LOG_GAMMA[h] * TOK * (far - 1)), 0.0
            )
        back_in[h - 2] = total.astype(BF)
        factor = jnp.where(doc_rows == doc_last, jnp.exp((TOK - place).astype(F32) * LOG_GAMMA[h]), 0.0)
        key = key + factor * dot_nt(values[h, HALO:], back_in[h - 2])
        finish_key(h, key)
        grad_v = grad_v + factor * dot_nn(k_h(slice(HALO, HALO + TOK)), back_in[h - 2])
        wf[:, h * VH : (h + 1) * VH] = grad_v
    up.pump()
    out.pump()

    @pl.when(z < 3)
    def _():
        g_halo.wait_recv()

    tail = slice(TOK, TOK + HALO)
    for h in (0, 1):
        cols_h = slice(h * KEYH, (h + 1) * KEYH)
        parts_q, parts_k, parts_v = [], [], []
        for b in (0, 1):
            rows, ext = slice(256 * b, 256 * b + 256), slice(256 * b, 256 * b + 384)
            grad = dot_nt(rgrad[h, rows], values[h, ext])
            decay = decay_block(h, 256, 384, 256 * b, 256 * b - HALO, start, docs, windows[0, h])
            grad = (grad * decay).astype(BF)
            parts_q.append(dot_nn(grad, keys[ext, cols_h]))
            parts_k.append(dot_tn(grad, queries[rows, cols_h]))
            parts_v.append(dot_tn(w01[h, b], rgrad[h, rows]))
        decay = decay_block(h, HALO, HALO, TOK, TOK - HALO, start, docs, windows[0, h])
        far_w = (dot_nt(qnext[:, cols_h], keys[tail, cols_h]) * decay).astype(BF)
        far_s = (dot_nt(gnext[h], values[h, tail]) * decay).astype(BF)

        def joined(parts, far):
            return jnp.concatenate(
                [
                    parts[0][HALO : 2 * HALO],
                    parts[0][2 * HALO :] + parts[1][:HALO],
                    parts[1][HALO : 2 * HALO],
                    parts[1][2 * HALO :] + far,
                ],
                axis=0,
            )

        finish_query(h, jnp.concatenate(parts_q, axis=0))
        finish_key(h, joined(parts_k, dot_tn(far_s, qnext[:, cols_h])))
        wf[:, h * VH : (h + 1) * VH] = joined(parts_v, dot_tn(far_w, gnext[h]))

    query_pair = halves(w_ref, 512, x2, 0)
    key_pair = halves(cot, 512, x2, 512)

    def store_value(rows):
        u_ref[rows] = jnp.concatenate([wf[rows, 0:VD].astype(BF), jnp.zeros((32, WIDE - VD), BF)], axis=1)

    row_loop(TOK, 32, store_value)
    pl.semaphore_wait(pair_credit.at[2], 1)
    value_pair = halves(u_ref, HALF, x1, 0)
    load("tokens", tokens_hbm, keys.at[pl.ds(0, TOK)])
    gate.pump()
    out.pump()

    ready("wg")
    wf[:, 0:D] = dot_nn(wide[:, 0:VD], wu[...])
    up.reduced()
    arrived(value_pair)
    for half in (0, 1):
        stage_columns(stage1, dot_tn(x1[:, 0:HALF], x3[:, 512 * half : 512 * half + 512]), 2 * half)
    value.start()
    gate.pump()
    arrived(query_pair)
    arrived(key_pair)
    out.reduced()
    stage_square(stage2, dot_tn(x3[...], x2[:, 0:512]), 0)
    stage_square(stage2, dot_tn(x3[...], x2[:, 512:1024]), 64)
    qk.start()
    load("wq", wq_hbm, x2)
    load("wk", wk_hbm, x3)
    gate.pump()
    down.pump()
    ready("wv")
    wf[:, 0:D] = wf[:, 0:D] + dot_nn(u_ref[:, 0:VD], wo[...])
    value.pump()
    up.pump()
    ready("wq", "wk")
    wf[:, 0:D] = wf[:, 0:D] + dot_nt(w_ref[:, 0:QK], x2[...])
    qk.pump()
    gate.pump()
    wf[:, 0:D] = wf[:, 0:D] + dot_nt(cot[...], x3[...])
    value.pump()
    out.pump()
    ready("tokens")

    def back_one(i, sums):
        rows = pl.ds(pl.multiple_of(i * 32, 32), 32)
        grad = wf[rows, 0:D]
        inverse = stats[rows, 1:2]
        scaled = (keys[rows].astype(F32) - stats[rows, 0:1]) * inverse
        e = grad * gain1[...]
        inner = e - jnp.mean(e, axis=-1, keepdims=True) - scaled * jnp.mean(e * scaled, axis=-1, keepdims=True)
        queries[rows] = (hidden[rows] + inverse * inner).astype(BF)
        return (sums[0] + fold(grad * scaled), sums[1] + fold(grad))

    gain_sum, bias_sum = lax.fori_loop(0, TOK // 32, back_one, (zero, zero))
    final = pltpu.make_async_copy(queries, out_tokens, save_sems.at[len(local_copies)])
    final.start()
    vec_rows[0:1] = jnp.sum(gain_sum, axis=0, keepdims=True)
    vec_rows[1:2] = jnp.sum(bias_sum, axis=0, keepdims=True)
    for block in range(4):
        for j in range(4):
            for t in range(2):
                first = 256 * block + 128 * t
                vec[block, 2 * j + t : 2 * j + t + 1] = vec_rows[j : j + 1, first : first + 128]
    vectors = vector_steps(at, vec, vec_core, vec_z, vec_y, vec_x, vec_out, (vec_send, vec_recv), 0)
    next(vectors)
    qk.pump()

    todo = [value, qk, gate, out, up, down]
    vectors_open = True
    while todo or vectors_open:
        todo = [unit for unit in todo if unit.pump()]
        if vectors_open:
            vectors_open = next(vectors, 0) is None
    last = pltpu.make_async_copy(vec_out, out_vec, save_sems.at[len(local_copies) + 1])
    last.start()

    @pl.when(z > 0)
    def _():
        g_halo.wait_send()

    for far in (1, 2, 3):

        @pl.when(z >= far)
        def _():
            passing[far - 1].wait_send()

    final.wait()
    last.wait()


def backward(arrays, gain1, gain2, lengths, windows):
    vmem = pl.BlockSpec(memory_space=pltpu.VMEM)
    smem = pl.BlockSpec(memory_space=pltpu.SMEM)
    anywhere = pl.BlockSpec(memory_space=pl.ANY)
    shape = jax.ShapeDtypeStruct
    outs = [shape((TOK, D), BF), shape((8, 128), F32)] + [shape((2, 4, 4, UNIT_ROWS[n], 128), BF) for n in UNITS]
    scratch = [
        pltpu.VMEM((2 * TOK, VD), BF), pltpu.VMEM((2 * TOK, D), BF), pltpu.VMEM((2 * TOK, D), BF), pltpu.VMEM((2 * TOK, HALF), BF),
        pltpu.VMEM((2 * TOK, 512), BF), pltpu.VMEM((TOK, WIDE), BF), pltpu.VMEM((TOK, D), BF), pltpu.VMEM((TOK, VD), BF),
        pltpu.VMEM((TOK, WIDE), BF), pltpu.VMEM((TOK, WIDE), BF), pltpu.VMEM((TOK, QK), BF), pltpu.VMEM((HALO + TOK, QK), BF),
        pltpu.VMEM((HEADS, HALO + TOK, VH), BF), pltpu.VMEM((2, 2, 256, 384), BF), pltpu.VMEM((2, TOK, TOK), BF),
        pltpu.VMEM((2, KEYH, VH), BF), pltpu.VMEM((2, KEYH, VH), BF), pltpu.VMEM((2, KEYH, VH), BF),
        pltpu.VMEM((3, 2, KEYH, VH), BF), pltpu.VMEM((HEADS, TOK, VH), BF), pltpu.VMEM((TOK, D), F32),
        pltpu.VMEM((TOK, WIDE), F32), pltpu.VMEM((VD, D), BF), pltpu.VMEM((VD, D), BF), pltpu.VMEM((TOK, 512), F32),
        pltpu.VMEM((TOK, 128), F32), pltpu.VMEM((HALO, 2 * KEYH), BF), pltpu.VMEM((2, HALO, VH), BF), pltpu.VMEM((8, D), F32),
        pltpu.VMEM((4, 8, 128), F32), pltpu.VMEM((4, 8, 128), F32), pltpu.VMEM((4, 8, 128), F32), pltpu.VMEM((4, 8, 128), F32),
        pltpu.VMEM((4, 8, 128), F32), pltpu.VMEM((8, 128), F32),
    ]
    scratch += [pltpu.VMEM((4, 4, 4, r, 128), BF) for r in SET_ROWS]
    for r in SET_ROWS:
        for count in PART_ROWS[r]:
            scratch += [pltpu.VMEM(s, BF) for s in landing_shapes(count)]
    for name in UNITS:
        scratch += [pltpu.VMEM((count, 128), BF) for count in PART_ROWS[UNIT_ROWS[name]]]
    dma, regular = pltpu.SemaphoreType.DMA, pltpu.SemaphoreType.REGULAR
    scratch += [dma((28,)), dma((8,)), dma((6,)), dma((6,)), dma((4,)), dma((4,)), dma((10,)), dma((10,))]
    scratch += [dma((18 * COPIES,)), dma((18 * COPIES,)), dma((18,)), regular((9,)), regular((3,))]
    return pl.pallas_call(
        backward_kernel,
        out_shape=outs,
        in_specs=[anywhere] * 28 + [vmem] * 2 + [smem] * 2,
        out_specs=[anywhere] * len(outs),
        scratch_shapes=scratch,
        compiler_params=pltpu.CompilerParams(collective_id=2, has_side_effects=True, vmem_limit_bytes=62 * 2**20),
        cost_estimate=pl.CostEstimate(flops=26 * 10**9, bytes_accessed=70 * 10**6, transcendentals=10**6),
        name="backward",
    )(*arrays, gain1.reshape(1, D), gain2.reshape(1, D), lengths, windows.reshape(1, HEADS))


def unpack_kernel(down, up, out, gate, value, qk, g_down, g_up, g_out, g_gate, g_value, g_query, g_key):
    for x in range(4):
        cols = slice(128 * x, 128 * x + 128)
        for source, target in ((down, g_down), (out, g_out)):
            target[:, cols] = source[0, 0, x].astype(F32)
        g_query[:, cols] = qk[0, 0, x, 0:64].astype(F32)
        g_key[:, cols] = qk[0, 0, x, 64:128].astype(F32)
        xr, xc = x // 2, x % 2
        for source, target in ((up, g_up), (gate, g_gate), (value, g_value)):
            target[BIG * xr : BIG * xr + BIG, 128 * xc : 128 * xc + 128] = source[0, 0, x].astype(F32)


def unpack(gathered):
    def source(rows):
        return pl.BlockSpec((1, 1, 4, rows, 128), lambda c, y: (c, y, 0, 0, 0))

    tall = pl.BlockSpec((BIG, 512), lambda c, y: (y, c))
    turned = pl.BlockSpec((2 * BIG, 256), lambda c, y: (4 * c + y, 0))
    square = pl.BlockSpec((64, 512), lambda c, y: (y, c))
    shape = jax.ShapeDtypeStruct
    return pl.pallas_call(
        unpack_kernel,
        grid=(2, 4),
        out_shape=[
            shape((VH, D), F32), shape((FF, 256), F32), shape((VH, D), F32), shape((VD, 256), F32), shape((VD, 256), F32),
            shape((256, QK), F32), shape((256, QK), F32),
        ],
        in_specs=[source(UNIT_ROWS[n]) for n in UNITS],
        out_specs=[tall, turned, tall, turned, turned, square, square],
        compiler_params=pltpu.CompilerParams(vmem_limit_bytes=32 * 2**20),
        name="unpack",
    )(*gathered)


def body(
    tokens, ln_gain1, ln_bias1, w_query, w_key, w_value, w_gate, w_out, ln_gain2, ln_bias2, w_up, w_down, doc_lengths, windows, cotangent
):
    table = jnp.asarray(rotary_constants())
    (
        result, first, second, mixed, act, cot_half, lift_half, lift, q, k, v, w01, w23, s_in, heads, u, w, hidden, stats, qnext,
    ) = forward(
        tokens[0], cotangent[0], ln_gain1, ln_bias1, ln_gain2, ln_bias2, doc_lengths, windows, table,
        w_query, w_key, w_value, w_gate, w_out, w_up, w_down,
    )

    def pair(a):
        return a.reshape(2 * TOK, a.shape[2])

    arrays = (
        pair(act), pair(cot_half), pair(lift_half), pair(second), pair(first), pair(mixed), lift, cotangent[0], hidden, stats,
        u, w, heads, q, k, v, w01, w23, s_in, qnext, tokens[0], table,
        w_query, w_key, w_value.T, w_gate.T, w_out, w_up.T,
    )
    grad_tokens, vectors, *gathered = backward(arrays, ln_gain1, ln_gain2, doc_lengths, windows)
    g_down, g_up, g_out, g_gate, g_value, g_query, g_key = unpack(gathered)
    vectors = vectors.reshape(4, 256)
    return (
        result.reshape(1, TOK, D),
        grad_tokens.reshape(1, TOK, D),
        vectors[0],
        vectors[1],
        g_query,
        g_key,
        g_value.T,
        g_gate.T,
        g_out,
        vectors[2],
        vectors[3],
        g_up.T,
        g_down,
    )


def solution(mesh):
    in_specs = (P("batch", "head", None),) + (P(),) * 11 + (P("batch", None), P(), P("batch", "head", None))
    rows, vector = P("head", None), P("head")
    out_specs = (
        P("batch", "head", None), P("batch", "head", None), vector, vector, rows, rows, rows, rows, rows, vector, vector, rows, rows,
    )
    return jax.shard_map(body, mesh=mesh, in_specs=in_specs, out_specs=out_specs, check_vma=False)
```

```python
import functools
import math

import jax
import jax.numpy as jnp
import numpy as np
from jax import lax
from jax.experimental import pallas as pl
from jax.experimental.pallas import tpu as pltpu
from jax.sharding import PartitionSpec as P

D = 1024
HEADS = 4
KEYH = 256
VH = 432
FF = 1728
QK = 1024
VD = 1728
TOK = 512
SEQ = 2048
HALO = 128
WIDE = 1792

epsilon = 1e-05
retention_floor = 1.0
BF = jnp.bfloat16
F32 = jnp.float32
MESH = pl.DeviceIdType.MESH


ORDERS = ((0, 1, 2), (1, 0, 2), (2, 0, 1))
GATHERS = ((1, 2), (2, 1), (1, 2))
BIG, PAIRED = 112, 128
CUTS = {BIG: ((0, 32), (32, 48), (80, 32)), PAIRED: ((0, 32), (32, 48), (80, 48))}
COPIES = 20


def coordinates():
    z = lax.axis_index("head")
    b = lax.axis_index("batch")
    return [z, lax.div(b, 8), lax.rem(lax.div(b, 2), 4), lax.rem(b, 2)]


def shifted(at, axis, step):
    place = list(at)
    if axis == 3:
        place[3] = 1 - place[3]
    else:
        place[axis] = lax.rem(place[axis] + step, 4)
    return (place[0], (place[1] * 4 + place[2]) * 2 + place[3])


def away(p, step):
    return lax.rem(p + step, 4)


LOW, HIGH = pl.ds(0, 2), pl.ds(2, 2)


def landing_shapes(r):
    return [(2, 4, r, 128)] * 2 + [(4, 4, r, 128)] * 2 + [(3, 4, r, 128), (3, r, 128)]


LANDINGS = 6


class Part:
    def __init__(self, at, stage, lands, mine, out, rows, order, gather, sems, base, credit_in, credit_out):
        self.at, self.stage, self.out = at, stage, out
        self.first, self.count = rows
        self.lands = [land.at[..., pl.ds(0, self.count), :] for land in lands]
        self.mine = mine.at[pl.ds(0, self.count)]
        self.order, self.gather = order, gather
        self.send_sems, self.recv_sems, self.copy_sem = sems
        self.slot = base
        self.credit_in, self.credit_out = credit_in, credit_out
        self.pending = []

    def send(self, source, target, axis, step):
        copy = pltpu.make_async_remote_copy(
            src_ref=source, dst_ref=target, send_sem=self.send_sems.at[self.slot], recv_sem=self.recv_sems.at[self.slot],
            device_id=shifted(self.at, axis, step), device_id_type=MESH,
        )
        self.slot += 1
        copy.start()
        self.pending.append(copy)
        return copy

    def flush(self):
        for copy in self.pending:
            copy.wait_send()
        self.pending = []

    def pick(self, axes):
        index = [slice(None)] * 3
        for axis, value in axes.items():
            index[axis] = value
        return self.stage.at[tuple(index) + (pl.ds(self.first, self.count), slice(None))]

    def writers(self):
        a1, a2, a3 = self.order
        return [(a1, 1), (a1, 3)] + [(axis, step) for axis in (a2, a3) for step in (1, 2, 3)]

    def steps(self):
        at, lands = self.at, self.lands
        a1, a2, a3 = self.order
        p1, p2, p3 = at[a1], at[a2], at[a3]
        if self.credit_in is not None:
            pl.semaphore_wait(self.credit_in, len(self.writers()))
        one = self.send(self.pick({a1: away(p1, 2), a2: LOW}), lands[0], a1, 1)
        two = self.send(self.pick({a1: away(p1, 2), a2: HIGH}), lands[1], a1, 3)
        yield
        one.wait_recv()
        there = self.pick({a1: away(p1, 1), a2: LOW})
        there[...] = there[...] + lands[0][...]
        one = self.send(self.pick({a1: away(p1, 1)}), lands[2], a1, 1)
        two.wait_recv()
        there = self.pick({a1: away(p1, 3), a2: HIGH})
        there[...] = there[...] + lands[1][...]
        two = self.send(self.pick({a1: away(p1, 3)}), lands[3], a1, 3)
        yield
        one.wait_recv()
        two.wait_recv()
        own = self.pick({a1: p1})
        own[...] = (own[...].astype(F32) + lands[2][...].astype(F32) + lands[3][...].astype(F32)).astype(BF)
        three = [self.send(self.pick({a1: p1, a2: away(p2, s)}), lands[4].at[s - 1], a2, s) for s in (1, 2, 3)]
        yield
        for copy in three:
            copy.wait_recv()
        own = self.pick({a1: p1, a2: p2})
        total = own[...].astype(F32)
        for step in range(3):
            total = total + lands[4][step].astype(F32)
        own[...] = total.astype(BF)
        three = [self.send(self.pick({a1: p1, a2: p2, a3: away(p3, s)}), lands[5].at[s - 1], a3, s) for s in (1, 2, 3)]
        yield
        for copy in three:
            copy.wait_recv()
        total = self.pick({a1: p1, a2: p2, a3: p3})[...].astype(F32)
        for step in range(3):
            total = total + lands[5][step].astype(F32)
        self.mine[...] = total.astype(BF)
        self.flush()
        if self.credit_out is not None:
            for axis, step in self.writers():
                pl.semaphore_signal(self.credit_out, inc=1, device_id=shifted(at, axis, step), device_id_type=MESH)

        rows = pl.ds(self.first, self.count)
        g1, g2 = self.gather
        target = self.out.at[at[3], at[1], at[2], rows]
        local = pltpu.make_async_copy(self.mine, target, self.copy_sem)
        local.start()
        three = [self.send(self.mine, target, g1, step) for step in (1, 2, 3)]
        yield
        for copy in three:
            copy.wait_recv()
        local.wait()

        def block(place):
            if g2 == 1:
                return self.out.at[at[3], place, :, rows]
            return self.out.at[at[3], :, place, rows]

        q = at[g2]
        three = [self.send(block(q), block(q), g2, step) for step in (1, 2, 3)]
        four = [self.send(block(q), block(q), 3, 1)]
        yield
        for step, copy in zip((1, 2, 3), three):
            copy.wait_recv()
            source = block(away(q, 4 - step))
            four.append(self.send(source, source, 3, 1))
        yield
        for copy in four:
            copy.wait_recv()
        self.flush()


class Unit:
    RS_STEPS = 5

    def __init__(self, parts):
        self.parts = parts
        self.running = None
        self.done = 0

    def start(self):
        self.running = [part.steps() for part in self.parts]
        self.pump()

    def pump(self, times=1):
        for _ in range(times):
            if not self.running:
                return False
            self.running = [steps for steps in self.running if next(steps, 0) is None]
            self.done += 1
        return bool(self.running)

    def reduced(self):
        while self.done < self.RS_STEPS:
            self.pump()


def vector_steps(at, mine, land_core, land_z, land_y, land_x, final, sems, base):
    send_sems, recv_sems = sems
    slots = iter(range(base, base + 10))

    def send(source, target, axis, step):
        slot = next(slots)
        copy = pltpu.make_async_remote_copy(
            src_ref=source, dst_ref=target, send_sem=send_sems.at[slot], recv_sem=recv_sems.at[slot],
            device_id=shifted(at, axis, step), device_id_type=MESH,
        )
        copy.start()
        return copy

    z, y, x, _ = at
    copies = [send(mine, land_core, 3, 1)]
    yield
    copies[0].wait()
    mine[...] = mine[...] + land_core[...]
    copies = [send(mine.at[away(z, s)], land_z.at[z], 0, s) for s in (1, 2, 3)]
    land_z[z] = mine[z]
    yield
    for axis, here, land in ((1, y, land_y), (2, x, land_x)):
        for copy in copies:
            copy.wait()
        source = land_z if axis == 1 else land_y
        total = (source[0] + source[1]) + (source[2] + source[3])
        land[here] = total
        copies = [send(land.at[here], land.at[here], axis, s) for s in (1, 2, 3)]
        yield
    for copy in copies:
        copy.wait()
    final[...] = (land_x[0] + land_x[1]) + (land_x[2] + land_x[3])


def greet(at):
    barrier = pltpu.get_barrier_semaphore()
    partners = [(axis, step) for axis in (0, 1, 2) for step in (1, 2, 3)] + [(3, 1)]
    for axis, step in partners:
        pl.semaphore_signal(barrier, inc=1, device_id=shifted(at, axis, step), device_id_type=MESH)
    pl.semaphore_wait(barrier, len(partners))


class Passing:
    PIECES = ((0, 0), (0, 1), (1, 0), (1, 1))

    def __init__(self, at, way, own, near, far, joined, sems, base):
        self.at, self.way = at, way
        self.rank = at[0] if way == 1 else 3 - at[0]
        self.own, self.near, self.far, self.joined = own, near, far, joined
        self.send_sems, self.recv_sems = sems
        self.base = base

    ROWS = (slice(0, 224), slice(224, VH))

    def piece(self, ref, p):
        head, half = self.PIECES[p]
        rows = self.ROWS[half]
        return ref.at[head, pl.ds(rows.start, rows.stop - rows.start)]

    def copy(self, source, target, p, kind):
        step = {0: self.way, 1: -self.way, 2: -self.way}[kind] % 4
        slot = self.base + 4 * min(kind, 1) + p
        return pltpu.make_async_remote_copy(
            src_ref=self.piece(source, p), dst_ref=self.piece(target, p), send_sem=self.send_sems.at[slot],
            recv_sem=self.recv_sems.at[slot], device_id=shifted(self.at, 0, step), device_id_type=MESH,
        )

    def clear(self):
        @pl.when(self.rank == 0)
        def _():
            self.near[...] = jnp.zeros(self.near.shape, BF)

        @pl.when(self.rank < 2)
        def _():
            self.far[...] = jnp.zeros(self.far.shape, BF)

    def begin(self, p):
        @pl.when(self.rank < 2)
        def _():
            self.copy(self.own, self.near, p, 0).start()

        @pl.when(self.rank == 0)
        def _():
            self.copy(self.own, self.far, p, 1).start()

    def forward(self, p, decay):
        head, half = self.PIECES[p]
        rows = self.ROWS[half]

        @pl.when(self.rank == 2)
        def _():
            self.copy(self.own, self.near, p, 0).wait_recv()
            total = self.own[head, rows].astype(F32) + self.near[head, rows].astype(F32) * decay[head]
            self.joined[head, rows] = total.astype(BF)
            self.copy(self.joined, self.near, p, 0).start()

        @pl.when(self.rank == 3)
        def _():
            self.copy(self.far, self.far, p, 1).wait_recv()
            self.copy(self.far, self.far, p, 2).start()

    def finish(self):
        for p in range(4):

            @pl.when((self.rank == 1) | (self.rank == 3))
            def _():
                self.copy(self.own, self.near, p, 0).wait_recv()

            @pl.when(self.rank == 2)
            def _():
                self.copy(self.far, self.far, p, 1).wait_recv()

    def drain(self):
        for p in range(4):

            @pl.when(self.rank < 3)
            def _():
                self.copy(self.own, self.near, p, 0).wait_send()

            @pl.when((self.rank == 0) | (self.rank == 3))
            def _():
                self.copy(self.own, self.far, p, 1).wait_send()


LOG_GAMMA = tuple(math.log(1.0 - 2.0 ** (-5.0 - h)) for h in range(HEADS))
HALF = WIDE // 2


def rotary_constants():
    half = KEYH // 2
    ladder = np.arange(half, dtype=np.float64)
    theta = 10000.0 ** (-ladder / half)
    place = np.arange(SEQ, dtype=np.float64)[:, None]
    zeta = (2.0 * ladder + 0.4 * KEYH) / (1.4 * KEYH)
    grow = zeta[None, :] ** (place / 512.0)
    cosine, sine = np.cos(place * theta), np.sin(place * theta)
    small = KEYH ** (-0.5)
    table = np.concatenate([cosine * grow, sine * grow, cosine / grow * small, sine / grow * small], axis=1)
    return np.concatenate([np.zeros((HALO, 4 * half)), table]).astype(np.float32)


def dot_nn(a, b):
    return lax.dot_general(a, b, (((1,), (0,)), ((), ())), preferred_element_type=F32)


def dot_nt(a, b):
    return lax.dot_general(a, b, (((1,), (1,)), ((), ())), preferred_element_type=F32)


def dot_tn(a, b):
    return lax.dot_general(a, b, (((0,), (0,)), ((), ())), preferred_element_type=F32)


def row_loop(total, step, work):
    def one(i, carry):
        work(pl.ds(pl.multiple_of(i * step, step), step))
        return carry

    lax.fori_loop(0, total // step, one, 0)


class Documents:
    def __init__(self, lengths_ref):
        ends = []
        total = 0
        for i in range(5):
            total = total + lengths_ref[0, i]
            ends.append(total)
        self.ends = ends

    def of(self, where):
        found = jnp.zeros(where.shape, jnp.int32) if hasattr(where, "shape") and where.shape else 0
        for end in self.ends:
            found = found + jnp.where(where >= end, 1, 0)
        return found


def column(count, first=0):
    return lax.broadcasted_iota(jnp.int32, (count, 1), 0) + first


def line(count, first=0):
    return lax.broadcasted_iota(jnp.int32, (1, count), 1) + first


def decay_block(h, rows, cols, row_first, col_first, start, docs, window):
    i, j = column(rows, row_first), line(cols, col_first)
    base = min(row_first, col_first)
    seen = (i >= j) & (docs.of(i + start) == docs.of(j + start))
    if window is not None:
        seen = seen & (i - j < window)
    if col_first < 0:
        seen = seen & (j + start >= 0)
    down = jnp.exp((i - base).astype(F32) * LOG_GAMMA[h])
    up = jnp.exp((j - base).astype(F32) * (-LOG_GAMMA[h]))
    return jnp.where(seen, down * up, 0.0)


def rotated(raw, cosine, sine):
    front, behind = raw[:, :128], raw[:, 128:]
    return jnp.concatenate([front * cosine - behind * sine, front * sine + behind * cosine], axis=1)


def forward_kernel(
    tokens_hbm, cot_hbm, gain1, bias1, gain2, bias2, lengths, windows, table_hbm,
    wq_hbm, wk_hbm, wv_hbm, wg_hbm, wo_hbm, wu_hbm, wd_hbm,
    out_result, out_first, out_second, out_mixed, out_act, out_cot, out_lhalf, out_lift,
    out_q, out_k, out_v, out_w01, out_w23, out_sin, out_heads, out_u, out_w, out_hidden, out_stats, out_qnext,
    tokens, cot, table, wq, wk, wv, wg, wo, wu, wd,
    first, queries, keys, values, wide_f32, down_grad, kept, w01, w23, state, state_near, state_far, state_join, state_in,
    heads, u_ref, w_ref, mixed, hidden, second, lift, act, stats,
    load_sems, save_sems, send_sems, recv_sems, pass_send, pass_recv,
):
    at = coordinates()
    z, core = at[0], at[3]
    start = z * TOK
    loads = {}
    for slot, (name, source, target) in enumerate(
        [
            ("tokens", tokens_hbm, tokens.at[pl.ds(HALO, TOK)]),
            ("wk", wk_hbm, wk),
            ("table", table_hbm.at[pl.ds(pl.multiple_of(z * TOK, TOK), HALO + TOK)], table),
            ("wv", wv_hbm, wv),
            ("wq", wq_hbm, wq),
            ("wg", wg_hbm, wg),
            ("cot", cot_hbm, cot),
            ("wd", wd_hbm, wd),
            ("wo", wo_hbm, wo),
            ("wu", wu_hbm, wu),
        ]
    ):
        loads[name] = pltpu.make_async_copy(source, target, load_sems.at[slot])
        loads[name].start()
    partners = [(3, 1), (0, 1), (0, 3)]
    barrier = pltpu.get_barrier_semaphore()
    for axis, step in partners:
        pl.semaphore_signal(barrier, inc=1, device_id=shifted(at, axis, step), device_id_type=MESH)

    saves, sends = [], []

    def save(source, target):
        copy = pltpu.make_async_copy(source, target, save_sems.at[len(saves)])
        copy.start()
        saves.append(copy)

    def remote(source, target, axis, step):
        slot = len(sends)
        copy = pltpu.make_async_remote_copy(
            src_ref=source, dst_ref=target, send_sem=send_sems.at[slot], recv_sem=recv_sems.at[slot],
            device_id=shifted(at, axis, step), device_id_type=MESH,
        )
        sends.append(copy)
        return copy

    def share(source, target):
        save(source, target.at[core])
        remote(source, target.at[core], 3, 1).start()
        return (saves[-1], sends[-1])

    loads["tokens"].wait()

    pl.semaphore_wait(barrier, len(partners))
    t_halo = remote(tokens.at[pl.ds(TOK, HALO)], tokens.at[pl.ds(0, HALO)], 0, 1)

    @pl.when(z < 3)
    def _():
        t_halo.start()

    @pl.when(z == 0)
    def _():
        tokens[0:HALO] = jnp.zeros((HALO, D), BF)

    def normalized(x):
        mean = jnp.mean(x, axis=-1, keepdims=True)
        center = x - mean
        inverse = lax.rsqrt(jnp.mean(center * center, axis=-1, keepdims=True) + epsilon)
        return center * inverse, mean, inverse

    def norm_one(i, carry):
        rows = pl.ds(pl.multiple_of(i * 64, 64), 64)
        scaled, mean, inverse = normalized(tokens[pl.ds(HALO + i * 64, 64)].astype(F32))
        first[pl.ds(HALO + i * 64, 64)] = (scaled * gain1[...] + bias1[...]).astype(BF)
        stats[rows, 0:1] = mean
        stats[rows, 1:2] = inverse
        return carry

    lax.fori_loop(0, TOK // 64, norm_one, 0)
    share(first.at[pl.ds(HALO, TOK)], out_first)

    docs = Documents(lengths)
    doc_before = docs.of(start - 1)
    doc_last = docs.of(start + TOK - 1)
    place = column(TOK)
    doc_rows = docs.of(place + start)

    def project(h, begin):
        cols = slice(h * KEYH, (h + 1) * KEYH)
        raw = dot_nn(first[begin:], wk[:, cols])
        keys[begin:, cols] = rotated(raw, table[begin:, 256:384], table[begin:, 384:512]).astype(BF)
        values[h, begin:] = dot_nt(first[begin:], wv[h * VH : (h + 1) * VH]).astype(BF)

    loads["wk"].wait()
    loads["table"].wait()
    loads["wv"].wait()
    passing = Passing(at, 1, state, state_near, state_far, state_join, (pass_send, pass_recv), 0)
    joins = [jnp.where(doc_before == doc_last, math.exp(LOG_GAMMA[h] * TOK), 0.0) for h in (2, 3)]
    for h in (2, 3):
        project(h, HALO)
        factor = jnp.where(doc_rows == doc_last, jnp.exp((TOK - place).astype(F32) * LOG_GAMMA[h]), 0.0)
        scaled = (keys[HALO:, h * KEYH : (h + 1) * KEYH].astype(F32) * factor).astype(BF)
        state[h - 2] = dot_tn(values[h, HALO:], scaled).astype(BF)
        passing.begin(2 * h - 4)
        passing.begin(2 * h - 3)
    passing.clear()
    loads["wq"].wait()
    for h in range(HEADS):
        raw = dot_nn(first[HALO:], wq[:, h * KEYH : (h + 1) * KEYH])
        queries[:, h * KEYH : (h + 1) * KEYH] = rotated(raw, table[HALO:, 0:128], table[HALO:, 128:256]).astype(BF)
    save(queries, out_q)
    q_halo = remote(queries.at[pl.ds(0, HALO), pl.ds(0, 2 * KEYH)], out_qnext, 0, 3)

    @pl.when(z > 0)
    def _():
        q_halo.start()

    loads["wg"].wait()
    passing.forward(0, joins)
    for h in range(HEADS):
        wide_f32[:, 0:VH] = dot_nt(first[HALO:], wg[h * VH : (h + 1) * VH])

        def swish(rows):
            gate = wide_f32[rows, 0:VH]
            sigma = 0.5 * jnp.tanh(0.5 * gate) + 0.5
            u_ref[h, rows] = (gate * sigma).astype(BF)
            w_ref[h, rows] = (sigma * (1.0 + gate * (1.0 - sigma))).astype(BF)

        row_loop(TOK, 128, swish)
        if h == 1:
            passing.forward(1, joins)
    save(u_ref, out_u)
    save(w_ref, out_w)
    loads["cot"].wait()
    save(cot.at[:, pl.ds(pl.multiple_of(core * 512, 512), 512)], out_cot.at[core])
    remote(cot.at[:, pl.ds(pl.multiple_of((1 - core) * 512, 512), 512)], out_cot.at[core], 3, 1).start()
    loads["wd"].wait()
    down_grad[...] = dot_nt(cot[...], wd[...]).astype(BF)
    passing.forward(2, joins)

    for h in (2, 3):
        for b in (0, 1):
            rows, cols = slice(256 * b, 256 * b + 256), 256 * b + 256
            q_h = queries[rows, h * KEYH : (h + 1) * KEYH]
            scores = dot_nt(q_h, keys[HALO : HALO + cols, h * KEYH : (h + 1) * KEYH])
            weight = (scores * decay_block(h, 256, cols, 256 * b, 0, start, docs, None)).astype(BF)
            w23[h - 2, rows, 0:cols] = weight
            kept[h, rows] = dot_nn(weight, values[h, HALO : HALO + cols])

    passing.forward(3, joins)

    @pl.when(z > 0)
    def _():
        t_halo.wait_recv()

    for block in (slice(0, 64), slice(64, 128)):
        first[block] = (normalized(tokens[block].astype(F32))[0] * gain1[...] + bias1[...]).astype(BF)
    for h in (0, 1):
        project(h, 0)

    save(keys, out_k)
    save(values, out_v)
    for h in (0, 1):
        for b in (0, 1):
            rows = slice(256 * b, 256 * b + 256)
            q_h = queries[rows, h * KEYH : (h + 1) * KEYH]
            scores = dot_nt(q_h, keys[256 * b : 256 * b + 384, h * KEYH : (h + 1) * KEYH])
            decay = decay_block(h, 256, 384, 256 * b, 256 * b - HALO, start, docs, windows[0, h])
            weight = (scores * decay).astype(BF)
            w01[h, b] = weight
            kept[h, rows] = dot_nn(weight, values[h, 256 * b : 256 * b + 384])
    save(w01, out_w01)
    save(w23, out_w23)

    passing.finish()
    from_first = docs.of(TOK - 1) == doc_before
    for h in (2, 3):
        power = jnp.where(z == 3, math.exp(2 * TOK * LOG_GAMMA[h]), math.exp(TOK * LOG_GAMMA[h]))
        total = state_near[h - 2].astype(F32) + state_far[h - 2].astype(F32) * jnp.where(from_first, power, 0.0)
        state_in[h - 2] = total.astype(BF)
        factor = jnp.where(doc_rows == doc_before, jnp.exp(place.astype(F32) * LOG_GAMMA[h]), 0.0)
        kept[h] = kept[h] + factor * dot_nt(queries[:, h * KEYH : (h + 1) * KEYH], state_in[h - 2])
    save(state_in, out_sin)

    def mix(rows):
        parts = []
        for h in range(HEADS):
            x = kept[h, rows]
            center = x - jnp.mean(x, axis=-1, keepdims=True)
            inverse = lax.rsqrt(jnp.mean(center * center, axis=-1, keepdims=True) + retention_floor)
            stats[rows, 4 + h : 5 + h] = inverse
            low = (center * inverse).astype(BF)
            heads[h, rows] = low
            parts.append(low.astype(F32) * u_ref[h, rows].astype(F32))
        mixed[rows] = jnp.concatenate(parts, axis=1).astype(BF)

    row_loop(TOK, 64, mix)
    mixed_away = share(mixed, out_mixed)
    save(heads, out_heads)

    loads["wo"].wait()
    hidden[...] = dot_nn(mixed[...], wo[...])

    def norm_two(i, carry):
        rows = pl.ds(pl.multiple_of(i * 64, 64), 64)
        x = hidden[rows] + tokens[pl.ds(HALO + i * 64, 64)].astype(F32)
        hidden[rows] = x
        scaled, mean, inverse = normalized(x)
        second[rows] = (scaled * gain2[...] + bias2[...]).astype(BF)
        stats[rows, 2:3] = mean
        stats[rows, 3:4] = inverse
        return carry

    lax.fori_loop(0, TOK // 64, norm_two, 0)
    share(second, out_second)
    save(hidden, out_hidden)
    save(stats, out_stats)

    loads["wu"].wait()
    for first_col in range(0, FF, 256):
        width = min(256, FF - first_col)
        cols = slice(first_col, first_col + width)
        wide_f32[:, cols] = dot_nt(second[...], wu[cols])

    def activate(rows):
        x = wide_f32[rows]
        phi = 0.5 * (1.0 + lax.erf(x * math.sqrt(0.5)))
        slope = phi + x * jnp.exp(-0.5 * x * x) * (1.0 / math.sqrt(2.0 * math.pi))
        act[rows] = (x * phi).astype(BF)
        grad = (down_grad[rows].astype(F32) * slope).astype(BF)
        lift[rows] = jnp.concatenate([grad, jnp.zeros((grad.shape[0], WIDE - FF), BF)], axis=1)

    row_loop(TOK, 32, activate)
    share(act, out_act)
    save(lift, out_lift)
    save(lift.at[:, pl.ds(pl.multiple_of(core * HALF, HALF), HALF)], out_lhalf.at[core])
    remote(lift.at[:, pl.ds(pl.multiple_of((1 - core) * HALF, HALF), HALF)], out_lhalf.at[core], 3, 1).start()
    for copy in mixed_away:
        copy.wait()
    mixed[:, 0:D] = (hidden[...] + dot_nn(act[...], wd[...])).astype(BF)
    save(mixed.at[:, pl.ds(0, D)], out_result)

    for copy in sends:
        if not any(copy is other for other in (t_halo, q_halo) + mixed_away):
            copy.wait()

    @pl.when(z > 0)
    def _():
        q_halo.wait_send()

    @pl.when(z < 3)
    def _():
        q_halo.wait_recv()
        t_halo.wait_send()

    passing.drain()
    for copy in saves:
        if copy is not mixed_away[0]:
            copy.wait()


def forward(tokens, cot, gain1, bias1, gain2, bias2, lengths, windows, table, wq, wk, wv, wg, wo, wu, wd):
    vmem = pl.BlockSpec(memory_space=pltpu.VMEM)
    smem = pl.BlockSpec(memory_space=pltpu.SMEM)
    anywhere = pl.BlockSpec(memory_space=pl.ANY)
    shape = jax.ShapeDtypeStruct
    outs = [
        shape((TOK, D), BF), shape((2, TOK, D), BF), shape((2, TOK, D), BF), shape((2, TOK, VD), BF), shape((2, TOK, FF), BF),
        shape((2, TOK, 512), BF), shape((2, TOK, HALF), BF), shape((TOK, WIDE), BF),
        shape((TOK, QK), BF), shape((HALO + TOK, QK), BF), shape((HEADS, HALO + TOK, VH), BF),
        shape((2, 2, 256, 384), BF), shape((2, TOK, TOK), BF), shape((2, VH, KEYH), BF),
        shape((HEADS, TOK, VH), BF), shape((HEADS, TOK, VH), BF), shape((HEADS, TOK, VH), BF), shape((TOK, D), F32), shape((TOK, 128), F32),
        shape((HALO, 2 * KEYH), BF),
    ]
    scratch = [
        pltpu.VMEM((HALO + TOK, D), BF), pltpu.VMEM((TOK, D), BF), pltpu.VMEM((HALO + TOK, 512), F32),
        pltpu.VMEM((D, QK), BF), pltpu.VMEM((D, QK), BF), pltpu.VMEM((VD, D), BF), pltpu.VMEM((VD, D), BF),
        pltpu.VMEM((VD, D), BF), pltpu.VMEM((FF, D), BF), pltpu.VMEM((FF, D), BF),
        pltpu.VMEM((HALO + TOK, D), BF), pltpu.VMEM((TOK, QK), BF), pltpu.VMEM((HALO + TOK, QK), BF),
        pltpu.VMEM((HEADS, HALO + TOK, VH), BF), pltpu.VMEM((TOK, FF), F32), pltpu.VMEM((TOK, FF), BF),
        pltpu.VMEM((HEADS, TOK, VH), F32), pltpu.VMEM((2, 2, 256, 384), BF), pltpu.VMEM((2, TOK, TOK), BF),
        pltpu.VMEM((2, VH, KEYH), BF), pltpu.VMEM((2, VH, KEYH), BF), pltpu.VMEM((2, VH, KEYH), BF), pltpu.VMEM((2, VH, KEYH), BF),
        pltpu.VMEM((2, VH, KEYH), BF),
        pltpu.VMEM((HEADS, TOK, VH), BF), pltpu.VMEM((HEADS, TOK, VH), BF), pltpu.VMEM((HEADS, TOK, VH), BF), pltpu.VMEM((TOK, VD), BF),
        pltpu.VMEM((TOK, D), F32), pltpu.VMEM((TOK, D), BF), pltpu.VMEM((TOK, WIDE), BF), pltpu.VMEM((TOK, FF), BF),
        pltpu.VMEM((TOK, 128), F32),
        pltpu.SemaphoreType.DMA((10,)), pltpu.SemaphoreType.DMA((20,)),
        pltpu.SemaphoreType.DMA((16,)), pltpu.SemaphoreType.DMA((16,)),
        pltpu.SemaphoreType.DMA((8,)), pltpu.SemaphoreType.DMA((8,)),
    ]
    return pl.pallas_call(
        forward_kernel,
        out_shape=outs,
        in_specs=[anywhere] * 2 + [vmem] * 4 + [smem] * 2 + [anywhere] * 8,
        out_specs=[anywhere] * len(outs),
        scratch_shapes=scratch,
        compiler_params=pltpu.CompilerParams(collective_id=1, has_side_effects=True, vmem_limit_bytes=62 * 2**20),
        cost_estimate=pl.CostEstimate(flops=14 * 10**9, bytes_accessed=50 * 10**6, transcendentals=2 * 10**6),
        name="forward",
    )(
        tokens, cot, gain1.reshape(1, D), bias1.reshape(1, D), gain2.reshape(1, D), bias2.reshape(1, D),
        lengths, windows.reshape(1, HEADS), table, wq, wk, wv.T, wg.T, wo, wu.T, wd,
    )


UNITS = ("down", "up", "out", "gate", "value", "qk")
UNIT_ROWS = {"down": BIG, "up": BIG, "out": BIG, "gate": BIG, "value": BIG, "qk": PAIRED}
UNIT_SET = {"down": 0, "up": 1, "out": 2, "gate": 3, "value": 0, "qk": 1}
SET_ROWS = (BIG, PAIRED, BIG, BIG)
SCHEDULE = (
    (0,), (1,), (), (0,), (), (1,), (0,), (0,), (), (), (0,), (), (), (0, 1, 2, 3,), (0, 1,), (), (2,), (), (1, 2, 3,), (5,), (4,), (), (), (1, 2,), (3,), (1,),
)
TAIL = (5, 4, 3, 2, 5, 3, 4, 2, 5, 2, 3, 4, 5, 3, 4, 5, 4, 5, 4)
PART_ROWS = {rows: tuple(count for _, count in cuts) for rows, cuts in CUTS.items()}


def stage_rows(stage, result, first_x):
    for z in range(4):
        for y in range(4):
            n = min(BIG, VH - BIG * y)
            for i in range(result.shape[1] // 128):
                piece = result[VH * z + BIG * y : VH * z + BIG * y + n, 128 * i : 128 * i + 128].astype(BF)
                stage[z, y, first_x + i, 0:n] = piece
                if n < BIG:
                    stage[z, y, first_x + i, n:BIG] = jnp.zeros((BIG - n, 128), BF)


def stage_columns(stage, result, first_z):
    for i in range(result.shape[1] // 128):
        z, xc = first_z + i // 2, i % 2
        for y in range(4):
            for xr in range(2):
                first = 224 * y + BIG * xr
                stage[z, y, 2 * xr + xc, 0:BIG] = result[first : first + BIG, 128 * i : 128 * i + 128].astype(BF)


def stage_square(stage, result, first_row):
    for z in range(4):
        for y in range(4):
            for x in range(4):
                piece = result[256 * z + 64 * y : 256 * z + 64 * y + 64, 128 * x : 128 * x + 128].astype(BF)
                stage[z, y, x, first_row : first_row + 64] = piece


def fold(rows):
    return jnp.sum(rows.reshape(rows.shape[0] // 8, 8, rows.shape[1]), axis=0)


def unrotated(grad, cosine, sine):
    grad = grad.astype(BF).astype(F32)
    front, behind = grad[:, :128], grad[:, 128:]
    return jnp.concatenate([front * cosine + behind * sine, behind * cosine - front * sine], axis=1).astype(BF)


def backward_kernel(
    act_hbm, coth_hbm, lhalf_hbm, second_hbm, first_hbm, mixed_hbm, lift_hbm, cot_hbm, hidden_hbm, stats_hbm,
    u_hbm, w_hbm, heads_hbm, q_hbm, k_hbm, v_hbm, w01_hbm, w23_hbm, sin_hbm, qnext_hbm, tokens_hbm, table_hbm,
    wq_hbm, wk_hbm, wv_hbm, wg_hbm, wo_hbm, wu_hbm, gain1, gain2, lengths, windows,
    out_tokens, out_vec, out_down, out_up, out_out, out_gate, out_value, out_qk,
    x1, x2, x3, y1, ch, wide, cot, heads, u_ref, w_ref, queries, keys, values, w01, w23, state_in,
    back_state, back_near, back_far, back_join, rgrad, hidden, wf, wu, wo, table, stats, qnext, gnext, vec_rows,
    vec, vec_core, vec_z, vec_y, vec_x, vec_out,
    stage0, stage1, stage2, stage3, *rest,
):
    lands = [[rest[(3 * s + p) * LANDINGS : (3 * s + p + 1) * LANDINGS] for p in range(3)] for s in range(4)]
    rest = rest[12 * LANDINGS :]
    mines = rest[0:18]
    load_sems, save_sems, pair_send, pair_recv, z_send, z_recv, vec_send, vec_recv = rest[18:26]
    unit_send, unit_recv, unit_copy, credits, pair_credit, pass_send, pass_recv = rest[26:]
    stages = (stage0, stage1, stage2, stage3)
    at = coordinates()
    z, core = at[0], at[3]
    start = z * TOK

    loading = {}

    def load(name, source, target):
        copy = pltpu.make_async_copy(source, target, load_sems.at[len(loading)])
        copy.start()
        loading[name] = copy

    def ready(*names):
        for name in names:
            loading[name].wait()

    load("act", act_hbm, x1)
    load("coth", coth_hbm, ch)
    load("lhalf", lhalf_hbm, y1)
    load("second", second_hbm, x2)
    load("lift", lift_hbm, wide)
    load("wu", wu_hbm, wu)
    greet(at)

    outs = dict(zip(UNITS, (out_down, out_up, out_out, out_gate, out_value, out_qk)))
    units = {}
    for n, name in enumerate(UNITS):
        s, parts = UNIT_SET[name], []
        for p in range(3):
            slot = 3 * n + p
            parts.append(
                Part(
                    at, stages[s], lands[s][p], mines[slot], outs[name], CUTS[UNIT_ROWS[name]][p], ORDERS[p], GATHERS[p],
                    (unit_send, unit_recv, unit_copy.at[slot]), slot * COPIES,
                    credits.at[slot - 12] if n >= 4 else None, credits.at[slot] if n < 2 else None,
                )
            )
        units[name] = Unit(parts)
    down, up, out, gate, value, qk = (units[name] for name in UNITS)
    numbered = [units[name] for name in UNITS]
    ticks = iter(SCHEDULE)

    def tick():
        for n in next(ticks):
            numbered[n].pump()

    pairs = []

    def to_sibling(source, target):
        copy = pltpu.make_async_remote_copy(
            src_ref=source, dst_ref=target, send_sem=pair_send.at[len(pairs)], recv_sem=pair_recv.at[len(pairs)],
            device_id=shifted(at, 3, 1), device_id_type=MESH,
        )
        copy.start()
        pairs.append(copy)
        return copy

    local_copies = []

    def halves(source, width, landing, lane):
        rows = pl.ds(pl.multiple_of(core * TOK, TOK), TOK)
        lanes = pl.ds(lane, width)
        mine = source.at[:, pl.ds(pl.multiple_of(core * width, width), width)]
        other = source.at[:, pl.ds(pl.multiple_of((1 - core) * width, width), width)]
        remote = to_sibling(other, landing.at[rows, lanes])
        local = pltpu.make_async_copy(mine, landing.at[rows, lanes], save_sems.at[len(local_copies)])
        local.start()
        local_copies.append(local)
        return remote, local

    def arrived(pair):
        pair[0].wait()
        pair[1].wait()

    def tell_sibling(slot):
        pl.semaphore_signal(pair_credit.at[slot], inc=1, device_id=shifted(at, 3, 1), device_id_type=MESH)

    ready("act", "coth")
    load("cot", cot_hbm, cot)
    load("hidden", hidden_hbm, hidden)
    load("stats", stats_hbm, stats)
    load("wo", wo_hbm, wo)
    for half in (0, 1):
        stage_rows(stage0, dot_tn(x1[...], ch[:, 256 * half : 256 * half + 256]), 2 * half)
    down.start()
    load("mixed", mixed_hbm, x1)
    load("u", u_hbm, u_ref)
    load("w", w_hbm, w_ref)
    load("heads", heads_hbm, heads)
    tell_sibling(0)

    ready("lhalf", "second")
    for half in (0, 1):
        stage_columns(stage1, dot_tn(y1[...], x2[:, 512 * half : 512 * half + 512]), 2 * half)
    up.start()
    tell_sibling(1)
    load("first", first_hbm, x3)
    load("q", q_hbm, queries)
    load("k", k_hbm, keys)
    load("v", v_hbm, values)
    load("w01", w01_hbm, w01)
    load("w23", w23_hbm, w23)
    load("sin", sin_hbm, state_in)
    load("qnext", qnext_hbm, qnext)
    load("table", table_hbm.at[pl.ds(pl.multiple_of(z * TOK + HALO, HALO), TOK)], table)

    ready("lift", "wu")
    for half in (0, 1):
        cols = slice(512 * half, 512 * half + 512)
        wf[:, cols] = dot_nn(wide[:, 0:FF], wu[:, cols])
        tick()
    load("wg", wg_hbm, wu)
    ready("cot", "hidden", "stats")

    def back_two(i, sums):
        rows = pl.ds(pl.multiple_of(i * 64, 64), 64)
        grad = wf[rows]
        inverse = stats[rows, 3:4]
        scaled = (hidden[rows] - stats[rows, 2:3]) * inverse
        e = grad * gain2[...]
        inner = e - jnp.mean(e, axis=-1, keepdims=True) - scaled * jnp.mean(e * scaled, axis=-1, keepdims=True)
        total = cot[rows].astype(F32) + inverse * inner
        hidden[rows] = total
        cot[rows] = total.astype(BF)
        return (sums[0] + fold(grad * scaled), sums[1] + fold(grad))

    zero = jnp.zeros((8, D), F32)
    gain_sum, bias_sum = lax.fori_loop(0, TOK // 64, back_two, (zero, zero))
    vec_rows[2:3] = jnp.sum(gain_sum, axis=0, keepdims=True)
    vec_rows[3:4] = jnp.sum(bias_sum, axis=0, keepdims=True)
    pl.semaphore_wait(pair_credit.at[0], 1)
    low_pair = halves(cot, 512, ch, 0)
    tick()

    ready("wo", "u", "w", "heads")

    def mixed_grad(first_head):
        for h in (first_head, first_head + 1):
            lane = 512 * (h - first_head)
            wf[:, lane : lane + VH] = dot_nt(cot[...], wo[h * VH : (h + 1) * VH])

    def back_head(h, lane, rows):
        grad = wf[rows, lane : lane + VH]
        c = heads[h, rows].astype(F32)
        gated = grad * c * w_ref[h, rows].astype(F32)
        e = (grad * u_ref[h, rows].astype(F32)).astype(BF).astype(F32)
        inner = e - jnp.mean(e, axis=-1, keepdims=True) - c * jnp.mean(e * c, axis=-1, keepdims=True)
        rgrad[h, rows] = (inner * stats[rows, 4 + h : 5 + h]).astype(BF)
        return gated

    def mix_late(rows):
        for h in (2, 3):
            w_ref[h, rows] = back_head(h, 512 * (h - 2), rows).astype(BF)

    def mix_early(rows):
        parts = [back_head(h, 512 * h, rows) for h in (0, 1)] + [w_ref[h, rows].astype(F32) for h in (2, 3)]
        gated = jnp.concatenate(parts, axis=1).astype(BF)
        wide[rows] = jnp.concatenate([gated, jnp.zeros((gated.shape[0], WIDE - VD), BF)], axis=1)

    mixed_grad(2)
    tick()
    row_loop(TOK, 64, mix_late)
    tick()

    ready("qnext", "q")
    docs = Documents(lengths)
    doc_before = docs.of(start - 1)
    doc_last = docs.of(start + TOK - 1)
    place = column(TOK)
    doc_rows = docs.of(place + start)

    def row_factor(h):
        return jnp.where(doc_rows == doc_before, jnp.exp(place.astype(F32) * LOG_GAMMA[h]), 0.0)

    passing = Passing(at, -1, back_state, back_near, back_far, back_join, (pass_send, pass_recv), 0)
    joins = [jnp.where(doc_before == doc_last, math.exp(LOG_GAMMA[h] * TOK), 0.0) for h in (2, 3)]
    for h in (2, 3):
        scaled = (queries[:, h * KEYH : (h + 1) * KEYH].astype(F32) * row_factor(h)).astype(BF)
        back_state[h - 2] = dot_tn(rgrad[h], scaled).astype(BF)
        passing.begin(2 * h - 4)
        passing.begin(2 * h - 3)
    passing.clear()

    mixed_grad(0)
    tick()
    row_loop(TOK, 64, mix_early)
    load("wv", wv_hbm, wo)
    g_halo = pltpu.make_async_remote_copy(
        src_ref=rgrad.at[pl.ds(0, 2), pl.ds(0, HALO)], dst_ref=gnext, send_sem=z_send.at[0], recv_sem=z_recv.at[0],
        device_id=shifted(at, 0, 3), device_id_type=MESH,
    )

    @pl.when(z > 0)
    def _():
        g_halo.start()

    @pl.when(z == 3)
    def _():
        gnext[...] = jnp.zeros((2, HALO, VH), BF)
        qnext[...] = jnp.zeros((HALO, 2 * KEYH), BF)

    pl.semaphore_wait(pair_credit.at[1], 1)
    gate_pair = halves(wide, HALF, y1, 0)
    tick()

    ready("mixed")
    arrived(low_pair)
    for half in (0, 1):
        stage_rows(stage2, dot_tn(x1[...], ch[:, 256 * half : 256 * half + 256]), 2 * half)
    out.start()
    tell_sibling(2)
    passing.forward(0, joins)
    tick()

    ready("first")
    arrived(gate_pair)
    for half in (0, 1):
        stage_columns(stage3, dot_tn(y1[...], x3[:, 512 * half : 512 * half + 512]), 2 * half)
    gate.start()
    passing.forward(1, joins)
    tick()

    ready("wg")
    for half in (0, 1):
        cols = slice(512 * half, 512 * half + 512)
        wf[:, cols] = dot_nn(wide[:, 0:VD], wu[:, cols])
        tick()
    passing.forward(2, joins)

    ready("k", "v", "w01", "w23", "sin", "table")
    grad_v = u_ref

    def finish_query(h, grad):
        queries[:, h * KEYH : (h + 1) * KEYH] = unrotated(grad, table[:, 0:128], table[:, 128:256])

    def finish_key(h, grad):
        cot[:, h * KEYH : (h + 1) * KEYH] = unrotated(grad, table[:, 256:384], table[:, 384:512])

    for h in (2, 3):
        cols_h = slice(h * KEYH, (h + 1) * KEYH)
        score = []
        for b in (0, 1):
            rows, cols = slice(256 * b, 256 * b + 256), 256 * b + 256
            grad = dot_nt(rgrad[h, rows], values[h, HALO : HALO + cols])
            grad = (grad * decay_block(h, 256, cols, 256 * b, 0, start, docs, None)).astype(BF)
            score.append(grad)
        late = dot_tn(score[1], queries[256:512, cols_h])
        early = dot_tn(score[0], queries[0:256, cols_h])
        cot[:, cols_h] = jnp.concatenate([early + late[:256], late[256:]], axis=0).astype(BF)
        query = jnp.concatenate([dot_nn(score[b], keys[HALO : HALO + 256 * b + 256, cols_h]) for b in (0, 1)], axis=0)
        query = query + row_factor(h) * dot_nn(rgrad[h], state_in[h - 2])
        finish_query(h, query)
        late = dot_tn(w23[h - 2, 256:512], rgrad[h, 256:512])
        early = dot_tn(w23[h - 2, 0:256, 0:256], rgrad[h, 0:256])
        grad_v[h] = jnp.concatenate([early + late[:256], late[256:]], axis=0).astype(BF)
        if h == 2:
            passing.forward(3, joins)
        tick()
    @pl.when(z < 3)
    def _():
        g_halo.wait_recv()

    tail = slice(TOK, TOK + HALO)
    for h in (0, 1):
        cols_h = slice(h * KEYH, (h + 1) * KEYH)
        parts_q, parts_k, parts_v = [], [], []
        for b in (0, 1):
            rows, ext = slice(256 * b, 256 * b + 256), slice(256 * b, 256 * b + 384)
            grad = dot_nt(rgrad[h, rows], values[h, ext])
            decay = decay_block(h, 256, 384, 256 * b, 256 * b - HALO, start, docs, windows[0, h])
            grad = (grad * decay).astype(BF)
            parts_q.append(dot_nn(grad, keys[ext, cols_h]))
            parts_k.append(dot_tn(grad, queries[rows, cols_h]))
            parts_v.append(dot_tn(w01[h, b], rgrad[h, rows]))
        decay = decay_block(h, HALO, HALO, TOK, TOK - HALO, start, docs, windows[0, h])
        far_w = (dot_nt(qnext[:, cols_h], keys[tail, cols_h]) * decay).astype(BF)
        far_s = (dot_nt(gnext[h], values[h, tail]) * decay).astype(BF)

        def joined(parts, far):
            return jnp.concatenate(
                [
                    parts[0][HALO : 2 * HALO],
                    parts[0][2 * HALO :] + parts[1][:HALO],
                    parts[1][HALO : 2 * HALO],
                    parts[1][2 * HALO :] + far,
                ],
                axis=0,
            )

        finish_query(h, jnp.concatenate(parts_q, axis=0))
        finish_key(h, joined(parts_k, dot_tn(far_s, qnext[:, cols_h])))
        grad_v[h] = joined(parts_v, dot_tn(far_w, gnext[h])).astype(BF)
        if h == 1:
            query_pair = halves(queries, 512, x2, 0)
        tick()

    passing.finish()
    from_last = docs.of(3 * TOK - 1) == doc_last
    for h in (2, 3):
        cols_h = slice(h * KEYH, (h + 1) * KEYH)
        power = jnp.where(z == 0, math.exp(2 * TOK * LOG_GAMMA[h]), math.exp(TOK * LOG_GAMMA[h]))
        total = back_near[h - 2].astype(F32) + back_far[h - 2].astype(F32) * jnp.where(from_last, power, 0.0)
        state_in[h - 2] = total.astype(BF)
        factor = jnp.where(doc_rows == doc_last, jnp.exp((TOK - place).astype(F32) * LOG_GAMMA[h]), 0.0)
        finish_key(h, cot[:, cols_h].astype(F32) + factor * dot_nn(values[h, HALO:], state_in[h - 2]))
        grad_v[h] = (grad_v[h].astype(F32) + factor * dot_nt(keys[HALO:, cols_h], state_in[h - 2])).astype(BF)
    key_pair = halves(cot, 512, x2, 512)
    tick()


    def store_value(rows):
        parts = [grad_v[h, rows].astype(F32) for h in range(HEADS)]
        joint = jnp.concatenate(parts, axis=1).astype(BF)
        wide[rows] = jnp.concatenate([joint, jnp.zeros((joint.shape[0], WIDE - VD), BF)], axis=1)

    row_loop(TOK, 64, store_value)
    pl.semaphore_wait(pair_credit.at[2], 1)
    value_pair = halves(wide, HALF, x1, 0)
    load("tokens", tokens_hbm, keys.at[pl.ds(0, TOK)])
    tick()

    up.reduced()
    arrived(query_pair)
    arrived(key_pair)
    stage_square(stage1, dot_tn(x3[...], x2[:, 0:512]), 0)
    stage_square(stage1, dot_tn(x3[...], x2[:, 512:1024]), 64)
    qk.start()
    load("wq", wq_hbm, x2)
    tick()
    down.reduced()
    arrived(value_pair)
    for half in (0, 1):
        stage_columns(stage0, dot_tn(x1[:, 0:HALF], x3[:, 512 * half : 512 * half + 512]), 2 * half)
    value.start()
    load("wk", wk_hbm, x3)
    tick()
    ready("wv")
    for half in (0, 1):
        cols = slice(512 * half, 512 * half + 512)
        wf[:, cols] = wf[:, cols] + dot_nn(wide[:, 0:VD], wo[:, cols])
        tick()
    ready("wq", "wk")
    for half in (0, 1):
        cols = slice(512 * half, 512 * half + 512)
        wf[:, cols] = wf[:, cols] + dot_nt(queries[...], x2[cols])
        tick()
    for half in (0, 1):
        cols = slice(512 * half, 512 * half + 512)
        wf[:, cols] = wf[:, cols] + dot_nt(cot[...], x3[cols])
        tick()
    ready("tokens")

    def back_one(i, sums):
        rows = pl.ds(pl.multiple_of(i * 64, 64), 64)
        grad = wf[rows]
        inverse = stats[rows, 1:2]
        scaled = (keys[rows].astype(F32) - stats[rows, 0:1]) * inverse
        e = grad * gain1[...]
        inner = e - jnp.mean(e, axis=-1, keepdims=True) - scaled * jnp.mean(e * scaled, axis=-1, keepdims=True)
        keys[rows] = (hidden[rows] + inverse * inner).astype(BF)
        return (sums[0] + fold(grad * scaled), sums[1] + fold(grad))

    gain_sum, bias_sum = lax.fori_loop(0, TOK // 64, back_one, (zero, zero))
    final = pltpu.make_async_copy(keys.at[pl.ds(0, TOK)], out_tokens, save_sems.at[len(local_copies)])
    final.start()
    vec_rows[0:1] = jnp.sum(gain_sum, axis=0, keepdims=True)
    vec_rows[1:2] = jnp.sum(bias_sum, axis=0, keepdims=True)
    for block in range(4):
        for j in range(4):
            for t in range(2):
                first = 256 * block + 128 * t
                vec[block, 2 * j + t : 2 * j + t + 1] = vec_rows[j : j + 1, first : first + 128]
    vectors = vector_steps(at, vec, vec_core, vec_z, vec_y, vec_x, vec_out, (vec_send, vec_recv), 0)
    next(vectors)
    tick()

    for n in TAIL:
        numbered[n].pump()
        next(vectors, 0)
    todo = [qk, value, gate, out, up, down]
    vectors_open = True
    while todo or vectors_open:
        todo = [unit for unit in todo if unit.pump()]
        vectors_open = next(vectors, 0) is None
    last = pltpu.make_async_copy(vec_out, out_vec, save_sems.at[len(local_copies) + 1])
    last.start()

    @pl.when(z > 0)
    def _():
        g_halo.wait_send()

    passing.drain()
    final.wait()
    last.wait()


def backward(arrays, gain1, gain2, lengths, windows):
    vmem = pl.BlockSpec(memory_space=pltpu.VMEM)
    smem = pl.BlockSpec(memory_space=pltpu.SMEM)
    anywhere = pl.BlockSpec(memory_space=pl.ANY)
    shape = jax.ShapeDtypeStruct
    outs = [shape((TOK, D), BF), shape((8, 128), F32)] + [shape((2, 4, 4, UNIT_ROWS[n], 128), BF) for n in UNITS]
    scratch = [
        pltpu.VMEM((2 * TOK, VD), BF), pltpu.VMEM((2 * TOK, D), BF), pltpu.VMEM((2 * TOK, D), BF), pltpu.VMEM((2 * TOK, HALF), BF),
        pltpu.VMEM((2 * TOK, 512), BF), pltpu.VMEM((TOK, WIDE), BF), pltpu.VMEM((TOK, D), BF), pltpu.VMEM((HEADS, TOK, VH), BF),
        pltpu.VMEM((HEADS, TOK, VH), BF), pltpu.VMEM((HEADS, TOK, VH), BF), pltpu.VMEM((TOK, QK), BF), pltpu.VMEM((HALO + TOK, QK), BF),
        pltpu.VMEM((HEADS, HALO + TOK, VH), BF), pltpu.VMEM((2, 2, 256, 384), BF), pltpu.VMEM((2, TOK, TOK), BF),
        pltpu.VMEM((2, VH, KEYH), BF), pltpu.VMEM((2, VH, KEYH), BF),
        pltpu.VMEM((2, VH, KEYH), BF), pltpu.VMEM((2, VH, KEYH), BF), pltpu.VMEM((2, VH, KEYH), BF),
        pltpu.VMEM((HEADS, TOK, VH), BF), pltpu.VMEM((TOK, D), F32),
        pltpu.VMEM((TOK, D), F32), pltpu.VMEM((VD, D), BF), pltpu.VMEM((VD, D), BF), pltpu.VMEM((TOK, 512), F32),
        pltpu.VMEM((TOK, 128), F32), pltpu.VMEM((HALO, 2 * KEYH), BF), pltpu.VMEM((2, HALO, VH), BF), pltpu.VMEM((8, D), F32),
        pltpu.VMEM((4, 8, 128), F32), pltpu.VMEM((4, 8, 128), F32), pltpu.VMEM((4, 8, 128), F32), pltpu.VMEM((4, 8, 128), F32),
        pltpu.VMEM((4, 8, 128), F32), pltpu.VMEM((8, 128), F32),
    ]
    scratch += [pltpu.VMEM((4, 4, 4, r, 128), BF) for r in SET_ROWS]
    for r in SET_ROWS:
        for count in PART_ROWS[r]:
            scratch += [pltpu.VMEM(s, BF) for s in landing_shapes(count)]
    for name in UNITS:
        scratch += [pltpu.VMEM((count, 128), BF) for count in PART_ROWS[UNIT_ROWS[name]]]
    dma, regular = pltpu.SemaphoreType.DMA, pltpu.SemaphoreType.REGULAR
    scratch += [dma((28,)), dma((8,)), dma((6,)), dma((6,)), dma((4,)), dma((4,)), dma((10,)), dma((10,))]
    scratch += [dma((18 * COPIES,)), dma((18 * COPIES,)), dma((18,)), regular((6,)), regular((3,)), dma((8,)), dma((8,))]
    return pl.pallas_call(
        backward_kernel,
        out_shape=outs,
        in_specs=[anywhere] * 28 + [vmem] * 2 + [smem] * 2,
        out_specs=[anywhere] * len(outs),
        scratch_shapes=scratch,
        compiler_params=pltpu.CompilerParams(collective_id=2, has_side_effects=True, vmem_limit_bytes=62 * 2**20),
        cost_estimate=pl.CostEstimate(flops=26 * 10**9, bytes_accessed=70 * 10**6, transcendentals=10**6),
        name="backward",
    )(*arrays, gain1.reshape(1, D), gain2.reshape(1, D), lengths, windows.reshape(1, HEADS))


def unpack_kernel(down, up, out, gate, value, qk, g_down, g_up, g_out, g_gate, g_value, g_query, g_key):
    for x in range(4):
        cols = slice(128 * x, 128 * x + 128)
        for source, target in ((down, g_down), (out, g_out)):
            target[:, cols] = source[0, 0, x].astype(F32)
        g_query[:, cols] = qk[0, 0, x, 0:64].astype(F32)
        g_key[:, cols] = qk[0, 0, x, 64:128].astype(F32)
        xr, xc = x // 2, x % 2
        for source, target in ((up, g_up), (gate, g_gate), (value, g_value)):
            target[BIG * xr : BIG * xr + BIG, 128 * xc : 128 * xc + 128] = source[0, 0, x].astype(F32)


def unpack(gathered):
    def source(rows):
        return pl.BlockSpec((1, 1, 4, rows, 128), lambda c, y: (c, y, 0, 0, 0))

    tall = pl.BlockSpec((BIG, 512), lambda c, y: (y, c))
    turned = pl.BlockSpec((2 * BIG, 256), lambda c, y: (4 * c + y, 0))
    square = pl.BlockSpec((64, 512), lambda c, y: (y, c))
    shape = jax.ShapeDtypeStruct
    return pl.pallas_call(
        unpack_kernel,
        grid=(2, 4),
        out_shape=[
            shape((VH, D), F32), shape((FF, 256), F32), shape((VH, D), F32), shape((VD, 256), F32), shape((VD, 256), F32),
            shape((256, QK), F32), shape((256, QK), F32),
        ],
        in_specs=[source(UNIT_ROWS[n]) for n in UNITS],
        out_specs=[tall, turned, tall, turned, turned, square, square],
        compiler_params=pltpu.CompilerParams(vmem_limit_bytes=62 * 2**20),
        name="unpack",
    )(*gathered)


def body(
    tokens, ln_gain1, ln_bias1, w_query, w_key, w_value, w_gate, w_out, ln_gain2, ln_bias2, w_up, w_down, doc_lengths, windows, cotangent
):
    table = jnp.asarray(rotary_constants())
    (
        result, first, second, mixed, act, cot_half, lift_half, lift, q, k, v, w01, w23, s_in, heads, u, w, hidden, stats, qnext,
    ) = forward(
        tokens[0], cotangent[0], ln_gain1, ln_bias1, ln_gain2, ln_bias2, doc_lengths, windows, table,
        w_query, w_key, w_value, w_gate, w_out, w_up, w_down,
    )

    def pair(a):
        return a.reshape(2 * TOK, a.shape[2])

    arrays = (
        pair(act), pair(cot_half), pair(lift_half), pair(second), pair(first), pair(mixed), lift, cotangent[0], hidden, stats,
        u, w, heads, q, k, v, w01, w23, s_in, qnext, tokens[0], table,
        w_query, w_key, w_value.T, w_gate.T, w_out, w_up.T,
    )
    grad_tokens, vectors, *gathered = backward(arrays, ln_gain1, ln_gain2, doc_lengths, windows)
    g_down, g_up, g_out, g_gate, g_value, g_query, g_key = unpack(gathered)
    vectors = vectors.reshape(4, 256)
    return (
        result.reshape(1, TOK, D),
        grad_tokens.reshape(1, TOK, D),
        vectors[0],
        vectors[1],
        g_query,
        g_key,
        g_value.T,
        g_gate.T,
        g_out,
        vectors[2],
        vectors[3],
        g_up.T,
        g_down,
    )


def solution(mesh):
    in_specs = (P("batch", "head", None),) + (P(),) * 11 + (P("batch", None), P(), P("batch", "head", None))
    rows, vector = P("head", None), P("head")
    out_specs = (
        P("batch", "head", None), P("batch", "head", None), vector, vector, rows, rows, rows, rows, rows, vector, vector, rows, rows,
    )
    return jax.shard_map(body, mesh=mesh, in_specs=in_specs, out_specs=out_specs, check_vma=False)
```

```python
import functools
import math

import jax
import jax.numpy as jnp
import numpy as np
from jax import lax
from jax.experimental import pallas as pl
from jax.experimental.pallas import tpu as pltpu
from jax.sharding import PartitionSpec as P

D = 1024
HEADS = 4
KEYH = 256
VH = 432
FF = 1728
QK = 1024
VD = 1728
TOK = 512
SEQ = 2048
HALO = 128
WIDE = 1792

epsilon = 1e-05
retention_floor = 1.0
BF = jnp.bfloat16
F32 = jnp.float32
MESH = pl.DeviceIdType.MESH


BIG, PAIRED = 112, 128
CUTS = {BIG: ((0, 48), (48, 32), (80, 32)), PAIRED: ((0, 48), (48, 48), (96, 32))}
ARRIVALS = 7


def coordinates():
    z = lax.axis_index("head")
    b = lax.axis_index("batch")
    return [z, lax.div(b, 8), lax.rem(lax.div(b, 2), 4), lax.rem(b, 2)]


def shifted(at, axis, step):
    place = list(at)
    if axis == 3:
        place[3] = 1 - place[3]
    else:
        place[axis] = lax.rem(place[axis] + step, 4)
    return (place[0], (place[1] * 4 + place[2]) * 2 + place[3])


def away(p, step):
    return lax.rem(p + step, 4)


LOW, HIGH = pl.ds(0, 2), pl.ds(2, 2)


def landing_shapes(r):
    return [(2, 2, 4, r, 128), (2, 4, 4, r, 128), (3, 4, r, 128), (3, r, 128)]


LANDINGS = 4


class Part:
    def __init__(self, at, stage, lands, mine, out, rows, order, gather, sems, slot, credit_in, credit_out, next_order):
        self.at, self.stage, self.out = at, stage, out
        self.first, self.count = rows
        self.lands = [land.at[..., pl.ds(0, self.count), :] for land in lands]
        self.mine = mine.at[pl.ds(0, self.count)]
        self.order, self.gather = order, gather
        send_sems, recv_sems, copy_sems = sems
        self.send_sem, self.copy_sem = send_sems.at[slot], copy_sems.at[slot]
        self.recv_sems = [recv_sems.at[ARRIVALS * slot + n] for n in range(ARRIVALS)]
        self.credit_in, self.credit_out, self.next_order = credit_in, credit_out, next_order

    def copy(self, source, target, axis, step, arrival):
        return pltpu.make_async_remote_copy(
            src_ref=source, dst_ref=target, send_sem=self.send_sem, recv_sem=self.recv_sems[arrival],
            device_id=shifted(self.at, axis, step), device_id_type=MESH,
        )

    def send(self, source, target, axis, step, arrival):
        self.copy(source, target, axis, step, arrival).start()

    def arrived(self, size, arrival):
        whole = self.copy(size, size, 3, 1, arrival)
        whole.wait_recv()
        whole.wait_send()

    def pick(self, axes):
        index = [slice(None)] * 3
        for axis, value in axes.items():
            index[axis] = value
        return self.stage.at[tuple(index) + (pl.ds(self.first, self.count), slice(None))]

    @staticmethod
    def writers(order):
        a1, a2, a3 = order
        return [(a1, 1), (a1, 3)] + [(axis, step) for axis in (a2, a3) for step in (1, 2, 3)]

    def steps(self):
        at, lands = self.at, self.lands
        a1, a2, a3 = self.order
        p1, p2, p3 = at[a1], at[a2], at[a3]
        cut = min(a2, a3)
        if self.credit_in is not None:
            pl.semaphore_wait(self.credit_in, len(self.writers(self.order)))
        self.send(self.pick({a1: away(p1, 2), cut: LOW}), lands[0].at[0], a1, 1, 0)
        self.send(self.pick({a1: away(p1, 2), cut: HIGH}), lands[0].at[1], a1, 3, 0)
        yield
        self.arrived(lands[0], 0)
        for n, step, part in ((0, 1, LOW), (1, 3, HIGH)):
            there = self.pick({a1: away(p1, step), cut: part})
            there[...] = there[...] + lands[0][n]
            self.send(self.pick({a1: away(p1, step)}), lands[1].at[n], a1, step, 1)
        yield
        self.arrived(lands[1], 1)
        own = self.pick({a1: p1})
        own[...] = (own[...].astype(F32) + lands[1][0].astype(F32) + lands[1][1].astype(F32)).astype(BF)
        for s in (1, 2, 3):
            self.send(self.pick({a1: p1, a2: away(p2, s)}), lands[2].at[s - 1], a2, s, 2)
        yield
        self.arrived(lands[2], 2)
        own = self.pick({a1: p1, a2: p2})
        total = own[...].astype(F32)
        for step in range(3):
            total = total + lands[2][step].astype(F32)
        own[...] = total.astype(BF)
        for s in (1, 2, 3):
            self.send(self.pick({a1: p1, a2: p2, a3: away(p3, s)}), lands[3].at[s - 1], a3, s, 3)
        yield
        self.arrived(lands[3], 3)
        total = self.pick({a1: p1, a2: p2, a3: p3})[...].astype(F32)
        for step in range(3):
            total = total + lands[3][step].astype(F32)
        self.mine[...] = total.astype(BF)
        if self.credit_out is not None:
            for axis, step in self.writers(self.next_order):
                pl.semaphore_signal(self.credit_out, inc=1, device_id=shifted(at, axis, step), device_id_type=MESH)

        rows = pl.ds(self.first, self.count)
        g1, g2 = self.gather
        target = self.out.at[at[3], at[1], at[2], rows]
        local = pltpu.make_async_copy(self.mine, target, self.copy_sem)
        local.start()
        for s in (1, 2, 3):
            self.send(self.mine, target, g1, s, 4)
        yield
        self.arrived(lands[3], 4)
        local.wait()

        def block(place):
            if g2 == 1:
                return self.out.at[at[3], place, :, rows]
            return self.out.at[at[3], :, place, rows]

        q = at[g2]
        for s in (1, 2, 3):
            self.send(block(q), block(q), g2, s, 5)
        yield
        self.arrived(lands[2], 5)
        for place in range(4):
            self.send(block(place), block(place), 3, 1, 6)
        yield
        self.arrived(lands[1].at[0], 6)


class Unit:
    RS_STEPS = 5

    def __init__(self, parts):
        self.parts = parts
        self.running = None
        self.done = 0

    def start(self):
        self.running = [part.steps() for part in self.parts]
        self.pump()

    def pump(self, times=1):
        for _ in range(times):
            if not self.running:
                return False
            self.running = [steps for steps in self.running if next(steps, 0) is None]
            self.done += 1
        return bool(self.running)

    def reduced(self):
        while self.done < self.RS_STEPS:
            self.pump()


def vector_steps(at, mine, land_core, land_z, land_y, land_x, final, sems, base):
    send_sems, recv_sems = sems
    slots = iter(range(base, base + 10))

    def send(source, target, axis, step):
        slot = next(slots)
        copy = pltpu.make_async_remote_copy(
            src_ref=source, dst_ref=target, send_sem=send_sems.at[slot], recv_sem=recv_sems.at[slot],
            device_id=shifted(at, axis, step), device_id_type=MESH,
        )
        copy.start()
        return copy

    z, y, x, _ = at
    copies = [send(mine, land_core, 3, 1)]
    yield
    copies[0].wait()
    mine[...] = mine[...] + land_core[...]
    copies = [send(mine.at[away(z, s)], land_z.at[z], 0, s) for s in (1, 2, 3)]
    land_z[z] = mine[z]
    yield
    for axis, here, land in ((1, y, land_y), (2, x, land_x)):
        for copy in copies:
            copy.wait()
        source = land_z if axis == 1 else land_y
        total = (source[0] + source[1]) + (source[2] + source[3])
        land[here] = total
        copies = [send(land.at[here], land.at[here], axis, s) for s in (1, 2, 3)]
        yield
    for copy in copies:
        copy.wait()
    final[...] = (land_x[0] + land_x[1]) + (land_x[2] + land_x[3])


def greet(at):
    barrier = pltpu.get_barrier_semaphore()
    partners = [(axis, step) for axis in (0, 1, 2) for step in (1, 2, 3)] + [(3, 1)]
    for axis, step in partners:
        pl.semaphore_signal(barrier, inc=1, device_id=shifted(at, axis, step), device_id_type=MESH)
    pl.semaphore_wait(barrier, len(partners))


class Passing:
    PIECES = ((0, 0), (0, 1), (1, 0), (1, 1))

    def __init__(self, at, way, own, near, far, joined, sems, base):
        self.at, self.way = at, way
        self.rank = at[0] if way == 1 else 3 - at[0]
        self.own, self.near, self.far, self.joined = own, near, far, joined
        self.send_sems, self.recv_sems = sems
        self.base = base

    ROWS = (slice(0, 224), slice(224, VH))

    def piece(self, ref, p):
        head, half = self.PIECES[p]
        rows = self.ROWS[half]
        return ref.at[head, pl.ds(rows.start, rows.stop - rows.start)]

    def copy(self, source, target, p, kind):
        step = {0: self.way, 1: -self.way, 2: -self.way}[kind] % 4
        slot = self.base + 4 * min(kind, 1) + p
        return pltpu.make_async_remote_copy(
            src_ref=self.piece(source, p), dst_ref=self.piece(target, p), send_sem=self.send_sems.at[slot],
            recv_sem=self.recv_sems.at[slot], device_id=shifted(self.at, 0, step), device_id_type=MESH,
        )

    def clear(self):
        @pl.when(self.rank == 0)
        def _():
            self.near[...] = jnp.zeros(self.near.shape, BF)

        @pl.when(self.rank < 2)
        def _():
            self.far[...] = jnp.zeros(self.far.shape, BF)

    def begin(self, p):
        @pl.when(self.rank < 2)
        def _():
            self.copy(self.own, self.near, p, 0).start()

        @pl.when(self.rank == 0)
        def _():
            self.copy(self.own, self.far, p, 1).start()

    def forward(self, p, decay):
        head, half = self.PIECES[p]
        rows = self.ROWS[half]

        @pl.when(self.rank == 2)
        def _():
            self.copy(self.own, self.near, p, 0).wait_recv()
            total = self.own[head, rows].astype(F32) + self.near[head, rows].astype(F32) * decay[head]
            self.joined[head, rows] = total.astype(BF)
            self.copy(self.joined, self.near, p, 0).start()

        @pl.when(self.rank == 3)
        def _():
            self.copy(self.far, self.far, p, 1).wait_recv()
            self.copy(self.far, self.far, p, 2).start()

    def finish(self):
        for p in range(4):

            @pl.when((self.rank == 1) | (self.rank == 3))
            def _():
                self.copy(self.own, self.near, p, 0).wait_recv()

            @pl.when(self.rank == 2)
            def _():
                self.copy(self.far, self.far, p, 1).wait_recv()

    def drain(self):
        for p in range(4):

            @pl.when(self.rank < 3)
            def _():
                self.copy(self.own, self.near, p, 0).wait_send()

            @pl.when((self.rank == 0) | (self.rank == 3))
            def _():
                self.copy(self.own, self.far, p, 1).wait_send()


LOG_GAMMA = tuple(math.log(1.0 - 2.0 ** (-5.0 - h)) for h in range(HEADS))
HALF = WIDE // 2


def rotary_constants():
    half = KEYH // 2
    ladder = np.arange(half, dtype=np.float64)
    theta = 10000.0 ** (-ladder / half)
    place = np.arange(SEQ, dtype=np.float64)[:, None]
    zeta = (2.0 * ladder + 0.4 * KEYH) / (1.4 * KEYH)
    grow = zeta[None, :] ** (place / 512.0)
    cosine, sine = np.cos(place * theta), np.sin(place * theta)
    small = KEYH ** (-0.5)
    table = np.concatenate([cosine * grow, sine * grow, cosine / grow * small, sine / grow * small], axis=1)
    return np.concatenate([np.zeros((HALO, 4 * half)), table]).astype(np.float32)


def dot_nn(a, b):
    return lax.dot_general(a, b, (((1,), (0,)), ((), ())), preferred_element_type=F32)


def dot_nt(a, b):
    return lax.dot_general(a, b, (((1,), (1,)), ((), ())), preferred_element_type=F32)


def dot_tn(a, b):
    return lax.dot_general(a, b, (((0,), (0,)), ((), ())), preferred_element_type=F32)


def row_loop(total, step, work):
    def one(i, carry):
        work(pl.ds(pl.multiple_of(i * step, step), step))
        return carry

    lax.fori_loop(0, total // step, one, 0)


class Documents:
    def __init__(self, lengths_ref):
        ends = []
        total = 0
        for i in range(5):
            total = total + lengths_ref[0, i]
            ends.append(total)
        self.ends = ends

    def of(self, where):
        found = jnp.zeros(where.shape, jnp.int32) if hasattr(where, "shape") and where.shape else 0
        for end in self.ends:
            found = found + jnp.where(where >= end, 1, 0)
        return found


def column(count, first=0):
    return lax.broadcasted_iota(jnp.int32, (count, 1), 0) + first


def line(count, first=0):
    return lax.broadcasted_iota(jnp.int32, (1, count), 1) + first


def decay_block(h, rows, cols, row_first, col_first, start, docs, window):
    i, j = column(rows, row_first), line(cols, col_first)
    base = min(row_first, col_first)
    seen = (i >= j) & (docs.of(i + start) == docs.of(j + start))
    if window is not None:
        seen = seen & (i - j < window)
    if col_first < 0:
        seen = seen & (j + start >= 0)
    down = jnp.exp((i - base).astype(F32) * LOG_GAMMA[h])
    up = jnp.exp((j - base).astype(F32) * (-LOG_GAMMA[h]))
    return jnp.where(seen, down * up, 0.0)


def rotated(raw, cosine, sine):
    front, behind = raw[:, :128], raw[:, 128:]
    return jnp.concatenate([front * cosine - behind * sine, front * sine + behind * cosine], axis=1)


def forward_kernel(
    tokens_hbm, cot_hbm, gain1, bias1, gain2, bias2, lengths, windows, table_hbm,
    wq_hbm, wk_hbm, wv_hbm, wg_hbm, wo_hbm, wu_hbm, wd_hbm,
    out_result, out_first, out_second, out_mixed, out_act, out_cot, out_lhalf, out_lift,
    out_q, out_k, out_v, out_w01, out_w23, out_sin, out_heads, out_u, out_w, out_hidden, out_stats, out_qnext,
    tokens, cot, table, wq, wk, wv, wg, wo, wu, wd,
    first, queries, keys, values, wide_f32, down_grad, kept, w01, w23, state, state_near, state_far, state_join, state_in,
    heads, u_ref, w_ref, mixed, hidden, second, lift, act, stats,
    load_sems, save_sems, send_sems, recv_sems, pass_send, pass_recv,
):
    at = coordinates()
    z, core = at[0], at[3]
    start = z * TOK
    loads = {}
    for slot, (name, source, target) in enumerate(
        [
            ("tokens", tokens_hbm, tokens.at[pl.ds(HALO, TOK)]),
            ("wk", wk_hbm, wk),
            ("table", table_hbm.at[pl.ds(pl.multiple_of(z * TOK, TOK), HALO + TOK)], table),
            ("wv", wv_hbm, wv),
            ("wq", wq_hbm, wq),
            ("wg", wg_hbm, wg),
            ("cot", cot_hbm, cot),
            ("wd", wd_hbm, wd),
            ("wo", wo_hbm, wo),
            ("wu", wu_hbm, wu),
        ]
    ):
        loads[name] = pltpu.make_async_copy(source, target, load_sems.at[slot])
        loads[name].start()
    partners = [(3, 1), (0, 1), (0, 3)]
    barrier = pltpu.get_barrier_semaphore()
    for axis, step in partners:
        pl.semaphore_signal(barrier, inc=1, device_id=shifted(at, axis, step), device_id_type=MESH)

    saves, sends = [], []

    def save(source, target):
        copy = pltpu.make_async_copy(source, target, save_sems.at[len(saves)])
        copy.start()
        saves.append(copy)

    def remote(source, target, axis, step):
        slot = len(sends)
        copy = pltpu.make_async_remote_copy(
            src_ref=source, dst_ref=target, send_sem=send_sems.at[slot], recv_sem=recv_sems.at[slot],
            device_id=shifted(at, axis, step), device_id_type=MESH,
        )
        sends.append(copy)
        return copy

    def share(source, target):
        save(source, target.at[core])
        remote(source, target.at[core], 3, 1).start()
        return (saves[-1], sends[-1])

    loads["tokens"].wait()

    pl.semaphore_wait(barrier, len(partners))
    t_halo = remote(tokens.at[pl.ds(TOK, HALO)], tokens.at[pl.ds(0, HALO)], 0, 1)

    @pl.when(z < 3)
    def _():
        t_halo.start()

    @pl.when(z == 0)
    def _():
        tokens[0:HALO] = jnp.zeros((HALO, D), BF)

    def normalized(x):
        mean = jnp.mean(x, axis=-1, keepdims=True)
        center = x - mean
        inverse = lax.rsqrt(jnp.mean(center * center, axis=-1, keepdims=True) + epsilon)
        return center * inverse, mean, inverse

    def norm_one(i, carry):
        rows = pl.ds(pl.multiple_of(i * 64, 64), 64)
        scaled, mean, inverse = normalized(tokens[pl.ds(HALO + i * 64, 64)].astype(F32))
        first[pl.ds(HALO + i * 64, 64)] = (scaled * gain1[...] + bias1[...]).astype(BF)
        stats[rows, 0:1] = mean
        stats[rows, 1:2] = inverse
        return carry

    lax.fori_loop(0, TOK // 64, norm_one, 0)
    share(first.at[pl.ds(HALO, TOK)], out_first)

    docs = Documents(lengths)
    doc_before = docs.of(start - 1)
    doc_last = docs.of(start + TOK - 1)
    place = column(TOK)
    doc_rows = docs.of(place + start)

    def project(h, begin):
        cols = slice(h * KEYH, (h + 1) * KEYH)
        raw = dot_nn(first[begin:], wk[:, cols])
        keys[begin:, cols] = rotated(raw, table[begin:, 256:384], table[begin:, 384:512]).astype(BF)
        values[h, begin:] = dot_nt(first[begin:], wv[h * VH : (h + 1) * VH]).astype(BF)

    loads["wk"].wait()
    loads["table"].wait()
    loads["wv"].wait()
    passing = Passing(at, 1, state, state_near, state_far, state_join, (pass_send, pass_recv), 0)
    joins = [jnp.where(doc_before == doc_last, math.exp(LOG_GAMMA[h] * TOK), 0.0) for h in (2, 3)]
    for h in (2, 3):
        project(h, HALO)
        factor = jnp.where(doc_rows == doc_last, jnp.exp((TOK - place).astype(F32) * LOG_GAMMA[h]), 0.0)
        scaled = (keys[HALO:, h * KEYH : (h + 1) * KEYH].astype(F32) * factor).astype(BF)
        state[h - 2] = dot_tn(values[h, HALO:], scaled).astype(BF)
        passing.begin(2 * h - 4)
        passing.begin(2 * h - 3)
    passing.clear()
    loads["wq"].wait()
    for h in range(HEADS):
        raw = dot_nn(first[HALO:], wq[:, h * KEYH : (h + 1) * KEYH])
        queries[:, h * KEYH : (h + 1) * KEYH] = rotated(raw, table[HALO:, 0:128], table[HALO:, 128:256]).astype(BF)
    save(queries, out_q)
    q_halo = remote(queries.at[pl.ds(0, HALO), pl.ds(0, 2 * KEYH)], out_qnext, 0, 3)

    @pl.when(z > 0)
    def _():
        q_halo.start()

    loads["wg"].wait()
    passing.forward(0, joins)
    for h in range(HEADS):
        wide_f32[:, 0:VH] = dot_nt(first[HALO:], wg[h * VH : (h + 1) * VH])

        def swish(rows):
            gate = wide_f32[rows, 0:VH]
            sigma = 0.5 * jnp.tanh(0.5 * gate) + 0.5
            u_ref[h, rows] = (gate * sigma).astype(BF)
            w_ref[h, rows] = (sigma * (1.0 + gate * (1.0 - sigma))).astype(BF)

        row_loop(TOK, 128, swish)
        if h == 1:
            passing.forward(1, joins)
    save(u_ref, out_u)
    save(w_ref, out_w)
    loads["cot"].wait()
    save(cot.at[:, pl.ds(pl.multiple_of(core * 512, 512), 512)], out_cot.at[core])
    remote(cot.at[:, pl.ds(pl.multiple_of((1 - core) * 512, 512), 512)], out_cot.at[core], 3, 1).start()
    loads["wd"].wait()
    down_grad[...] = dot_nt(cot[...], wd[...]).astype(BF)
    passing.forward(2, joins)

    for h in (2, 3):
        for b in (0, 1):
            rows, cols = slice(256 * b, 256 * b + 256), 256 * b + 256
            q_h = queries[rows, h * KEYH : (h + 1) * KEYH]
            scores = dot_nt(q_h, keys[HALO : HALO + cols, h * KEYH : (h + 1) * KEYH])
            weight = (scores * decay_block(h, 256, cols, 256 * b, 0, start, docs, None)).astype(BF)
            w23[h - 2, rows, 0:cols] = weight
            kept[h, rows] = dot_nn(weight, values[h, HALO : HALO + cols])

    passing.forward(3, joins)

    @pl.when(z > 0)
    def _():
        t_halo.wait_recv()

    for block in (slice(0, 64), slice(64, 128)):
        first[block] = (normalized(tokens[block].astype(F32))[0] * gain1[...] + bias1[...]).astype(BF)
    for h in (0, 1):
        project(h, 0)

    save(keys, out_k)
    save(values, out_v)
    for h in (0, 1):
        for b in (0, 1):
            rows = slice(256 * b, 256 * b + 256)
            q_h = queries[rows, h * KEYH : (h + 1) * KEYH]
            scores = dot_nt(q_h, keys[256 * b : 256 * b + 384, h * KEYH : (h + 1) * KEYH])
            decay = decay_block(h, 256, 384, 256 * b, 256 * b - HALO, start, docs, windows[0, h])
            weight = (scores * decay).astype(BF)
            w01[h, b] = weight
            kept[h, rows] = dot_nn(weight, values[h, 256 * b : 256 * b + 384])
    save(w01, out_w01)
    save(w23, out_w23)

    passing.finish()
    from_first = docs.of(TOK - 1) == doc_before
    for h in (2, 3):
        power = jnp.where(z == 3, math.exp(2 * TOK * LOG_GAMMA[h]), math.exp(TOK * LOG_GAMMA[h]))
        total = state_near[h - 2].astype(F32) + state_far[h - 2].astype(F32) * jnp.where(from_first, power, 0.0)
        state_in[h - 2] = total.astype(BF)
        factor = jnp.where(doc_rows == doc_before, jnp.exp(place.astype(F32) * LOG_GAMMA[h]), 0.0)
        kept[h] = kept[h] + factor * dot_nt(queries[:, h * KEYH : (h + 1) * KEYH], state_in[h - 2])
    save(state_in, out_sin)

    def mix(rows):
        parts = []
        for h in range(HEADS):
            x = kept[h, rows]
            center = x - jnp.mean(x, axis=-1, keepdims=True)
            inverse = lax.rsqrt(jnp.mean(center * center, axis=-1, keepdims=True) + retention_floor)
            stats[rows, 4 + h : 5 + h] = inverse
            low = (center * inverse).astype(BF)
            heads[h, rows] = low
            parts.append(low.astype(F32) * u_ref[h, rows].astype(F32))
        mixed[rows] = jnp.concatenate(parts, axis=1).astype(BF)

    row_loop(TOK, 64, mix)
    mixed_away = share(mixed, out_mixed)
    save(heads, out_heads)

    loads["wo"].wait()
    hidden[...] = dot_nn(mixed[...], wo[...])

    def norm_two(i, carry):
        rows = pl.ds(pl.multiple_of(i * 64, 64), 64)
        x = hidden[rows] + tokens[pl.ds(HALO + i * 64, 64)].astype(F32)
        hidden[rows] = x
        scaled, mean, inverse = normalized(x)
        second[rows] = (scaled * gain2[...] + bias2[...]).astype(BF)
        stats[rows, 2:3] = mean
        stats[rows, 3:4] = inverse
        return carry

    lax.fori_loop(0, TOK // 64, norm_two, 0)
    share(second, out_second)
    save(hidden, out_hidden)
    save(stats, out_stats)

    loads["wu"].wait()
    for first_col in range(0, FF, 256):
        width = min(256, FF - first_col)
        cols = slice(first_col, first_col + width)
        wide_f32[:, cols] = dot_nt(second[...], wu[cols])

    def activate(rows):
        x = wide_f32[rows]
        phi = 0.5 * (1.0 + lax.erf(x * math.sqrt(0.5)))
        slope = phi + x * jnp.exp(-0.5 * x * x) * (1.0 / math.sqrt(2.0 * math.pi))
        act[rows] = (x * phi).astype(BF)
        grad = (down_grad[rows].astype(F32) * slope).astype(BF)
        lift[rows] = jnp.concatenate([grad, jnp.zeros((grad.shape[0], WIDE - FF), BF)], axis=1)

    row_loop(TOK, 32, activate)
    share(act, out_act)
    save(lift, out_lift)
    save(lift.at[:, pl.ds(pl.multiple_of(core * HALF, HALF), HALF)], out_lhalf.at[core])
    remote(lift.at[:, pl.ds(pl.multiple_of((1 - core) * HALF, HALF), HALF)], out_lhalf.at[core], 3, 1).start()
    for copy in mixed_away:
        copy.wait()
    mixed[:, 0:D] = (hidden[...] + dot_nn(act[...], wd[...])).astype(BF)
    save(mixed.at[:, pl.ds(0, D)], out_result)

    for copy in sends:
        if not any(copy is other for other in (t_halo, q_halo) + mixed_away):
            copy.wait()

    @pl.when(z > 0)
    def _():
        q_halo.wait_send()

    @pl.when(z < 3)
    def _():
        q_halo.wait_recv()
        t_halo.wait_send()

    passing.drain()
    for copy in saves:
        if copy is not mixed_away[0]:
            copy.wait()


def forward(tokens, cot, gain1, bias1, gain2, bias2, lengths, windows, table, wq, wk, wv, wg, wo, wu, wd):
    vmem = pl.BlockSpec(memory_space=pltpu.VMEM)
    smem = pl.BlockSpec(memory_space=pltpu.SMEM)
    anywhere = pl.BlockSpec(memory_space=pl.ANY)
    shape = jax.ShapeDtypeStruct
    outs = [
        shape((TOK, D), BF), shape((2, TOK, D), BF), shape((2, TOK, D), BF), shape((2, TOK, VD), BF), shape((2, TOK, FF), BF),
        shape((2, TOK, 512), BF), shape((2, TOK, HALF), BF), shape((TOK, WIDE), BF),
        shape((TOK, QK), BF), shape((HALO + TOK, QK), BF), shape((HEADS, HALO + TOK, VH), BF),
        shape((2, 2, 256, 384), BF), shape((2, TOK, TOK), BF), shape((2, VH, KEYH), BF),
        shape((HEADS, TOK, VH), BF), shape((HEADS, TOK, VH), BF), shape((HEADS, TOK, VH), BF), shape((TOK, D), F32), shape((TOK, 128), F32),
        shape((HALO, 2 * KEYH), BF),
    ]
    scratch = [
        pltpu.VMEM((HALO + TOK, D), BF), pltpu.VMEM((TOK, D), BF), pltpu.VMEM((HALO + TOK, 512), F32),
        pltpu.VMEM((D, QK), BF), pltpu.VMEM((D, QK), BF), pltpu.VMEM((VD, D), BF), pltpu.VMEM((VD, D), BF),
        pltpu.VMEM((VD, D), BF), pltpu.VMEM((FF, D), BF), pltpu.VMEM((FF, D), BF),
        pltpu.VMEM((HALO + TOK, D), BF), pltpu.VMEM((TOK, QK), BF), pltpu.VMEM((HALO + TOK, QK), BF),
        pltpu.VMEM((HEADS, HALO + TOK, VH), BF), pltpu.VMEM((TOK, FF), F32), pltpu.VMEM((TOK, FF), BF),
        pltpu.VMEM((HEADS, TOK, VH), F32), pltpu.VMEM((2, 2, 256, 384), BF), pltpu.VMEM((2, TOK, TOK), BF),
        pltpu.VMEM((2, VH, KEYH), BF), pltpu.VMEM((2, VH, KEYH), BF), pltpu.VMEM((2, VH, KEYH), BF), pltpu.VMEM((2, VH, KEYH), BF),
        pltpu.VMEM((2, VH, KEYH), BF),
        pltpu.VMEM((HEADS, TOK, VH), BF), pltpu.VMEM((HEADS, TOK, VH), BF), pltpu.VMEM((HEADS, TOK, VH), BF), pltpu.VMEM((TOK, VD), BF),
        pltpu.VMEM((TOK, D), F32), pltpu.VMEM((TOK, D), BF), pltpu.VMEM((TOK, WIDE), BF), pltpu.VMEM((TOK, FF), BF),
        pltpu.VMEM((TOK, 128), F32),
        pltpu.SemaphoreType.DMA((10,)), pltpu.SemaphoreType.DMA((20,)),
        pltpu.SemaphoreType.DMA((16,)), pltpu.SemaphoreType.DMA((16,)),
        pltpu.SemaphoreType.DMA((8,)), pltpu.SemaphoreType.DMA((8,)),
    ]
    return pl.pallas_call(
        forward_kernel,
        out_shape=outs,
        in_specs=[anywhere] * 2 + [vmem] * 4 + [smem] * 2 + [anywhere] * 8,
        out_specs=[anywhere] * len(outs),
        scratch_shapes=scratch,
        compiler_params=pltpu.CompilerParams(collective_id=1, has_side_effects=True, vmem_limit_bytes=62 * 2**20),
        cost_estimate=pl.CostEstimate(flops=14 * 10**9, bytes_accessed=50 * 10**6, transcendentals=2 * 10**6),
        name="forward",
    )(
        tokens, cot, gain1.reshape(1, D), bias1.reshape(1, D), gain2.reshape(1, D), bias2.reshape(1, D),
        lengths, windows.reshape(1, HEADS), table, wq, wk, wv.T, wg.T, wo, wu.T, wd,
    )


UNITS = ("down", "up", "out", "gate", "value", "qk")
UNIT_ROWS = {"down": BIG, "up": BIG, "out": BIG, "gate": BIG, "value": BIG, "qk": PAIRED}
UNIT_SET = {"down": 0, "up": 1, "out": 2, "gate": 3, "value": 0, "qk": 1}
SET_ROWS = (BIG, PAIRED, BIG, BIG)
FOLLOWER = {"down": "value", "up": "qk"}
PLAN = {
    "down": (((1, 2, 0), (1, 2)), ((2, 1, 0), (2, 1)), ((0, 2, 1), (1, 2))),
    "up": (((2, 1, 0), (1, 2)), ((1, 2, 0), (2, 1)), ((1, 2, 0), (2, 1))),
    "out": (((1, 0, 2), (2, 1)), ((2, 1, 0), (1, 2)), ((2, 0, 1), (1, 2))),
    "gate": (((2, 0, 1), (2, 1)), ((1, 2, 0), (1, 2)), ((1, 0, 2), (1, 2))),
    "value": (((0, 2, 1), (1, 2)), ((2, 1, 0), (2, 1)), ((2, 1, 0), (2, 1))),
    "qk": (((0, 1, 2), (2, 1)), ((1, 0, 2), (1, 2)), ((1, 2, 0), (1, 2))),
}
BLOCKS = (
    "up", "down", "second", "norm2", "mixl", "states", "mixe", "fg", "gate", "out", "full", "band", "cross", "store", "qk", "value", "fq", "fv", "fk", "n1",
)
SCHEDULE = (
    (), (), (), (), (1,), (0,), (), (), (), (1,), (6,), (), (7, 0), (8, 9, 1), (3,), (), (0,), (2,), (1,), (3, 0), (), (), (2,), (), (1,), (5, 3, 0), (), (4,), (),
)
TAIL = (1, 2, 1, 5, 3, 4, 0, 2, 5, 0, 3, 4, 5, 2, 4, 3, 5, 3, 2, 4, 2, 5, 4, 5, 4)
PART_ROWS = {rows: tuple(count for _, count in cuts) for rows, cuts in CUTS.items()}


def stage_rows(stage, result, first_x):
    for z in range(4):
        for y in range(4):
            n = min(BIG, VH - BIG * y)
            for i in range(result.shape[1] // 128):
                piece = result[VH * z + BIG * y : VH * z + BIG * y + n, 128 * i : 128 * i + 128].astype(BF)
                stage[z, y, first_x + i, 0:n] = piece
                if n < BIG:
                    stage[z, y, first_x + i, n:BIG] = jnp.zeros((BIG - n, 128), BF)


def stage_columns(stage, result, first_z):
    for i in range(result.shape[1] // 128):
        z, xc = first_z + i // 2, i % 2
        for y in range(4):
            for xr in range(2):
                first = 224 * y + BIG * xr
                stage[z, y, 2 * xr + xc, 0:BIG] = result[first : first + BIG, 128 * i : 128 * i + 128].astype(BF)


def stage_square(stage, result, first_row):
    for z in range(4):
        for y in range(4):
            for x in range(4):
                piece = result[256 * z + 64 * y : 256 * z + 64 * y + 64, 128 * x : 128 * x + 128].astype(BF)
                stage[z, y, x, first_row : first_row + 64] = piece


def fold(rows):
    return jnp.sum(rows.reshape(rows.shape[0] // 8, 8, rows.shape[1]), axis=0)


def unrotated(grad, cosine, sine):
    grad = grad.astype(BF).astype(F32)
    front, behind = grad[:, :128], grad[:, 128:]
    return jnp.concatenate([front * cosine + behind * sine, behind * cosine - front * sine], axis=1).astype(BF)


def backward_kernel(
    act_hbm, coth_hbm, lhalf_hbm, second_hbm, first_hbm, mixed_hbm, lift_hbm, cot_hbm, hidden_hbm, stats_hbm,
    u_hbm, w_hbm, heads_hbm, q_hbm, k_hbm, v_hbm, w01_hbm, w23_hbm, sin_hbm, qnext_hbm, tokens_hbm, table_hbm,
    wq_hbm, wk_hbm, wv_hbm, wg_hbm, wo_hbm, wu_hbm, gain1, gain2, lengths, windows,
    out_tokens, out_vec, out_down, out_up, out_out, out_gate, out_value, out_qk,
    x1, x2, x3, y1, ch, wide, cot, heads, u_ref, w_ref, queries, keys, values, w01, w23, state_in,
    back_state, back_near, back_far, back_join, rgrad, hidden, wf, wu, wo, table, stats, qnext, gnext, vec_rows,
    vec, vec_core, vec_z, vec_y, vec_x, vec_out,
    stage0, stage1, stage2, stage3, *rest,
):
    lands = [[rest[(3 * s + p) * LANDINGS : (3 * s + p + 1) * LANDINGS] for p in range(3)] for s in range(4)]
    rest = rest[12 * LANDINGS :]
    mines = rest[0:18]
    load_sems, save_sems, pair_send, pair_recv, z_send, z_recv, vec_send, vec_recv = rest[18:26]
    unit_send, unit_recv, unit_copy, credits, pair_credit, pass_send, pass_recv = rest[26:]
    stages = (stage0, stage1, stage2, stage3)
    at = coordinates()
    z, core = at[0], at[3]
    start = z * TOK

    loading = {}

    def load(name, source, target):
        copy = pltpu.make_async_copy(source, target, load_sems.at[len(loading)])
        copy.start()
        loading[name] = copy

    def ready(*names):
        for name in names:
            loading[name].wait()

    waited = set()

    def ready_once(*names):
        for name in names:
            if name not in waited:
                waited.add(name)
                loading[name].wait()

    load("act", act_hbm, x1)
    load("coth", coth_hbm, ch)
    load("lhalf", lhalf_hbm, y1)
    load("second", second_hbm, x2)
    load("lift", lift_hbm, wide)
    load("wu", wu_hbm, wu)
    greet(at)

    outs = dict(zip(UNITS, (out_down, out_up, out_out, out_gate, out_value, out_qk)))
    units = {}
    for n, name in enumerate(UNITS):
        s, parts = UNIT_SET[name], []
        for p in range(3):
            slot = 3 * n + p
            order, gather = PLAN[name][p]
            follower = FOLLOWER.get(name)
            parts.append(
                Part(
                    at, stages[s], lands[s][p], mines[slot], outs[name], CUTS[UNIT_ROWS[name]][p], order, gather,
                    (unit_send, unit_recv, unit_copy), slot,
                    credits.at[slot - 12] if n >= 4 else None, credits.at[slot] if follower else None,
                    PLAN[follower][p][0] if follower else None,
                )
            )
        units[name] = Unit(parts)
    down, up, out, gate, value, qk = (units[name] for name in UNITS)
    numbered = [units[name] for name in UNITS]
    ticks = iter(SCHEDULE)

    def tick():
        for n in next(ticks):
            if n < len(UNITS):
                numbered[n].pump()
            else:
                passing.forward(n - len(UNITS), joins)

    pairs = []

    def to_sibling(source, target):
        copy = pltpu.make_async_remote_copy(
            src_ref=source, dst_ref=target, send_sem=pair_send.at[len(pairs)], recv_sem=pair_recv.at[len(pairs)],
            device_id=shifted(at, 3, 1), device_id_type=MESH,
        )
        copy.start()
        pairs.append(copy)
        return copy

    local_copies = []

    def halves(source, width, landing, lane):
        rows = pl.ds(pl.multiple_of(core * TOK, TOK), TOK)
        lanes = pl.ds(lane, width)
        mine = source.at[:, pl.ds(pl.multiple_of(core * width, width), width)]
        other = source.at[:, pl.ds(pl.multiple_of((1 - core) * width, width), width)]
        remote = to_sibling(other, landing.at[rows, lanes])
        local = pltpu.make_async_copy(mine, landing.at[rows, lanes], save_sems.at[len(local_copies)])
        local.start()
        local_copies.append(local)
        return remote, local

    def arrived(pair):
        pair[0].wait()
        pair[1].wait()

    def tell_sibling(slot):
        pl.semaphore_signal(pair_credit.at[slot], inc=1, device_id=shifted(at, 3, 1), device_id_type=MESH)

    docs = Documents(lengths)
    doc_before = docs.of(start - 1)
    doc_last = docs.of(start + TOK - 1)
    place = column(TOK)
    doc_rows = docs.of(place + start)
    joins = [jnp.where(doc_before == doc_last, math.exp(LOG_GAMMA[h] * TOK), 0.0) for h in (2, 3)]
    passing = Passing(at, -1, back_state, back_near, back_far, back_join, (pass_send, pass_recv), 0)
    zero = jnp.zeros((8, D), F32)
    grad_v = u_ref
    pair = {}
    g_halo = pltpu.make_async_remote_copy(
        src_ref=rgrad.at[pl.ds(0, 2), pl.ds(0, HALO)], dst_ref=gnext, send_sem=z_send.at[0], recv_sem=z_recv.at[0],
        device_id=shifted(at, 0, 3), device_id_type=MESH,
    )

    def head_cols(h):
        return slice(h * KEYH, (h + 1) * KEYH)

    def row_factor(h):
        return jnp.where(doc_rows == doc_before, jnp.exp(place.astype(F32) * LOG_GAMMA[h]), 0.0)

    def two_halves(work):
        for half in (0, 1):
            cols = slice(512 * half, 512 * half + 512)
            wf[:, cols] = work(cols)
            tick()

    def block_down():
        ready("act", "coth")
        for half in (0, 1):
            stage_rows(stage0, dot_tn(x1[...], ch[:, 256 * half : 256 * half + 256]), 2 * half)
        down.start()
        load("mixed", mixed_hbm, x1)
        tell_sibling(0)
        tick()

    def block_up():
        ready("lhalf", "second")
        for half in (0, 1):
            stage_columns(stage1, dot_tn(y1[...], x2[:, 512 * half : 512 * half + 512]), 2 * half)
        up.start()
        tell_sibling(1)
        tick()

    def block_second():
        ready("lift", "wu")
        two_halves(lambda cols: dot_nn(wide[:, 0:FF], wu[:, cols]))
        load("wg", wg_hbm, wu)

    def block_norm2():
        ready("cot", "hidden", "stats")

        def back_two(i, sums):
            rows = pl.ds(pl.multiple_of(i * 64, 64), 64)
            grad = wf[rows]
            inverse = stats[rows, 3:4]
            scaled = (hidden[rows] - stats[rows, 2:3]) * inverse
            e = grad * gain2[...]
            inner = e - jnp.mean(e, axis=-1, keepdims=True) - scaled * jnp.mean(e * scaled, axis=-1, keepdims=True)
            total = cot[rows].astype(F32) + inverse * inner
            hidden[rows] = total
            cot[rows] = total.astype(BF)
            return (sums[0] + fold(grad * scaled), sums[1] + fold(grad))

        gain_sum, bias_sum = lax.fori_loop(0, TOK // 64, back_two, (zero, zero))
        pl.semaphore_wait(pair_credit.at[0], 1)
        pair["low"] = halves(cot, 512, ch, 0)
        vec_rows[2:3] = jnp.sum(gain_sum, axis=0, keepdims=True)
        vec_rows[3:4] = jnp.sum(bias_sum, axis=0, keepdims=True)
        tick()

    def mixed_grad(first_head):
        ready_once("wo", "u", "w", "heads")
        for h in (first_head, first_head + 1):
            lane = 512 * (h - first_head)
            wf[:, lane : lane + VH] = dot_nt(cot[...], wo[h * VH : (h + 1) * VH])

    def back_head(h, lane, rows):
        grad = wf[rows, lane : lane + VH]
        c = heads[h, rows].astype(F32)
        gated = grad * c * w_ref[h, rows].astype(F32)
        e = (grad * u_ref[h, rows].astype(F32)).astype(BF).astype(F32)
        inner = e - jnp.mean(e, axis=-1, keepdims=True) - c * jnp.mean(e * c, axis=-1, keepdims=True)
        rgrad[h, rows] = (inner * stats[rows, 4 + h : 5 + h]).astype(BF)
        return gated

    def block_mixl():
        def mix_late(rows):
            for h in (2, 3):
                w_ref[h, rows] = back_head(h, 512 * (h - 2), rows).astype(BF)

        mixed_grad(2)
        tick()
        row_loop(TOK, 64, mix_late)
        tick()

    def block_states():
        ready("q")
        for h in (2, 3):
            scaled = (queries[:, head_cols(h)].astype(F32) * row_factor(h)).astype(BF)
            back_state[h - 2] = dot_tn(rgrad[h], scaled).astype(BF)
            passing.begin(2 * h - 4)
            passing.begin(2 * h - 3)
        passing.clear()
        tick()

    def block_mixe():
        def mix_early(rows):
            parts = [back_head(h, 512 * h, rows) for h in (0, 1)] + [w_ref[h, rows].astype(F32) for h in (2, 3)]
            gated = jnp.concatenate(parts, axis=1).astype(BF)
            wide[rows] = jnp.concatenate([gated, jnp.zeros((gated.shape[0], WIDE - VD), BF)], axis=1)

        mixed_grad(0)
        load("wv", wv_hbm, wo)
        tick()
        row_loop(TOK, 64, mix_early)
        ready("qnext")

        @pl.when(z > 0)
        def _():
            g_halo.start()

        @pl.when(z == 3)
        def _():
            gnext[...] = jnp.zeros((2, HALO, VH), BF)
            qnext[...] = jnp.zeros((HALO, 2 * KEYH), BF)

        pl.semaphore_wait(pair_credit.at[1], 1)
        pair["gate"] = halves(wide, HALF, y1, 0)
        tick()

    def block_out():
        ready("mixed")
        arrived(pair["low"])
        for half in (0, 1):
            stage_rows(stage2, dot_tn(x1[...], ch[:, 256 * half : 256 * half + 256]), 2 * half)
        out.start()
        tell_sibling(2)
        tick()

    def block_gate():
        ready("first")
        arrived(pair["gate"])
        for half in (0, 1):
            stage_columns(stage3, dot_tn(y1[...], x3[:, 512 * half : 512 * half + 512]), 2 * half)
        gate.start()
        tick()

    def block_fg():
        ready("wg")
        two_halves(lambda cols: dot_nn(wide[:, 0:VD], wu[:, cols]))

    def finish_query(h, grad):
        queries[:, head_cols(h)] = unrotated(grad, table[:, 0:128], table[:, 128:256])

    def finish_key(h, grad):
        cot[:, head_cols(h)] = unrotated(grad, table[:, 256:384], table[:, 384:512])

    def block_full():
        ready_once("k", "v", "w01", "w23", "sin", "table")
        for h in (2, 3):
            cols_h = head_cols(h)
            score = []
            for b in (0, 1):
                rows, cols = slice(256 * b, 256 * b + 256), 256 * b + 256
                grad = dot_nt(rgrad[h, rows], values[h, HALO : HALO + cols])
                grad = (grad * decay_block(h, 256, cols, 256 * b, 0, start, docs, None)).astype(BF)
                score.append(grad)
            late = dot_tn(score[1], queries[256:512, cols_h])
            early = dot_tn(score[0], queries[0:256, cols_h])
            ch[0:TOK, head_cols(h - 2)] = jnp.concatenate([early + late[:256], late[256:]], axis=0).astype(BF)
            query = jnp.concatenate([dot_nn(score[b], keys[HALO : HALO + 256 * b + 256, cols_h]) for b in (0, 1)], axis=0)
            query = query + row_factor(h) * dot_nn(rgrad[h], state_in[h - 2])
            finish_query(h, query)
            late = dot_tn(w23[h - 2, 256:512], rgrad[h, 256:512])
            early = dot_tn(w23[h - 2, 0:256, 0:256], rgrad[h, 0:256])
            grad_v[h] = jnp.concatenate([early + late[:256], late[256:]], axis=0).astype(BF)
            tick()

    def block_band():
        ready_once("k", "v", "w01", "w23", "sin", "table")

        @pl.when(z < 3)
        def _():
            g_halo.wait_recv()

        tail = slice(TOK, TOK + HALO)
        for h in (0, 1):
            cols_h = head_cols(h)
            parts_q, parts_k, parts_v = [], [], []
            for b in (0, 1):
                rows, ext = slice(256 * b, 256 * b + 256), slice(256 * b, 256 * b + 384)
                grad = dot_nt(rgrad[h, rows], values[h, ext])
                decay = decay_block(h, 256, 384, 256 * b, 256 * b - HALO, start, docs, windows[0, h])
                grad = (grad * decay).astype(BF)
                parts_q.append(dot_nn(grad, keys[ext, cols_h]))
                parts_k.append(dot_tn(grad, queries[rows, cols_h]))
                parts_v.append(dot_tn(w01[h, b], rgrad[h, rows]))
            decay = decay_block(h, HALO, HALO, TOK, TOK - HALO, start, docs, windows[0, h])
            far_w = (dot_nt(qnext[:, cols_h], keys[tail, cols_h]) * decay).astype(BF)
            far_s = (dot_nt(gnext[h], values[h, tail]) * decay).astype(BF)

            def joined(parts, far):
                return jnp.concatenate(
                    [
                        parts[0][HALO : 2 * HALO],
                        parts[0][2 * HALO :] + parts[1][:HALO],
                        parts[1][HALO : 2 * HALO],
                        parts[1][2 * HALO :] + far,
                    ],
                    axis=0,
                )

            finish_query(h, jnp.concatenate(parts_q, axis=0))
            finish_key(h, joined(parts_k, dot_tn(far_s, qnext[:, cols_h])))
            grad_v[h] = joined(parts_v, dot_tn(far_w, gnext[h])).astype(BF)
            if h == 1:
                share_keys()
            tick()

    def block_cross():
        passing.finish()
        from_last = docs.of(3 * TOK - 1) == doc_last
        for h in (2, 3):
            cols_h = head_cols(h)
            power = jnp.where(z == 0, math.exp(2 * TOK * LOG_GAMMA[h]), math.exp(TOK * LOG_GAMMA[h]))
            total = back_near[h - 2].astype(F32) + back_far[h - 2].astype(F32) * jnp.where(from_last, power, 0.0)
            state_in[h - 2] = total.astype(BF)
            factor = jnp.where(doc_rows == doc_last, jnp.exp((TOK - place).astype(F32) * LOG_GAMMA[h]), 0.0)
            grad = ch[0:TOK, head_cols(h - 2)].astype(F32)
            finish_key(h, grad + factor * dot_nn(values[h, HALO:], state_in[h - 2]))
            grad_v[h] = (grad_v[h].astype(F32) + factor * dot_nt(keys[HALO:, cols_h], state_in[h - 2])).astype(BF)
        share_keys()
        tick()

    retained = []

    def share_keys():
        retained.append(0)
        if len(retained) == 2:
            pair["query"] = halves(queries, 512, x2, 0)
            pair["key"] = halves(cot, 512, x2, 512)

    def block_store():
        def store_value(rows):
            joint = jnp.concatenate([grad_v[h, rows].astype(F32) for h in range(HEADS)], axis=1).astype(BF)
            wide[rows] = jnp.concatenate([joint, jnp.zeros((joint.shape[0], WIDE - VD), BF)], axis=1)

        row_loop(TOK, 64, store_value)
        pl.semaphore_wait(pair_credit.at[2], 1)
        pair["value"] = halves(wide, HALF, x1, 0)
        load("tokens", tokens_hbm, keys.at[pl.ds(0, TOK)])
        tick()

    def block_qk():
        up.reduced()
        arrived(pair["query"])
        arrived(pair["key"])
        stage_square(stage1, dot_tn(x3[...], x2[:, 0:512]), 0)
        stage_square(stage1, dot_tn(x3[...], x2[:, 512:1024]), 64)
        qk.start()
        load("wq", wq_hbm, x2)
        tick()

    def block_value():
        down.reduced()
        arrived(pair["value"])
        for half in (0, 1):
            stage_columns(stage0, dot_tn(x1[:, 0:HALF], x3[:, 512 * half : 512 * half + 512]), 2 * half)
        value.start()
        load("wk", wk_hbm, x3)
        tick()

    def block_fv():
        ready("wv")
        two_halves(lambda cols: wf[:, cols] + dot_nn(wide[:, 0:VD], wo[:, cols]))

    def block_fq():
        ready("wq")
        two_halves(lambda cols: wf[:, cols] + dot_nt(queries[...], x2[cols]))

    def block_fk():
        ready("wk")
        two_halves(lambda cols: wf[:, cols] + dot_nt(cot[...], x3[cols]))

    def block_n1():
        ready("tokens")

        def back_one(i, sums):
            rows = pl.ds(pl.multiple_of(i * 64, 64), 64)
            grad = wf[rows]
            inverse = stats[rows, 1:2]
            scaled = (keys[rows].astype(F32) - stats[rows, 0:1]) * inverse
            e = grad * gain1[...]
            inner = e - jnp.mean(e, axis=-1, keepdims=True) - scaled * jnp.mean(e * scaled, axis=-1, keepdims=True)
            keys[rows] = (hidden[rows] + inverse * inner).astype(BF)
            return (sums[0] + fold(grad * scaled), sums[1] + fold(grad))

        gain_sum, bias_sum = lax.fori_loop(0, TOK // 64, back_one, (zero, zero))
        pair["tokens"] = pltpu.make_async_copy(keys.at[pl.ds(0, TOK)], out_tokens, save_sems.at[len(local_copies)])
        pair["tokens"].start()
        vec_rows[0:1] = jnp.sum(gain_sum, axis=0, keepdims=True)
        vec_rows[1:2] = jnp.sum(bias_sum, axis=0, keepdims=True)
        for block in range(4):
            for j in range(4):
                for t in range(2):
                    first = 256 * block + 128 * t
                    vec[block, 2 * j + t : 2 * j + t + 1] = vec_rows[j : j + 1, first : first + 128]
        next(vectors)
        tick()

    vectors = vector_steps(at, vec, vec_core, vec_z, vec_y, vec_x, vec_out, (vec_send, vec_recv), 0)
    known = {
        "down": block_down, "up": block_up, "second": block_second, "norm2": block_norm2, "mixl": block_mixl, "states": block_states,
        "mixe": block_mixe, "out": block_out, "gate": block_gate, "fg": block_fg, "full": block_full, "band": block_band,
        "cross": block_cross, "store": block_store, "qk": block_qk, "value": block_value, "fv": block_fv, "fq": block_fq,
        "fk": block_fk, "n1": block_n1,
    }
    for number, name in enumerate(BLOCKS):
        known[name]()
        if number == 0:
            load("cot", cot_hbm, cot)
            load("hidden", hidden_hbm, hidden)
            load("stats", stats_hbm, stats)
            load("wo", wo_hbm, wo)
            load("u", u_hbm, u_ref)
            load("w", w_hbm, w_ref)
            load("heads", heads_hbm, heads)
            load("q", q_hbm, queries)
            load("qnext", qnext_hbm, qnext)
        if number == 1:
            load("first", first_hbm, x3)
            load("k", k_hbm, keys)
            load("v", v_hbm, values)
            load("sin", sin_hbm, state_in)
            load("w23", w23_hbm, w23)
            load("w01", w01_hbm, w01)
            load("table", table_hbm.at[pl.ds(pl.multiple_of(z * TOK + HALO, HALO), TOK)], table)

    for n in TAIL:
        numbered[n].pump()
        next(vectors, 0)
    todo = [qk, value, gate, out, up, down]
    vectors_open = True
    while todo or vectors_open:
        todo = [unit for unit in todo if unit.pump()]
        vectors_open = next(vectors, 0) is None
    last = pltpu.make_async_copy(vec_out, out_vec, save_sems.at[len(local_copies) + 1])
    last.start()

    @pl.when(z > 0)
    def _():
        g_halo.wait_send()

    passing.drain()
    pair["tokens"].wait()
    last.wait()


def backward(arrays, gain1, gain2, lengths, windows):
    vmem = pl.BlockSpec(memory_space=pltpu.VMEM)
    smem = pl.BlockSpec(memory_space=pltpu.SMEM)
    anywhere = pl.BlockSpec(memory_space=pl.ANY)
    shape = jax.ShapeDtypeStruct
    outs = [shape((TOK, D), BF), shape((8, 128), F32)] + [shape((2, 4, 4, UNIT_ROWS[n], 128), BF) for n in UNITS]
    scratch = [
        pltpu.VMEM((2 * TOK, VD), BF), pltpu.VMEM((2 * TOK, D), BF), pltpu.VMEM((2 * TOK, D), BF), pltpu.VMEM((2 * TOK, HALF), BF),
        pltpu.VMEM((2 * TOK, 512), BF), pltpu.VMEM((TOK, WIDE), BF), pltpu.VMEM((TOK, D), BF), pltpu.VMEM((HEADS, TOK, VH), BF),
        pltpu.VMEM((HEADS, TOK, VH), BF), pltpu.VMEM((HEADS, TOK, VH), BF), pltpu.VMEM((TOK, QK), BF), pltpu.VMEM((HALO + TOK, QK), BF),
        pltpu.VMEM((HEADS, HALO + TOK, VH), BF), pltpu.VMEM((2, 2, 256, 384), BF), pltpu.VMEM((2, TOK, TOK), BF),
        pltpu.VMEM((2, VH, KEYH), BF), pltpu.VMEM((2, VH, KEYH), BF),
        pltpu.VMEM((2, VH, KEYH), BF), pltpu.VMEM((2, VH, KEYH), BF), pltpu.VMEM((2, VH, KEYH), BF),
        pltpu.VMEM((HEADS, TOK, VH), BF), pltpu.VMEM((TOK, D), F32),
        pltpu.VMEM((TOK, D), F32), pltpu.VMEM((VD, D), BF), pltpu.VMEM((VD, D), BF), pltpu.VMEM((TOK, 512), F32),
        pltpu.VMEM((TOK, 128), F32), pltpu.VMEM((HALO, 2 * KEYH), BF), pltpu.VMEM((2, HALO, VH), BF), pltpu.VMEM((8, D), F32),
        pltpu.VMEM((4, 8, 128), F32), pltpu.VMEM((4, 8, 128), F32), pltpu.VMEM((4, 8, 128), F32), pltpu.VMEM((4, 8, 128), F32),
        pltpu.VMEM((4, 8, 128), F32), pltpu.VMEM((8, 128), F32),
    ]
    scratch += [pltpu.VMEM((4, 4, 4, r, 128), BF) for r in SET_ROWS]
    for r in SET_ROWS:
        for count in PART_ROWS[r]:
            scratch += [pltpu.VMEM(s, BF) for s in landing_shapes(count)]
    for name in UNITS:
        scratch += [pltpu.VMEM((count, 128), BF) for count in PART_ROWS[UNIT_ROWS[name]]]
    dma, regular = pltpu.SemaphoreType.DMA, pltpu.SemaphoreType.REGULAR
    scratch += [dma((28,)), dma((8,)), dma((6,)), dma((6,)), dma((4,)), dma((4,)), dma((10,)), dma((10,))]
    scratch += [dma((18,)), dma((18 * ARRIVALS,)), dma((18,)), regular((6,)), regular((3,)), dma((8,)), dma((8,))]
    return pl.pallas_call(
        backward_kernel,
        out_shape=outs,
        in_specs=[anywhere] * 28 + [vmem] * 2 + [smem] * 2,
        out_specs=[anywhere] * len(outs),
        scratch_shapes=scratch,
        compiler_params=pltpu.CompilerParams(collective_id=2, has_side_effects=True, vmem_limit_bytes=62 * 2**20),
        cost_estimate=pl.CostEstimate(flops=26 * 10**9, bytes_accessed=70 * 10**6, transcendentals=10**6),
        name="backward",
    )(*arrays, gain1.reshape(1, D), gain2.reshape(1, D), lengths, windows.reshape(1, HEADS))


def unpack_kernel(down, up, out, gate, value, qk, g_down, g_up, g_out, g_gate, g_value, g_query, g_key):
    for x in range(4):
        cols = slice(128 * x, 128 * x + 128)
        for source, target in ((down, g_down), (out, g_out)):
            target[:, cols] = source[0, 0, x].astype(F32)
        g_query[:, cols] = qk[0, 0, x, 0:64].astype(F32)
        g_key[:, cols] = qk[0, 0, x, 64:128].astype(F32)
        xr, xc = x // 2, x % 2
        for source, target in ((up, g_up), (gate, g_gate), (value, g_value)):
            target[BIG * xr : BIG * xr + BIG, 128 * xc : 128 * xc + 128] = source[0, 0, x].astype(F32)


def unpack(gathered):
    def source(rows):
        return pl.BlockSpec((1, 1, 4, rows, 128), lambda c, y: (c, y, 0, 0, 0))

    tall = pl.BlockSpec((BIG, 512), lambda c, y: (y, c))
    turned = pl.BlockSpec((2 * BIG, 256), lambda c, y: (4 * c + y, 0))
    square = pl.BlockSpec((64, 512), lambda c, y: (y, c))
    shape = jax.ShapeDtypeStruct
    return pl.pallas_call(
        unpack_kernel,
        grid=(2, 4),
        out_shape=[
            shape((VH, D), F32), shape((FF, 256), F32), shape((VH, D), F32), shape((VD, 256), F32), shape((VD, 256), F32),
            shape((256, QK), F32), shape((256, QK), F32),
        ],
        in_specs=[source(UNIT_ROWS[n]) for n in UNITS],
        out_specs=[tall, turned, tall, turned, turned, square, square],
        compiler_params=pltpu.CompilerParams(vmem_limit_bytes=62 * 2**20),
        name="unpack",
    )(*gathered)


def body(
    tokens, ln_gain1, ln_bias1, w_query, w_key, w_value, w_gate, w_out, ln_gain2, ln_bias2, w_up, w_down, doc_lengths, windows, cotangent
):
    table = jnp.asarray(rotary_constants())
    (
        result, first, second, mixed, act, cot_half, lift_half, lift, q, k, v, w01, w23, s_in, heads, u, w, hidden, stats, qnext,
    ) = forward(
        tokens[0], cotangent[0], ln_gain1, ln_bias1, ln_gain2, ln_bias2, doc_lengths, windows, table,
        w_query, w_key, w_value, w_gate, w_out, w_up, w_down,
    )

    def pair(a):
        return a.reshape(2 * TOK, a.shape[2])

    arrays = (
        pair(act), pair(cot_half), pair(lift_half), pair(second), pair(first), pair(mixed), lift, cotangent[0], hidden, stats,
        u, w, heads, q, k, v, w01, w23, s_in, qnext, tokens[0], table,
        w_query, w_key, w_value.T, w_gate.T, w_out, w_up.T,
    )
    grad_tokens, vectors, *gathered = backward(arrays, ln_gain1, ln_gain2, doc_lengths, windows)
    g_down, g_up, g_out, g_gate, g_value, g_query, g_key = unpack(gathered)
    vectors = vectors.reshape(4, 256)
    return (
        result.reshape(1, TOK, D),
        grad_tokens.reshape(1, TOK, D),
        vectors[0],
        vectors[1],
        g_query,
        g_key,
        g_value.T,
        g_gate.T,
        g_out,
        vectors[2],
        vectors[3],
        g_up.T,
        g_down,
    )


def solution(mesh):
    in_specs = (P("batch", "head", None),) + (P(),) * 11 + (P("batch", None), P(), P("batch", "head", None))
    rows, vector = P("head", None), P("head")
    out_specs = (
        P("batch", "head", None), P("batch", "head", None), vector, vector, rows, rows, rows, rows, rows, vector, vector, rows, rows,
    )
    return jax.shard_map(body, mesh=mesh, in_specs=in_specs, out_specs=out_specs, check_vma=False)
```

```python
import functools
import math

import jax
import jax.numpy as jnp
import numpy as np
from jax import lax
from jax.experimental import pallas as pl
from jax.experimental.pallas import tpu as pltpu
from jax.sharding import PartitionSpec as P

D = 1024
HEADS = 4
KEYH = 256
VH = 432
FF = 1728
QK = 1024
VD = 1728
TOK = 512
SEQ = 2048
HALO = 128
WIDE = 1792

epsilon = 1e-05
retention_floor = 1.0
BF = jnp.bfloat16
F32 = jnp.float32
MESH = pl.DeviceIdType.MESH


BIG, PAIRED = 112, 128
CUTS = {BIG: ((0, 48), (48, 32), (80, 32)), PAIRED: ((0, 48), (48, 48), (96, 32))}
ARRIVALS = 9


def coordinates():
    z = lax.axis_index("head")
    b = lax.axis_index("batch")
    return [z, lax.div(b, 8), lax.rem(lax.div(b, 2), 4), lax.rem(b, 2)]


def shifted(at, axis, step):
    place = list(at)
    if axis == 3:
        place[3] = 1 - place[3]
    else:
        place[axis] = lax.rem(place[axis] + step, 4)
    return (place[0], (place[1] * 4 + place[2]) * 2 + place[3])


def away(p, step):
    return lax.rem(p + step, 4)


LOW, HIGH = pl.ds(0, 2), pl.ds(2, 2)


def landing_shapes(r):
    return [(2, 2, 4, r, 128), (2, 4, 4, r, 128), (3, 4, r, 128), (3, r, 128)]


LANDINGS = 4


class Part:
    def __init__(self, at, stage, lands, mine, out, rows, order, gather, sems, slot, credit_in, credit_out, next_order, thrifty):
        self.at, self.stage, self.out = at, stage, out
        self.first, self.count = rows
        self.lands = [land.at[..., pl.ds(0, self.count), :] for land in lands]
        self.mine = mine.at[pl.ds(0, self.count)]
        self.order, self.gather = order, gather
        send_sems, recv_sems, copy_sems = sems
        self.send_sem, self.copy_sem = send_sems.at[slot], copy_sems.at[slot]
        self.recv_sems = [recv_sems.at[ARRIVALS * slot + n] for n in range(ARRIVALS)]
        self.credit_in, self.credit_out, self.next_order = credit_in, credit_out, next_order
        self.thrifty = thrifty

    def copy(self, source, target, axis, step, arrival):
        return pltpu.make_async_remote_copy(
            src_ref=source, dst_ref=target, send_sem=self.send_sem, recv_sem=self.recv_sems[arrival],
            device_id=shifted(self.at, axis, step), device_id_type=MESH,
        )

    def send(self, source, target, axis, step, arrival):
        self.copy(source, target, axis, step, arrival).start()

    def arrived(self, size, arrival):
        whole = self.copy(size, size, 3, 1, arrival)
        whole.wait_recv()
        whole.wait_send()

    def pick(self, axes):
        index = [slice(None)] * 3
        for axis, value in axes.items():
            index[axis] = value
        return self.stage.at[tuple(index) + (pl.ds(self.first, self.count), slice(None))]

    @staticmethod
    def writers(order):
        a1, a2, a3 = order
        return [(a1, 1), (a1, 3)] + [(axis, step) for axis in (a2, a3) for step in (1, 2, 3)]

    def steps(self):
        at, lands = self.at, self.lands
        a1, a2, a3 = self.order
        p1, p2, p3 = at[a1], at[a2], at[a3]
        cut = min(a2, a3)
        if self.credit_in is not None:
            pl.semaphore_wait(self.credit_in, len(self.writers(self.order)))
        self.send(self.pick({a1: away(p1, 2), cut: LOW}), lands[0].at[0], a1, 1, 0)
        self.send(self.pick({a1: away(p1, 2), cut: HIGH}), lands[0].at[1], a1, 3, 0)
        yield
        self.arrived(lands[0], 0)
        for n, step, part in ((0, 1, LOW), (1, 3, HIGH)):
            there = self.pick({a1: away(p1, step), cut: part})
            there[...] = there[...] + lands[0][n]
            self.send(self.pick({a1: away(p1, step)}), lands[1].at[n], a1, step, 1)
        yield
        self.arrived(lands[1], 1)
        own = self.pick({a1: p1})
        own[...] = (own[...].astype(F32) + lands[1][0].astype(F32) + lands[1][1].astype(F32)).astype(BF)
        if self.thrifty:
            self.send(self.pick({a1: p1, a2: away(p2, 2), a3: LOW}), lands[2].at[0, LOW], a2, 1, 2)
            self.send(self.pick({a1: p1, a2: away(p2, 2), a3: HIGH}), lands[2].at[0, HIGH], a2, 3, 2)
            yield
            self.arrived(lands[2].at[0], 2)
            for n, step, part in ((1, 1, LOW), (2, 3, HIGH)):
                there = self.pick({a1: p1, a2: away(p2, step), a3: part})
                there[...] = there[...] + lands[2][0, 2 * n - 2 : 2 * n]
                self.send(self.pick({a1: p1, a2: away(p2, step)}), lands[2].at[n], a2, step, 7)
            yield
            self.arrived(lands[2].at[pl.ds(1, 2)], 7)
            come = (1, 2)
        else:
            for s in (1, 2, 3):
                self.send(self.pick({a1: p1, a2: away(p2, s)}), lands[2].at[s - 1], a2, s, 2)
            yield
            self.arrived(lands[2], 2)
            come = (0, 1, 2)
        own = self.pick({a1: p1, a2: p2})
        total = own[...].astype(F32)
        for step in come:
            total = total + lands[2][step].astype(F32)
        own[...] = total.astype(BF)
        for s in (1, 2, 3):
            self.send(self.pick({a1: p1, a2: p2, a3: away(p3, s)}), lands[3].at[s - 1], a3, s, 3)
        yield
        self.arrived(lands[3], 3)
        total = self.pick({a1: p1, a2: p2, a3: p3})[...].astype(F32)
        for step in range(3):
            total = total + lands[3][step].astype(F32)
        self.mine[...] = total.astype(BF)
        if self.credit_out is not None:
            for axis, step in self.writers(self.next_order):
                pl.semaphore_signal(self.credit_out, inc=1, device_id=shifted(at, axis, step), device_id_type=MESH)

        rows = pl.ds(self.first, self.count)
        g1, g2 = self.gather
        target = self.out.at[at[3], at[1], at[2], rows]
        local = pltpu.make_async_copy(self.mine, target, self.copy_sem)
        local.start()
        for s in (1, 2, 3):
            self.send(self.mine, target, g1, s, 4)
        yield
        self.arrived(lands[3], 4)
        local.wait()

        def block(place, part=slice(None)):
            if g2 == 1:
                return self.out.at[at[3], place, part, rows]
            return self.out.at[at[3], part, place, rows]

        q = at[g2]
        if self.thrifty:
            for s in (1, 3):
                self.send(block(q), block(q), g2, s, 5)
            yield
            self.arrived(lands[2].at[pl.ds(0, 2)], 5)
            for s, part in ((1, LOW), (3, HIGH)):
                source = block(away(q, 4 - s), part)
                self.send(source, source, g2, s, 8)
            yield
            self.arrived(lands[2].at[0], 8)
        else:
            for s in (1, 2, 3):
                self.send(block(q), block(q), g2, s, 5)
            yield
            self.arrived(lands[2], 5)
        for place in range(4):
            self.send(block(place), block(place), 3, 1, 6)
        yield
        self.arrived(lands[1].at[0], 6)


class Unit:
    def __init__(self, parts, thrifty):
        self.parts = parts
        self.steps_to_reduce = 6 if thrifty else 5
        self.running = None
        self.done = 0

    def start(self):
        self.running = [part.steps() for part in self.parts]
        self.pump()

    def pump(self, times=1):
        for _ in range(times):
            if not self.running:
                return False
            self.running = [steps for steps in self.running if next(steps, 0) is None]
            self.done += 1
        return bool(self.running)

    def reduced(self):
        while self.done < self.steps_to_reduce:
            self.pump()


def vector_steps(at, mine, land_core, land_z, land_y, land_x, final, sems, base):
    send_sems, recv_sems = sems
    slots = iter(range(base, base + 10))

    def send(source, target, axis, step):
        slot = next(slots)
        copy = pltpu.make_async_remote_copy(
            src_ref=source, dst_ref=target, send_sem=send_sems.at[slot], recv_sem=recv_sems.at[slot],
            device_id=shifted(at, axis, step), device_id_type=MESH,
        )
        copy.start()
        return copy

    z, y, x, _ = at
    copies = [send(mine, land_core, 3, 1)]
    yield
    copies[0].wait()
    mine[...] = mine[...] + land_core[...]
    copies = [send(mine.at[away(z, s)], land_z.at[z], 0, s) for s in (1, 2, 3)]
    land_z[z] = mine[z]
    yield
    for axis, here, land in ((1, y, land_y), (2, x, land_x)):
        for copy in copies:
            copy.wait()
        source = land_z if axis == 1 else land_y
        total = (source[0] + source[1]) + (source[2] + source[3])
        land[here] = total
        copies = [send(land.at[here], land.at[here], axis, s) for s in (1, 2, 3)]
        yield
    for copy in copies:
        copy.wait()
    final[...] = (land_x[0] + land_x[1]) + (land_x[2] + land_x[3])


def greet(at):
    barrier = pltpu.get_barrier_semaphore()
    partners = [(axis, step) for axis in (0, 1, 2) for step in (1, 2, 3)] + [(3, 1)]
    for axis, step in partners:
        pl.semaphore_signal(barrier, inc=1, device_id=shifted(at, axis, step), device_id_type=MESH)
    pl.semaphore_wait(barrier, len(partners))


class Passing:
    PIECES = ((0, 0), (0, 1), (1, 0), (1, 1))

    def __init__(self, at, way, own, near, far, sems, base):
        self.at, self.way = at, way
        self.rank = at[0] if way == 1 else 3 - at[0]
        self.own, self.near, self.far = own, near, far
        self.send_sems, self.recv_sems = sems
        self.base = base

    ROWS = (slice(0, 224), slice(224, VH))

    def piece(self, ref, p):
        head, half = self.PIECES[p]
        rows = self.ROWS[half]
        return ref.at[head, pl.ds(rows.start, rows.stop - rows.start)]

    def copy(self, source, target, p, kind):
        step = {0: self.way, 1: -self.way, 2: -self.way}[kind] % 4
        slot = self.base + 4 * min(kind, 1) + p
        return pltpu.make_async_remote_copy(
            src_ref=self.piece(source, p), dst_ref=self.piece(target, p), send_sem=self.send_sems.at[slot],
            recv_sem=self.recv_sems.at[slot], device_id=shifted(self.at, 0, step), device_id_type=MESH,
        )

    def clear(self):
        @pl.when(self.rank == 0)
        def _():
            self.near[...] = jnp.zeros(self.near.shape, BF)

        @pl.when(self.rank < 2)
        def _():
            self.far[...] = jnp.zeros(self.far.shape, BF)

    def begin(self, p):
        @pl.when(self.rank < 2)
        def _():
            self.copy(self.own, self.near, p, 0).start()

        @pl.when(self.rank == 0)
        def _():
            self.copy(self.own, self.far, p, 1).start()

    def forward(self, p, decay):
        head, half = self.PIECES[p]
        rows = self.ROWS[half]

        @pl.when(self.rank == 2)
        def _():
            self.copy(self.own, self.near, p, 0).wait_recv()
            total = self.own[head, rows].astype(F32) + self.near[head, rows].astype(F32) * decay[head]
            self.own[head, rows] = total.astype(BF)
            self.copy(self.own, self.near, p, 0).start()

        @pl.when(self.rank == 3)
        def _():
            self.copy(self.far, self.far, p, 1).wait_recv()
            self.copy(self.far, self.far, p, 2).start()

    def finish(self):
        for p in range(4):

            @pl.when((self.rank == 1) | (self.rank == 3))
            def _():
                self.copy(self.own, self.near, p, 0).wait_recv()

            @pl.when(self.rank == 2)
            def _():
                self.copy(self.far, self.far, p, 1).wait_recv()

    def drain(self):
        for p in range(4):

            @pl.when(self.rank < 3)
            def _():
                self.copy(self.own, self.near, p, 0).wait_send()

            @pl.when((self.rank == 0) | (self.rank == 3))
            def _():
                self.copy(self.own, self.far, p, 1).wait_send()


LOG_GAMMA = tuple(math.log(1.0 - 2.0 ** (-5.0 - h)) for h in range(HEADS))
HALF = WIDE // 2


def rotary_constants():
    half = KEYH // 2
    ladder = np.arange(half, dtype=np.float64)
    theta = 10000.0 ** (-ladder / half)
    place = np.arange(SEQ, dtype=np.float64)[:, None]
    zeta = (2.0 * ladder + 0.4 * KEYH) / (1.4 * KEYH)
    grow = zeta[None, :] ** (place / 512.0)
    cosine, sine = np.cos(place * theta), np.sin(place * theta)
    small = KEYH ** (-0.5)
    table = np.concatenate([cosine * grow, sine * grow, cosine / grow * small, sine / grow * small], axis=1)
    return np.concatenate([np.zeros((HALO, 4 * half)), table]).astype(np.float32)


def dot_nn(a, b):
    return lax.dot_general(a, b, (((1,), (0,)), ((), ())), preferred_element_type=F32)


def dot_nt(a, b):
    return lax.dot_general(a, b, (((1,), (1,)), ((), ())), preferred_element_type=F32)


def dot_tn(a, b):
    return lax.dot_general(a, b, (((0,), (0,)), ((), ())), preferred_element_type=F32)


def row_loop(total, step, work):
    def one(i, carry):
        work(pl.ds(pl.multiple_of(i * step, step), step))
        return carry

    lax.fori_loop(0, total // step, one, 0)


class Documents:
    def __init__(self, lengths_ref):
        ends = []
        total = 0
        for i in range(5):
            total = total + lengths_ref[0, i]
            ends.append(total)
        self.ends = ends

    def of(self, where):
        found = jnp.zeros(where.shape, jnp.int32) if hasattr(where, "shape") and where.shape else 0
        for end in self.ends:
            found = found + jnp.where(where >= end, 1, 0)
        return found


def column(count, first=0):
    return lax.broadcasted_iota(jnp.int32, (count, 1), 0) + first


def line(count, first=0):
    return lax.broadcasted_iota(jnp.int32, (1, count), 1) + first


def decay_block(h, rows, cols, row_first, col_first, start, docs, window):
    i, j = column(rows, row_first), line(cols, col_first)
    base = min(row_first, col_first)
    seen = (i >= j) & (docs.of(i + start) == docs.of(j + start))
    if window is not None:
        seen = seen & (i - j < window)
    if col_first < 0:
        seen = seen & (j + start >= 0)
    down = jnp.exp((i - base).astype(F32) * LOG_GAMMA[h])
    up = jnp.exp((j - base).astype(F32) * (-LOG_GAMMA[h]))
    return jnp.where(seen, down * up, 0.0)


def rotated(raw, cosine, sine):
    front, behind = raw[:, :128], raw[:, 128:]
    return jnp.concatenate([front * cosine - behind * sine, front * sine + behind * cosine], axis=1)


def forward_kernel(
    tokens_hbm, cot_hbm, gain1, bias1, gain2, bias2, lengths, windows, table_hbm,
    wq_hbm, wk_hbm, wv_hbm, wg_hbm, wo_hbm, wu_hbm, wd_hbm,
    out_result, out_first, out_second, out_mixed, out_act, out_cot, out_lhalf, out_lift,
    out_q, out_k, out_v, out_w01, out_w23, out_sin, out_heads, out_u, out_w, out_hidden, out_stats, out_qnext,
    tokens, cot, table, wq, wk, wv, wg, wo, wu, wd,
    first, queries, keys, values, wide_f32, down_grad, kept, w01, w23, state, state_near, state_far, state_in,
    heads, u_ref, w_ref, mixed, hidden, second, lift, act, stats,
    load_sems, save_sems, send_sems, recv_sems, pass_send, pass_recv,
):
    at = coordinates()
    z, core = at[0], at[3]
    start = z * TOK
    loads = {}
    for slot, (name, source, target) in enumerate(
        [
            ("tokens", tokens_hbm, tokens.at[pl.ds(HALO, TOK)]),
            ("wk", wk_hbm, wk),
            ("table", table_hbm.at[pl.ds(pl.multiple_of(z * TOK, TOK), HALO + TOK)], table),
            ("wv", wv_hbm, wv),
            ("wq", wq_hbm, wq),
            ("wg", wg_hbm, wg),
            ("cot", cot_hbm, cot),
            ("wd", wd_hbm, wd),
            ("wo", wo_hbm, wo),
            ("wu", wu_hbm, wu),
        ]
    ):
        loads[name] = pltpu.make_async_copy(source, target, load_sems.at[slot])
        loads[name].start()
    partners = [(3, 1), (0, 1), (0, 3)]
    barrier = pltpu.get_barrier_semaphore()
    for axis, step in partners:
        pl.semaphore_signal(barrier, inc=1, device_id=shifted(at, axis, step), device_id_type=MESH)

    saves, sends = [], []

    def save(source, target):
        copy = pltpu.make_async_copy(source, target, save_sems.at[len(saves)])
        copy.start()
        saves.append(copy)

    def remote(source, target, axis, step):
        slot = len(sends)
        copy = pltpu.make_async_remote_copy(
            src_ref=source, dst_ref=target, send_sem=send_sems.at[slot], recv_sem=recv_sems.at[slot],
            device_id=shifted(at, axis, step), device_id_type=MESH,
        )
        sends.append(copy)
        return copy

    def share(source, target):
        save(source, target.at[core])
        remote(source, target.at[core], 3, 1).start()
        return (saves[-1], sends[-1])

    loads["tokens"].wait()

    pl.semaphore_wait(barrier, len(partners))
    t_halo = remote(tokens.at[pl.ds(TOK, HALO)], tokens.at[pl.ds(0, HALO)], 0, 1)

    @pl.when(z < 3)
    def _():
        t_halo.start()

    @pl.when(z == 0)
    def _():
        tokens[0:HALO] = jnp.zeros((HALO, D), BF)

    def normalized(x):
        mean = jnp.mean(x, axis=-1, keepdims=True)
        center = x - mean
        inverse = lax.rsqrt(jnp.mean(center * center, axis=-1, keepdims=True) + epsilon)
        return center * inverse, mean, inverse

    def norm_one(i, carry):
        rows = pl.ds(pl.multiple_of(i * 64, 64), 64)
        scaled, mean, inverse = normalized(tokens[pl.ds(HALO + i * 64, 64)].astype(F32))
        first[pl.ds(HALO + i * 64, 64)] = (scaled * gain1[...] + bias1[...]).astype(BF)
        stats[rows, 0:1] = mean
        stats[rows, 1:2] = inverse
        return carry

    lax.fori_loop(0, TOK // 64, norm_one, 0)
    share(first.at[pl.ds(HALO, TOK)], out_first)

    docs = Documents(lengths)
    doc_before = docs.of(start - 1)
    doc_last = docs.of(start + TOK - 1)
    place = column(TOK)
    doc_rows = docs.of(place + start)

    def project(h, begin):
        cols = slice(h * KEYH, (h + 1) * KEYH)
        raw = dot_nn(first[begin:], wk[:, cols])
        keys[begin:, cols] = rotated(raw, table[begin:, 256:384], table[begin:, 384:512]).astype(BF)
        values[h, begin:] = dot_nt(first[begin:], wv[h * VH : (h + 1) * VH]).astype(BF)

    loads["wk"].wait()
    loads["table"].wait()
    loads["wv"].wait()
    passing = Passing(at, 1, state, state_near, state_far, (pass_send, pass_recv), 0)
    joins = [jnp.where(doc_before == doc_last, math.exp(LOG_GAMMA[h] * TOK), 0.0) for h in (2, 3)]
    for h in (2, 3):
        project(h, HALO)
        factor = jnp.where(doc_rows == doc_last, jnp.exp((TOK - place).astype(F32) * LOG_GAMMA[h]), 0.0)
        scaled = (keys[HALO:, h * KEYH : (h + 1) * KEYH].astype(F32) * factor).astype(BF)
        state[h - 2] = dot_tn(values[h, HALO:], scaled).astype(BF)
        passing.begin(2 * h - 4)
        passing.begin(2 * h - 3)
    passing.clear()
    loads["wq"].wait()
    for h in range(HEADS):
        raw = dot_nn(first[HALO:], wq[:, h * KEYH : (h + 1) * KEYH])
        queries[:, h * KEYH : (h + 1) * KEYH] = rotated(raw, table[HALO:, 0:128], table[HALO:, 128:256]).astype(BF)
    save(queries, out_q)
    q_halo = remote(queries.at[pl.ds(0, HALO), pl.ds(0, 2 * KEYH)], out_qnext, 0, 3)

    @pl.when(z > 0)
    def _():
        q_halo.start()

    loads["wg"].wait()
    passing.forward(0, joins)

    def swish(h, rows):
        lane = 512 * (h % 2)
        gate = wide_f32[rows, lane : lane + VH]
        sigma = 0.5 * jnp.tanh(0.5 * gate) + 0.5
        u_ref[h, rows] = (gate * sigma).astype(BF)
        w_ref[h, rows] = (sigma * (1.0 + gate * (1.0 - sigma))).astype(BF)

    for h in range(HEADS + 1):
        if h < HEADS:
            lane = 512 * (h % 2)
            wide_f32[:, lane : lane + VH] = dot_nt(first[HALO:], wg[h * VH : (h + 1) * VH])
        if h > 0:
            for row in range(0, TOK, 64):
                swish(h - 1, slice(row, row + 64))
        if h == 2:
            passing.forward(1, joins)
    save(u_ref, out_u)
    save(w_ref, out_w)
    loads["cot"].wait()
    save(cot.at[:, pl.ds(pl.multiple_of(core * 512, 512), 512)], out_cot.at[core])
    remote(cot.at[:, pl.ds(pl.multiple_of((1 - core) * 512, 512), 512)], out_cot.at[core], 3, 1).start()
    loads["wd"].wait()
    down_grad[...] = dot_nt(cot[...], wd[...]).astype(BF)
    passing.forward(2, joins)

    for h in (2, 3):
        for b in (0, 1):
            rows, cols = slice(256 * b, 256 * b + 256), 256 * b + 256
            q_h = queries[rows, h * KEYH : (h + 1) * KEYH]
            scores = dot_nt(q_h, keys[HALO : HALO + cols, h * KEYH : (h + 1) * KEYH])
            weight = (scores * decay_block(h, 256, cols, 256 * b, 0, start, docs, None)).astype(BF)
            w23[h - 2, rows, 0:cols] = weight
            kept[h, rows] = dot_nn(weight, values[h, HALO : HALO + cols])

    passing.forward(3, joins)

    @pl.when(z > 0)
    def _():
        t_halo.wait_recv()

    for block in (slice(0, 64), slice(64, 128)):
        first[block] = (normalized(tokens[block].astype(F32))[0] * gain1[...] + bias1[...]).astype(BF)
    for h in (0, 1):
        project(h, 0)

    save(keys, out_k)
    save(values, out_v)
    for h in (0, 1):
        for b in (0, 1):
            rows = slice(256 * b, 256 * b + 256)
            q_h = queries[rows, h * KEYH : (h + 1) * KEYH]
            scores = dot_nt(q_h, keys[256 * b : 256 * b + 384, h * KEYH : (h + 1) * KEYH])
            decay = decay_block(h, 256, 384, 256 * b, 256 * b - HALO, start, docs, windows[0, h])
            weight = (scores * decay).astype(BF)
            w01[h, b] = weight
            kept[h, rows] = dot_nn(weight, values[h, 256 * b : 256 * b + 384])
    save(w01, out_w01)
    save(w23, out_w23)

    passing.finish()
    from_first = docs.of(TOK - 1) == doc_before
    for h in (2, 3):
        power = jnp.where(z == 3, math.exp(2 * TOK * LOG_GAMMA[h]), math.exp(TOK * LOG_GAMMA[h]))
        total = state_near[h - 2].astype(F32) + state_far[h - 2].astype(F32) * jnp.where(from_first, power, 0.0)
        state_in[h - 2] = total.astype(BF)
        factor = jnp.where(doc_rows == doc_before, jnp.exp(place.astype(F32) * LOG_GAMMA[h]), 0.0)
        kept[h] = kept[h] + factor * dot_nt(queries[:, h * KEYH : (h + 1) * KEYH], state_in[h - 2])
    save(state_in, out_sin)

    def mix(rows):
        parts = []
        for h in range(HEADS):
            x = kept[h, rows]
            center = x - jnp.mean(x, axis=-1, keepdims=True)
            inverse = lax.rsqrt(jnp.mean(center * center, axis=-1, keepdims=True) + retention_floor)
            stats[rows, 4 + h : 5 + h] = inverse
            low = (center * inverse).astype(BF)
            heads[h, rows] = low
            parts.append(low.astype(F32) * u_ref[h, rows].astype(F32))
        mixed[rows] = jnp.concatenate(parts, axis=1).astype(BF)

    row_loop(TOK, 64, mix)
    mixed_away = share(mixed, out_mixed)
    save(heads, out_heads)

    loads["wo"].wait()
    hidden[...] = dot_nn(mixed[...], wo[...])

    def norm_two(i, carry):
        rows = pl.ds(pl.multiple_of(i * 64, 64), 64)
        x = hidden[rows] + tokens[pl.ds(HALO + i * 64, 64)].astype(F32)
        hidden[rows] = x
        scaled, mean, inverse = normalized(x)
        second[rows] = (scaled * gain2[...] + bias2[...]).astype(BF)
        stats[rows, 2:3] = mean
        stats[rows, 3:4] = inverse
        return carry

    lax.fori_loop(0, TOK // 64, norm_two, 0)
    share(second, out_second)
    save(hidden, out_hidden)
    save(stats, out_stats)

    loads["wu"].wait()

    def activate(cols, rows):
        x = wide_f32[rows, cols]
        phi = 0.5 * (1.0 + lax.erf(x * math.sqrt(0.5)))
        slope = phi + x * jnp.exp(-0.5 * x * x) * (1.0 / math.sqrt(2.0 * math.pi))
        act[rows, cols] = (x * phi).astype(BF)
        grad = (down_grad[rows, cols].astype(F32) * slope).astype(BF)
        if cols.stop == FF:
            grad = jnp.concatenate([grad, jnp.zeros((grad.shape[0], WIDE - FF), BF)], axis=1)
        lift[rows, cols.start : cols.start + grad.shape[1]] = grad

    blocks = [slice(first_col, min(first_col + 256, FF)) for first_col in range(0, FF, 256)]
    for n in range(len(blocks) + 1):
        if n < len(blocks):
            wide_f32[:, blocks[n]] = dot_nt(second[...], wu[blocks[n]])
        if n > 0:
            for row in range(0, TOK, 64):
                activate(blocks[n - 1], slice(row, row + 64))
    save(act, out_act)
    save(lift, out_lift)
    save(lift.at[:, pl.ds(pl.multiple_of(core * HALF, HALF), HALF)], out_lhalf.at[core])
    remote(lift.at[:, pl.ds(pl.multiple_of((1 - core) * HALF, HALF), HALF)], out_lhalf.at[core], 3, 1).start()
    for copy in mixed_away:
        copy.wait()
    mixed[:, 0:D] = (hidden[...] + dot_nn(act[...], wd[...])).astype(BF)
    save(mixed.at[:, pl.ds(0, D)], out_result)

    for copy in sends:
        if not any(copy is other for other in (t_halo, q_halo) + mixed_away):
            copy.wait()

    @pl.when(z > 0)
    def _():
        q_halo.wait_send()

    @pl.when(z < 3)
    def _():
        q_halo.wait_recv()
        t_halo.wait_send()

    passing.drain()
    for copy in saves:
        if copy is not mixed_away[0]:
            copy.wait()


def forward(tokens, cot, gain1, bias1, gain2, bias2, lengths, windows, table, wq, wk, wv, wg, wo, wu, wd):
    vmem = pl.BlockSpec(memory_space=pltpu.VMEM)
    smem = pl.BlockSpec(memory_space=pltpu.SMEM)
    anywhere = pl.BlockSpec(memory_space=pl.ANY)
    shape = jax.ShapeDtypeStruct
    outs = [
        shape((TOK, D), BF), shape((2, TOK, D), BF), shape((2, TOK, D), BF), shape((2, TOK, VD), BF), shape((TOK, FF), BF),
        shape((2, TOK, 512), BF), shape((2, TOK, HALF), BF), shape((TOK, WIDE), BF),
        shape((TOK, QK), BF), shape((HALO + TOK, QK), BF), shape((HEADS, HALO + TOK, VH), BF),
        shape((2, 2, 256, 384), BF), shape((2, TOK, TOK), BF), shape((2, VH, KEYH), BF),
        shape((HEADS, TOK, VH), BF), shape((HEADS, TOK, VH), BF), shape((HEADS, TOK, VH), BF), shape((TOK, D), F32), shape((TOK, 128), F32),
        shape((HALO, 2 * KEYH), BF),
    ]
    scratch = [
        pltpu.VMEM((HALO + TOK, D), BF), pltpu.VMEM((TOK, D), BF), pltpu.VMEM((HALO + TOK, 512), F32),
        pltpu.VMEM((D, QK), BF), pltpu.VMEM((D, QK), BF), pltpu.VMEM((VD, D), BF), pltpu.VMEM((VD, D), BF),
        pltpu.VMEM((VD, D), BF), pltpu.VMEM((FF, D), BF), pltpu.VMEM((FF, D), BF),
        pltpu.VMEM((HALO + TOK, D), BF), pltpu.VMEM((TOK, QK), BF), pltpu.VMEM((HALO + TOK, QK), BF),
        pltpu.VMEM((HEADS, HALO + TOK, VH), BF), pltpu.VMEM((TOK, FF), F32), pltpu.VMEM((TOK, FF), BF),
        pltpu.VMEM((HEADS, TOK, VH), F32), pltpu.VMEM((2, 2, 256, 384), BF), pltpu.VMEM((2, TOK, TOK), BF),
        pltpu.VMEM((2, VH, KEYH), BF), pltpu.VMEM((2, VH, KEYH), BF), pltpu.VMEM((2, VH, KEYH), BF), pltpu.VMEM((2, VH, KEYH), BF),
        pltpu.VMEM((HEADS, TOK, VH), BF), pltpu.VMEM((HEADS, TOK, VH), BF), pltpu.VMEM((HEADS, TOK, VH), BF), pltpu.VMEM((TOK, VD), BF),
        pltpu.VMEM((TOK, D), F32), pltpu.VMEM((TOK, D), BF), pltpu.VMEM((TOK, WIDE), BF), pltpu.VMEM((TOK, FF), BF),
        pltpu.VMEM((TOK, 128), F32),
        pltpu.SemaphoreType.DMA((10,)), pltpu.SemaphoreType.DMA((20,)),
        pltpu.SemaphoreType.DMA((16,)), pltpu.SemaphoreType.DMA((16,)),
        pltpu.SemaphoreType.DMA((8,)), pltpu.SemaphoreType.DMA((8,)),
    ]
    return pl.pallas_call(
        forward_kernel,
        out_shape=outs,
        in_specs=[anywhere] * 2 + [vmem] * 4 + [smem] * 2 + [anywhere] * 8,
        out_specs=[anywhere] * len(outs),
        scratch_shapes=scratch,
        compiler_params=pltpu.CompilerParams(collective_id=1, has_side_effects=True, vmem_limit_bytes=62 * 2**20),
        cost_estimate=pl.CostEstimate(flops=14 * 10**9, bytes_accessed=50 * 10**6, transcendentals=2 * 10**6),
        name="forward",
    )(
        tokens, cot, gain1.reshape(1, D), bias1.reshape(1, D), gain2.reshape(1, D), bias2.reshape(1, D),
        lengths, windows.reshape(1, HEADS), table, wq, wk, wv.T, wg.T, wo, wu.T, wd,
    )


LAST = TOK - HALO
UNITS = ("down", "up", "out", "gate", "value", "qk")
UNIT_ROWS = {"down": BIG, "up": BIG, "out": BIG, "gate": BIG, "value": BIG, "qk": PAIRED}
UNIT_SET = {"down": 0, "up": 1, "out": 2, "gate": 3, "value": 0, "qk": 1}
SET_ROWS = (BIG, PAIRED, BIG, BIG)
FOLLOWER = {"down": "value", "up": "qk"}
PLAN = {
    "down": (((2, 1, 0), (2, 1)), ((1, 2, 0), (1, 2)), ((0, 1, 2), (2, 1))),
    "up": (((0, 2, 1), (1, 2)), ((2, 1, 0), (2, 1)), ((1, 2, 0), (1, 2))),
    "out": (((0, 1, 2), (1, 2)), ((2, 0, 1), (2, 1)), ((1, 0, 2), (2, 1))),
    "gate": (((2, 0, 1), (1, 2)), ((1, 0, 2), (2, 1)), ((1, 2, 0), (1, 2))),
    "value": (((0, 2, 1), (1, 2)), ((2, 1, 0), (2, 1)), ((1, 0, 2), (2, 1))),
    "qk": (((1, 2, 0), (2, 1)), ((2, 0, 1), (1, 2)), ((0, 1, 2), (1, 2))),
}
THRIFTY = ("down", "up", "gate")
BLOCKS = (
    "up", "down", "second", "norm2", "mixl", "states", "mixe", "gate", "fg", "out", "band", "far", "full", "cross", "store", "qk", "value", "fq", "fk", "fv", "n1",
)
SCHEDULE = (
    (), (), (), (1,), (0,), (), (), (1,), (), (0, 1), (6, 7, 0, 1), (8,), (9, 3), (0,), (), (1,), (), (), (3,), (2,), (0, 1), (3,), (2,), (0,), (1,), (), (5,), (3,), (4,), (0, 1, 2),
)
TAIL = (1, 5, 3, 4, 2, 0, 5, 3, 0, 4, 5, 2, 4, 3, 5, 2, 4, 3, 2, 5, 3, 4, 5, 4)
PART_ROWS = {rows: tuple(count for _, count in cuts) for rows, cuts in CUTS.items()}


def stage_rows(stage, result, first_x):
    for z in range(4):
        for y in range(4):
            n = min(BIG, VH - BIG * y)
            for i in range(result.shape[1] // 128):
                piece = result[VH * z + BIG * y : VH * z + BIG * y + n, 128 * i : 128 * i + 128].astype(BF)
                stage[z, y, first_x + i, 0:n] = piece
                if n < BIG:
                    stage[z, y, first_x + i, n:BIG] = jnp.zeros((BIG - n, 128), BF)


def stage_columns(stage, result, first_z):
    for i in range(result.shape[1] // 128):
        z, xc = first_z + i // 2, i % 2
        for y in range(4):
            for xr in range(2):
                first = 224 * y + BIG * xr
                stage[z, y, 2 * xr + xc, 0:BIG] = result[first : first + BIG, 128 * i : 128 * i + 128].astype(BF)


def stage_square(stage, result, first_row):
    for z in range(4):
        for y in range(4):
            for x in range(4):
                piece = result[256 * z + 64 * y : 256 * z + 64 * y + 64, 128 * x : 128 * x + 128].astype(BF)
                stage[z, y, x, first_row : first_row + 64] = piece


def fold(rows):
    return jnp.sum(rows.reshape(rows.shape[0] // 8, 8, rows.shape[1]), axis=0)


def unrotated(grad, cosine, sine):
    grad = grad.astype(BF).astype(F32)
    front, behind = grad[:, :128], grad[:, 128:]
    return jnp.concatenate([front * cosine + behind * sine, behind * cosine - front * sine], axis=1).astype(BF)


def backward_kernel(
    act_hbm, coth_hbm, lhalf_hbm, second_hbm, first_hbm, mixed_hbm, lift_hbm, cot_hbm, hidden_hbm, stats_hbm,
    u_hbm, w_hbm, heads_hbm, q_hbm, k_hbm, v_hbm, w01_hbm, w23_hbm, sin_hbm, qnext_hbm, tokens_hbm, table_hbm,
    wq_hbm, wk_hbm, wv_hbm, wg_hbm, wo_hbm, wu_hbm, gain1, gain2, lengths, windows,
    out_tokens, out_vec, out_down, out_up, out_out, out_gate, out_value, out_qk,
    x1, x2, x3, y1, ch, wide, cot, heads, u_ref, w_ref, queries, keys, values, w01, w23, state_in,
    back_state, back_near, back_far, rgrad, hidden, wf, wu, wo, table, stats, qnext, gnext, vec_rows,
    vec, vec_core, vec_z, vec_y, vec_x, vec_out,
    stage0, stage1, stage2, stage3, *rest,
):
    lands = [[rest[(3 * s + p) * LANDINGS : (3 * s + p + 1) * LANDINGS] for p in range(3)] for s in range(4)]
    rest = rest[12 * LANDINGS :]
    mines = rest[0:18]
    load_sems, save_sems, pair_send, pair_recv, z_send, z_recv, vec_send, vec_recv = rest[18:26]
    unit_send, unit_recv, unit_copy, credits, pair_credit, pass_send, pass_recv = rest[26:]
    stages = (stage0, stage1, stage2, stage3)
    at = coordinates()
    z, core = at[0], at[3]
    start = z * TOK

    loading = {}

    def load(name, source, target):
        copy = pltpu.make_async_copy(source, target, load_sems.at[len(loading)])
        copy.start()
        loading[name] = copy

    def ready(*names):
        for name in names:
            loading[name].wait()

    waited = set()

    def ready_once(*names):
        for name in names:
            if name not in waited:
                waited.add(name)
                loading[name].wait()

    own_rows = pl.ds(pl.multiple_of(core * TOK, TOK), TOK)
    load("act", act_hbm, x1.at[own_rows])
    load("lhalf", lhalf_hbm, y1)
    load("second", second_hbm, x2)
    load("coth", coth_hbm, ch)
    load("lift", lift_hbm, wide)
    load("wu", wu_hbm, wu)
    greet(at)

    outs = dict(zip(UNITS, (out_down, out_up, out_out, out_gate, out_value, out_qk)))
    units = {}
    for n, name in enumerate(UNITS):
        s, parts = UNIT_SET[name], []
        for p in range(3):
            slot = 3 * n + p
            order, gather = PLAN[name][p]
            follower = FOLLOWER.get(name)
            parts.append(
                Part(
                    at, stages[s], lands[s][p], mines[slot], outs[name], CUTS[UNIT_ROWS[name]][p], order, gather,
                    (unit_send, unit_recv, unit_copy), slot,
                    credits.at[slot - 12] if n >= 4 else None, credits.at[slot] if follower else None,
                    PLAN[follower][p][0] if follower else None, name in THRIFTY,
                )
            )
        units[name] = Unit(parts, name in THRIFTY)
    down, up, out, gate, value, qk = (units[name] for name in UNITS)
    numbered = [units[name] for name in UNITS]
    ticks = iter(SCHEDULE)

    def tick():
        for n in next(ticks):
            if n < len(UNITS):
                numbered[n].pump()
            else:
                passing.forward(n - len(UNITS), joins)

    pairs = []

    def to_sibling(source, target):
        copy = pltpu.make_async_remote_copy(
            src_ref=source, dst_ref=target, send_sem=pair_send.at[len(pairs)], recv_sem=pair_recv.at[len(pairs)],
            device_id=shifted(at, 3, 1), device_id_type=MESH,
        )
        copy.start()
        pairs.append(copy)
        return copy

    local_copies = []

    def halves(source, width, landing, lane):
        rows = pl.ds(pl.multiple_of(core * TOK, TOK), TOK)
        lanes = pl.ds(lane, width)
        mine = source.at[:, pl.ds(pl.multiple_of(core * width, width), width)]
        other = source.at[:, pl.ds(pl.multiple_of((1 - core) * width, width), width)]
        remote = to_sibling(other, landing.at[rows, lanes])
        local = pltpu.make_async_copy(mine, landing.at[rows, lanes], save_sems.at[len(local_copies)])
        local.start()
        local_copies.append(local)
        return remote, local

    def arrived(pair):
        pair[0].wait()
        pair[1].wait()

    ready("act")
    act_pair = to_sibling(x1.at[own_rows], x1.at[own_rows])

    def tell_sibling(slot):
        pl.semaphore_signal(pair_credit.at[slot], inc=1, device_id=shifted(at, 3, 1), device_id_type=MESH)

    docs = Documents(lengths)
    doc_before = docs.of(start - 1)
    doc_last = docs.of(start + TOK - 1)
    place = column(TOK)
    doc_rows = docs.of(place + start)
    joins = [jnp.where(doc_before == doc_last, math.exp(LOG_GAMMA[h] * TOK), 0.0) for h in (2, 3)]
    passing = Passing(at, -1, back_state, back_near, back_far, (pass_send, pass_recv), 0)
    zero = jnp.zeros((8, D), F32)
    grad_v = u_ref
    pair = {}
    g_halo = pltpu.make_async_remote_copy(
        src_ref=rgrad.at[pl.ds(0, 2), pl.ds(0, HALO)], dst_ref=gnext, send_sem=z_send.at[0], recv_sem=z_recv.at[0],
        device_id=shifted(at, 0, 3), device_id_type=MESH,
    )

    def head_cols(h):
        return slice(h * KEYH, (h + 1) * KEYH)

    def row_factor(h):
        return jnp.where(doc_rows == doc_before, jnp.exp(place.astype(F32) * LOG_GAMMA[h]), 0.0)

    def two_halves(work):
        for half in (0, 1):
            cols = slice(512 * half, 512 * half + 512)
            wf[:, cols] = work(cols)
            tick()

    def block_down():
        ready("coth")
        act_pair.wait()
        for half in (0, 1):
            stage_rows(stage0, dot_tn(x1[...], ch[:, 256 * half : 256 * half + 256]), 2 * half)
        down.start()
        load("mixed", mixed_hbm, x1)
        tell_sibling(0)
        tick()

    def block_up():
        ready("lhalf", "second")
        for half in (0, 1):
            stage_columns(stage1, dot_tn(y1[...], x2[:, 512 * half : 512 * half + 512]), 2 * half)
        up.start()
        tell_sibling(1)
        tick()

    def block_second():
        ready("lift", "wu")
        two_halves(lambda cols: dot_nn(wide[:, 0:FF], wu[:, cols]))
        load("wg", wg_hbm, wu)

    def block_norm2():
        ready("cot", "hidden", "stats")

        def back_two(i, sums):
            rows = pl.ds(pl.multiple_of(i * 64, 64), 64)
            grad = wf[rows]
            inverse = stats[rows, 3:4]
            scaled = (hidden[rows] - stats[rows, 2:3]) * inverse
            e = grad * gain2[...]
            inner = e - jnp.mean(e, axis=-1, keepdims=True) - scaled * jnp.mean(e * scaled, axis=-1, keepdims=True)
            total = cot[rows].astype(F32) + inverse * inner
            hidden[rows] = total
            cot[rows] = total.astype(BF)
            return (sums[0] + fold(grad * scaled), sums[1] + fold(grad))

        gain_sum, bias_sum = lax.fori_loop(0, TOK // 64, back_two, (zero, zero))
        pl.semaphore_wait(pair_credit.at[0], 1)
        pair["low"] = halves(cot, 512, ch, 0)
        vec_rows[2:3] = jnp.sum(gain_sum, axis=0, keepdims=True)
        vec_rows[3:4] = jnp.sum(bias_sum, axis=0, keepdims=True)
        tick()

    def mixed_grad(h):
        ready_once("wo", "u", "w", "heads")
        lane = 512 * (h % 2)
        wf[:, lane : lane + VH] = dot_nt(cot[...], wo[h * VH : (h + 1) * VH])

    def back_head(h, rows):
        lane = 512 * (h % 2)
        grad = wf[rows, lane : lane + VH]
        c = heads[h, rows].astype(F32)
        gated = grad * c * w_ref[h, rows].astype(F32)
        e = (grad * u_ref[h, rows].astype(F32)).astype(BF).astype(F32)
        inner = e - jnp.mean(e, axis=-1, keepdims=True) - c * jnp.mean(e * c, axis=-1, keepdims=True)
        rgrad[h, rows] = (inner * stats[rows, 4 + h : 5 + h]).astype(BF)
        return gated

    def block_mixl():
        mixed_grad(2)
        mixed_grad(3)
        for h in (2, 3):
            for row in range(0, TOK, 64):
                rows = slice(row, row + 64)
                w_ref[h, rows] = back_head(h, rows).astype(BF)
            tick()

    def block_states():
        ready("q")
        for h in (2, 3):
            scaled = (queries[:, head_cols(h)].astype(F32) * row_factor(h)).astype(BF)
            back_state[h - 2] = dot_tn(rgrad[h], scaled).astype(BF)
            passing.begin(2 * h - 4)
            passing.begin(2 * h - 3)
        passing.clear()
        tick()

    def block_mixe():
        mixed_grad(0)
        mixed_grad(1)
        load("wv", wv_hbm, wo)
        for row in range(0, TOK, 64):
            rows = slice(row, row + 64)
            parts = [back_head(h, rows) for h in (0, 1)] + [w_ref[h, rows].astype(F32) for h in (2, 3)]
            gated = jnp.concatenate(parts, axis=1).astype(BF)
            wide[rows] = jnp.concatenate([gated, jnp.zeros((64, WIDE - VD), BF)], axis=1)
            if row == TOK // 2 - 64:
                tick()
        ready("qnext")

        @pl.when(z > 0)
        def _():
            g_halo.start()

        @pl.when(z == 3)
        def _():
            gnext[...] = jnp.zeros((2, HALO, VH), BF)
            qnext[...] = jnp.zeros((HALO, 2 * KEYH), BF)

        pl.semaphore_wait(pair_credit.at[1], 1)
        pair["gate"] = halves(wide, HALF, y1, 0)
        tick()

    def block_out():
        ready("mixed")
        arrived(pair["low"])
        for half in (0, 1):
            stage_rows(stage2, dot_tn(x1[...], ch[:, 256 * half : 256 * half + 256]), 2 * half)
        out.start()
        tell_sibling(2)
        tick()

    def block_gate():
        ready("first")
        arrived(pair["gate"])
        for half in (0, 1):
            stage_columns(stage3, dot_tn(y1[...], x3[:, 512 * half : 512 * half + 512]), 2 * half)
        gate.start()
        tick()

    def block_fg():
        ready("wg")
        two_halves(lambda cols: dot_nn(wide[:, 0:VD], wu[:, cols]))

    def finish_query(h, grad):
        queries[:, head_cols(h)] = unrotated(grad, table[:, 0:128], table[:, 128:256])

    def finish_key(h, grad, rows=slice(0, TOK)):
        cot[rows, head_cols(h)] = unrotated(grad, table[rows, 256:384], table[rows, 384:512])

    def block_full():
        ready_once("k", "v", "w01", "w23", "sin", "table")
        for h in (2, 3):
            cols_h = head_cols(h)
            score = []
            for b in (0, 1):
                rows, cols = slice(256 * b, 256 * b + 256), 256 * b + 256
                grad = dot_nt(rgrad[h, rows], values[h, HALO : HALO + cols])
                grad = (grad * decay_block(h, 256, cols, 256 * b, 0, start, docs, None)).astype(BF)
                score.append(grad)
            late = dot_tn(score[1], queries[256:512, cols_h])
            early = dot_tn(score[0], queries[0:256, cols_h])
            ch[0:TOK, head_cols(h - 2)] = jnp.concatenate([early + late[:256], late[256:]], axis=0).astype(BF)
            query = jnp.concatenate([dot_nn(score[b], keys[HALO : HALO + 256 * b + 256, cols_h]) for b in (0, 1)], axis=0)
            query = query + row_factor(h) * dot_nn(rgrad[h], state_in[h - 2])
            finish_query(h, query)
            late = dot_tn(w23[h - 2, 256:512], rgrad[h, 256:512])
            early = dot_tn(w23[h - 2, 0:256, 0:256], rgrad[h, 0:256])
            grad_v[h] = jnp.concatenate([early + late[:256], late[256:]], axis=0).astype(BF)
            tick()

    def block_band():
        ready_once("k", "v", "w01", "w23", "sin", "table")
        for h in (0, 1):
            cols_h = head_cols(h)
            parts_q, parts_k, parts_v = [], [], []
            for b in (0, 1):
                rows, ext = slice(256 * b, 256 * b + 256), slice(256 * b, 256 * b + 384)
                grad = dot_nt(rgrad[h, rows], values[h, ext])
                decay = decay_block(h, 256, 384, 256 * b, 256 * b - HALO, start, docs, windows[0, h])
                grad = (grad * decay).astype(BF)
                parts_q.append(dot_nn(grad, keys[ext, cols_h]))
                parts_k.append(dot_tn(grad, queries[rows, cols_h]))
                parts_v.append(dot_tn(w01[h, b], rgrad[h, rows]))

            def joined(parts):
                return jnp.concatenate(
                    [parts[0][HALO : 2 * HALO], parts[0][2 * HALO :] + parts[1][:HALO], parts[1][HALO:]], axis=0
                )

            finish_query(h, jnp.concatenate(parts_q, axis=0))
            key = joined(parts_k)
            finish_key(h, key[:LAST], slice(0, LAST))
            ch[TOK : TOK + HALO, cols_h] = key[LAST:].astype(BF)
            grad_v[h] = joined(parts_v).astype(BF)
            tick()

    def block_far():
        @pl.when(z < 3)
        def _():
            g_halo.wait_recv()

        tail = slice(TOK, TOK + HALO)
        for h in (0, 1):
            cols_h = head_cols(h)
            decay = decay_block(h, HALO, HALO, TOK, LAST, start, docs, windows[0, h])
            far_w = (dot_nt(qnext[:, cols_h], keys[tail, cols_h]) * decay).astype(BF)
            far_s = (dot_nt(gnext[h], values[h, tail]) * decay).astype(BF)
            key = ch[TOK : TOK + HALO, cols_h].astype(F32) + dot_tn(far_s, qnext[:, cols_h])
            finish_key(h, key, slice(LAST, TOK))
            grad_v[h, LAST:] = (grad_v[h, LAST:].astype(F32) + dot_tn(far_w, gnext[h])).astype(BF)
        share_keys()
        tick()

    def block_cross():
        passing.finish()
        from_last = docs.of(3 * TOK - 1) == doc_last
        for h in (2, 3):
            cols_h = head_cols(h)
            power = jnp.where(z == 0, math.exp(2 * TOK * LOG_GAMMA[h]), math.exp(TOK * LOG_GAMMA[h]))
            total = back_near[h - 2].astype(F32) + back_far[h - 2].astype(F32) * jnp.where(from_last, power, 0.0)
            state_in[h - 2] = total.astype(BF)
            factor = jnp.where(doc_rows == doc_last, jnp.exp((TOK - place).astype(F32) * LOG_GAMMA[h]), 0.0)
            grad = ch[0:TOK, head_cols(h - 2)].astype(F32)
            finish_key(h, grad + factor * dot_nn(values[h, HALO:], state_in[h - 2]))
            grad_v[h] = (grad_v[h].astype(F32) + factor * dot_nt(keys[HALO:, cols_h], state_in[h - 2])).astype(BF)
        share_keys()
        tick()

    retained = []

    def share_keys():
        retained.append(0)
        if len(retained) == 2:
            pair["query"] = halves(queries, 512, x2, 0)
            pair["key"] = halves(cot, 512, x2, 512)

    def block_store():
        def store_value(rows):
            joint = jnp.concatenate([grad_v[h, rows].astype(F32) for h in range(HEADS)], axis=1).astype(BF)
            wide[rows] = jnp.concatenate([joint, jnp.zeros((joint.shape[0], WIDE - VD), BF)], axis=1)

        row_loop(TOK, 64, store_value)
        pl.semaphore_wait(pair_credit.at[2], 1)
        pair["value"] = halves(wide, HALF, x1, 0)
        load("tokens", tokens_hbm, keys.at[pl.ds(0, TOK)])
        tick()

    def block_qk():
        up.reduced()
        arrived(pair["query"])
        arrived(pair["key"])
        stage_square(stage1, dot_tn(x3[...], x2[:, 0:512]), 0)
        stage_square(stage1, dot_tn(x3[...], x2[:, 512:1024]), 64)
        qk.start()
        load("wq", wq_hbm, x2)
        tick()

    def block_value():
        down.reduced()
        arrived(pair["value"])
        for half in (0, 1):
            stage_columns(stage0, dot_tn(x1[:, 0:HALF], x3[:, 512 * half : 512 * half + 512]), 2 * half)
        value.start()
        load("wk", wk_hbm, x3)
        tick()

    def block_fv():
        ready("wv")
        two_halves(lambda cols: wf[:, cols] + dot_nn(wide[:, 0:VD], wo[:, cols]))

    def block_fq():
        ready("wq")
        two_halves(lambda cols: wf[:, cols] + dot_nt(queries[...], x2[cols]))

    def block_fk():
        ready("wk")
        two_halves(lambda cols: wf[:, cols] + dot_nt(cot[...], x3[cols]))

    def block_n1():
        ready("tokens")

        def back_one(i, sums):
            rows = pl.ds(pl.multiple_of(i * 64, 64), 64)
            grad = wf[rows]
            inverse = stats[rows, 1:2]
            scaled = (keys[rows].astype(F32) - stats[rows, 0:1]) * inverse
            e = grad * gain1[...]
            inner = e - jnp.mean(e, axis=-1, keepdims=True) - scaled * jnp.mean(e * scaled, axis=-1, keepdims=True)
            keys[rows] = (hidden[rows] + inverse * inner).astype(BF)
            return (sums[0] + fold(grad * scaled), sums[1] + fold(grad))

        gain_sum, bias_sum = lax.fori_loop(0, TOK // 64, back_one, (zero, zero))
        pair["tokens"] = pltpu.make_async_copy(keys.at[pl.ds(0, TOK)], out_tokens, save_sems.at[len(local_copies)])
        pair["tokens"].start()
        vec_rows[0:1] = jnp.sum(gain_sum, axis=0, keepdims=True)
        vec_rows[1:2] = jnp.sum(bias_sum, axis=0, keepdims=True)
        for block in range(4):
            for j in range(4):
                for t in range(2):
                    first = 256 * block + 128 * t
                    vec[block, 2 * j + t : 2 * j + t + 1] = vec_rows[j : j + 1, first : first + 128]
        next(vectors)
        tick()

    vectors = vector_steps(at, vec, vec_core, vec_z, vec_y, vec_x, vec_out, (vec_send, vec_recv), 0)
    known = {
        "down": block_down, "up": block_up, "second": block_second, "norm2": block_norm2, "mixl": block_mixl, "states": block_states,
        "mixe": block_mixe, "out": block_out, "gate": block_gate, "fg": block_fg, "full": block_full, "band": block_band, "far": block_far,
        "cross": block_cross, "store": block_store, "qk": block_qk, "value": block_value, "fv": block_fv, "fq": block_fq,
        "fk": block_fk, "n1": block_n1,
    }
    for number, name in enumerate(BLOCKS):
        known[name]()
        if number == 0:
            load("cot", cot_hbm, cot)
            load("hidden", hidden_hbm, hidden)
            load("stats", stats_hbm, stats)
            load("wo", wo_hbm, wo)
            load("u", u_hbm, u_ref)
            load("w", w_hbm, w_ref)
            load("heads", heads_hbm, heads)
            load("q", q_hbm, queries)
            load("qnext", qnext_hbm, qnext)
        if number == 1:
            load("first", first_hbm, x3)
            load("k", k_hbm, keys)
            load("v", v_hbm, values)
            load("sin", sin_hbm, state_in)
            load("w23", w23_hbm, w23)
            load("w01", w01_hbm, w01)
            load("table", table_hbm.at[pl.ds(pl.multiple_of(z * TOK + HALO, HALO), TOK)], table)

    for count, n in enumerate(TAIL):
        numbered[n].pump()
        if count % 4 == 3:
            next(vectors, 0)
    todo = [qk, value, gate, out, up, down]
    vectors_open = True
    while todo or vectors_open:
        todo = [unit for unit in todo if unit.pump()]
        vectors_open = next(vectors, 0) is None
    last = pltpu.make_async_copy(vec_out, out_vec, save_sems.at[len(local_copies) + 1])
    last.start()

    @pl.when(z > 0)
    def _():
        g_halo.wait_send()

    passing.drain()
    pair["tokens"].wait()
    last.wait()


def backward(arrays, gain1, gain2, lengths, windows):
    vmem = pl.BlockSpec(memory_space=pltpu.VMEM)
    smem = pl.BlockSpec(memory_space=pltpu.SMEM)
    anywhere = pl.BlockSpec(memory_space=pl.ANY)
    shape = jax.ShapeDtypeStruct
    outs = [shape((TOK, D), BF), shape((8, 128), F32)] + [shape((2, 4, 4, UNIT_ROWS[n], 128), BF) for n in UNITS]
    scratch = [
        pltpu.VMEM((2 * TOK, VD), BF), pltpu.VMEM((2 * TOK, D), BF), pltpu.VMEM((2 * TOK, D), BF), pltpu.VMEM((2 * TOK, HALF), BF),
        pltpu.VMEM((2 * TOK, 512), BF), pltpu.VMEM((TOK, WIDE), BF), pltpu.VMEM((TOK, D), BF), pltpu.VMEM((HEADS, TOK, VH), BF),
        pltpu.VMEM((HEADS, TOK, VH), BF), pltpu.VMEM((HEADS, TOK, VH), BF), pltpu.VMEM((TOK, QK), BF), pltpu.VMEM((HALO + TOK, QK), BF),
        pltpu.VMEM((HEADS, HALO + TOK, VH), BF), pltpu.VMEM((2, 2, 256, 384), BF), pltpu.VMEM((2, TOK, TOK), BF),
        pltpu.VMEM((2, VH, KEYH), BF), pltpu.VMEM((2, VH, KEYH), BF),
        pltpu.VMEM((2, VH, KEYH), BF), pltpu.VMEM((2, VH, KEYH), BF),
        pltpu.VMEM((HEADS, TOK, VH), BF), pltpu.VMEM((TOK, D), F32),
        pltpu.VMEM((TOK, D), F32), pltpu.VMEM((VD, D), BF), pltpu.VMEM((VD, D), BF), pltpu.VMEM((TOK, 512), F32),
        pltpu.VMEM((TOK, 128), F32), pltpu.VMEM((HALO, 2 * KEYH), BF), pltpu.VMEM((2, HALO, VH), BF), pltpu.VMEM((8, D), F32),
        pltpu.VMEM((4, 8, 128), F32), pltpu.VMEM((4, 8, 128), F32), pltpu.VMEM((4, 8, 128), F32), pltpu.VMEM((4, 8, 128), F32),
        pltpu.VMEM((4, 8, 128), F32), pltpu.VMEM((8, 128), F32),
    ]
    scratch += [pltpu.VMEM((4, 4, 4, r, 128), BF) for r in SET_ROWS]
    for r in SET_ROWS:
        for count in PART_ROWS[r]:
            scratch += [pltpu.VMEM(s, BF) for s in landing_shapes(count)]
    for name in UNITS:
        scratch += [pltpu.VMEM((count, 128), BF) for count in PART_ROWS[UNIT_ROWS[name]]]
    dma, regular = pltpu.SemaphoreType.DMA, pltpu.SemaphoreType.REGULAR
    scratch += [dma((28,)), dma((8,)), dma((6,)), dma((6,)), dma((4,)), dma((4,)), dma((10,)), dma((10,))]
    scratch += [dma((18,)), dma((18 * ARRIVALS,)), dma((18,)), regular((6,)), regular((3,)), dma((8,)), dma((8,))]
    return pl.pallas_call(
        backward_kernel,
        out_shape=outs,
        in_specs=[anywhere] * 28 + [vmem] * 2 + [smem] * 2,
        out_specs=[anywhere] * len(outs),
        scratch_shapes=scratch,
        compiler_params=pltpu.CompilerParams(collective_id=2, has_side_effects=True, vmem_limit_bytes=63 * 2**20),
        cost_estimate=pl.CostEstimate(flops=26 * 10**9, bytes_accessed=70 * 10**6, transcendentals=10**6),
        name="backward",
    )(*arrays, gain1.reshape(1, D), gain2.reshape(1, D), lengths, windows.reshape(1, HEADS))


def unpack_kernel(down, up, out, gate, value, qk, result, tokens, vectors, *outs):
    g_down, g_up, g_out, g_gate, g_value, g_query, g_key, out_result, out_tokens = outs[:9]
    for y in range(4):
        for x in range(4):
            cols = slice(128 * x, 128 * x + 128)
            for source, target in ((down, g_down), (out, g_out)):
                target[BIG * y : BIG * y + BIG, cols] = source[0, y, x].astype(F32)
            g_query[64 * y : 64 * y + 64, cols] = qk[0, y, x, 0:64].astype(F32)
            g_key[64 * y : 64 * y + 64, cols] = qk[0, y, x, 64:128].astype(F32)
            first, lane = 2 * BIG * y + BIG * (x // 2), 128 * (x % 2)
            for source, target in ((up, g_up), (gate, g_gate), (value, g_value)):
                target[first : first + BIG, lane : lane + 128] = source[0, y, x].astype(F32)
    out_result[...] = result[...]
    out_tokens[...] = tokens[...]
    for j, target in enumerate(outs[9:]):
        target[...] = vectors[2 * j : 2 * j + 2]


def unpack(gathered, result, grad_tokens, vectors):
    def source(rows):
        return pl.BlockSpec((1, 4, 4, rows, 128), lambda c: (c, 0, 0, 0, 0))

    tall = pl.BlockSpec((4 * BIG, 512), lambda c: (0, c))
    turned = pl.BlockSpec((WIDE // 2, 256), lambda c: (c, 0))
    square = pl.BlockSpec((256, 512), lambda c: (0, c))
    plain = pl.BlockSpec((TOK // 2, D), lambda c: (c, 0))
    shape = jax.ShapeDtypeStruct
    return pl.pallas_call(
        unpack_kernel,
        grid=(2,),
        out_shape=[
            shape((VH, D), F32), shape((FF, 256), F32), shape((VH, D), F32), shape((VD, 256), F32), shape((VD, 256), F32),
            shape((256, QK), F32), shape((256, QK), F32), shape((TOK, D), BF), shape((TOK, D), BF),
        ]
        + [shape((2, 128), F32)] * 4,
        in_specs=[source(UNIT_ROWS[n]) for n in UNITS] + [plain, plain, pl.BlockSpec((8, 128), lambda c: (0, 0))],
        out_specs=[tall, turned, tall, turned, turned, square, square, plain, plain] + [pl.BlockSpec((2, 128), lambda c: (0, 0))] * 4,
        compiler_params=pltpu.CompilerParams(vmem_limit_bytes=62 * 2**20),
        name="unpack",
    )(*gathered, result, grad_tokens, vectors)


def body(
    tokens, ln_gain1, ln_bias1, w_query, w_key, w_value, w_gate, w_out, ln_gain2, ln_bias2, w_up, w_down, doc_lengths, windows, cotangent
):
    table = jnp.asarray(rotary_constants())
    (
        result, first, second, mixed, act, cot_half, lift_half, lift, q, k, v, w01, w23, s_in, heads, u, w, hidden, stats, qnext,
    ) = forward(
        tokens[0], cotangent[0], ln_gain1, ln_bias1, ln_gain2, ln_bias2, doc_lengths, windows, table,
        w_query, w_key, w_value, w_gate, w_out, w_up, w_down,
    )

    def pair(a):
        return a.reshape(2 * TOK, a.shape[2])

    arrays = (
        act, pair(cot_half), pair(lift_half), pair(second), pair(first), pair(mixed), lift, cotangent[0], hidden, stats,
        u, w, heads, q, k, v, w01, w23, s_in, qnext, tokens[0], table,
        w_query, w_key, w_value.T, w_gate.T, w_out, w_up.T,
    )
    grad_tokens, vectors, *gathered = backward(arrays, ln_gain1, ln_gain2, doc_lengths, windows)
    g_down, g_up, g_out, g_gate, g_value, g_query, g_key, result, grad_tokens, *vectors = unpack(
        gathered, result, grad_tokens, vectors
    )
    gain1, bias1, gain2, bias2 = (vector.reshape(256) for vector in vectors)
    return (
        result.reshape(1, TOK, D), grad_tokens.reshape(1, TOK, D), gain1, bias1, g_query, g_key, g_value.T, g_gate.T, g_out,
        gain2, bias2, g_up.T, g_down,
    )


def solution(mesh):
    in_specs = (P("batch", "head", None),) + (P(),) * 11 + (P("batch", None), P(), P("batch", "head", None))
    rows, vector = P("head", None), P("head")
    out_specs = (
        P("batch", "head", None), P("batch", "head", None), vector, vector, rows, rows, rows, rows, rows, vector, vector, rows, rows,
    )
    return jax.shard_map(body, mesh=mesh, in_specs=in_specs, out_specs=out_specs, check_vma=False)
```

```python
import functools
import math

import jax
import jax.numpy as jnp
import numpy as np
from jax import lax
from jax.experimental import pallas as pl
from jax.experimental.pallas import tpu as pltpu
from jax.sharding import PartitionSpec as P

D = 1024
HEADS = 4
KEYH = 256
VH = 432
FF = 1728
QK = 1024
VD = 1728
TOK = 512
SEQ = 2048
HALO = 128
WIDE = 1792

epsilon = 1e-05
retention_floor = 1.0
BF = jnp.bfloat16
F32 = jnp.float32
MESH = pl.DeviceIdType.MESH


BIG, PAIRED = 112, 128
CUTS = {BIG: ((0, 48), (48, 32), (80, 32)), PAIRED: ((0, 48), (48, 48), (96, 32))}
ARRIVALS = 9


def coordinates():
    z = lax.axis_index("head")
    b = lax.axis_index("batch")
    return [z, lax.div(b, 8), lax.rem(lax.div(b, 2), 4), lax.rem(b, 2)]


def shifted(at, axis, step):
    place = list(at)
    if axis == 3:
        place[3] = 1 - place[3]
    else:
        place[axis] = lax.rem(place[axis] + step, 4)
    return (place[0], (place[1] * 4 + place[2]) * 2 + place[3])


def away(p, step):
    return lax.rem(p + step, 4)


LOW, HIGH = pl.ds(0, 2), pl.ds(2, 2)


def landing_shapes(r):
    return [(2, 2, 4, r, 128), (2, 4, 4, r, 128), (3, 4, r, 128), (3, r, 128)]


LANDINGS = 4


class Part:
    def __init__(self, at, stage, lands, mine, out, rows, order, gather, sems, slot, credit_in, credit_out, next_order, thrifty, joint):
        self.at, self.stage, self.out = at, stage, out
        self.first, self.count = rows
        self.lands = [land.at[..., pl.ds(0, self.count), :] for land in lands]
        self.mine = mine.at[pl.ds(0, self.count)]
        self.order, self.gather = order, gather
        send_sems, recv_sems, copy_sems = sems
        self.send_sem, self.copy_sem = send_sems.at[slot], copy_sems.at[slot]
        self.recv_sems = [recv_sems.at[ARRIVALS * slot + n] for n in range(ARRIVALS)]
        self.credit_in, self.credit_out, self.next_order = credit_in, credit_out, next_order
        self.thrifty = thrifty
        self.joint = joint
        self.lend = None

    def copy(self, source, target, axis, step, arrival):
        return pltpu.make_async_remote_copy(
            src_ref=source, dst_ref=target, send_sem=self.send_sem, recv_sem=self.recv_sems[arrival],
            device_id=shifted(self.at, axis, step), device_id_type=MESH,
        )

    def send(self, source, target, axis, step, arrival):
        self.copy(source, target, axis, step, arrival).start()

    def arrived(self, size, arrival):
        whole = self.copy(size, size, 3, 1, arrival)
        whole.wait_recv()
        whole.wait_send()

    def pick(self, axes):
        index = [slice(None)] * 3
        for axis, value in axes.items():
            index[axis] = value
        return self.stage.at[tuple(index) + (pl.ds(self.first, self.count), slice(None))]

    @staticmethod
    def writers(order):
        a1, a2, a3 = order
        return [(a1, 1), (a1, 3)] + [(axis, step) for axis in (a2, a3) for step in (1, 2, 3)]

    def steps(self):
        at, lands = self.at, self.lands
        a1, a2, a3 = self.order
        p1, p2, p3 = at[a1], at[a2], at[a3]
        cut = min(a2, a3)
        if self.credit_in is not None:
            pl.semaphore_wait(self.credit_in, len(self.writers(self.order)))
        self.send(self.pick({a1: away(p1, 2), cut: LOW}), lands[0].at[0], a1, 1, 0)
        self.send(self.pick({a1: away(p1, 2), cut: HIGH}), lands[0].at[1], a1, 3, 0)
        yield
        self.arrived(lands[0], 0)
        for n, step, part in ((0, 1, LOW), (1, 3, HIGH)):
            there = self.pick({a1: away(p1, step), cut: part})
            there[...] = there[...] + lands[0][n]
            self.send(self.pick({a1: away(p1, step)}), lands[1].at[n], a1, step, 1)
        yield
        self.arrived(lands[1], 1)
        own = self.pick({a1: p1})
        own[...] = (own[...].astype(F32) + lands[1][0].astype(F32) + lands[1][1].astype(F32)).astype(BF)
        if self.thrifty:
            self.send(self.pick({a1: p1, a2: away(p2, 2), a3: LOW}), lands[2].at[0, LOW], a2, 1, 2)
            self.send(self.pick({a1: p1, a2: away(p2, 2), a3: HIGH}), lands[2].at[0, HIGH], a2, 3, 2)
            yield
            self.arrived(lands[2].at[0], 2)
            for n, step, part in ((1, 1, LOW), (2, 3, HIGH)):
                there = self.pick({a1: p1, a2: away(p2, step), a3: part})
                there[...] = there[...] + lands[2][0, 2 * n - 2 : 2 * n]
                self.send(self.pick({a1: p1, a2: away(p2, step)}), lands[2].at[n], a2, step, 7)
            yield
            self.arrived(lands[2].at[pl.ds(1, 2)], 7)
            come = (1, 2)
        else:
            for s in (1, 2, 3):
                self.send(self.pick({a1: p1, a2: away(p2, s)}), lands[2].at[s - 1], a2, s, 2)
            yield
            self.arrived(lands[2], 2)
            come = (0, 1, 2)
        own = self.pick({a1: p1, a2: p2})
        total = own[...].astype(F32)
        for step in come:
            total = total + lands[2][step].astype(F32)
        own[...] = total.astype(BF)
        if self.lend is not None:
            credit, axis = self.lend
            for step in (1, 2, 3):
                pl.semaphore_signal(credit, inc=1, device_id=shifted(at, axis, step), device_id_type=MESH)
        if self.joint is not None:
            yield from self.joint_steps(own)
            return
        for s in (1, 2, 3):
            self.send(self.pick({a1: p1, a2: p2, a3: away(p3, s)}), lands[3].at[s - 1], a3, s, 3)
        yield
        self.arrived(lands[3], 3)
        total = self.pick({a1: p1, a2: p2, a3: p3})[...].astype(F32)
        for step in range(3):
            total = total + lands[3][step].astype(F32)
        self.mine[...] = total.astype(BF)
        if self.credit_out is not None:
            for axis, step in self.writers(self.next_order):
                pl.semaphore_signal(self.credit_out, inc=1, device_id=shifted(at, axis, step), device_id_type=MESH)

        rows = pl.ds(self.first, self.count)
        g1, g2 = self.gather
        target = self.out.at[at[3], at[1], at[2], rows]
        local = pltpu.make_async_copy(self.mine, target, self.copy_sem)
        local.start()
        for s in (1, 2, 3):
            self.send(self.mine, target, g1, s, 4)
        yield
        self.arrived(lands[3], 4)
        local.wait()

        def block(place, part=slice(None)):
            if g2 == 1:
                return self.out.at[at[3], place, part, rows]
            return self.out.at[at[3], part, place, rows]

        q = at[g2]
        if self.thrifty:
            for s in (1, 3):
                self.send(block(q), block(q), g2, s, 5)
            yield
            self.arrived(lands[2].at[pl.ds(0, 2)], 5)
            for s, part in ((1, LOW), (3, HIGH)):
                source = block(away(q, 4 - s), part)
                self.send(source, source, g2, s, 8)
            yield
            self.arrived(lands[2].at[0], 8)
        else:
            for s in (1, 2, 3):
                self.send(block(q), block(q), g2, s, 5)
            yield
            self.arrived(lands[2], 5)
        for place in range(4):
            self.send(block(place), block(place), 3, 1, 6)
        yield
        self.arrived(lands[1].at[0], 6)


    def joint_steps(self, own):
        at, (borrowed, credit) = self.at, self.joint
        axis, (g1, g2) = self.order[2], self.gather
        rows = pl.ds(self.first, self.count)
        borrowed = borrowed.at[..., pl.ds(0, self.count), :]
        pl.semaphore_wait(credit, 3)
        for s in (1, 2, 3):
            self.send(own, borrowed.at[s - 1], axis, s, 3)
        yield
        self.arrived(borrowed, 3)
        first = own[...].astype(F32) + borrowed[1].astype(F32)
        second = borrowed[0].astype(F32) + borrowed[2].astype(F32)
        own[...] = (first + second).astype(BF)

        def block(place):
            if g2 == 1:
                return self.out.at[at[3], place, :, rows]
            return self.out.at[at[3], :, place, rows]

        q = at[g2]
        local = pltpu.make_async_copy(own, block(q), self.copy_sem)
        local.start()
        for s in (1, 2, 3):
            self.send(own, block(q), g2, s, 5)
        yield
        self.arrived(self.lands[2], 5)
        local.wait()
        for place in range(4):
            self.send(block(place), block(place), 3, 1, 6)
        yield
        self.arrived(self.lands[1].at[0], 6)


class Unit:
    def __init__(self, parts, thrifty):
        self.parts = parts
        self.steps_to_reduce = 6 if thrifty else 5
        self.running = [None] * len(parts)
        self.done = [0] * len(parts)

    def start(self):
        for n, part in enumerate(self.parts):
            self.running[n] = part.steps()
            self.pump(n)

    def pump(self, n):
        if self.running[n] is not None and next(self.running[n], 0) == 0:
            self.running[n] = None
        self.done[n] += 1

    def reduced(self):
        for n in range(len(self.parts)):
            while self.done[n] < self.steps_to_reduce:
                self.pump(n)

    def finish(self):
        for n in range(len(self.parts)):
            while self.running[n] is not None:
                self.pump(n)


def vector_steps(at, mine, land_core, land_z, land_y, land_x, final, sems, base):
    send_sems, recv_sems = sems
    slots = iter(range(base, base + 10))

    def send(source, target, axis, step):
        slot = next(slots)
        copy = pltpu.make_async_remote_copy(
            src_ref=source, dst_ref=target, send_sem=send_sems.at[slot], recv_sem=recv_sems.at[slot],
            device_id=shifted(at, axis, step), device_id_type=MESH,
        )
        copy.start()
        return copy

    z, y, x, _ = at
    copies = [send(mine, land_core, 3, 1)]
    yield
    copies[0].wait()
    mine[...] = mine[...] + land_core[...]
    copies = [send(mine.at[away(z, s)], land_z.at[z], 0, s) for s in (1, 2, 3)]
    land_z[z] = mine[z]
    yield
    for axis, here, land in ((1, y, land_y), (2, x, land_x)):
        for copy in copies:
            copy.wait()
        source = land_z if axis == 1 else land_y
        total = (source[0] + source[1]) + (source[2] + source[3])
        land[here] = total
        copies = [send(land.at[here], land.at[here], axis, s) for s in (1, 2, 3)]
        yield
    for copy in copies:
        copy.wait()
    final[...] = (land_x[0] + land_x[1]) + (land_x[2] + land_x[3])


def greet(at):
    barrier = pltpu.get_barrier_semaphore()
    partners = [(axis, step) for axis in (0, 1, 2) for step in (1, 2, 3)] + [(3, 1)]
    for axis, step in partners:
        pl.semaphore_signal(barrier, inc=1, device_id=shifted(at, axis, step), device_id_type=MESH)
    pl.semaphore_wait(barrier, len(partners))


class Passing:
    PIECES = ((0, 0), (0, 1), (1, 0), (1, 1))

    def __init__(self, at, way, own, near, far, sems, base):
        self.at, self.way = at, way
        self.rank = at[0] if way == 1 else 3 - at[0]
        self.own, self.near, self.far = own, near, far
        self.send_sems, self.recv_sems = sems
        self.base = base

    ROWS = (slice(0, 224), slice(224, VH))

    def piece(self, ref, p):
        head, half = self.PIECES[p]
        rows = self.ROWS[half]
        return ref.at[head, pl.ds(rows.start, rows.stop - rows.start)]

    def copy(self, source, target, p, kind):
        step = {0: self.way, 1: -self.way, 2: -self.way}[kind] % 4
        slot = self.base + 4 * min(kind, 1) + p
        return pltpu.make_async_remote_copy(
            src_ref=self.piece(source, p), dst_ref=self.piece(target, p), send_sem=self.send_sems.at[slot],
            recv_sem=self.recv_sems.at[slot], device_id=shifted(self.at, 0, step), device_id_type=MESH,
        )

    def clear(self):
        @pl.when(self.rank == 0)
        def _():
            self.near[...] = jnp.zeros(self.near.shape, BF)

        @pl.when(self.rank < 2)
        def _():
            self.far[...] = jnp.zeros(self.far.shape, BF)

    def begin(self, p):
        @pl.when(self.rank < 2)
        def _():
            self.copy(self.own, self.near, p, 0).start()

        @pl.when(self.rank == 0)
        def _():
            self.copy(self.own, self.far, p, 1).start()

    def forward(self, p, decay):
        head, half = self.PIECES[p]
        rows = self.ROWS[half]

        @pl.when(self.rank == 2)
        def _():
            self.copy(self.own, self.near, p, 0).wait_recv()
            total = self.own[head, rows].astype(F32) + self.near[head, rows].astype(F32) * decay[head]
            self.own[head, rows] = total.astype(BF)
            self.copy(self.own, self.near, p, 0).start()

        @pl.when(self.rank == 3)
        def _():
            self.copy(self.far, self.far, p, 1).wait_recv()
            self.copy(self.far, self.far, p, 2).start()

    def finish(self):
        for p in range(4):

            @pl.when((self.rank == 1) | (self.rank == 3))
            def _():
                self.copy(self.own, self.near, p, 0).wait_recv()

            @pl.when(self.rank == 2)
            def _():
                self.copy(self.far, self.far, p, 1).wait_recv()

    def drain(self):
        for p in range(4):

            @pl.when(self.rank < 3)
            def _():
                self.copy(self.own, self.near, p, 0).wait_send()

            @pl.when((self.rank == 0) | (self.rank == 3))
            def _():
                self.copy(self.own, self.far, p, 1).wait_send()


LOG_GAMMA = tuple(math.log(1.0 - 2.0 ** (-5.0 - h)) for h in range(HEADS))
HALF = WIDE // 2


def rotary_constants():
    half = KEYH // 2
    ladder = np.arange(half, dtype=np.float64)
    theta = 10000.0 ** (-ladder / half)
    place = np.arange(SEQ, dtype=np.float64)[:, None]
    zeta = (2.0 * ladder + 0.4 * KEYH) / (1.4 * KEYH)
    grow = zeta[None, :] ** (place / 512.0)
    cosine, sine = np.cos(place * theta), np.sin(place * theta)
    small = KEYH ** (-0.5)
    table = np.concatenate([cosine * grow, sine * grow, cosine / grow * small, sine / grow * small], axis=1)
    return np.concatenate([np.zeros((HALO, 4 * half)), table]).astype(np.float32)


def dot_nn(a, b):
    return lax.dot_general(a, b, (((1,), (0,)), ((), ())), preferred_element_type=F32)


def dot_nt(a, b):
    return lax.dot_general(a, b, (((1,), (1,)), ((), ())), preferred_element_type=F32)


def dot_tn(a, b):
    return lax.dot_general(a, b, (((0,), (0,)), ((), ())), preferred_element_type=F32)


def row_loop(total, step, work):
    def one(i, carry):
        work(pl.ds(pl.multiple_of(i * step, step), step))
        return carry

    lax.fori_loop(0, total // step, one, 0)


class Documents:
    def __init__(self, lengths_ref):
        ends = []
        total = 0
        for i in range(5):
            total = total + lengths_ref[0, i]
            ends.append(total)
        self.ends = ends

    def of(self, where):
        found = jnp.zeros(where.shape, jnp.int32) if hasattr(where, "shape") and where.shape else 0
        for end in self.ends:
            found = found + jnp.where(where >= end, 1, 0)
        return found


def column(count, first=0):
    return lax.broadcasted_iota(jnp.int32, (count, 1), 0) + first


def line(count, first=0):
    return lax.broadcasted_iota(jnp.int32, (1, count), 1) + first


def decay_block(h, rows, cols, row_first, col_first, start, docs, window):
    i, j = column(rows, row_first), line(cols, col_first)
    base = min(row_first, col_first)
    seen = (i >= j) & (docs.of(i + start) == docs.of(j + start))
    if window is not None:
        seen = seen & (i - j < window)
    if col_first < 0:
        seen = seen & (j + start >= 0)
    down = jnp.exp((i - base).astype(F32) * LOG_GAMMA[h])
    up = jnp.exp((j - base).astype(F32) * (-LOG_GAMMA[h]))
    return jnp.where(seen, down * up, 0.0)


def rotated(raw, cosine, sine):
    front, behind = raw[:, :128], raw[:, 128:]
    return jnp.concatenate([front * cosine - behind * sine, front * sine + behind * cosine], axis=1)


def forward_kernel(
    tokens_hbm, cot_hbm, gain1, bias1, gain2, bias2, lengths, windows, table_hbm,
    wq_hbm, wk_hbm, wv_hbm, wg_hbm, wo_hbm, wu_hbm, wd_hbm,
    out_result, out_first, out_second, out_mixed, out_act, out_cot, out_lhalf, out_lift,
    out_q, out_k, out_v, out_w01, out_w23, out_sin, out_heads, out_u, out_w, out_hidden, out_stats, out_qnext,
    tokens, cot, table, wq, wk, wv, wg, wo, wu, wd,
    first, queries, keys, values, wide_f32, down_grad, kept, w01, w23, state, state_near, state_far, state_in,
    heads, u_ref, w_ref, mixed, hidden, second, lift, act, stats,
    load_sems, save_sems, send_sems, recv_sems, pass_send, pass_recv,
):
    at = coordinates()
    z, core = at[0], at[3]
    start = z * TOK
    loads = {}
    for slot, (name, source, target) in enumerate(
        [
            ("tokens", tokens_hbm, tokens.at[pl.ds(HALO, TOK)]),
            ("wk", wk_hbm, wk),
            ("table", table_hbm.at[pl.ds(pl.multiple_of(z * TOK, TOK), HALO + TOK)], table),
            ("wv", wv_hbm, wv),
            ("wq", wq_hbm, wq),
            ("wg", wg_hbm, wg),
            ("cot", cot_hbm, cot),
            ("wd", wd_hbm, wd),
            ("wo", wo_hbm, wo),
            ("wu", wu_hbm, wu),
        ]
    ):
        loads[name] = pltpu.make_async_copy(source, target, load_sems.at[slot])
        loads[name].start()
    partners = [(3, 1), (0, 1), (0, 3)]
    barrier = pltpu.get_barrier_semaphore()
    for axis, step in partners:
        pl.semaphore_signal(barrier, inc=1, device_id=shifted(at, axis, step), device_id_type=MESH)

    saves, sends = [], []

    def save(source, target):
        copy = pltpu.make_async_copy(source, target, save_sems.at[len(saves)])
        copy.start()
        saves.append(copy)

    def remote(source, target, axis, step):
        slot = len(sends)
        copy = pltpu.make_async_remote_copy(
            src_ref=source, dst_ref=target, send_sem=send_sems.at[slot], recv_sem=recv_sems.at[slot],
            device_id=shifted(at, axis, step), device_id_type=MESH,
        )
        sends.append(copy)
        return copy

    def share(source, target):
        save(source, target.at[core])
        remote(source, target.at[core], 3, 1).start()
        return (saves[-1], sends[-1])

    loads["tokens"].wait()

    pl.semaphore_wait(barrier, len(partners))
    t_halo = remote(tokens.at[pl.ds(TOK, HALO)], tokens.at[pl.ds(0, HALO)], 0, 1)

    @pl.when(z < 3)
    def _():
        t_halo.start()

    @pl.when(z == 0)
    def _():
        tokens[0:HALO] = jnp.zeros((HALO, D), BF)

    def normalized(x):
        mean = jnp.mean(x, axis=-1, keepdims=True)
        center = x - mean
        inverse = lax.rsqrt(jnp.mean(center * center, axis=-1, keepdims=True) + epsilon)
        return center * inverse, mean, inverse

    def norm_one(i, carry):
        rows = pl.ds(pl.multiple_of(i * 64, 64), 64)
        scaled, mean, inverse = normalized(tokens[pl.ds(HALO + i * 64, 64)].astype(F32))
        first[pl.ds(HALO + i * 64, 64)] = (scaled * gain1[...] + bias1[...]).astype(BF)
        stats[rows, 0:1] = mean
        stats[rows, 1:2] = inverse
        return carry

    lax.fori_loop(0, TOK // 64, norm_one, 0)
    share(first.at[pl.ds(HALO, TOK)], out_first)

    docs = Documents(lengths)
    doc_before = docs.of(start - 1)
    doc_last = docs.of(start + TOK - 1)
    place = column(TOK)
    doc_rows = docs.of(place + start)

    def project(h, begin):
        cols = slice(h * KEYH, (h + 1) * KEYH)
        raw = dot_nn(first[begin:], wk[:, cols])
        keys[begin:, cols] = rotated(raw, table[begin:, 256:384], table[begin:, 384:512]).astype(BF)
        values[h, begin:] = dot_nt(first[begin:], wv[h * VH : (h + 1) * VH]).astype(BF)

    loads["wk"].wait()
    loads["table"].wait()
    loads["wv"].wait()
    passing = Passing(at, 1, state, state_near, state_far, (pass_send, pass_recv), 0)
    joins = [jnp.where(doc_before == doc_last, math.exp(LOG_GAMMA[h] * TOK), 0.0) for h in (2, 3)]
    for h in (2, 3):
        project(h, HALO)
        factor = jnp.where(doc_rows == doc_last, jnp.exp((TOK - place).astype(F32) * LOG_GAMMA[h]), 0.0)
        scaled = (keys[HALO:, h * KEYH : (h + 1) * KEYH].astype(F32) * factor).astype(BF)
        state[h - 2] = dot_tn(values[h, HALO:], scaled).astype(BF)
        passing.begin(2 * h - 4)
        passing.begin(2 * h - 3)
    passing.clear()
    loads["wq"].wait()
    for h in range(HEADS):
        raw = dot_nn(first[HALO:], wq[:, h * KEYH : (h + 1) * KEYH])
        queries[:, h * KEYH : (h + 1) * KEYH] = rotated(raw, table[HALO:, 0:128], table[HALO:, 128:256]).astype(BF)
    save(queries, out_q)
    q_halo = remote(queries.at[pl.ds(0, HALO), pl.ds(0, 2 * KEYH)], out_qnext, 0, 3)

    @pl.when(z > 0)
    def _():
        q_halo.start()

    loads["wg"].wait()

    def swish(h, rows):
        lane = 512 * (h % 2)
        gate = wide_f32[rows, lane : lane + VH]
        sigma = 0.5 * jnp.tanh(0.5 * gate) + 0.5
        u_ref[h, rows] = (gate * sigma).astype(BF)
        w_ref[h, rows] = (sigma * (1.0 + gate * (1.0 - sigma))).astype(BF)

    for h in range(HEADS + 1):
        if h < HEADS:
            lane = 512 * (h % 2)
            wide_f32[:, lane : lane + VH] = dot_nt(first[HALO:], wg[h * VH : (h + 1) * VH])
        if h > 0:
            for row in range(0, TOK, 64):
                swish(h - 1, slice(row, row + 64))
        if h == 2:
            passing.forward(0, joins)
    passing.forward(1, joins)
    save(u_ref, out_u)
    save(w_ref, out_w)
    loads["cot"].wait()
    save(cot.at[:, pl.ds(pl.multiple_of(core * 512, 512), 512)], out_cot.at[core])
    remote(cot.at[:, pl.ds(pl.multiple_of((1 - core) * 512, 512), 512)], out_cot.at[core], 3, 1).start()
    loads["wd"].wait()
    down_grad[...] = dot_nt(cot[...], wd[...]).astype(BF)
    passing.forward(2, joins)

    for h in (2, 3):
        for b in (0, 1):
            rows, cols = slice(256 * b, 256 * b + 256), 256 * b + 256
            q_h = queries[rows, h * KEYH : (h + 1) * KEYH]
            scores = dot_nt(q_h, keys[HALO : HALO + cols, h * KEYH : (h + 1) * KEYH])
            weight = (scores * decay_block(h, 256, cols, 256 * b, 0, start, docs, None)).astype(BF)
            w23[h - 2, rows, 0:cols] = weight
            kept[h, rows] = dot_nn(weight, values[h, HALO : HALO + cols])

    passing.forward(3, joins)

    @pl.when(z > 0)
    def _():
        t_halo.wait_recv()

    for block in (slice(0, 64), slice(64, 128)):
        first[block] = (normalized(tokens[block].astype(F32))[0] * gain1[...] + bias1[...]).astype(BF)
    for h in (0, 1):
        project(h, 0)

    save(keys, out_k)
    save(values, out_v)
    for h in (0, 1):
        for b in (0, 1):
            rows = slice(256 * b, 256 * b + 256)
            q_h = queries[rows, h * KEYH : (h + 1) * KEYH]
            scores = dot_nt(q_h, keys[256 * b : 256 * b + 384, h * KEYH : (h + 1) * KEYH])
            decay = decay_block(h, 256, 384, 256 * b, 256 * b - HALO, start, docs, windows[0, h])
            weight = (scores * decay).astype(BF)
            w01[h, b] = weight
            kept[h, rows] = dot_nn(weight, values[h, 256 * b : 256 * b + 384])
    save(w01, out_w01)
    save(w23, out_w23)

    passing.finish()
    from_first = docs.of(TOK - 1) == doc_before
    for h in (2, 3):
        power = jnp.where(z == 3, math.exp(2 * TOK * LOG_GAMMA[h]), math.exp(TOK * LOG_GAMMA[h]))
        total = state_near[h - 2].astype(F32) + state_far[h - 2].astype(F32) * jnp.where(from_first, power, 0.0)
        state_in[h - 2] = total.astype(BF)
        factor = jnp.where(doc_rows == doc_before, jnp.exp(place.astype(F32) * LOG_GAMMA[h]), 0.0)
        kept[h] = kept[h] + factor * dot_nt(queries[:, h * KEYH : (h + 1) * KEYH], state_in[h - 2])
    save(state_in, out_sin)

    def mix(rows):
        parts = []
        for h in range(HEADS):
            x = kept[h, rows]
            center = x - jnp.mean(x, axis=-1, keepdims=True)
            inverse = lax.rsqrt(jnp.mean(center * center, axis=-1, keepdims=True) + retention_floor)
            stats[rows, 4 + h : 5 + h] = inverse
            low = (center * inverse).astype(BF)
            heads[h, rows] = low
            parts.append(low.astype(F32) * u_ref[h, rows].astype(F32))
        mixed[rows] = jnp.concatenate(parts, axis=1).astype(BF)

    row_loop(TOK, 64, mix)
    mixed_away = share(mixed, out_mixed)
    save(heads, out_heads)

    loads["wo"].wait()
    hidden[...] = dot_nn(mixed[...], wo[...])

    def norm_two(i, carry):
        rows = pl.ds(pl.multiple_of(i * 64, 64), 64)
        x = hidden[rows] + tokens[pl.ds(HALO + i * 64, 64)].astype(F32)
        hidden[rows] = x
        scaled, mean, inverse = normalized(x)
        second[rows] = (scaled * gain2[...] + bias2[...]).astype(BF)
        stats[rows, 2:3] = mean
        stats[rows, 3:4] = inverse
        return carry

    lax.fori_loop(0, TOK // 64, norm_two, 0)
    share(second, out_second)
    save(hidden, out_hidden)
    save(stats, out_stats)

    loads["wu"].wait()

    def activate(cols, rows):
        x = wide_f32[rows, cols]
        phi = 0.5 * (1.0 + lax.erf(x * math.sqrt(0.5)))
        slope = phi + x * jnp.exp(-0.5 * x * x) * (1.0 / math.sqrt(2.0 * math.pi))
        act[rows, cols] = (x * phi).astype(BF)
        grad = (down_grad[rows, cols].astype(F32) * slope).astype(BF)
        if cols.stop == FF:
            grad = jnp.concatenate([grad, jnp.zeros((grad.shape[0], WIDE - FF), BF)], axis=1)
        lift[rows, cols.start : cols.start + grad.shape[1]] = grad

    blocks = [slice(first_col, min(first_col + 256, FF)) for first_col in range(0, FF, 256)]
    for n in range(len(blocks) + 1):
        if n < len(blocks):
            wide_f32[:, blocks[n]] = dot_nt(second[...], wu[blocks[n]])
        if n > 0:
            for row in range(0, TOK, 64):
                activate(blocks[n - 1], slice(row, row + 64))
    save(act, out_act)
    save(lift, out_lift)
    save(lift.at[:, pl.ds(pl.multiple_of(core * HALF, HALF), HALF)], out_lhalf.at[core])
    remote(lift.at[:, pl.ds(pl.multiple_of((1 - core) * HALF, HALF), HALF)], out_lhalf.at[core], 3, 1).start()
    for copy in mixed_away:
        copy.wait()
    mixed[:, 0:D] = (hidden[...] + dot_nn(act[...], wd[...])).astype(BF)
    save(mixed.at[:, pl.ds(0, D)], out_result)

    for copy in sends:
        if not any(copy is other for other in (t_halo, q_halo) + mixed_away):
            copy.wait()

    @pl.when(z > 0)
    def _():
        q_halo.wait_send()

    @pl.when(z < 3)
    def _():
        q_halo.wait_recv()
        t_halo.wait_send()

    passing.drain()
    for copy in saves:
        if copy is not mixed_away[0]:
            copy.wait()


def forward(tokens, cot, gain1, bias1, gain2, bias2, lengths, windows, table, wq, wk, wv, wg, wo, wu, wd):
    vmem = pl.BlockSpec(memory_space=pltpu.VMEM)
    smem = pl.BlockSpec(memory_space=pltpu.SMEM)
    anywhere = pl.BlockSpec(memory_space=pl.ANY)
    shape = jax.ShapeDtypeStruct
    outs = [
        shape((TOK, D), BF), shape((2, TOK, D), BF), shape((2, TOK, D), BF), shape((2, TOK, VD), BF), shape((TOK, FF), BF),
        shape((2, TOK, 512), BF), shape((2, TOK, HALF), BF), shape((TOK, WIDE), BF),
        shape((TOK, QK), BF), shape((HALO + TOK, QK), BF), shape((HEADS, HALO + TOK, VH), BF),
        shape((2, 2, 256, 384), BF), shape((2, TOK, TOK), BF), shape((2, VH, KEYH), BF),
        shape((HEADS, TOK, VH), BF), shape((HEADS, TOK, VH), BF), shape((HEADS, TOK, VH), BF), shape((TOK, D), F32), shape((TOK, 128), F32),
        shape((HALO, 2 * KEYH), BF),
    ]
    scratch = [
        pltpu.VMEM((HALO + TOK, D), BF), pltpu.VMEM((TOK, D), BF), pltpu.VMEM((HALO + TOK, 512), F32),
        pltpu.VMEM((D, QK), BF), pltpu.VMEM((D, QK), BF), pltpu.VMEM((VD, D), BF), pltpu.VMEM((VD, D), BF),
        pltpu.VMEM((VD, D), BF), pltpu.VMEM((FF, D), BF), pltpu.VMEM((FF, D), BF),
        pltpu.VMEM((HALO + TOK, D), BF), pltpu.VMEM((TOK, QK), BF), pltpu.VMEM((HALO + TOK, QK), BF),
        pltpu.VMEM((HEADS, HALO + TOK, VH), BF), pltpu.VMEM((TOK, FF), F32), pltpu.VMEM((TOK, FF), BF),
        pltpu.VMEM((HEADS, TOK, VH), F32), pltpu.VMEM((2, 2, 256, 384), BF), pltpu.VMEM((2, TOK, TOK), BF),
        pltpu.VMEM((2, VH, KEYH), BF), pltpu.VMEM((2, VH, KEYH), BF), pltpu.VMEM((2, VH, KEYH), BF), pltpu.VMEM((2, VH, KEYH), BF),
        pltpu.VMEM((HEADS, TOK, VH), BF), pltpu.VMEM((HEADS, TOK, VH), BF), pltpu.VMEM((HEADS, TOK, VH), BF), pltpu.VMEM((TOK, VD), BF),
        pltpu.VMEM((TOK, D), F32), pltpu.VMEM((TOK, D), BF), pltpu.VMEM((TOK, WIDE), BF), pltpu.VMEM((TOK, FF), BF),
        pltpu.VMEM((TOK, 128), F32),
        pltpu.SemaphoreType.DMA((10,)), pltpu.SemaphoreType.DMA((20,)),
        pltpu.SemaphoreType.DMA((16,)), pltpu.SemaphoreType.DMA((16,)),
        pltpu.SemaphoreType.DMA((8,)), pltpu.SemaphoreType.DMA((8,)),
    ]
    return pl.pallas_call(
        forward_kernel,
        out_shape=outs,
        in_specs=[anywhere] * 2 + [vmem] * 4 + [smem] * 2 + [anywhere] * 8,
        out_specs=[anywhere] * len(outs),
        scratch_shapes=scratch,
        compiler_params=pltpu.CompilerParams(collective_id=1, has_side_effects=True, vmem_limit_bytes=62 * 2**20),
        cost_estimate=pl.CostEstimate(flops=14 * 10**9, bytes_accessed=50 * 10**6, transcendentals=2 * 10**6),
        name="forward",
    )(
        tokens, cot, gain1.reshape(1, D), bias1.reshape(1, D), gain2.reshape(1, D), bias2.reshape(1, D),
        lengths, windows.reshape(1, HEADS), table, wq, wk, wv.T, wg.T, wo, wu.T, wd,
    )


LAST = TOK - HALO
UNITS = ("down", "up", "out", "gate", "value", "qk")
UNIT_ROWS = {"down": BIG, "up": BIG, "out": BIG, "gate": BIG, "value": BIG, "qk": PAIRED}
UNIT_SET = {"down": 0, "up": 1, "out": 2, "gate": 3, "value": 0, "qk": 1}
SET_ROWS = (BIG, PAIRED, BIG, BIG)
FOLLOWER = {"down": "value", "up": "qk"}
LENDER = {"value": "gate", "qk": "out"}
PLAN = {
    "down": (((0, 1, 2), (1, 2)), ((2, 1, 0), (1, 2)), ((1, 0, 2), (2, 1))),
    "up": (((1, 2, 0), (1, 2)), ((2, 1, 0), (2, 1)), ((0, 2, 1), (1, 2))),
    "out": (((2, 0, 1), (2, 1)), ((2, 1, 0), (1, 2)), ((1, 2, 0), (2, 1))),
    "gate": (((2, 0, 1), (1, 2)), ((1, 0, 2), (1, 2)), ((1, 0, 2), (2, 1))),
    "value": (((2, 0, 1), (1, 2)), ((1, 0, 2), (2, 1)), ((0, 2, 1), (1, 2))),
    "qk": (((0, 2, 1), (1, 2)), ((1, 0, 2), (2, 1)), ((0, 1, 2), (2, 1))),
}
THRIFTY = ("down", "out")
BLOCKS = (
    "up", "second", "down", "norm2", "mixl", "out", "states", "mixe", "gate", "fg", "band", "far", "full", "cross", "store", "qk", "value", "fq", "fk", "fv", "n1",
)
SCHEDULE = (
    (), (), (), (3, 4, 5), (), (1, 2), (0,), (4, 5), (3,), (1, 2), (0, 6, 8), (18, 19, 0, 1, 3, 4, 5, 7), (20, 8), (10,), (21, 2, 6, 11), (0, 1, 9), (5, 7, 8, 10), (0, 3, 4), (11,), (2, 5, 6, 7, 9), (0, 1, 3, 4, 8, 10), (2, 6, 7, 11), (0, 1, 4, 5, 8, 9), (3, 10), (2, 4, 11, 15, 16), (5, 6, 17), (3, 7, 12, 13), (0, 9, 10, 14), (1, 2, 6, 8, 11), (0, 15, 16),
)
TAIL = (7, 12, 17, 13, 10, 1, 9, 2, 14, 10, 6, 15, 1, 8, 7, 2, 16, 11, 17, 9, 6, 12, 11, 14, 13, 7, 15, 9, 8, 6, 16, 7, 8, 17, 12, 13, 14, 15, 16, 17, 12, 15, 16, 13, 14, 17, 12, 13, 14)
PART_ROWS = {rows: tuple(count for _, count in cuts) for rows, cuts in CUTS.items()}


def stage_rows(stage, result, first_x):
    for z in range(4):
        for y in range(4):
            n = min(BIG, VH - BIG * y)
            for i in range(result.shape[1] // 128):
                piece = result[VH * z + BIG * y : VH * z + BIG * y + n, 128 * i : 128 * i + 128].astype(BF)
                stage[z, y, first_x + i, 0:n] = piece
                if n < BIG:
                    stage[z, y, first_x + i, n:BIG] = jnp.zeros((BIG - n, 128), BF)


def stage_columns(stage, result, first_z):
    for i in range(result.shape[1] // 128):
        z, xc = first_z + i // 2, i % 2
        for y in range(4):
            for xr in range(2):
                first = 224 * y + BIG * xr
                stage[z, y, 2 * xr + xc, 0:BIG] = result[first : first + BIG, 128 * i : 128 * i + 128].astype(BF)


def stage_square(stage, result, first_row):
    for z in range(4):
        for y in range(4):
            for x in range(4):
                piece = result[256 * z + 64 * y : 256 * z + 64 * y + 64, 128 * x : 128 * x + 128].astype(BF)
                stage[z, y, x, first_row : first_row + 64] = piece


def fold(rows):
    return jnp.sum(rows.reshape(rows.shape[0] // 8, 8, rows.shape[1]), axis=0)


def unrotated(grad, cosine, sine):
    grad = grad.astype(BF).astype(F32)
    front, behind = grad[:, :128], grad[:, 128:]
    return jnp.concatenate([front * cosine + behind * sine, behind * cosine - front * sine], axis=1).astype(BF)


def backward_kernel(
    act_hbm, coth_hbm, lhalf_hbm, second_hbm, first_hbm, mixed_hbm, lift_hbm, cot_hbm, hidden_hbm, stats_hbm,
    u_hbm, w_hbm, heads_hbm, q_hbm, k_hbm, v_hbm, w01_hbm, w23_hbm, sin_hbm, qnext_hbm, tokens_hbm, table_hbm,
    wq_hbm, wk_hbm, wv_hbm, wg_hbm, wo_hbm, wu_hbm, gain1, gain2, lengths, windows,
    out_tokens, out_vec, out_down, out_up, out_out, out_gate, out_value, out_qk,
    x1, x2, x3, y1, ch, wide, cot, heads, u_ref, w_ref, queries, keys, values, w01, w23, state_in,
    back_state, back_near, back_far, rgrad, hidden, wf, wu, wo, table, stats, qnext, gnext, vec_rows,
    vec, vec_core, vec_z, vec_y, vec_x, vec_out,
    stage0, stage1, stage2, stage3, *rest,
):
    lands = [[rest[(3 * s + p) * LANDINGS : (3 * s + p + 1) * LANDINGS] for p in range(3)] for s in range(4)]
    rest = rest[12 * LANDINGS :]
    mines = rest[0:18]
    load_sems, save_sems, pair_send, pair_recv, z_send, z_recv, vec_send, vec_recv = rest[18:26]
    unit_send, unit_recv, unit_copy, credits, pair_credit, pass_send, pass_recv, joint_credits = rest[26:]
    stages = (stage0, stage1, stage2, stage3)
    at = coordinates()
    z, core = at[0], at[3]
    start = z * TOK

    loading = {}

    def load(name, source, target):
        copy = pltpu.make_async_copy(source, target, load_sems.at[len(loading)])
        copy.start()
        loading[name] = copy

    def ready(*names):
        for name in names:
            loading[name].wait()

    waited = set()

    def ready_once(*names):
        for name in names:
            if name not in waited:
                waited.add(name)
                loading[name].wait()

    own_rows = pl.ds(pl.multiple_of(core * TOK, TOK), TOK)
    load("act", act_hbm, x1.at[own_rows])
    load("lhalf", lhalf_hbm, y1)
    load("second", second_hbm, x2)
    load("coth", coth_hbm, ch)
    load("lift", lift_hbm, wide)
    load("wu", wu_hbm, wu)
    greet(at)

    outs = dict(zip(UNITS, (out_down, out_up, out_out, out_gate, out_value, out_qk)))
    units = {}
    for n, name in enumerate(UNITS):
        s, parts = UNIT_SET[name], []
        for p in range(3):
            slot = 3 * n + p
            order, gather = PLAN[name][p]
            follower = FOLLOWER.get(name)
            parts.append(
                Part(
                    at, stages[s], lands[s][p], mines[slot], outs[name], CUTS[UNIT_ROWS[name]][p], order, gather,
                    (unit_send, unit_recv, unit_copy), slot,
                    credits.at[slot - 12] if n >= 4 else None, credits.at[slot] if follower else None,
                    PLAN[follower][p][0] if follower else None, name in THRIFTY,
                    (lands[UNIT_SET[LENDER[name]]][p][2], joint_credits.at[slot - 12]) if n >= 4 else None,
                )
            )
        units[name] = Unit(parts, name in THRIFTY)
    for name, lender in LENDER.items():
        for p in range(3):
            slot = 3 * UNITS.index(name) + p
            units[lender].parts[p].lend = (joint_credits.at[slot - 12], PLAN[name][p][0][2])
    down, up, out, gate, value, qk = (units[name] for name in UNITS)
    numbered = [units[name] for name in UNITS]
    ticks = iter(SCHEDULE)

    def tick():
        for n in next(ticks):
            if n < 3 * len(UNITS):
                numbered[n // 3].pump(n % 3)
            else:
                passing.forward(n - 3 * len(UNITS), joins)

    pairs = []

    def to_sibling(source, target):
        copy = pltpu.make_async_remote_copy(
            src_ref=source, dst_ref=target, send_sem=pair_send.at[len(pairs)], recv_sem=pair_recv.at[len(pairs)],
            device_id=shifted(at, 3, 1), device_id_type=MESH,
        )
        copy.start()
        pairs.append(copy)
        return copy

    local_copies = []

    def halves(source, width, landing, lane):
        rows = pl.ds(pl.multiple_of(core * TOK, TOK), TOK)
        lanes = pl.ds(lane, width)
        mine = source.at[:, pl.ds(pl.multiple_of(core * width, width), width)]
        other = source.at[:, pl.ds(pl.multiple_of((1 - core) * width, width), width)]
        remote = to_sibling(other, landing.at[rows, lanes])
        local = pltpu.make_async_copy(mine, landing.at[rows, lanes], save_sems.at[len(local_copies)])
        local.start()
        local_copies.append(local)
        return remote, local

    def arrived(pair):
        pair[0].wait()
        pair[1].wait()

    ready("act")
    act_pair = to_sibling(x1.at[own_rows], x1.at[own_rows])

    def tell_sibling(slot):
        pl.semaphore_signal(pair_credit.at[slot], inc=1, device_id=shifted(at, 3, 1), device_id_type=MESH)

    docs = Documents(lengths)
    doc_before = docs.of(start - 1)
    doc_last = docs.of(start + TOK - 1)
    place = column(TOK)
    doc_rows = docs.of(place + start)
    joins = [jnp.where(doc_before == doc_last, math.exp(LOG_GAMMA[h] * TOK), 0.0) for h in (2, 3)]
    passing = Passing(at, -1, back_state, back_near, back_far, (pass_send, pass_recv), 0)
    zero = jnp.zeros((8, D), F32)
    grad_v = u_ref
    pair = {}
    g_halo = pltpu.make_async_remote_copy(
        src_ref=rgrad.at[pl.ds(0, 2), pl.ds(0, HALO)], dst_ref=gnext, send_sem=z_send.at[0], recv_sem=z_recv.at[0],
        device_id=shifted(at, 0, 3), device_id_type=MESH,
    )

    def head_cols(h):
        return slice(h * KEYH, (h + 1) * KEYH)

    def row_factor(h):
        return jnp.where(doc_rows == doc_before, jnp.exp(place.astype(F32) * LOG_GAMMA[h]), 0.0)

    def two_halves(work):
        for half in (0, 1):
            cols = slice(512 * half, 512 * half + 512)
            wf[:, cols] = work(cols)
            tick()

    def block_down():
        ready("coth")
        act_pair.wait()
        for half in (0, 1):
            stage_rows(stage0, dot_tn(x1[...], ch[:, 256 * half : 256 * half + 256]), 2 * half)
        down.start()
        load("mixed", mixed_hbm, x1)
        tell_sibling(0)
        tick()

    def block_up():
        ready("lhalf", "second")
        for half in (0, 1):
            stage_columns(stage1, dot_tn(y1[...], x2[:, 512 * half : 512 * half + 512]), 2 * half)
        up.start()
        tell_sibling(1)
        tick()

    def block_second():
        ready("lift", "wu")
        two_halves(lambda cols: dot_nn(wide[:, 0:FF], wu[:, cols]))
        load("wg", wg_hbm, wu)

    def block_norm2():
        ready("cot", "hidden", "stats")

        def back_two(i, sums):
            rows = pl.ds(pl.multiple_of(i * 64, 64), 64)
            grad = wf[rows]
            inverse = stats[rows, 3:4]
            scaled = (hidden[rows] - stats[rows, 2:3]) * inverse
            e = grad * gain2[...]
            inner = e - jnp.mean(e, axis=-1, keepdims=True) - scaled * jnp.mean(e * scaled, axis=-1, keepdims=True)
            total = cot[rows].astype(F32) + inverse * inner
            hidden[rows] = total
            cot[rows] = total.astype(BF)
            return (sums[0] + fold(grad * scaled), sums[1] + fold(grad))

        gain_sum, bias_sum = lax.fori_loop(0, TOK // 64, back_two, (zero, zero))
        pl.semaphore_wait(pair_credit.at[0], 1)
        pair["low"] = halves(cot, 512, ch, 0)
        vec_rows[2:3] = jnp.sum(gain_sum, axis=0, keepdims=True)
        vec_rows[3:4] = jnp.sum(bias_sum, axis=0, keepdims=True)
        tick()

    def mixed_grad(h):
        ready_once("wo", "u", "w", "heads")
        lane = 512 * (h % 2)
        wf[:, lane : lane + VH] = dot_nt(cot[...], wo[h * VH : (h + 1) * VH])

    def back_head(h, rows):
        lane = 512 * (h % 2)
        grad = wf[rows, lane : lane + VH]
        c = heads[h, rows].astype(F32)
        gated = grad * c * w_ref[h, rows].astype(F32)
        e = (grad * u_ref[h, rows].astype(F32)).astype(BF).astype(F32)
        inner = e - jnp.mean(e, axis=-1, keepdims=True) - c * jnp.mean(e * c, axis=-1, keepdims=True)
        rgrad[h, rows] = (inner * stats[rows, 4 + h : 5 + h]).astype(BF)
        return gated

    def block_mixl():
        mixed_grad(2)
        mixed_grad(3)
        for h in (2, 3):
            for row in range(0, TOK, 64):
                rows = slice(row, row + 64)
                w_ref[h, rows] = back_head(h, rows).astype(BF)
            tick()

    def block_states():
        ready("q")
        for h in (2, 3):
            scaled = (queries[:, head_cols(h)].astype(F32) * row_factor(h)).astype(BF)
            back_state[h - 2] = dot_tn(rgrad[h], scaled).astype(BF)
            passing.begin(2 * h - 4)
            passing.begin(2 * h - 3)
        passing.clear()
        tick()

    def block_mixe():
        mixed_grad(0)
        mixed_grad(1)
        load("wv", wv_hbm, wo)
        for row in range(0, TOK, 64):
            rows = slice(row, row + 64)
            parts = [back_head(h, rows) for h in (0, 1)] + [w_ref[h, rows].astype(F32) for h in (2, 3)]
            gated = jnp.concatenate(parts, axis=1).astype(BF)
            wide[rows] = jnp.concatenate([gated, jnp.zeros((64, WIDE - VD), BF)], axis=1)
            if row == TOK // 2 - 64:
                tick()
        ready("qnext")

        @pl.when(z > 0)
        def _():
            g_halo.start()

        @pl.when(z == 3)
        def _():
            gnext[...] = jnp.zeros((2, HALO, VH), BF)
            qnext[...] = jnp.zeros((HALO, 2 * KEYH), BF)

        pl.semaphore_wait(pair_credit.at[1], 1)
        pair["gate"] = halves(wide, HALF, y1, 0)
        tick()

    def block_out():
        ready("mixed")
        arrived(pair["low"])
        for half in (0, 1):
            stage_rows(stage2, dot_tn(x1[...], ch[:, 256 * half : 256 * half + 256]), 2 * half)
        out.start()
        tell_sibling(2)
        tick()

    def block_gate():
        ready("first")
        arrived(pair["gate"])
        for half in (0, 1):
            stage_columns(stage3, dot_tn(y1[...], x3[:, 512 * half : 512 * half + 512]), 2 * half)
        gate.start()
        tick()

    def block_fg():
        ready("wg")
        two_halves(lambda cols: dot_nn(wide[:, 0:VD], wu[:, cols]))

    def finish_query(h, grad):
        queries[:, head_cols(h)] = unrotated(grad, table[:, 0:128], table[:, 128:256])

    def finish_key(h, grad, rows=slice(0, TOK)):
        cot[rows, head_cols(h)] = unrotated(grad, table[rows, 256:384], table[rows, 384:512])

    def block_full():
        ready_once("k", "v", "w01", "w23", "sin", "table")
        for h in (2, 3):
            cols_h = head_cols(h)
            score = []
            for b in (0, 1):
                rows, cols = slice(256 * b, 256 * b + 256), 256 * b + 256
                grad = dot_nt(rgrad[h, rows], values[h, HALO : HALO + cols])
                grad = (grad * decay_block(h, 256, cols, 256 * b, 0, start, docs, None)).astype(BF)
                score.append(grad)
            late = dot_tn(score[1], queries[256:512, cols_h])
            early = dot_tn(score[0], queries[0:256, cols_h])
            ch[0:TOK, head_cols(h - 2)] = jnp.concatenate([early + late[:256], late[256:]], axis=0).astype(BF)
            query = jnp.concatenate([dot_nn(score[b], keys[HALO : HALO + 256 * b + 256, cols_h]) for b in (0, 1)], axis=0)
            query = query + row_factor(h) * dot_nn(rgrad[h], state_in[h - 2])
            finish_query(h, query)
            late = dot_tn(w23[h - 2, 256:512], rgrad[h, 256:512])
            early = dot_tn(w23[h - 2, 0:256, 0:256], rgrad[h, 0:256])
            grad_v[h] = jnp.concatenate([early + late[:256], late[256:]], axis=0).astype(BF)
            tick()

    def block_band():
        ready_once("k", "v", "w01", "w23", "sin", "table")
        for h in (0, 1):
            cols_h = head_cols(h)
            parts_q, parts_k, parts_v = [], [], []
            for b in (0, 1):
                rows, ext = slice(256 * b, 256 * b + 256), slice(256 * b, 256 * b + 384)
                grad = dot_nt(rgrad[h, rows], values[h, ext])
                decay = decay_block(h, 256, 384, 256 * b, 256 * b - HALO, start, docs, windows[0, h])
                grad = (grad * decay).astype(BF)
                parts_q.append(dot_nn(grad, keys[ext, cols_h]))
                parts_k.append(dot_tn(grad, queries[rows, cols_h]))
                parts_v.append(dot_tn(w01[h, b], rgrad[h, rows]))

            def joined(parts):
                return jnp.concatenate(
                    [parts[0][HALO : 2 * HALO], parts[0][2 * HALO :] + parts[1][:HALO], parts[1][HALO:]], axis=0
                )

            finish_query(h, jnp.concatenate(parts_q, axis=0))
            key = joined(parts_k)
            finish_key(h, key[:LAST], slice(0, LAST))
            ch[TOK : TOK + HALO, cols_h] = key[LAST:].astype(BF)
            grad_v[h] = joined(parts_v).astype(BF)
            tick()

    def block_far():
        @pl.when(z < 3)
        def _():
            g_halo.wait_recv()

        tail = slice(TOK, TOK + HALO)
        for h in (0, 1):
            cols_h = head_cols(h)
            decay = decay_block(h, HALO, HALO, TOK, LAST, start, docs, windows[0, h])
            far_w = (dot_nt(qnext[:, cols_h], keys[tail, cols_h]) * decay).astype(BF)
            far_s = (dot_nt(gnext[h], values[h, tail]) * decay).astype(BF)
            key = ch[TOK : TOK + HALO, cols_h].astype(F32) + dot_tn(far_s, qnext[:, cols_h])
            finish_key(h, key, slice(LAST, TOK))
            grad_v[h, LAST:] = (grad_v[h, LAST:].astype(F32) + dot_tn(far_w, gnext[h])).astype(BF)
        share_keys()
        tick()

    def block_cross():
        passing.finish()
        from_last = docs.of(3 * TOK - 1) == doc_last
        for h in (2, 3):
            cols_h = head_cols(h)
            power = jnp.where(z == 0, math.exp(2 * TOK * LOG_GAMMA[h]), math.exp(TOK * LOG_GAMMA[h]))
            total = back_near[h - 2].astype(F32) + back_far[h - 2].astype(F32) * jnp.where(from_last, power, 0.0)
            state_in[h - 2] = total.astype(BF)
            factor = jnp.where(doc_rows == doc_last, jnp.exp((TOK - place).astype(F32) * LOG_GAMMA[h]), 0.0)
            grad = ch[0:TOK, head_cols(h - 2)].astype(F32)
            finish_key(h, grad + factor * dot_nn(values[h, HALO:], state_in[h - 2]))
            grad_v[h] = (grad_v[h].astype(F32) + factor * dot_nt(keys[HALO:, cols_h], state_in[h - 2])).astype(BF)
        share_keys()
        tick()

    retained = []

    def share_keys():
        retained.append(0)
        if len(retained) == 2:
            pair["query"] = halves(queries, 512, x2, 0)
            pair["key"] = halves(cot, 512, x2, 512)

    def block_store():
        def store_value(rows):
            joint = jnp.concatenate([grad_v[h, rows].astype(F32) for h in range(HEADS)], axis=1).astype(BF)
            wide[rows] = jnp.concatenate([joint, jnp.zeros((joint.shape[0], WIDE - VD), BF)], axis=1)

        row_loop(TOK, 64, store_value)
        pl.semaphore_wait(pair_credit.at[2], 1)
        pair["value"] = halves(wide, HALF, x1, 0)
        load("tokens", tokens_hbm, keys.at[pl.ds(0, TOK)])
        tick()

    def block_qk():
        up.reduced()
        arrived(pair["query"])
        arrived(pair["key"])
        stage_square(stage1, dot_tn(x3[...], x2[:, 0:512]), 0)
        stage_square(stage1, dot_tn(x3[...], x2[:, 512:1024]), 64)
        qk.start()
        load("wq", wq_hbm, x2)
        tick()

    def block_value():
        down.reduced()
        arrived(pair["value"])
        for half in (0, 1):
            stage_columns(stage0, dot_tn(x1[:, 0:HALF], x3[:, 512 * half : 512 * half + 512]), 2 * half)
        value.start()
        load("wk", wk_hbm, x3)
        tick()

    def block_fv():
        ready("wv")
        two_halves(lambda cols: wf[:, cols] + dot_nn(wide[:, 0:VD], wo[:, cols]))

    def block_fq():
        ready("wq")
        two_halves(lambda cols: wf[:, cols] + dot_nt(queries[...], x2[cols]))

    def block_fk():
        ready("wk")
        two_halves(lambda cols: wf[:, cols] + dot_nt(cot[...], x3[cols]))

    def block_n1():
        ready("tokens")

        def back_one(i, sums):
            rows = pl.ds(pl.multiple_of(i * 64, 64), 64)
            grad = wf[rows]
            inverse = stats[rows, 1:2]
            scaled = (keys[rows].astype(F32) - stats[rows, 0:1]) * inverse
            e = grad * gain1[...]
            inner = e - jnp.mean(e, axis=-1, keepdims=True) - scaled * jnp.mean(e * scaled, axis=-1, keepdims=True)
            keys[rows] = (hidden[rows] + inverse * inner).astype(BF)
            return (sums[0] + fold(grad * scaled), sums[1] + fold(grad))

        gain_sum, bias_sum = lax.fori_loop(0, TOK // 64, back_one, (zero, zero))
        pair["tokens"] = pltpu.make_async_copy(keys.at[pl.ds(0, TOK)], out_tokens, save_sems.at[len(local_copies)])
        pair["tokens"].start()
        vec_rows[0:1] = jnp.sum(gain_sum, axis=0, keepdims=True)
        vec_rows[1:2] = jnp.sum(bias_sum, axis=0, keepdims=True)
        for block in range(4):
            for j in range(4):
                for t in range(2):
                    first = 256 * block + 128 * t
                    vec[block, 2 * j + t : 2 * j + t + 1] = vec_rows[j : j + 1, first : first + 128]
        next(vectors)
        tick()

    vectors = vector_steps(at, vec, vec_core, vec_z, vec_y, vec_x, vec_out, (vec_send, vec_recv), 0)
    known = {
        "down": block_down, "up": block_up, "second": block_second, "norm2": block_norm2, "mixl": block_mixl, "states": block_states,
        "mixe": block_mixe, "out": block_out, "gate": block_gate, "fg": block_fg, "full": block_full, "band": block_band, "far": block_far,
        "cross": block_cross, "store": block_store, "qk": block_qk, "value": block_value, "fv": block_fv, "fq": block_fq,
        "fk": block_fk, "n1": block_n1,
    }
    for number, name in enumerate(BLOCKS):
        known[name]()
        if number == 0:
            load("cot", cot_hbm, cot)
            load("hidden", hidden_hbm, hidden)
            load("stats", stats_hbm, stats)
            load("wo", wo_hbm, wo)
            load("u", u_hbm, u_ref)
            load("w", w_hbm, w_ref)
            load("heads", heads_hbm, heads)
            load("q", q_hbm, queries)
            load("qnext", qnext_hbm, qnext)
        if number == 1:
            load("first", first_hbm, x3)
            load("k", k_hbm, keys)
            load("v", v_hbm, values)
            load("sin", sin_hbm, state_in)
            load("w23", w23_hbm, w23)
            load("w01", w01_hbm, w01)
            load("table", table_hbm.at[pl.ds(pl.multiple_of(z * TOK + HALO, HALO), TOK)], table)

    for count, n in enumerate(TAIL):
        numbered[n // 3].pump(n % 3)
        if count % 12 == 11:
            next(vectors, 0)
    for unit in numbered:
        unit.finish()
    for _ in vectors:
        pass
    last = pltpu.make_async_copy(vec_out, out_vec, save_sems.at[len(local_copies) + 1])
    last.start()

    @pl.when(z > 0)
    def _():
        g_halo.wait_send()

    passing.drain()
    pair["tokens"].wait()
    last.wait()


def backward(arrays, gain1, gain2, lengths, windows):
    vmem = pl.BlockSpec(memory_space=pltpu.VMEM)
    smem = pl.BlockSpec(memory_space=pltpu.SMEM)
    anywhere = pl.BlockSpec(memory_space=pl.ANY)
    shape = jax.ShapeDtypeStruct
    outs = [shape((TOK, D), BF), shape((8, 128), F32)] + [shape((2, 4, 4, UNIT_ROWS[n], 128), BF) for n in UNITS]
    scratch = [
        pltpu.VMEM((2 * TOK, VD), BF), pltpu.VMEM((2 * TOK, D), BF), pltpu.VMEM((2 * TOK, D), BF), pltpu.VMEM((2 * TOK, HALF), BF),
        pltpu.VMEM((2 * TOK, 512), BF), pltpu.VMEM((TOK, WIDE), BF), pltpu.VMEM((TOK, D), BF), pltpu.VMEM((HEADS, TOK, VH), BF),
        pltpu.VMEM((HEADS, TOK, VH), BF), pltpu.VMEM((HEADS, TOK, VH), BF), pltpu.VMEM((TOK, QK), BF), pltpu.VMEM((HALO + TOK, QK), BF),
        pltpu.VMEM((HEADS, HALO + TOK, VH), BF), pltpu.VMEM((2, 2, 256, 384), BF), pltpu.VMEM((2, TOK, TOK), BF),
        pltpu.VMEM((2, VH, KEYH), BF), pltpu.VMEM((2, VH, KEYH), BF),
        pltpu.VMEM((2, VH, KEYH), BF), pltpu.VMEM((2, VH, KEYH), BF),
        pltpu.VMEM((HEADS, TOK, VH), BF), pltpu.VMEM((TOK, D), F32),
        pltpu.VMEM((TOK, D), F32), pltpu.VMEM((VD, D), BF), pltpu.VMEM((VD, D), BF), pltpu.VMEM((TOK, 512), F32),
        pltpu.VMEM((TOK, 128), F32), pltpu.VMEM((HALO, 2 * KEYH), BF), pltpu.VMEM((2, HALO, VH), BF), pltpu.VMEM((8, D), F32),
        pltpu.VMEM((4, 8, 128), F32), pltpu.VMEM((4, 8, 128), F32), pltpu.VMEM((4, 8, 128), F32), pltpu.VMEM((4, 8, 128), F32),
        pltpu.VMEM((4, 8, 128), F32), pltpu.VMEM((8, 128), F32),
    ]
    scratch += [pltpu.VMEM((4, 4, 4, r, 128), BF) for r in SET_ROWS]
    for n, r in enumerate(SET_ROWS):
        for count, paired in zip(PART_ROWS[r], PART_ROWS[PAIRED]):
            shapes = landing_shapes(count)
            if n == UNIT_SET[LENDER["qk"]]:
                shapes[2] = landing_shapes(paired)[2]
            scratch += [pltpu.VMEM(s, BF) for s in shapes]
    for name in UNITS:
        scratch += [pltpu.VMEM((count, 128), BF) for count in PART_ROWS[UNIT_ROWS[name]]]
    dma, regular = pltpu.SemaphoreType.DMA, pltpu.SemaphoreType.REGULAR
    scratch += [dma((28,)), dma((8,)), dma((6,)), dma((6,)), dma((4,)), dma((4,)), dma((10,)), dma((10,))]
    scratch += [dma((18,)), dma((18 * ARRIVALS,)), dma((18,)), regular((6,)), regular((3,)), dma((8,)), dma((8,)), regular((6,))]
    return pl.pallas_call(
        backward_kernel,
        out_shape=outs,
        in_specs=[anywhere] * 28 + [vmem] * 2 + [smem] * 2,
        out_specs=[anywhere] * len(outs),
        scratch_shapes=scratch,
        compiler_params=pltpu.CompilerParams(collective_id=2, has_side_effects=True, vmem_limit_bytes=63 * 2**20),
        cost_estimate=pl.CostEstimate(flops=26 * 10**9, bytes_accessed=70 * 10**6, transcendentals=10**6),
        name="backward",
    )(*arrays, gain1.reshape(1, D), gain2.reshape(1, D), lengths, windows.reshape(1, HEADS))


def unpack_kernel(down, up, out, gate, value, qk, result, tokens, vectors, *outs):
    g_down, g_up, g_out, g_gate, g_value, g_query, g_key, out_result, out_tokens = outs[:9]
    for y in range(4):
        for x in range(4):
            cols = slice(128 * x, 128 * x + 128)
            for source, target in ((down, g_down), (out, g_out)):
                target[BIG * y : BIG * y + BIG, cols] = source[0, y, x].astype(F32)
            g_query[64 * y : 64 * y + 64, cols] = qk[0, y, x, 0:64].astype(F32)
            g_key[64 * y : 64 * y + 64, cols] = qk[0, y, x, 64:128].astype(F32)
            first, lane = 2 * BIG * y + BIG * (x // 2), 128 * (x % 2)
            for source, target in ((up, g_up), (gate, g_gate), (value, g_value)):
                target[first : first + BIG, lane : lane + 128] = source[0, y, x].astype(F32)
    out_result[...] = result[...]
    out_tokens[...] = tokens[...]
    for j, target in enumerate(outs[9:]):
        target[...] = vectors[2 * j : 2 * j + 2]


def unpack(gathered, result, grad_tokens, vectors):
    def source(rows):
        return pl.BlockSpec((1, 4, 4, rows, 128), lambda c: (c, 0, 0, 0, 0))

    tall = pl.BlockSpec((4 * BIG, 512), lambda c: (0, c))
    turned = pl.BlockSpec((WIDE // 2, 256), lambda c: (c, 0))
    square = pl.BlockSpec((256, 512), lambda c: (0, c))
    plain = pl.BlockSpec((TOK // 2, D), lambda c: (c, 0))
    shape = jax.ShapeDtypeStruct
    return pl.pallas_call(
        unpack_kernel,
        grid=(2,),
        out_shape=[
            shape((VH, D), F32), shape((FF, 256), F32), shape((VH, D), F32), shape((VD, 256), F32), shape((VD, 256), F32),
            shape((256, QK), F32), shape((256, QK), F32), shape((TOK, D), BF), shape((TOK, D), BF),
        ]
        + [shape((2, 128), F32)] * 4,
        in_specs=[source(UNIT_ROWS[n]) for n in UNITS] + [plain, plain, pl.BlockSpec((8, 128), lambda c: (0, 0))],
        out_specs=[tall, turned, tall, turned, turned, square, square, plain, plain] + [pl.BlockSpec((2, 128), lambda c: (0, 0))] * 4,
        compiler_params=pltpu.CompilerParams(vmem_limit_bytes=62 * 2**20),
        name="unpack",
    )(*gathered, result, grad_tokens, vectors)


def body(
    tokens, ln_gain1, ln_bias1, w_query, w_key, w_value, w_gate, w_out, ln_gain2, ln_bias2, w_up, w_down, doc_lengths, windows, cotangent
):
    table = jnp.asarray(rotary_constants())
    (
        result, first, second, mixed, act, cot_half, lift_half, lift, q, k, v, w01, w23, s_in, heads, u, w, hidden, stats, qnext,
    ) = forward(
        tokens[0], cotangent[0], ln_gain1, ln_bias1, ln_gain2, ln_bias2, doc_lengths, windows, table,
        w_query, w_key, w_value, w_gate, w_out, w_up, w_down,
    )

    def pair(a):
        return a.reshape(2 * TOK, a.shape[2])

    arrays = (
        act, pair(cot_half), pair(lift_half), pair(second), pair(first), pair(mixed), lift, cotangent[0], hidden, stats,
        u, w, heads, q, k, v, w01, w23, s_in, qnext, tokens[0], table,
        w_query, w_key, w_value.T, w_gate.T, w_out, w_up.T,
    )
    grad_tokens, vectors, *gathered = backward(arrays, ln_gain1, ln_gain2, doc_lengths, windows)
    g_down, g_up, g_out, g_gate, g_value, g_query, g_key, result, grad_tokens, *vectors = unpack(
        gathered, result, grad_tokens, vectors
    )
    gain1, bias1, gain2, bias2 = (vector.reshape(256) for vector in vectors)
    return (
        result.reshape(1, TOK, D), grad_tokens.reshape(1, TOK, D), gain1, bias1, g_query, g_key, g_value.T, g_gate.T, g_out,
        gain2, bias2, g_up.T, g_down,
    )


def solution(mesh):
    in_specs = (P("batch", "head", None),) + (P(),) * 11 + (P("batch", None), P(), P("batch", "head", None))
    rows, vector = P("head", None), P("head")
    out_specs = (
        P("batch", "head", None), P("batch", "head", None), vector, vector, rows, rows, rows, rows, rows, vector, vector, rows, rows,
    )
    return jax.shard_map(body, mesh=mesh, in_specs=in_specs, out_specs=out_specs, check_vma=False)
```

```python
import functools
import math

import jax
import jax.numpy as jnp
import numpy as np
from jax import lax
from jax.experimental import pallas as pl
from jax.experimental.pallas import tpu as pltpu
from jax.sharding import PartitionSpec as P

D = 1024
HEADS = 4
KEYH = 256
VH = 432
FF = 1728
QK = 1024
VD = 1728
TOK = 512
SEQ = 2048
HALO = 128
WIDE = 1792

epsilon = 1e-05
retention_floor = 1.0
BF = jnp.bfloat16
F32 = jnp.float32
MESH = pl.DeviceIdType.MESH


BIG, PAIRED = 112, 128
CUTS = {BIG: ((0, 48), (48, 32), (80, 32)), PAIRED: ((0, 48), (48, 48), (96, 32))}
ARRIVALS = 9


def coordinates():
    z = lax.axis_index("head")
    b = lax.axis_index("batch")
    return [z, lax.div(b, 8), lax.rem(lax.div(b, 2), 4), lax.rem(b, 2)]


def shifted(at, axis, step):
    place = list(at)
    if axis == 3:
        place[3] = 1 - place[3]
    else:
        place[axis] = lax.rem(place[axis] + step, 4)
    return (place[0], (place[1] * 4 + place[2]) * 2 + place[3])


def away(p, step):
    return lax.rem(p + step, 4)


LOW, HIGH = pl.ds(0, 2), pl.ds(2, 2)


def landing_shapes(r):
    return [(2, 2, 4, r, 128), (2, 4, 4, r, 128), (3, 4, r, 128), (3, r, 128)]


LANDINGS = 4


class Part:
    def __init__(self, at, stage, lands, mine, out, rows, order, gather, sems, slot, credit_in, credit_out, next_order, thrifty, joint):
        self.at, self.stage, self.out = at, stage, out
        self.first, self.count = rows
        self.lands = [land.at[..., pl.ds(0, self.count), :] for land in lands]
        self.mine = mine.at[pl.ds(0, self.count)]
        self.order, self.gather = order, gather
        send_sems, recv_sems, copy_sems = sems
        self.send_sem, self.copy_sem = send_sems.at[slot], copy_sems.at[slot]
        self.recv_sems = [recv_sems.at[ARRIVALS * slot + n] for n in range(ARRIVALS)]
        self.credit_in, self.credit_out, self.next_order = credit_in, credit_out, next_order
        self.thrifty = thrifty
        self.joint = joint
        self.lend = None

    def copy(self, source, target, axis, step, arrival):
        return pltpu.make_async_remote_copy(
            src_ref=source, dst_ref=target, send_sem=self.send_sem, recv_sem=self.recv_sems[arrival],
            device_id=shifted(self.at, axis, step), device_id_type=MESH,
        )

    def send(self, source, target, axis, step, arrival):
        self.copy(source, target, axis, step, arrival).start()

    def arrived(self, size, arrival):
        whole = self.copy(size, size, 3, 1, arrival)
        whole.wait_recv()
        whole.wait_send()

    def pick(self, axes):
        index = [slice(None)] * 3
        for axis, value in axes.items():
            index[axis] = value
        return self.stage.at[tuple(index) + (pl.ds(self.first, self.count), slice(None))]

    @staticmethod
    def writers(order):
        a1, a2, a3 = order
        return [(a1, 1), (a1, 3)] + [(axis, step) for axis in (a2, a3) for step in (1, 2, 3)]

    def steps(self):
        at, lands = self.at, self.lands
        a1, a2, a3 = self.order
        p1, p2, p3 = at[a1], at[a2], at[a3]
        cut = min(a2, a3)
        if self.credit_in is not None:
            pl.semaphore_wait(self.credit_in, len(self.writers(self.order)))
        self.send(self.pick({a1: away(p1, 2), cut: LOW}), lands[0].at[0], a1, 1, 0)
        self.send(self.pick({a1: away(p1, 2), cut: HIGH}), lands[0].at[1], a1, 3, 0)
        yield
        self.arrived(lands[0], 0)
        for n, step, part in ((0, 1, LOW), (1, 3, HIGH)):
            there = self.pick({a1: away(p1, step), cut: part})
            there[...] = there[...] + lands[0][n]
            self.send(self.pick({a1: away(p1, step)}), lands[1].at[n], a1, step, 1)
        yield
        self.arrived(lands[1], 1)
        own = self.pick({a1: p1})
        own[...] = (own[...].astype(F32) + lands[1][0].astype(F32) + lands[1][1].astype(F32)).astype(BF)
        if self.thrifty:
            self.send(self.pick({a1: p1, a2: away(p2, 2), a3: LOW}), lands[2].at[0, LOW], a2, 1, 2)
            self.send(self.pick({a1: p1, a2: away(p2, 2), a3: HIGH}), lands[2].at[0, HIGH], a2, 3, 2)
            yield
            self.arrived(lands[2].at[0], 2)
            for n, step, part in ((1, 1, LOW), (2, 3, HIGH)):
                there = self.pick({a1: p1, a2: away(p2, step), a3: part})
                there[...] = there[...] + lands[2][0, 2 * n - 2 : 2 * n]
                self.send(self.pick({a1: p1, a2: away(p2, step)}), lands[2].at[n], a2, step, 7)
            yield
            self.arrived(lands[2].at[pl.ds(1, 2)], 7)
            come = (1, 2)
        else:
            for s in (1, 2, 3):
                self.send(self.pick({a1: p1, a2: away(p2, s)}), lands[2].at[s - 1], a2, s, 2)
            yield
            self.arrived(lands[2], 2)
            come = (0, 1, 2)
        own = self.pick({a1: p1, a2: p2})
        total = own[...].astype(F32)
        for step in come:
            total = total + lands[2][step].astype(F32)
        own[...] = total.astype(BF)
        if self.lend is not None:
            credit, axis = self.lend
            for step in (1, 2, 3):
                pl.semaphore_signal(credit, inc=1, device_id=shifted(at, axis, step), device_id_type=MESH)
        if self.joint is not None:
            yield from self.joint_steps(own)
            return
        for s in (1, 2, 3):
            self.send(self.pick({a1: p1, a2: p2, a3: away(p3, s)}), lands[3].at[s - 1], a3, s, 3)
        yield
        self.arrived(lands[3], 3)
        total = self.pick({a1: p1, a2: p2, a3: p3})[...].astype(F32)
        for step in range(3):
            total = total + lands[3][step].astype(F32)
        self.mine[...] = total.astype(BF)
        if self.credit_out is not None:
            for axis, step in self.writers(self.next_order):
                pl.semaphore_signal(self.credit_out, inc=1, device_id=shifted(at, axis, step), device_id_type=MESH)

        rows = pl.ds(self.first, self.count)
        g1, g2 = self.gather
        target = self.out.at[at[3], at[1], at[2], rows]
        local = pltpu.make_async_copy(self.mine, target, self.copy_sem)
        local.start()
        for s in (1, 2, 3):
            self.send(self.mine, target, g1, s, 4)
        yield
        self.arrived(lands[3], 4)
        local.wait()

        def block(place, part=slice(None)):
            if g2 == 1:
                return self.out.at[at[3], place, part, rows]
            return self.out.at[at[3], part, place, rows]

        q = at[g2]
        if self.thrifty:
            for s in (1, 3):
                self.send(block(q), block(q), g2, s, 5)
            yield
            self.arrived(lands[2].at[pl.ds(0, 2)], 5)
            for s, part in ((1, LOW), (3, HIGH)):
                source = block(away(q, 4 - s), part)
                self.send(source, source, g2, s, 8)
            yield
            self.arrived(lands[2].at[0], 8)
        else:
            for s in (1, 2, 3):
                self.send(block(q), block(q), g2, s, 5)
            yield
            self.arrived(lands[2], 5)
        for place in range(4):
            self.send(block(place), block(place), 3, 1, 6)
        yield
        self.arrived(lands[1].at[0], 6)


    def joint_steps(self, own):
        at, (borrowed, credit) = self.at, self.joint
        axis, (g1, g2) = self.order[2], self.gather
        rows = pl.ds(self.first, self.count)
        borrowed = borrowed.at[..., pl.ds(0, self.count), :]
        pl.semaphore_wait(credit, 3)
        for s in (1, 2, 3):
            self.send(own, borrowed.at[s - 1], axis, s, 3)
        yield
        self.arrived(borrowed, 3)
        first = own[...].astype(F32) + borrowed[1].astype(F32)
        second = borrowed[0].astype(F32) + borrowed[2].astype(F32)
        own[...] = (first + second).astype(BF)

        def block(place):
            if g2 == 1:
                return self.out.at[at[3], place, :, rows]
            return self.out.at[at[3], :, place, rows]

        q = at[g2]
        local = pltpu.make_async_copy(own, block(q), self.copy_sem)
        local.start()
        for s in (1, 2, 3):
            self.send(own, block(q), g2, s, 5)
        yield
        self.arrived(self.lands[2], 5)
        local.wait()
        for place in range(4):
            self.send(block(place), block(place), 3, 1, 6)
        yield
        self.arrived(self.lands[1].at[0], 6)


class Unit:
    def __init__(self, parts, thrifty):
        self.parts = parts
        self.steps_to_reduce = 6 if thrifty else 5
        self.running = [None] * len(parts)
        self.done = [0] * len(parts)

    def start(self):
        for n, part in enumerate(self.parts):
            self.running[n] = part.steps()
            self.pump(n)

    def pump(self, n):
        if self.running[n] is not None and next(self.running[n], 0) == 0:
            self.running[n] = None
        self.done[n] += 1

    def reduced(self):
        for n in range(len(self.parts)):
            while self.done[n] < self.steps_to_reduce:
                self.pump(n)

    def finish(self):
        for n in range(len(self.parts)):
            while self.running[n] is not None:
                self.pump(n)


def vector_steps(at, mine, land_core, land_z, land_y, land_x, final, sems, base):
    send_sems, recv_sems = sems
    slots = iter(range(base, base + 10))

    def send(source, target, axis, step):
        slot = next(slots)
        copy = pltpu.make_async_remote_copy(
            src_ref=source, dst_ref=target, send_sem=send_sems.at[slot], recv_sem=recv_sems.at[slot],
            device_id=shifted(at, axis, step), device_id_type=MESH,
        )
        copy.start()
        return copy

    z, y, x, _ = at
    copies = [send(mine, land_core, 3, 1)]
    yield
    copies[0].wait()
    mine[...] = mine[...] + land_core[...]
    copies = [send(mine.at[away(z, s)], land_z.at[z], 0, s) for s in (1, 2, 3)]
    land_z[z] = mine[z]
    yield
    for axis, here, land in ((1, y, land_y), (2, x, land_x)):
        for copy in copies:
            copy.wait()
        source = land_z if axis == 1 else land_y
        total = (source[0] + source[1]) + (source[2] + source[3])
        land[here] = total
        copies = [send(land.at[here], land.at[here], axis, s) for s in (1, 2, 3)]
        yield
    for copy in copies:
        copy.wait()
    final[...] = (land_x[0] + land_x[1]) + (land_x[2] + land_x[3])


def greet(at):
    barrier = pltpu.get_barrier_semaphore()
    partners = [(axis, step) for axis in (0, 1, 2) for step in (1, 2, 3)] + [(3, 1)]
    for axis, step in partners:
        pl.semaphore_signal(barrier, inc=1, device_id=shifted(at, axis, step), device_id_type=MESH)
    pl.semaphore_wait(barrier, len(partners))


class Passing:
    PIECES = ((0, 0), (0, 1), (1, 0), (1, 1))

    def __init__(self, at, way, own, near, far, sems, base):
        self.at, self.way = at, way
        self.rank = at[0] if way == 1 else 3 - at[0]
        self.own, self.near, self.far = own, near, far
        self.send_sems, self.recv_sems = sems
        self.base = base

    ROWS = (slice(0, 224), slice(224, VH))

    def piece(self, ref, p):
        head, half = self.PIECES[p]
        rows = self.ROWS[half]
        return ref.at[head, pl.ds(rows.start, rows.stop - rows.start)]

    def copy(self, source, target, p, kind):
        step = {0: self.way, 1: -self.way, 2: -self.way}[kind] % 4
        slot = self.base + 4 * min(kind, 1) + p
        return pltpu.make_async_remote_copy(
            src_ref=self.piece(source, p), dst_ref=self.piece(target, p), send_sem=self.send_sems.at[slot],
            recv_sem=self.recv_sems.at[slot], device_id=shifted(self.at, 0, step), device_id_type=MESH,
        )

    def clear(self):
        @pl.when(self.rank == 0)
        def _():
            self.near[...] = jnp.zeros(self.near.shape, BF)

        @pl.when(self.rank < 2)
        def _():
            self.far[...] = jnp.zeros(self.far.shape, BF)

    def begin(self, p):
        @pl.when(self.rank < 2)
        def _():
            self.copy(self.own, self.near, p, 0).start()

        @pl.when(self.rank == 0)
        def _():
            self.copy(self.own, self.far, p, 1).start()

    def forward(self, p, decay):
        head, half = self.PIECES[p]
        rows = self.ROWS[half]

        @pl.when(self.rank == 2)
        def _():
            self.copy(self.own, self.near, p, 0).wait_recv()
            total = self.own[head, rows].astype(F32) + self.near[head, rows].astype(F32) * decay[head]
            self.own[head, rows] = total.astype(BF)
            self.copy(self.own, self.near, p, 0).start()

        @pl.when(self.rank == 3)
        def _():
            self.copy(self.far, self.far, p, 1).wait_recv()
            self.copy(self.far, self.far, p, 2).start()

    def finish(self):
        for p in range(4):

            @pl.when((self.rank == 1) | (self.rank == 3))
            def _():
                self.copy(self.own, self.near, p, 0).wait_recv()

            @pl.when(self.rank == 2)
            def _():
                self.copy(self.far, self.far, p, 1).wait_recv()

    def drain(self):
        for p in range(4):

            @pl.when(self.rank < 3)
            def _():
                self.copy(self.own, self.near, p, 0).wait_send()

            @pl.when((self.rank == 0) | (self.rank == 3))
            def _():
                self.copy(self.own, self.far, p, 1).wait_send()


LOG_GAMMA = tuple(math.log(1.0 - 2.0 ** (-5.0 - h)) for h in range(HEADS))
HALF = WIDE // 2


def rotary_constants():
    half = KEYH // 2
    ladder = np.arange(half, dtype=np.float64)
    theta = 10000.0 ** (-ladder / half)
    place = np.arange(SEQ, dtype=np.float64)[:, None]
    zeta = (2.0 * ladder + 0.4 * KEYH) / (1.4 * KEYH)
    grow = zeta[None, :] ** (place / 512.0)
    cosine, sine = np.cos(place * theta), np.sin(place * theta)
    small = KEYH ** (-0.5)
    table = np.concatenate([cosine * grow, sine * grow, cosine / grow * small, sine / grow * small], axis=1)
    return np.concatenate([np.zeros((HALO, 4 * half)), table]).astype(np.float32)


def dot_nn(a, b):
    return lax.dot_general(a, b, (((1,), (0,)), ((), ())), preferred_element_type=F32)


def dot_nt(a, b):
    return lax.dot_general(a, b, (((1,), (1,)), ((), ())), preferred_element_type=F32)


def dot_tn(a, b):
    return lax.dot_general(a, b, (((0,), (0,)), ((), ())), preferred_element_type=F32)


def row_loop(total, step, work):
    def one(i, carry):
        work(pl.ds(pl.multiple_of(i * step, step), step))
        return carry

    lax.fori_loop(0, total // step, one, 0)


class Documents:
    def __init__(self, lengths_ref):
        ends = []
        total = 0
        for i in range(5):
            total = total + lengths_ref[0, i]
            ends.append(total)
        self.ends = ends

    def of(self, where):
        found = jnp.zeros(where.shape, jnp.int32) if hasattr(where, "shape") and where.shape else 0
        for end in self.ends:
            found = found + jnp.where(where >= end, 1, 0)
        return found


def column(count, first=0):
    return lax.broadcasted_iota(jnp.int32, (count, 1), 0) + first


def line(count, first=0):
    return lax.broadcasted_iota(jnp.int32, (1, count), 1) + first


def decay_block(h, rows, cols, row_first, col_first, start, docs, window):
    i, j = column(rows, row_first), line(cols, col_first)
    base = min(row_first, col_first)
    seen = (i >= j) & (docs.of(i + start) == docs.of(j + start))
    if window is not None:
        seen = seen & (i - j < window)
    if col_first < 0:
        seen = seen & (j + start >= 0)
    down = jnp.exp((i - base).astype(F32) * LOG_GAMMA[h])
    up = jnp.exp((j - base).astype(F32) * (-LOG_GAMMA[h]))
    return jnp.where(seen, down * up, 0.0)


def rotated(raw, cosine, sine):
    front, behind = raw[:, :128], raw[:, 128:]
    return jnp.concatenate([front * cosine - behind * sine, front * sine + behind * cosine], axis=1)


def forward_kernel(
    tokens_hbm, cot_hbm, gain1, bias1, gain2, bias2, lengths, windows, table_hbm,
    wq_hbm, wk_hbm, wv_hbm, wg_hbm, wo_hbm, wu_hbm, wd_hbm,
    out_result, out_first, out_second, out_mixed, out_act, out_cot, out_lhalf, out_lift,
    out_q, out_k, out_v, out_w01, out_w23, out_sin, out_heads, out_u, out_w, out_hidden, out_stats, out_qnext,
    tokens, cot, table, wq, wk, wv, wg, wo, wu, wd,
    first, queries, keys, values, wide_f32, down_grad, kept, w01, w23, state, state_near, state_far, state_in,
    heads, u_ref, w_ref, mixed, hidden, second, lift, act, stats,
    load_sems, save_sems, send_sems, recv_sems, pass_send, pass_recv,
):
    at = coordinates()
    z, core = at[0], at[3]
    start = z * TOK
    loads = {}
    for slot, (name, source, target) in enumerate(
        [
            ("tokens", tokens_hbm, tokens.at[pl.ds(HALO, TOK)]),
            ("wk", wk_hbm, wk),
            ("table", table_hbm.at[pl.ds(pl.multiple_of(z * TOK, TOK), HALO + TOK)], table),
            ("wv", wv_hbm, wv),
            ("wq", wq_hbm, wq),
            ("wg", wg_hbm, wg),
            ("cot", cot_hbm, cot),
            ("wd", wd_hbm, wd),
            ("wo", wo_hbm, wo),
            ("wu", wu_hbm, wu),
        ]
    ):
        loads[name] = pltpu.make_async_copy(source, target, load_sems.at[slot])
        loads[name].start()
    partners = [(3, 1), (0, 1), (0, 3)]
    barrier = pltpu.get_barrier_semaphore()
    for axis, step in partners:
        pl.semaphore_signal(barrier, inc=1, device_id=shifted(at, axis, step), device_id_type=MESH)

    saves, sends = [], []

    def save(source, target):
        copy = pltpu.make_async_copy(source, target, save_sems.at[len(saves)])
        copy.start()
        saves.append(copy)

    def remote(source, target, axis, step):
        slot = len(sends)
        copy = pltpu.make_async_remote_copy(
            src_ref=source, dst_ref=target, send_sem=send_sems.at[slot], recv_sem=recv_sems.at[slot],
            device_id=shifted(at, axis, step), device_id_type=MESH,
        )
        sends.append(copy)
        return copy

    def share(source, target):
        save(source, target.at[core])
        remote(source, target.at[core], 3, 1).start()
        return (saves[-1], sends[-1])

    loads["tokens"].wait()

    pl.semaphore_wait(barrier, len(partners))
    t_halo = remote(tokens.at[pl.ds(TOK, HALO)], tokens.at[pl.ds(0, HALO)], 0, 1)

    @pl.when(z < 3)
    def _():
        t_halo.start()

    @pl.when(z == 0)
    def _():
        tokens[0:HALO] = jnp.zeros((HALO, D), BF)

    def normalized(x):
        mean = jnp.mean(x, axis=-1, keepdims=True)
        center = x - mean
        inverse = lax.rsqrt(jnp.mean(center * center, axis=-1, keepdims=True) + epsilon)
        return center * inverse, mean, inverse

    def norm_one(i, carry):
        rows = pl.ds(pl.multiple_of(i * 64, 64), 64)
        scaled, mean, inverse = normalized(tokens[pl.ds(HALO + i * 64, 64)].astype(F32))
        first[pl.ds(HALO + i * 64, 64)] = (scaled * gain1[...] + bias1[...]).astype(BF)
        stats[rows, 0:1] = mean
        stats[rows, 1:2] = inverse
        return carry

    lax.fori_loop(0, TOK // 64, norm_one, 0)
    share(first.at[pl.ds(HALO, TOK)], out_first)

    docs = Documents(lengths)
    doc_before = docs.of(start - 1)
    doc_last = docs.of(start + TOK - 1)
    place = column(TOK)
    doc_rows = docs.of(place + start)

    def project(h, begin):
        cols = slice(h * KEYH, (h + 1) * KEYH)
        raw = dot_nn(first[begin:], wk[:, cols])
        keys[begin:, cols] = rotated(raw, table[begin:, 256:384], table[begin:, 384:512]).astype(BF)
        values[h, begin:] = dot_nt(first[begin:], wv[h * VH : (h + 1) * VH]).astype(BF)

    loads["wk"].wait()
    loads["table"].wait()
    loads["wv"].wait()
    passing = Passing(at, 1, state, state_near, state_far, (pass_send, pass_recv), 0)
    joins = [jnp.where(doc_before == doc_last, math.exp(LOG_GAMMA[h] * TOK), 0.0) for h in (2, 3)]
    for h in (2, 3):
        project(h, HALO)
        factor = jnp.where(doc_rows == doc_last, jnp.exp((TOK - place).astype(F32) * LOG_GAMMA[h]), 0.0)
        scaled = (keys[HALO:, h * KEYH : (h + 1) * KEYH].astype(F32) * factor).astype(BF)
        state[h - 2] = dot_tn(values[h, HALO:], scaled).astype(BF)
        passing.begin(2 * h - 4)
        passing.begin(2 * h - 3)
    passing.clear()
    loads["wq"].wait()
    for h in range(HEADS):
        raw = dot_nn(first[HALO:], wq[:, h * KEYH : (h + 1) * KEYH])
        queries[:, h * KEYH : (h + 1) * KEYH] = rotated(raw, table[HALO:, 0:128], table[HALO:, 128:256]).astype(BF)
    save(queries, out_q)
    q_halo = remote(queries.at[pl.ds(0, HALO), pl.ds(0, 2 * KEYH)], out_qnext, 0, 3)

    @pl.when(z > 0)
    def _():
        q_halo.start()

    loads["wg"].wait()

    def swish(h, rows):
        lane = 512 * (h % 2)
        gate = wide_f32[rows, lane : lane + VH]
        sigma = 0.5 * jnp.tanh(0.5 * gate) + 0.5
        u_ref[h, rows] = (gate * sigma).astype(BF)
        w_ref[h, rows] = (sigma * (1.0 + gate * (1.0 - sigma))).astype(BF)

    for h in range(HEADS + 1):
        if h < HEADS:
            lane = 512 * (h % 2)
            wide_f32[:, lane : lane + VH] = dot_nt(first[HALO:], wg[h * VH : (h + 1) * VH])
        if h > 0:
            for row in range(0, TOK, 64):
                swish(h - 1, slice(row, row + 64))
        if h == 2:
            passing.forward(0, joins)
    passing.forward(1, joins)
    save(u_ref, out_u)
    save(w_ref, out_w)
    loads["cot"].wait()
    save(cot.at[:, pl.ds(pl.multiple_of(core * 512, 512), 512)], out_cot.at[core])
    remote(cot.at[:, pl.ds(pl.multiple_of((1 - core) * 512, 512), 512)], out_cot.at[core], 3, 1).start()
    loads["wd"].wait()
    down_grad[...] = dot_nt(cot[...], wd[...]).astype(BF)
    passing.forward(2, joins)

    for h in (2, 3):
        for b in (0, 1):
            rows, cols = slice(256 * b, 256 * b + 256), 256 * b + 256
            q_h = queries[rows, h * KEYH : (h + 1) * KEYH]
            scores = dot_nt(q_h, keys[HALO : HALO + cols, h * KEYH : (h + 1) * KEYH])
            weight = (scores * decay_block(h, 256, cols, 256 * b, 0, start, docs, None)).astype(BF)
            w23[h - 2, rows, 0:cols] = weight
            kept[h, rows] = dot_nn(weight, values[h, HALO : HALO + cols])

    passing.forward(3, joins)

    @pl.when(z > 0)
    def _():
        t_halo.wait_recv()

    for block in (slice(0, 64), slice(64, 128)):
        first[block] = (normalized(tokens[block].astype(F32))[0] * gain1[...] + bias1[...]).astype(BF)
    for h in (0, 1):
        project(h, 0)

    save(keys, out_k)
    save(values, out_v)
    for h in (0, 1):
        for b in (0, 1):
            rows = slice(256 * b, 256 * b + 256)
            q_h = queries[rows, h * KEYH : (h + 1) * KEYH]
            scores = dot_nt(q_h, keys[256 * b : 256 * b + 384, h * KEYH : (h + 1) * KEYH])
            decay = decay_block(h, 256, 384, 256 * b, 256 * b - HALO, start, docs, windows[0, h])
            weight = (scores * decay).astype(BF)
            w01[h, b] = weight
            kept[h, rows] = dot_nn(weight, values[h, 256 * b : 256 * b + 384])
    save(w01, out_w01)
    save(w23, out_w23)

    passing.finish()
    from_first = docs.of(TOK - 1) == doc_before
    for h in (2, 3):
        power = jnp.where(z == 3, math.exp(2 * TOK * LOG_GAMMA[h]), math.exp(TOK * LOG_GAMMA[h]))
        total = state_near[h - 2].astype(F32) + state_far[h - 2].astype(F32) * jnp.where(from_first, power, 0.0)
        state_in[h - 2] = total.astype(BF)
        factor = jnp.where(doc_rows == doc_before, jnp.exp(place.astype(F32) * LOG_GAMMA[h]), 0.0)
        kept[h] = kept[h] + factor * dot_nt(queries[:, h * KEYH : (h + 1) * KEYH], state_in[h - 2])
    save(state_in, out_sin)

    def mix(rows):
        parts = []
        for h in range(HEADS):
            x = kept[h, rows]
            center = x - jnp.mean(x, axis=-1, keepdims=True)
            inverse = lax.rsqrt(jnp.mean(center * center, axis=-1, keepdims=True) + retention_floor)
            stats[rows, 4 + h : 5 + h] = inverse
            low = (center * inverse).astype(BF)
            heads[h, rows] = low
            parts.append(low.astype(F32) * u_ref[h, rows].astype(F32))
        mixed[rows] = jnp.concatenate(parts, axis=1).astype(BF)

    row_loop(TOK, 64, mix)
    mixed_away = share(mixed, out_mixed)
    save(heads, out_heads)

    loads["wo"].wait()
    hidden[...] = dot_nn(mixed[...], wo[...])

    def norm_two(i, carry):
        rows = pl.ds(pl.multiple_of(i * 64, 64), 64)
        x = hidden[rows] + tokens[pl.ds(HALO + i * 64, 64)].astype(F32)
        hidden[rows] = x
        scaled, mean, inverse = normalized(x)
        second[rows] = (scaled * gain2[...] + bias2[...]).astype(BF)
        stats[rows, 2:3] = mean
        stats[rows, 3:4] = inverse
        return carry

    lax.fori_loop(0, TOK // 64, norm_two, 0)
    share(second, out_second)
    save(hidden, out_hidden)
    save(stats, out_stats)

    loads["wu"].wait()

    def activate(cols, rows):
        x = wide_f32[rows, cols]
        phi = 0.5 * (1.0 + lax.erf(x * math.sqrt(0.5)))
        slope = phi + x * jnp.exp(-0.5 * x * x) * (1.0 / math.sqrt(2.0 * math.pi))
        act[rows, cols] = (x * phi).astype(BF)
        grad = (down_grad[rows, cols].astype(F32) * slope).astype(BF)
        if cols.stop == FF:
            grad = jnp.concatenate([grad, jnp.zeros((grad.shape[0], WIDE - FF), BF)], axis=1)
        lift[rows, cols.start : cols.start + grad.shape[1]] = grad

    blocks = [slice(first_col, min(first_col + 256, FF)) for first_col in range(0, FF, 256)]
    for n in range(len(blocks) + 1):
        if n < len(blocks):
            wide_f32[:, blocks[n]] = dot_nt(second[...], wu[blocks[n]])
        if n > 0:
            for row in range(0, TOK, 64):
                activate(blocks[n - 1], slice(row, row + 64))
    save(act, out_act)
    save(lift, out_lift)
    save(lift.at[:, pl.ds(pl.multiple_of(core * HALF, HALF), HALF)], out_lhalf.at[core])
    remote(lift.at[:, pl.ds(pl.multiple_of((1 - core) * HALF, HALF), HALF)], out_lhalf.at[core], 3, 1).start()
    for copy in mixed_away:
        copy.wait()
    mixed[:, 0:D] = (hidden[...] + dot_nn(act[...], wd[...])).astype(BF)
    save(mixed.at[:, pl.ds(0, D)], out_result)

    for copy in sends:
        if not any(copy is other for other in (t_halo, q_halo) + mixed_away):
            copy.wait()

    @pl.when(z > 0)
    def _():
        q_halo.wait_send()

    @pl.when(z < 3)
    def _():
        q_halo.wait_recv()
        t_halo.wait_send()

    passing.drain()
    for copy in saves:
        if copy is not mixed_away[0]:
            copy.wait()


def forward(tokens, cot, gain1, bias1, gain2, bias2, lengths, windows, table, wq, wk, wv, wg, wo, wu, wd):
    vmem = pl.BlockSpec(memory_space=pltpu.VMEM)
    smem = pl.BlockSpec(memory_space=pltpu.SMEM)
    anywhere = pl.BlockSpec(memory_space=pl.ANY)
    shape = jax.ShapeDtypeStruct
    outs = [
        shape((TOK, D), BF), shape((2, TOK, D), BF), shape((2, TOK, D), BF), shape((2, TOK, VD), BF), shape((TOK, FF), BF),
        shape((2, TOK, 512), BF), shape((2, TOK, HALF), BF), shape((TOK, WIDE), BF),
        shape((TOK, QK), BF), shape((HALO + TOK, QK), BF), shape((HEADS, HALO + TOK, VH), BF),
        shape((2, 2, 256, 384), BF), shape((2, TOK, TOK), BF), shape((2, VH, KEYH), BF),
        shape((HEADS, TOK, VH), BF), shape((HEADS, TOK, VH), BF), shape((HEADS, TOK, VH), BF), shape((TOK, D), F32), shape((TOK, 128), F32),
        shape((HALO, 2 * KEYH), BF),
    ]
    scratch = [
        pltpu.VMEM((HALO + TOK, D), BF), pltpu.VMEM((TOK, D), BF), pltpu.VMEM((HALO + TOK, 512), F32),
        pltpu.VMEM((D, QK), BF), pltpu.VMEM((D, QK), BF), pltpu.VMEM((VD, D), BF), pltpu.VMEM((VD, D), BF),
        pltpu.VMEM((VD, D), BF), pltpu.VMEM((FF, D), BF), pltpu.VMEM((FF, D), BF),
        pltpu.VMEM((HALO + TOK, D), BF), pltpu.VMEM((TOK, QK), BF), pltpu.VMEM((HALO + TOK, QK), BF),
        pltpu.VMEM((HEADS, HALO + TOK, VH), BF), pltpu.VMEM((TOK, FF), F32), pltpu.VMEM((TOK, FF), BF),
        pltpu.VMEM((HEADS, TOK, VH), F32), pltpu.VMEM((2, 2, 256, 384), BF), pltpu.VMEM((2, TOK, TOK), BF),
        pltpu.VMEM((2, VH, KEYH), BF), pltpu.VMEM((2, VH, KEYH), BF), pltpu.VMEM((2, VH, KEYH), BF), pltpu.VMEM((2, VH, KEYH), BF),
        pltpu.VMEM((HEADS, TOK, VH), BF), pltpu.VMEM((HEADS, TOK, VH), BF), pltpu.VMEM((HEADS, TOK, VH), BF), pltpu.VMEM((TOK, VD), BF),
        pltpu.VMEM((TOK, D), F32), pltpu.VMEM((TOK, D), BF), pltpu.VMEM((TOK, WIDE), BF), pltpu.VMEM((TOK, FF), BF),
        pltpu.VMEM((TOK, 128), F32),
        pltpu.SemaphoreType.DMA((10,)), pltpu.SemaphoreType.DMA((20,)),
        pltpu.SemaphoreType.DMA((16,)), pltpu.SemaphoreType.DMA((16,)),
        pltpu.SemaphoreType.DMA((8,)), pltpu.SemaphoreType.DMA((8,)),
    ]
    return pl.pallas_call(
        forward_kernel,
        out_shape=outs,
        in_specs=[anywhere] * 2 + [vmem] * 4 + [smem] * 2 + [anywhere] * 8,
        out_specs=[anywhere] * len(outs),
        scratch_shapes=scratch,
        compiler_params=pltpu.CompilerParams(collective_id=1, has_side_effects=True, vmem_limit_bytes=62 * 2**20),
        cost_estimate=pl.CostEstimate(flops=14 * 10**9, bytes_accessed=50 * 10**6, transcendentals=2 * 10**6),
        name="forward",
    )(
        tokens, cot, gain1.reshape(1, D), bias1.reshape(1, D), gain2.reshape(1, D), bias2.reshape(1, D),
        lengths, windows.reshape(1, HEADS), table, wq, wk, wv.T, wg.T, wo, wu.T, wd,
    )


LAST = TOK - HALO
UNITS = ("down", "up", "out", "gate", "value", "qk")
UNIT_ROWS = {"down": BIG, "up": BIG, "out": BIG, "gate": BIG, "value": BIG, "qk": PAIRED}
UNIT_SET = {"down": 0, "up": 1, "out": 2, "gate": 3, "value": 0, "qk": 1}
SET_ROWS = (BIG, PAIRED, BIG, BIG)
FOLLOWER = {"down": "value", "up": "qk"}
LENDER = {"value": "gate", "qk": "out"}
PLAN = {
    "down": (((0, 1, 2), (1, 2)), ((2, 1, 0), (1, 2)), ((1, 0, 2), (2, 1))),
    "up": (((1, 2, 0), (1, 2)), ((2, 1, 0), (2, 1)), ((0, 2, 1), (1, 2))),
    "out": (((2, 0, 1), (2, 1)), ((2, 1, 0), (1, 2)), ((1, 2, 0), (2, 1))),
    "gate": (((2, 0, 1), (1, 2)), ((1, 0, 2), (1, 2)), ((1, 0, 2), (2, 1))),
    "value": (((2, 0, 1), (1, 2)), ((1, 0, 2), (2, 1)), ((0, 2, 1), (1, 2))),
    "qk": (((0, 2, 1), (1, 2)), ((1, 0, 2), (2, 1)), ((0, 1, 2), (2, 1))),
}
THRIFTY = ("down", "out")
BLOCKS = (
    "up", "second", "down", "norm2", "mixl", "out", "states", "mixe", "gate", "fg", "band", "full", "far", "cross", "store", "qk", "value", "fq", "fk", "fv", "n1",
)
SCHEDULE = (
    (), (), (), (3, 4, 5), (), (1, 2), (0,), (4, 5), (3,), (1, 2), (0, 6, 8), (18, 19, 0, 1, 3, 4, 5, 7), (20, 8), (10,), (21, 2, 6, 11), (0, 1, 9), (5, 7, 8, 10), (0, 3, 4), (11,), (2, 5, 6, 7, 9), (0, 1, 3, 4, 8, 10), (2, 6, 7, 11), (0, 1, 4, 5, 8, 9), (3, 10), (2, 4, 11, 15, 16), (5, 6, 17), (3, 7, 12, 13), (0, 9, 10, 14), (1, 2, 6, 8, 11), (0, 15, 16),
)
TAIL = (7, 12, 17, 13, 10, 1, 9, 2, 14, 10, 6, 15, 1, 8, 7, 2, 16, 11, 17, 9, 6, 12, 11, 14, 13, 7, 15, 9, 8, 6, 16, 7, 8, 17, 12, 13, 14, 15, 16, 17, 12, 15, 16, 13, 14, 17, 12, 13, 14)
PART_ROWS = {rows: tuple(count for _, count in cuts) for rows, cuts in CUTS.items()}


def stage_rows(stage, result, first_x):
    for z in range(4):
        for y in range(4):
            n = min(BIG, VH - BIG * y)
            for i in range(result.shape[1] // 128):
                piece = result[VH * z + BIG * y : VH * z + BIG * y + n, 128 * i : 128 * i + 128].astype(BF)
                stage[z, y, first_x + i, 0:n] = piece
                if n < BIG:
                    stage[z, y, first_x + i, n:BIG] = jnp.zeros((BIG - n, 128), BF)


def stage_columns(stage, result, first_z):
    for i in range(result.shape[1] // 128):
        z, xc = first_z + i // 2, i % 2
        for y in range(4):
            for xr in range(2):
                first = 224 * y + BIG * xr
                stage[z, y, 2 * xr + xc, 0:BIG] = result[first : first + BIG, 128 * i : 128 * i + 128].astype(BF)


def stage_square(stage, result, first_row):
    for z in range(4):
        for y in range(4):
            for x in range(4):
                piece = result[256 * z + 64 * y : 256 * z + 64 * y + 64, 128 * x : 128 * x + 128].astype(BF)
                stage[z, y, x, first_row : first_row + 64] = piece


def fold(rows):
    return jnp.sum(rows.reshape(rows.shape[0] // 8, 8, rows.shape[1]), axis=0)


def unrotated(grad, cosine, sine):
    grad = grad.astype(BF).astype(F32)
    front, behind = grad[:, :128], grad[:, 128:]
    return jnp.concatenate([front * cosine + behind * sine, behind * cosine - front * sine], axis=1).astype(BF)


def backward_kernel(
    act_hbm, coth_hbm, lhalf_hbm, second_hbm, first_hbm, mixed_hbm, lift_hbm, cot_hbm, hidden_hbm, stats_hbm,
    u_hbm, w_hbm, heads_hbm, q_hbm, k_hbm, v_hbm, w01_hbm, w23_hbm, sin_hbm, qnext_hbm, tokens_hbm, table_hbm,
    wq_hbm, wk_hbm, wv_hbm, wg_hbm, wo_hbm, wu_hbm, gain1, gain2, lengths, windows,
    out_tokens, out_vec, out_down, out_up, out_out, out_gate, out_value, out_qk,
    x1, x2, x3, y1, ch, wide, cot, heads, u_ref, w_ref, queries, keys, values, w01, w23, state_in,
    back_state, back_near, back_far, rgrad, hidden, wf, wu, wo, table, stats, qnext, gnext, vec_rows,
    vec, vec_core, vec_z, vec_y, vec_x, vec_out,
    stage0, stage1, stage2, stage3, *rest,
):
    lands = [[rest[(3 * s + p) * LANDINGS : (3 * s + p + 1) * LANDINGS] for p in range(3)] for s in range(4)]
    rest = rest[12 * LANDINGS :]
    mines = rest[0:18]
    load_sems, save_sems, pair_send, pair_recv, z_send, z_recv, vec_send, vec_recv = rest[18:26]
    unit_send, unit_recv, unit_copy, credits, pair_credit, pass_send, pass_recv, joint_credits = rest[26:]
    stages = (stage0, stage1, stage2, stage3)
    at = coordinates()
    z, core = at[0], at[3]
    start = z * TOK

    loading = {}

    def load(name, source, target):
        copy = pltpu.make_async_copy(source, target, load_sems.at[len(loading)])
        copy.start()
        loading[name] = copy

    def ready(*names):
        for name in names:
            loading[name].wait()

    waited = set()

    def ready_once(*names):
        for name in names:
            if name not in waited:
                waited.add(name)
                loading[name].wait()

    own_rows = pl.ds(pl.multiple_of(core * TOK, TOK), TOK)
    load("act", act_hbm, x1.at[own_rows])
    load("lhalf", lhalf_hbm, y1)
    load("second", second_hbm, x2)
    load("coth", coth_hbm, ch)
    load("lift", lift_hbm, wide)
    load("wu", wu_hbm, wu)
    greet(at)

    outs = dict(zip(UNITS, (out_down, out_up, out_out, out_gate, out_value, out_qk)))
    units = {}
    for n, name in enumerate(UNITS):
        s, parts = UNIT_SET[name], []
        for p in range(3):
            slot = 3 * n + p
            order, gather = PLAN[name][p]
            follower = FOLLOWER.get(name)
            parts.append(
                Part(
                    at, stages[s], lands[s][p], mines[slot], outs[name], CUTS[UNIT_ROWS[name]][p], order, gather,
                    (unit_send, unit_recv, unit_copy), slot,
                    credits.at[slot - 12] if n >= 4 else None, credits.at[slot] if follower else None,
                    PLAN[follower][p][0] if follower else None, name in THRIFTY,
                    (lands[UNIT_SET[LENDER[name]]][p][2], joint_credits.at[slot - 12]) if n >= 4 else None,
                )
            )
        units[name] = Unit(parts, name in THRIFTY)
    for name, lender in LENDER.items():
        for p in range(3):
            slot = 3 * UNITS.index(name) + p
            units[lender].parts[p].lend = (joint_credits.at[slot - 12], PLAN[name][p][0][2])
    down, up, out, gate, value, qk = (units[name] for name in UNITS)
    numbered = [units[name] for name in UNITS]
    ticks = iter(SCHEDULE)

    def tick():
        for n in next(ticks):
            if n < 3 * len(UNITS):
                numbered[n // 3].pump(n % 3)
            else:
                passing.forward(n - 3 * len(UNITS), joins)

    pairs = []

    def to_sibling(source, target):
        copy = pltpu.make_async_remote_copy(
            src_ref=source, dst_ref=target, send_sem=pair_send.at[len(pairs)], recv_sem=pair_recv.at[len(pairs)],
            device_id=shifted(at, 3, 1), device_id_type=MESH,
        )
        copy.start()
        pairs.append(copy)
        return copy

    local_copies = []

    def halves(source, width, landing, lane):
        rows = pl.ds(pl.multiple_of(core * TOK, TOK), TOK)
        lanes = pl.ds(lane, width)
        mine = source.at[:, pl.ds(pl.multiple_of(core * width, width), width)]
        other = source.at[:, pl.ds(pl.multiple_of((1 - core) * width, width), width)]
        remote = to_sibling(other, landing.at[rows, lanes])
        local = pltpu.make_async_copy(mine, landing.at[rows, lanes], save_sems.at[len(local_copies)])
        local.start()
        local_copies.append(local)
        return remote, local

    def arrived(pair):
        pair[0].wait()
        pair[1].wait()

    ready("act")
    act_pair = to_sibling(x1.at[own_rows], x1.at[own_rows])

    def tell_sibling(slot):
        pl.semaphore_signal(pair_credit.at[slot], inc=1, device_id=shifted(at, 3, 1), device_id_type=MESH)

    docs = Documents(lengths)
    doc_before = docs.of(start - 1)
    doc_last = docs.of(start + TOK - 1)
    place = column(TOK)
    doc_rows = docs.of(place + start)
    joins = [jnp.where(doc_before == doc_last, math.exp(LOG_GAMMA[h] * TOK), 0.0) for h in (2, 3)]
    passing = Passing(at, -1, back_state, back_near, back_far, (pass_send, pass_recv), 0)
    zero = jnp.zeros((8, D), F32)
    grad_v = u_ref
    pair = {}
    g_halo = pltpu.make_async_remote_copy(
        src_ref=rgrad.at[pl.ds(0, 2), pl.ds(0, HALO)], dst_ref=gnext, send_sem=z_send.at[0], recv_sem=z_recv.at[0],
        device_id=shifted(at, 0, 3), device_id_type=MESH,
    )

    def head_cols(h):
        return slice(h * KEYH, (h + 1) * KEYH)

    def row_factor(h):
        return jnp.where(doc_rows == doc_before, jnp.exp(place.astype(F32) * LOG_GAMMA[h]), 0.0)

    def two_halves(work):
        for half in (0, 1):
            cols = slice(512 * half, 512 * half + 512)
            wf[:, cols] = work(cols)
            tick()

    def block_down():
        ready("coth")
        act_pair.wait()
        for half in (0, 1):
            stage_rows(stage0, dot_tn(x1[...], ch[:, 256 * half : 256 * half + 256]), 2 * half)
        down.start()
        load("mixed", mixed_hbm, x1)
        tell_sibling(0)
        tick()

    def block_up():
        ready("lhalf", "second")
        for half in (0, 1):
            stage_columns(stage1, dot_tn(y1[...], x2[:, 512 * half : 512 * half + 512]), 2 * half)
        up.start()
        tell_sibling(1)
        tick()

    def block_second():
        ready("lift", "wu")
        two_halves(lambda cols: dot_nn(wide[:, 0:FF], wu[:, cols]))
        load("wg", wg_hbm, wu)

    def block_norm2():
        ready("cot", "hidden", "stats")

        def back_two(i, sums):
            rows = pl.ds(pl.multiple_of(i * 64, 64), 64)
            grad = wf[rows]
            inverse = stats[rows, 3:4]
            scaled = (hidden[rows] - stats[rows, 2:3]) * inverse
            e = grad * gain2[...]
            inner = e - jnp.mean(e, axis=-1, keepdims=True) - scaled * jnp.mean(e * scaled, axis=-1, keepdims=True)
            total = cot[rows].astype(F32) + inverse * inner
            hidden[rows] = total
            cot[rows] = total.astype(BF)
            return (sums[0] + fold(grad * scaled), sums[1] + fold(grad))

        gain_sum, bias_sum = lax.fori_loop(0, TOK // 64, back_two, (zero, zero))
        pl.semaphore_wait(pair_credit.at[0], 1)
        pair["low"] = halves(cot, 512, ch, 0)
        vec_rows[2:3] = jnp.sum(gain_sum, axis=0, keepdims=True)
        vec_rows[3:4] = jnp.sum(bias_sum, axis=0, keepdims=True)
        tick()

    def mixed_grad(h):
        ready_once("wo", "u", "w", "heads")
        lane = 512 * (h % 2)
        wf[:, lane : lane + VH] = dot_nt(cot[...], wo[h * VH : (h + 1) * VH])

    def back_head(h, rows):
        lane = 512 * (h % 2)
        grad = wf[rows, lane : lane + VH]
        c = heads[h, rows].astype(F32)
        gated = grad * c * w_ref[h, rows].astype(F32)
        e = (grad * u_ref[h, rows].astype(F32)).astype(BF).astype(F32)
        inner = e - jnp.mean(e, axis=-1, keepdims=True) - c * jnp.mean(e * c, axis=-1, keepdims=True)
        rgrad[h, rows] = (inner * stats[rows, 4 + h : 5 + h]).astype(BF)
        return gated

    def block_mixl():
        mixed_grad(2)
        mixed_grad(3)
        for h in (2, 3):
            for row in range(0, TOK, 64):
                rows = slice(row, row + 64)
                w_ref[h, rows] = back_head(h, rows).astype(BF)
            tick()

    def block_states():
        ready("q")
        for h in (2, 3):
            scaled = (queries[:, head_cols(h)].astype(F32) * row_factor(h)).astype(BF)
            back_state[h - 2] = dot_tn(rgrad[h], scaled).astype(BF)
            passing.begin(2 * h - 4)
            passing.begin(2 * h - 3)
        passing.clear()
        tick()

    def block_mixe():
        mixed_grad(0)
        mixed_grad(1)
        load("wv", wv_hbm, wo)
        for row in range(0, TOK, 64):
            rows = slice(row, row + 64)
            parts = [back_head(h, rows) for h in (0, 1)] + [w_ref[h, rows].astype(F32) for h in (2, 3)]
            gated = jnp.concatenate(parts, axis=1).astype(BF)
            wide[rows] = jnp.concatenate([gated, jnp.zeros((64, WIDE - VD), BF)], axis=1)
            if row == TOK // 2 - 64:
                tick()
        ready("qnext")

        @pl.when(z > 0)
        def _():
            g_halo.start()

        @pl.when(z == 3)
        def _():
            gnext[...] = jnp.zeros((2, HALO, VH), BF)
            qnext[...] = jnp.zeros((HALO, 2 * KEYH), BF)

        pl.semaphore_wait(pair_credit.at[1], 1)
        pair["gate"] = halves(wide, HALF, y1, 0)
        tick()

    def block_out():
        ready("mixed")
        arrived(pair["low"])
        for half in (0, 1):
            stage_rows(stage2, dot_tn(x1[...], ch[:, 256 * half : 256 * half + 256]), 2 * half)
        out.start()
        tell_sibling(2)
        tick()

    def block_gate():
        ready("first")
        arrived(pair["gate"])
        for half in (0, 1):
            stage_columns(stage3, dot_tn(y1[...], x3[:, 512 * half : 512 * half + 512]), 2 * half)
        gate.start()
        tick()

    def block_fg():
        ready("wg")
        two_halves(lambda cols: dot_nn(wide[:, 0:VD], wu[:, cols]))

    def finish_query(h, grad):
        queries[:, head_cols(h)] = unrotated(grad, table[:, 0:128], table[:, 128:256])

    def finish_key(h, grad, rows=slice(0, TOK)):
        cot[rows, head_cols(h)] = unrotated(grad, table[rows, 256:384], table[rows, 384:512])

    def block_full():
        ready_once("k", "v", "w01", "w23", "sin", "table")
        for h in (2, 3):
            cols_h = head_cols(h)
            score = []
            for b in (0, 1):
                rows, cols = slice(256 * b, 256 * b + 256), 256 * b + 256
                grad = dot_nt(rgrad[h, rows], values[h, HALO : HALO + cols])
                grad = (grad * decay_block(h, 256, cols, 256 * b, 0, start, docs, None)).astype(BF)
                score.append(grad)
            late = dot_tn(score[1], queries[256:512, cols_h])
            early = dot_tn(score[0], queries[0:256, cols_h])
            ch[0:TOK, head_cols(h - 2)] = jnp.concatenate([early + late[:256], late[256:]], axis=0).astype(BF)
            query = jnp.concatenate([dot_nn(score[b], keys[HALO : HALO + 256 * b + 256, cols_h]) for b in (0, 1)], axis=0)
            query = query + row_factor(h) * dot_nn(rgrad[h], state_in[h - 2])
            finish_query(h, query)
            late = dot_tn(w23[h - 2, 256:512], rgrad[h, 256:512])
            early = dot_tn(w23[h - 2, 0:256, 0:256], rgrad[h, 0:256])
            grad_v[h] = jnp.concatenate([early + late[:256], late[256:]], axis=0).astype(BF)
            tick()

    def block_band():
        ready_once("k", "v", "w01", "w23", "sin", "table")
        for h in (0, 1):
            cols_h = head_cols(h)
            parts_q, parts_k, parts_v = [], [], []
            for b in (0, 1):
                rows, ext = slice(256 * b, 256 * b + 256), slice(256 * b, 256 * b + 384)
                grad = dot_nt(rgrad[h, rows], values[h, ext])
                decay = decay_block(h, 256, 384, 256 * b, 256 * b - HALO, start, docs, windows[0, h])
                grad = (grad * decay).astype(BF)
                parts_q.append(dot_nn(grad, keys[ext, cols_h]))
                parts_k.append(dot_tn(grad, queries[rows, cols_h]))
                parts_v.append(dot_tn(w01[h, b], rgrad[h, rows]))

            def joined(parts):
                return jnp.concatenate(
                    [parts[0][HALO : 2 * HALO], parts[0][2 * HALO :] + parts[1][:HALO], parts[1][HALO:]], axis=0
                )

            finish_query(h, jnp.concatenate(parts_q, axis=0))
            key = joined(parts_k)
            finish_key(h, key[:LAST], slice(0, LAST))
            ch[TOK : TOK + HALO, cols_h] = key[LAST:].astype(BF)
            grad_v[h] = joined(parts_v).astype(BF)
            tick()

    def block_far():
        @pl.when(z < 3)
        def _():
            g_halo.wait_recv()

        tail = slice(TOK, TOK + HALO)
        for h in (0, 1):
            cols_h = head_cols(h)
            decay = decay_block(h, HALO, HALO, TOK, LAST, start, docs, windows[0, h])
            far_w = (dot_nt(qnext[:, cols_h], keys[tail, cols_h]) * decay).astype(BF)
            far_s = (dot_nt(gnext[h], values[h, tail]) * decay).astype(BF)
            key = ch[TOK : TOK + HALO, cols_h].astype(F32) + dot_tn(far_s, qnext[:, cols_h])
            finish_key(h, key, slice(LAST, TOK))
            grad_v[h, LAST:] = (grad_v[h, LAST:].astype(F32) + dot_tn(far_w, gnext[h])).astype(BF)
        share_keys()
        tick()

    def block_cross():
        passing.finish()
        from_last = docs.of(3 * TOK - 1) == doc_last
        for h in (2, 3):
            cols_h = head_cols(h)
            power = jnp.where(z == 0, math.exp(2 * TOK * LOG_GAMMA[h]), math.exp(TOK * LOG_GAMMA[h]))
            total = back_near[h - 2].astype(F32) + back_far[h - 2].astype(F32) * jnp.where(from_last, power, 0.0)
            state_in[h - 2] = total.astype(BF)
            factor = jnp.where(doc_rows == doc_last, jnp.exp((TOK - place).astype(F32) * LOG_GAMMA[h]), 0.0)
            grad = ch[0:TOK, head_cols(h - 2)].astype(F32)
            finish_key(h, grad + factor * dot_nn(values[h, HALO:], state_in[h - 2]))
            grad_v[h] = (grad_v[h].astype(F32) + factor * dot_nt(keys[HALO:, cols_h], state_in[h - 2])).astype(BF)
        share_keys()
        tick()

    retained = []

    def share_keys():
        retained.append(0)
        if len(retained) == 2:
            pair["query"] = halves(queries, 512, x2, 0)
            pair["key"] = halves(cot, 512, x2, 512)

    def block_store():
        def store_value(rows):
            joint = jnp.concatenate([grad_v[h, rows].astype(F32) for h in range(HEADS)], axis=1).astype(BF)
            wide[rows] = jnp.concatenate([joint, jnp.zeros((joint.shape[0], WIDE - VD), BF)], axis=1)

        row_loop(TOK, 64, store_value)
        pl.semaphore_wait(pair_credit.at[2], 1)
        pair["value"] = halves(wide, HALF, x1, 0)
        load("tokens", tokens_hbm, keys.at[pl.ds(0, TOK)])
        tick()

    def block_qk():
        up.reduced()
        arrived(pair["query"])
        arrived(pair["key"])
        stage_square(stage1, dot_tn(x3[...], x2[:, 0:512]), 0)
        stage_square(stage1, dot_tn(x3[...], x2[:, 512:1024]), 64)
        qk.start()
        load("wq", wq_hbm, x2)
        tick()

    def block_value():
        down.reduced()
        arrived(pair["value"])
        for half in (0, 1):
            stage_columns(stage0, dot_tn(x1[:, 0:HALF], x3[:, 512 * half : 512 * half + 512]), 2 * half)
        value.start()
        load("wk", wk_hbm, x3)
        tick()

    def block_fv():
        ready("wv")
        two_halves(lambda cols: wf[:, cols] + dot_nn(wide[:, 0:VD], wo[:, cols]))

    def block_fq():
        ready("wq")
        two_halves(lambda cols: wf[:, cols] + dot_nt(queries[...], x2[cols]))

    def block_fk():
        ready("wk")
        two_halves(lambda cols: wf[:, cols] + dot_nt(cot[...], x3[cols]))

    def block_n1():
        ready("tokens")

        def back_one(i, sums):
            rows = pl.ds(pl.multiple_of(i * 64, 64), 64)
            grad = wf[rows]
            inverse = stats[rows, 1:2]
            scaled = (keys[rows].astype(F32) - stats[rows, 0:1]) * inverse
            e = grad * gain1[...]
            inner = e - jnp.mean(e, axis=-1, keepdims=True) - scaled * jnp.mean(e * scaled, axis=-1, keepdims=True)
            keys[rows] = (hidden[rows] + inverse * inner).astype(BF)
            return (sums[0] + fold(grad * scaled), sums[1] + fold(grad))

        gain_sum, bias_sum = lax.fori_loop(0, TOK // 64, back_one, (zero, zero))
        pair["tokens"] = pltpu.make_async_copy(keys.at[pl.ds(0, TOK)], out_tokens, save_sems.at[len(local_copies)])
        pair["tokens"].start()
        vec_rows[0:1] = jnp.sum(gain_sum, axis=0, keepdims=True)
        vec_rows[1:2] = jnp.sum(bias_sum, axis=0, keepdims=True)
        for block in range(4):
            for j in range(4):
                for t in range(2):
                    first = 256 * block + 128 * t
                    vec[block, 2 * j + t : 2 * j + t + 1] = vec_rows[j : j + 1, first : first + 128]
        next(vectors)
        tick()

    vectors = vector_steps(at, vec, vec_core, vec_z, vec_y, vec_x, vec_out, (vec_send, vec_recv), 0)
    known = {
        "down": block_down, "up": block_up, "second": block_second, "norm2": block_norm2, "mixl": block_mixl, "states": block_states,
        "mixe": block_mixe, "out": block_out, "gate": block_gate, "fg": block_fg, "full": block_full, "band": block_band, "far": block_far,
        "cross": block_cross, "store": block_store, "qk": block_qk, "value": block_value, "fv": block_fv, "fq": block_fq,
        "fk": block_fk, "n1": block_n1,
    }
    for number, name in enumerate(BLOCKS):
        known[name]()
        if number == 0:
            load("cot", cot_hbm, cot)
            load("hidden", hidden_hbm, hidden)
            load("stats", stats_hbm, stats)
            load("wo", wo_hbm, wo)
            load("u", u_hbm, u_ref)
            load("w", w_hbm, w_ref)
            load("heads", heads_hbm, heads)
            load("q", q_hbm, queries)
            load("qnext", qnext_hbm, qnext)
        if number == 1:
            load("first", first_hbm, x3)
            load("k", k_hbm, keys)
            load("v", v_hbm, values)
            load("sin", sin_hbm, state_in)
            load("w23", w23_hbm, w23)
            load("w01", w01_hbm, w01)
            load("table", table_hbm.at[pl.ds(pl.multiple_of(z * TOK + HALO, HALO), TOK)], table)

    for count, n in enumerate(TAIL):
        numbered[n // 3].pump(n % 3)
        if count % 12 == 11:
            next(vectors, 0)
    for unit in numbered:
        unit.finish()
    for _ in vectors:
        pass
    last = pltpu.make_async_copy(vec_out, out_vec, save_sems.at[len(local_copies) + 1])
    last.start()

    @pl.when(z > 0)
    def _():
        g_halo.wait_send()

    passing.drain()
    pair["tokens"].wait()
    last.wait()


def backward(arrays, gain1, gain2, lengths, windows):
    vmem = pl.BlockSpec(memory_space=pltpu.VMEM)
    smem = pl.BlockSpec(memory_space=pltpu.SMEM)
    anywhere = pl.BlockSpec(memory_space=pl.ANY)
    shape = jax.ShapeDtypeStruct
    outs = [shape((TOK, D), BF), shape((8, 128), F32)] + [shape((2, 4, 4, UNIT_ROWS[n], 128), BF) for n in UNITS]
    scratch = [
        pltpu.VMEM((2 * TOK, VD), BF), pltpu.VMEM((2 * TOK, D), BF), pltpu.VMEM((2 * TOK, D), BF), pltpu.VMEM((2 * TOK, HALF), BF),
        pltpu.VMEM((2 * TOK, 512), BF), pltpu.VMEM((TOK, WIDE), BF), pltpu.VMEM((TOK, D), BF), pltpu.VMEM((HEADS, TOK, VH), BF),
        pltpu.VMEM((HEADS, TOK, VH), BF), pltpu.VMEM((HEADS, TOK, VH), BF), pltpu.VMEM((TOK, QK), BF), pltpu.VMEM((HALO + TOK, QK), BF),
        pltpu.VMEM((HEADS, HALO + TOK, VH), BF), pltpu.VMEM((2, 2, 256, 384), BF), pltpu.VMEM((2, TOK, TOK), BF),
        pltpu.VMEM((2, VH, KEYH), BF), pltpu.VMEM((2, VH, KEYH), BF),
        pltpu.VMEM((2, VH, KEYH), BF), pltpu.VMEM((2, VH, KEYH), BF),
        pltpu.VMEM((HEADS, TOK, VH), BF), pltpu.VMEM((TOK, D), F32),
        pltpu.VMEM((TOK, D), F32), pltpu.VMEM((VD, D), BF), pltpu.VMEM((VD, D), BF), pltpu.VMEM((TOK, 512), F32),
        pltpu.VMEM((TOK, 128), F32), pltpu.VMEM((HALO, 2 * KEYH), BF), pltpu.VMEM((2, HALO, VH), BF), pltpu.VMEM((8, D), F32),
        pltpu.VMEM((4, 8, 128), F32), pltpu.VMEM((4, 8, 128), F32), pltpu.VMEM((4, 8, 128), F32), pltpu.VMEM((4, 8, 128), F32),
        pltpu.VMEM((4, 8, 128), F32), pltpu.VMEM((8, 128), F32),
    ]
    scratch += [pltpu.VMEM((4, 4, 4, r, 128), BF) for r in SET_ROWS]
    for n, r in enumerate(SET_ROWS):
        for count, paired in zip(PART_ROWS[r], PART_ROWS[PAIRED]):
            shapes = landing_shapes(count)
            if n == UNIT_SET[LENDER["qk"]]:
                shapes[2] = landing_shapes(paired)[2]
            scratch += [pltpu.VMEM(s, BF) for s in shapes]
    for name in UNITS:
        scratch += [pltpu.VMEM((count, 128), BF) for count in PART_ROWS[UNIT_ROWS[name]]]
    dma, regular = pltpu.SemaphoreType.DMA, pltpu.SemaphoreType.REGULAR
    scratch += [dma((28,)), dma((8,)), dma((6,)), dma((6,)), dma((4,)), dma((4,)), dma((10,)), dma((10,))]
    scratch += [dma((18,)), dma((18 * ARRIVALS,)), dma((18,)), regular((6,)), regular((3,)), dma((8,)), dma((8,)), regular((6,))]
    return pl.pallas_call(
        backward_kernel,
        out_shape=outs,
        in_specs=[anywhere] * 28 + [vmem] * 2 + [smem] * 2,
        out_specs=[anywhere] * len(outs),
        scratch_shapes=scratch,
        compiler_params=pltpu.CompilerParams(collective_id=2, has_side_effects=True, vmem_limit_bytes=63 * 2**20),
        cost_estimate=pl.CostEstimate(flops=26 * 10**9, bytes_accessed=70 * 10**6, transcendentals=10**6),
        name="backward",
    )(*arrays, gain1.reshape(1, D), gain2.reshape(1, D), lengths, windows.reshape(1, HEADS))


def unpack_kernel(down, up, out, gate, value, qk, result, tokens, vectors, *outs):
    g_down, g_up, g_out, g_gate, g_value, g_query, g_key, out_result, out_tokens = outs[:9]
    for y in range(4):
        for x in range(4):
            cols = slice(128 * x, 128 * x + 128)
            for source, target in ((down, g_down), (out, g_out)):
                target[BIG * y : BIG * y + BIG, cols] = source[0, y, x].astype(F32)
            g_query[64 * y : 64 * y + 64, cols] = qk[0, y, x, 0:64].astype(F32)
            g_key[64 * y : 64 * y + 64, cols] = qk[0, y, x, 64:128].astype(F32)
            first, lane = 2 * BIG * y + BIG * (x // 2), 128 * (x % 2)
            for source, target in ((up, g_up), (gate, g_gate), (value, g_value)):
                target[first : first + BIG, lane : lane + 128] = source[0, y, x].astype(F32)
    out_result[...] = result[...]
    out_tokens[...] = tokens[...]
    for j, target in enumerate(outs[9:]):
        target[...] = vectors[2 * j : 2 * j + 2]


def unpack(gathered, result, grad_tokens, vectors):
    def source(rows):
        return pl.BlockSpec((1, 4, 4, rows, 128), lambda c: (c, 0, 0, 0, 0))

    tall = pl.BlockSpec((4 * BIG, 512), lambda c: (0, c))
    turned = pl.BlockSpec((WIDE // 2, 256), lambda c: (c, 0))
    square = pl.BlockSpec((256, 512), lambda c: (0, c))
    plain = pl.BlockSpec((TOK // 2, D), lambda c: (c, 0))
    shape = jax.ShapeDtypeStruct
    return pl.pallas_call(
        unpack_kernel,
        grid=(2,),
        out_shape=[
            shape((VH, D), F32), shape((FF, 256), F32), shape((VH, D), F32), shape((VD, 256), F32), shape((VD, 256), F32),
            shape((256, QK), F32), shape((256, QK), F32), shape((TOK, D), BF), shape((TOK, D), BF),
        ]
        + [shape((2, 128), F32)] * 4,
        in_specs=[source(UNIT_ROWS[n]) for n in UNITS] + [plain, plain, pl.BlockSpec((8, 128), lambda c: (0, 0))],
        out_specs=[tall, turned, tall, turned, turned, square, square, plain, plain] + [pl.BlockSpec((2, 128), lambda c: (0, 0))] * 4,
        compiler_params=pltpu.CompilerParams(vmem_limit_bytes=62 * 2**20),
        name="unpack",
    )(*gathered, result, grad_tokens, vectors)


def body(
    tokens, ln_gain1, ln_bias1, w_query, w_key, w_value, w_gate, w_out, ln_gain2, ln_bias2, w_up, w_down, doc_lengths, windows, cotangent
):
    table = jnp.asarray(rotary_constants())
    (
        result, first, second, mixed, act, cot_half, lift_half, lift, q, k, v, w01, w23, s_in, heads, u, w, hidden, stats, qnext,
    ) = forward(
        tokens[0], cotangent[0], ln_gain1, ln_bias1, ln_gain2, ln_bias2, doc_lengths, windows, table,
        w_query, w_key, w_value, w_gate, w_out, w_up, w_down,
    )

    def pair(a):
        return a.reshape(2 * TOK, a.shape[2])

    arrays = (
        act, pair(cot_half), pair(lift_half), pair(second), pair(first), pair(mixed), lift, cotangent[0], hidden, stats,
        u, w, heads, q, k, v, w01, w23, s_in, qnext, tokens[0], table,
        w_query, w_key, w_value.T, w_gate.T, w_out, w_up.T,
    )
    grad_tokens, vectors, *gathered = backward(arrays, ln_gain1, ln_gain2, doc_lengths, windows)
    g_down, g_up, g_out, g_gate, g_value, g_query, g_key, result, grad_tokens, *vectors = unpack(
        gathered, result, grad_tokens, vectors
    )
    gain1, bias1, gain2, bias2 = (vector.reshape(256) for vector in vectors)
    return (
        result.reshape(1, TOK, D), grad_tokens.reshape(1, TOK, D), gain1, bias1, g_query, g_key, g_value.T, g_gate.T, g_out,
        gain2, bias2, g_up.T, g_down,
    )


def solution(mesh):
    in_specs = (P("batch", "head", None),) + (P(),) * 11 + (P("batch", None), P(), P("batch", "head", None))
    rows, vector = P("head", None), P("head")
    out_specs = (
        P("batch", "head", None), P("batch", "head", None), vector, vector, rows, rows, rows, rows, rows, vector, vector, rows, rows,
    )
    return jax.shard_map(body, mesh=mesh, in_specs=in_specs, out_specs=out_specs, check_vma=False)
```
